32 devices in a mesh: rows: 16 (over z, x, core), frames: 2 (over y).
Axes of the slice: x: 2, y: 2, z: 4, core: 2. Of those that a mesh axis runs over, the one named last changes fastest.
Arguments:
- frames_raw: float32 [4, 256, 4096], P('frames', 'rows'), may hold values from 0.1 to 5.2, as said below
- wind_off: float32 [2, 256, 4096], P('frames', 'rows'), may hold values from 0.12 to 14.8, as said below
- run_owner: int32 [16], P('rows'), may hold values from 0 to 1
- search_base: int32 [2, 2], P('frames'), may hold values from -8 to 8, as said below
Outputs:
- pressure: float32 [4, 256, 4096], P('frames', 'rows')
- frame_mean: float32 [4], P('frames')
- frame_rms: float32 [4], P('frames')
- time_mean: float32 [256, 4096], P('rows')
- time_rms: float32 [256, 4096], P('rows')
The draws below stay inside these ranges and needn't reach their ends.
Inputs may be any that keep to these rules, and one draw needn't show every extreme that they name: `frames_raw`: positive intensities. `wind_off`: positive intensities. `search_base`: entry 0 of a block is a row offset from -1 to 1, entry 1 a column offset from -8 to 8; in every draw some block has row offset -1, some +1, some column offset -8 and some +8.
All inputs are finite; a program needn't handle non-finite values.
Results may differ from the reference program's by a relative error of at most 0.0003.
Values sent between devices are 32-bit elements; how exact they have to be, the bound alone decides.
No kernel may reach another device: no remote copies, remote signals or barrier semaphores. Data moves between devices by JAX's collectives and lax.ppermute only.
A program may use at most 128 MiB of HBM per device.

```python
import jax
import jax.numpy as jnp
from jax import lax

NX = 4096
ROWS_DEV = 16
F_DEV = 2
NY = 256
FRAMES = 4
N_ROWS = 16
N_FRAMES = 2


def shared_texture(key):
    key_normal = jax.random.fold_in(key, 0)
    coarse_rows = (NY + 1) // 2
    coarse_cols = (NX + 3) // 4
    normal_part = jnp.clip(jax.random.normal(key_normal, (coarse_rows, coarse_cols), jnp.float32), -3.0, 3.0)
    coarse = normal_part
    widened = jnp.repeat(jnp.repeat(coarse, 2, axis=0), 4, axis=1)
    return widened[:NY, :NX]


def draw_frames_raw(key, part):
    texture = shared_texture(key)
    key = jax.random.fold_in(key, 3)
    key_move, key_gain, key_noise = jax.random.split(key, 3)
    moves = jax.random.randint(key_move, (FRAMES, 2), -3, 4)
    gains = jax.random.uniform(key_gain, (FRAMES,), jnp.float32, 0.7, 1.3)
    noise = jnp.clip(jax.random.normal(key_noise, (FRAMES, NY, NX), jnp.float32), -3.0, 3.0)
    moved = jax.vmap(lambda shift_pair: jnp.roll(texture, (shift_pair[0], shift_pair[1]), axis=(0, 1)))(moves)
    return gains[:, None, None] * (1.5 + 0.4 * moved) * (1.0 + 0.15 * noise)


def draw_wind_off(key, part):
    texture = shared_texture(key)
    key = jax.random.fold_in(key, 5)
    key_level, key_run = jax.random.split(key)
    run_levels = jax.random.uniform(key_level, (N_FRAMES,), jnp.float32, 0.6, 1.4)
    run_noise = jnp.clip(jax.random.normal(key_run, (N_FRAMES, NY, NX), jnp.float32), -3.0, 3.0)
    lighting = 1.0 + 2.0 * jnp.arange(NY, dtype=jnp.float32) / (NY - 1)
    return run_levels[:, None, None] * lighting[None, :, None] * (1.5 + 0.4 * texture)[None] * (1.0 + 0.1 * run_noise)


def draw_search_base(key, part):
    key = jax.random.fold_in(key, 7)
    key_rows, key_order, key_cols, key_order_two = jax.random.split(key, 4)
    row_offsets = jax.random.randint(key_rows, (N_FRAMES,), -1, 2)
    order = jax.random.permutation(key_order, N_FRAMES)
    row_offsets = row_offsets.at[order[0]].set(-1).at[order[1]].set(1)
    col_offsets = jax.random.randint(key_cols, (N_FRAMES,), -8, 9)
    order_two = jax.random.permutation(key_order_two, N_FRAMES)
    col_offsets = col_offsets.at[order_two[0]].set(-8).at[order_two[1]].set(8)
    return jnp.stack([row_offsets, col_offsets], 1).astype(jnp.int32)


def set_ends(array, key, least, high):
    place = [jax.random.randint(jax.random.fold_in(key, axis), (), 0, length) for axis, length in enumerate(array.shape)]
    main_axis = array.shape.index(max(array.shape))
    next_to = place[:main_axis] + [(place[main_axis] + 1) % array.shape[main_axis]] + place[main_axis + 1:]
    return array.at[tuple(place)].set(least).at[tuple(next_to)].set(high)


def setup_inputs(seed: int = 0) -> dict:
    seeds = jax.random.split(jax.random.key(seed), 5)
    frames_raw = draw_frames_raw(jax.random.fold_in(seeds[4], 71), 0)
    wind_off = draw_wind_off(jax.random.fold_in(seeds[4], 71), 0)
    run_owner = set_ends(jax.random.randint(seeds[2], (N_ROWS,), 0, N_FRAMES), jax.random.fold_in(seeds[2], 1), 0, N_FRAMES - 1).astype(jnp.int32)
    search_base = draw_search_base(jax.random.fold_in(seeds[4], 71), 0)
    return {"frames_raw": frames_raw, "wind_off": wind_off, "run_owner": run_owner, "search_base": search_base}


smoothing_taps = (1.0 / 256, 8.0 / 256, 28.0 / 256, 56.0 / 256, 70.0 / 256, 56.0 / 256, 28.0 / 256, 8.0 / 256, 1.0 / 256)
calib_zero = -0.25
calib_linear = 1.0
calib_square = 0.15

def smooth_columns(image_in):
    columns = image_in.shape[-1]
    padded = jnp.pad(image_in, [(0, 0)] * (image_in.ndim - 1) + [(4, 4)])
    running = smoothing_taps[0] * padded[..., 0:columns]
    for tap_index in range(1, 9):
        running = running + smoothing_taps[tap_index] * padded[..., tap_index:tap_index + columns]
    return running

def smooth_rows(image_in, row_count):
    running = smoothing_taps[0] * image_in[..., 0:row_count, :]
    for tap_index in range(1, 9):
        running = running + smoothing_taps[tap_index] * image_in[..., tap_index:tap_index + row_count, :]
    return running

def denoise(image_in):
    padded = jnp.pad(image_in, [(0, 0)] * (image_in.ndim - 2) + [(4, 4), (0, 0)])
    return smooth_rows(smooth_columns(padded), image_in.shape[-2])

def window_stack(padded, first_row, offset_cols, row_count, columns):
    slab = lax.dynamic_slice_in_dim(padded, first_row, row_count, 0)
    return jnp.stack([lax.dynamic_slice_in_dim(slab, 11 + offset_cols + col_step, columns, 1) for col_step in range(-3, 4)])

def blend_weights(matches, frame_power, ref_power):
    norm_product = jnp.sqrt((frame_power + 1e-06) * (ref_power + 1e-06))
    rho = matches / norm_product[:, None, None]
    squared = rho * rho
    weights = squared / (0.05 + lax.optimization_barrier(jnp.sum(squared, axis=(1, 2), keepdims=True)))
    remainder = 1.0 - lax.optimization_barrier(jnp.sum(weights, axis=(1, 2)))
    return weights.at[:, 3, 3].add(remainder)

def calibrate(ratio_in):
    return calib_zero + ratio_in * (calib_linear + calib_square * ratio_in)

def reference(frames_raw, wind_off, run_owner, search_base):
    owner_rows = jnp.repeat(run_owner.astype(jnp.int32), ROWS_DEV)
    reference_raw = jnp.take_along_axis(wind_off, owner_rows[None, :, None], axis=0)[0]
    ref_clean = denoise(reference_raw)
    ref_detail = reference_raw - ref_clean
    ref_power = jnp.sum(ref_detail * ref_detail)
    clean_pad = jnp.pad(ref_clean, ((4, 4), (11, 11)))
    detail_pad = jnp.pad(ref_detail, ((4, 4), (11, 11)))
    highest = lax.Precision.HIGHEST
    blocks = frames_raw.reshape(N_FRAMES, F_DEV, NY, NX)

    def one_block(block_item):
        frame_block, offsets = block_item
        offset_rows = offsets[0]
        offset_cols = offsets[1]
        smoothed = denoise(frame_block)
        detail = frame_block - smoothed
        matches = []
        for row_step in range(-3, 4):
            shifted = window_stack(detail_pad, 4 + offset_rows + row_step, offset_cols, NY, NX)
            matches.append(jnp.einsum('fyx,cyx->fc', detail, shifted, precision=highest))
        matches = jnp.stack(matches, 1)
        weights = blend_weights(matches, lax.optimization_barrier(jnp.sum(detail * detail, axis=(1, 2))), ref_power)
        registered = jnp.zeros((F_DEV, NY, NX), jnp.float32)
        for row_step in range(-3, 4):
            shifted = window_stack(clean_pad, 4 + offset_rows + row_step, offset_cols, NY, NX)
            registered = registered + jnp.einsum('fc,cyx->fyx', weights[:, row_step + 3, :], shifted, precision=highest)
        return calibrate(registered / smoothed)
    pressure = lax.map(one_block, (blocks, search_base)).reshape(FRAMES, NY, NX)
    frame_mean = lax.optimization_barrier(jnp.mean(pressure, axis=(1, 2)))
    frame_rms = jnp.sqrt(lax.optimization_barrier(jnp.mean(pressure * pressure, axis=(1, 2))) - frame_mean * frame_mean)
    time_mean = lax.optimization_barrier(jnp.mean(pressure, axis=0))
    time_rms = jnp.sqrt(jnp.maximum(lax.optimization_barrier(jnp.mean(pressure * pressure, axis=0)) - time_mean * time_mean, 0.0))
    return (pressure, frame_mean, frame_rms, time_mean, time_rms)
```

```python
import functools

import jax
import jax.numpy as jnp
from jax import lax
from jax.experimental import pallas as pl
from jax.experimental.pallas import tpu as pltpu
from jax.sharding import PartitionSpec as P

taps = (1.0 / 256, 8.0 / 256, 28.0 / 256, 56.0 / 256, 70.0 / 256)
calib_zero = -0.25
calib_linear = 1.0
calib_square = 0.15
lanes = 128
reach = 7
params = pltpu.CompilerParams(vmem_limit_bytes=24 * 1024 * 1024)
vmem = pl.BlockSpec(memory_space=pltpu.VMEM)
smem = pl.BlockSpec(memory_space=pltpu.SMEM)


def tile_of(index):
    return pl.ds(pl.multiple_of(index * lanes, lanes), lanes)


def vertical(load):
    total = taps[4] * load(4)
    for step in range(4):
        total = total + taps[step] * (load(step) + load(8 - step))
    return total


def horizontal(before, here, after):
    lane = lax.broadcasted_iota(jnp.int32, here.shape, here.ndim - 1)
    total = taps[4] * here
    for step in range(1, 5):
        right = pltpu.roll(jnp.where(lane < step, after, here), lanes - step, here.ndim - 1)
        left = pltpu.roll(jnp.where(lane >= lanes - step, before, here), step, here.ndim - 1)
        total = total + taps[4 - step] * (right + left)
    return total


def smooth_kernel(frames, top, bottom, smoothed, rows_in, half):
    count, rows, columns = frames.shape
    tiles = columns // lanes
    zero = jnp.zeros((rows, lanes), jnp.float32)
    for f in range(count):
        half[f, 0] = zero
        half[f, tiles + 1] = zero

    def load_step(t, carry):
        for f in range(count):
            rows_in[f, t, 4:8, :] = top[f, :, tile_of(t)]
            rows_in[f, t, 8 : 8 + rows, :] = frames[f, :, tile_of(t)]
            rows_in[f, t, 8 + rows : 12 + rows, :] = bottom[f, :, tile_of(t)]
        return carry

    def vertical_step(t, carry):
        for f in range(count):
            half[f, t + 1] = vertical(lambda s: rows_in[f, t, pl.ds(4 + s, rows), :])
        return carry

    def horizontal_step(t, carry):
        for f in range(count):
            smoothed[f, :, tile_of(t)] = horizontal(half[f, t], half[f, t + 1], half[f, t + 2])
        return carry

    by_tiles(load_step, tiles, 4)
    by_tiles(vertical_step, tiles, 4)
    by_tiles(horizontal_step, tiles, 4)


def by_tiles(step, tiles, group, init=()):
    def body(index, carry):
        for inner in range(group):
            carry = step(index * group + inner, carry)
        return carry

    return lax.fori_loop(0, tiles // group, body, init)


def shift_columns(source, shifted, base_col, tiles):
    def per_offset(j, carry):
        shift = base_col + j - 3
        negative = shift < 0
        first = jnp.where(negative, 0, 1)
        amount = jnp.where(negative, shift + lanes, shift)
        back = lax.rem(lanes - amount, lanes)

        def step(t, inner):
            here = source[t + first]
            after = source[t + first + 1]
            lane = lax.broadcasted_iota(jnp.int32, here.shape, 1)
            shifted[j, t] = pltpu.roll(jnp.where(lane < amount, after, here), back, 1)
            return inner

        by_tiles(step, tiles, 4)
        return carry

    lax.fori_loop(0, reach, per_offset, 0)


def match_kernel(
    base, owner, wind, other, top, bottom, frames, smoothed, clean, part, rows_in, half, fine, shifted, detail, sums
):
    count, rows, columns = frames.shape
    tiles = columns // lanes
    wide = rows + 8
    row_index = lax.axis_index("rows")
    last_row = lax.axis_size("rows") - 1
    mine = owner[0] == lax.axis_index("frames")
    blank = jnp.zeros((wide, lanes), jnp.float32)
    half[0] = blank
    half[tiles + 1] = blank
    for array in (clean, fine):
        array[0] = blank
        array[tiles + 1] = blank
    place = lax.broadcasted_iota(jnp.int32, (wide, lanes), 0)
    inside = ((place >= 4) | (row_index > 0)) & ((place < rows + 4) | (row_index < last_row))

    def load_step(t, carry):
        rows_in[t, 0:8, :] = top[:, tile_of(t)]
        rows_in[t, 8 : 8 + rows, :] = jnp.where(mine, wind[0, :, tile_of(t)], other[:, tile_of(t)])
        rows_in[t, 8 + rows : 16 + rows, :] = bottom[:, tile_of(t)]
        for f in range(count):
            detail[t, f] = frames[f, :, tile_of(t)] - smoothed[f, :, tile_of(t)]
        return carry

    def vertical_step(t, carry):
        half[t + 1] = vertical(lambda s: rows_in[t, pl.ds(s, wide), :])
        return carry

    def horizontal_step(t, carry):
        smooth = jnp.where(inside, horizontal(half[t], half[t + 1], half[t + 2]), 0.0)
        clean[t + 1] = smooth
        fine[t + 1] = rows_in[t, pl.ds(4, wide), :] - smooth
        return carry

    by_tiles(load_step, tiles, 4)
    by_tiles(vertical_step, tiles, 4)
    by_tiles(horizontal_step, tiles, 4)
    shift_columns(fine, shifted, base[0, 1], tiles)
    first_row = 1 + base[0, 0]
    zero = jnp.zeros((8, lanes), jnp.float32)

    def fold(product):
        return jnp.sum(product.reshape(rows // 8, 8, lanes), axis=0)

    def per_offset(j, carry):
        def step(t, totals):
            parts = [detail[t, f] for f in range(count)]
            result = []
            for i in range(reach):
                window = shifted[j, t, pl.ds(first_row + i, rows), :]
                for f in range(count):
                    result.append(totals[i * count + f] + fold(parts[f] * window))
            return tuple(result)

        totals = by_tiles(step, tiles, 2, (zero,) * (reach * count))
        for i in range(reach * count):
            sums[j * reach * count + i] = totals[i]
        return carry

    sums[...] = jnp.zeros(sums.shape, jnp.float32)
    lax.fori_loop(0, reach, per_offset, 0)

    def power_step(t, totals):
        own = fine[t + 1, pl.ds(4, rows), :]
        values = [detail[t, f] for f in range(count)] + [own]
        return tuple(total + fold(value * value) for total, value in zip(totals, values))

    powers = by_tiles(power_step, tiles, 4, (zero,) * (count + 1))
    for f in range(count + 1):
        sums[reach * reach * count + f] = powers[f]
    part[...] = lanes_from(jnp.sum(sums[...], axis=1), part.shape[0])


def lanes_from(columns_in, copies):
    ones = jnp.ones((copies, lanes), jnp.float32)
    return lax.dot_general(
        ones,
        columns_in,
        (((1,), (1,)), ((), ())),
        precision=lax.Precision.HIGHEST,
        preferred_element_type=jnp.float32,
    )


def blend_weights(totals, count):
    entry = lax.broadcasted_iota(jnp.int32, totals.shape, 1)
    used = reach * reach * count

    def pick(index):
        return jnp.sum(jnp.where(entry == index, totals, 0.0), axis=1, keepdims=True)

    ref_power = pick(used + count)
    weights = jnp.zeros_like(totals)
    middle = (reach * reach // 2) * count
    for f in range(count):
        member = (entry < used) & (lax.rem(entry, count) == f)
        norm_product = jnp.sqrt((pick(used + f) + 1e-06) * (ref_power + 1e-06))
        rho = jnp.where(member, totals, 0.0) / norm_product
        squared = rho * rho
        shares = squared / (0.05 + jnp.sum(squared, axis=1, keepdims=True))
        remainder = 1.0 - jnp.sum(shares, axis=1, keepdims=True)
        weights = weights + shares + jnp.where(entry == middle + f, remainder, 0.0)
    return weights


def pressure_kernel(base, parts, clean, smoothed, pressure, moments, part, shifted, splat, sums):
    count, rows, columns = smoothed.shape
    tiles = columns // lanes
    weights = blend_weights(jnp.sum(parts[...], axis=0, keepdims=True), count)
    square = (lanes, lanes)
    diagonal = lax.broadcasted_iota(jnp.int32, square, 0) == lax.broadcasted_iota(jnp.int32, square, 1)
    spread = jnp.where(diagonal, jnp.broadcast_to(weights, square), 0.0)
    spread = jnp.broadcast_to(jnp.sum(spread, axis=1, keepdims=True), square)
    for k in range(reach * reach * count):
        splat[k] = jnp.broadcast_to(spread[k : k + 1, :], (8, lanes))
    shift_columns(clean, shifted, base[0, 1], tiles)
    first_row = 1 + base[0, 0]
    zero = jnp.zeros((8, lanes), jnp.float32)
    groups = rows // 8
    pair = 2

    def step(t, totals):
        values = [[[zero] * groups for f in range(count)] for p in range(pair)]
        for j in range(reach):
            for i in range(reach):
                factor = [splat[(j * reach + i) * count + f] for f in range(count)]
                for p in range(pair):
                    for g in range(groups):
                        window = shifted[j, t * pair + p, pl.ds(first_row + i + 8 * g, 8), :]
                        for f in range(count):
                            values[p][f][g] = values[p][f][g] + factor[f] * window
        totals = list(totals)
        for p in range(pair):
            where = tile_of(t * pair + p)
            for g in range(groups):
                band = slice(8 * g, 8 * g + 8)
                first = zero
                second = zero
                for f in range(count):
                    ratio = values[p][f][g] / smoothed[f, band, where]
                    value = calib_zero + ratio * (calib_linear + calib_square * ratio)
                    squared = value * value
                    pressure[f, band, where] = value
                    first = first + value
                    second = second + squared
                    totals[f] = totals[f] + value
                    totals[count + f] = totals[count + f] + squared
                moments[0, band, where] = first
                moments[1, band, where] = second
        return tuple(totals)

    totals = lax.fori_loop(0, tiles // pair, step, (zero,) * (2 * count))
    sums[...] = jnp.zeros(sums.shape, jnp.float32)
    for k in range(2 * count):
        sums[k] = totals[k]
    part[...] = lanes_from(jnp.sum(sums[...], axis=1), part.shape[0])


def neighbours(value, axis, step):
    size = lax.axis_size(axis)
    pairs = [(i, i + step) for i in range(size) if 0 <= i + step < size]
    return lax.ppermute(value, axis, pairs)


def from_owner(shard, axis, root):
    mine = lax.axis_index(axis) == root
    if lax.axis_size(axis) == 2:
        return lax.ppermute(shard, axis, [(0, 1), (1, 0)])
    return lax.psum(jnp.where(mine, shard, jnp.zeros_like(shard)), axis)


def total_over(value, axis):
    size = lax.axis_size(axis)
    if size & (size - 1):
        return lax.psum(value, axis)
    step = 1
    while step < size:
        value = value + lax.ppermute(value, axis, [(i, i ^ step) for i in range(size)])
        step *= 2
    return value


def shards(frames_raw, wind_off, run_owner, search_base):
    count, rows, columns = frames_raw.shape
    tiles = columns // lanes
    wide = rows + 8
    size = lax.axis_size("rows")
    f32 = jnp.float32
    struct = functools.partial(jax.ShapeDtypeStruct, dtype=f32)
    other = from_owner(wind_off[0], "frames", run_owner[0])
    frames_top = neighbours(frames_raw[:, rows - 4 :], "rows", 1)
    frames_bottom = neighbours(frames_raw[:, :4], "rows", -1)
    mine = run_owner[0] == lax.axis_index("frames")
    ref_top = neighbours(jnp.where(mine, wind_off[0, rows - 8 :], other[rows - 8 :]), "rows", 1)
    ref_bottom = neighbours(jnp.where(mine, wind_off[0, :8], other[:8]), "rows", -1)
    smoothed = pl.pallas_call(
        smooth_kernel,
        out_shape=struct((count, rows, columns)),
        in_specs=[vmem] * 3,
        out_specs=vmem,
        scratch_shapes=[
            pltpu.VMEM((count, tiles, rows + 16, lanes), f32),
            pltpu.VMEM((count, tiles + 2, rows, lanes), f32),
        ],
        compiler_params=params,
        name="smooth",
    )(frames_raw, frames_top, frames_bottom)
    clean, part = pl.pallas_call(
        match_kernel,
        out_shape=(struct((tiles + 2, wide, lanes)), struct((size, lanes))),
        in_specs=[smem, smem] + [vmem] * 6,
        out_specs=(vmem, vmem),
        scratch_shapes=[
            pltpu.VMEM((tiles, rows + 16, lanes), f32),
            pltpu.VMEM((tiles + 2, wide, lanes), f32),
            pltpu.VMEM((tiles + 2, wide, lanes), f32),
            pltpu.VMEM((reach, tiles, wide, lanes), f32),
            pltpu.VMEM((tiles, count, rows, lanes), f32),
            pltpu.VMEM((lanes, 8, lanes), f32),
        ],
        compiler_params=params,
        name="match",
    )(search_base, run_owner, wind_off, other, ref_top, ref_bottom, frames_raw, smoothed)
    parts = lax.all_to_all(part, "rows", 0, 0, tiled=True)
    pressure, moments, part = pl.pallas_call(
        pressure_kernel,
        out_shape=(struct((count, rows, columns)), struct((2, rows, columns)), struct((8, lanes))),
        in_specs=[smem] + [vmem] * 3,
        out_specs=(vmem, vmem, vmem),
        scratch_shapes=[
            pltpu.VMEM((reach, tiles, wide, lanes), f32),
            pltpu.VMEM((reach * reach * count, 8, lanes), f32),
            pltpu.VMEM((lanes, 8, lanes), f32),
        ],
        compiler_params=params,
        name="pressure",
    )(search_base, parts, clean, smoothed)
    whole = total_over(moments, "frames")
    spatial = total_over(part[0], "rows")
    cell_count = rows * columns * size
    frame_mean = spatial[:count] / cell_count
    frame_rms = jnp.sqrt(spatial[count : 2 * count] / cell_count - frame_mean * frame_mean)
    total_frames = count * lax.axis_size("frames")
    time_mean = whole[0] / total_frames
    time_rms = jnp.sqrt(jnp.maximum(whole[1] / total_frames - time_mean * time_mean, 0.0))
    return (pressure, frame_mean, frame_rms, time_mean, time_rms)


def solution(mesh):
    placed = (P("frames", "rows", None), P("frames", "rows", None), P("rows"), P("frames", None))
    return jax.shard_map(
        shards,
        mesh=mesh,
        in_specs=placed,
        out_specs=(
            P("frames", "rows", None),
            P("frames"),
            P("frames"),
            P("rows", None),
            P("rows", None),
        ),
        check_vma=False,
    )
```

```python
import functools

import jax
import jax.numpy as jnp
from jax import lax
from jax.experimental import pallas as pl
from jax.experimental.pallas import tpu as pltpu
from jax.sharding import PartitionSpec as P

taps = (1.0 / 256, 8.0 / 256, 28.0 / 256, 56.0 / 256, 70.0 / 256)
calib_zero = -0.25
calib_linear = 1.0
calib_square = 0.15
lanes = 128
reach = 7
params = pltpu.CompilerParams(vmem_limit_bytes=24 * 1024 * 1024)
vmem = pl.BlockSpec(memory_space=pltpu.VMEM)
smem = pl.BlockSpec(memory_space=pltpu.SMEM)


def tile_of(index):
    return pl.ds(pl.multiple_of(index * lanes, lanes), lanes)


def vertical(load):
    total = taps[4] * load(4)
    for step in range(4):
        total = total + taps[step] * (load(step) + load(8 - step))
    return total


def horizontal(before, here, after):
    lane = lax.broadcasted_iota(jnp.int32, here.shape, here.ndim - 1)
    total = taps[4] * here
    for step in range(1, 5):
        right = pltpu.roll(jnp.where(lane < step, after, here), lanes - step, here.ndim - 1)
        left = pltpu.roll(jnp.where(lane >= lanes - step, before, here), step, here.ndim - 1)
        total = total + taps[4 - step] * (right + left)
    return total


def smooth_kernel(frames, from_odd, from_even, smoothed, rows_in, half):
    count, rows, columns = frames.shape
    tiles = columns // lanes
    odd = lax.axis_index("rows") % 2 == 1
    zero = jnp.zeros((rows, lanes), jnp.float32)
    for f in range(count):
        half[f, 0] = zero
        half[f, tiles + 1] = zero

    def load_step(t, carry):
        for f in range(count):
            outer = from_odd[f, :, tile_of(t)]
            inner = from_even[f, :, tile_of(t)]
            rows_in[f, t, 4:8, :] = jnp.where(odd, inner, outer)
            rows_in[f, t, 8 : 8 + rows, :] = frames[f, :, tile_of(t)]
            rows_in[f, t, 8 + rows : 12 + rows, :] = jnp.where(odd, outer, inner)
        return carry

    def vertical_step(t, carry):
        for f in range(count):
            half[f, t + 1] = vertical(lambda s: rows_in[f, t, pl.ds(4 + s, rows), :])
        return carry

    def horizontal_step(t, carry):
        for f in range(count):
            smoothed[f, :, tile_of(t)] = horizontal(half[f, t], half[f, t + 1], half[f, t + 2])
        return carry

    by_tiles(load_step, tiles, 8)
    by_tiles(vertical_step, tiles, 8)
    by_tiles(horizontal_step, tiles, 8)


def by_tiles(step, tiles, group, init=()):
    def body(index, carry):
        for inner in range(group):
            carry = step(index * group + inner, carry)
        return carry

    return lax.fori_loop(0, tiles // group, body, init)


def shift_columns(source, shifted, base_col, tiles):
    def per_offset(j, carry):
        shift = base_col + j - 3
        negative = shift < 0
        first = jnp.where(negative, 0, 1)
        amount = jnp.where(negative, shift + lanes, shift)
        back = lax.rem(lanes - amount, lanes)

        def step(t, inner):
            here = source[t + first]
            after = source[t + first + 1]
            lane = lax.broadcasted_iota(jnp.int32, here.shape, 1)
            shifted[j, t] = pltpu.roll(jnp.where(lane < amount, after, here), back, 1)
            return inner

        by_tiles(step, tiles, 32)
        return carry

    lax.fori_loop(0, reach, per_offset, 0)


def match_kernel(
    base, own_odd, own_even, from_odd, from_even, frames, smoothed, clean, part, rows_in, half, fine, shifted, detail, sums
):
    count, rows, columns = frames.shape
    tiles = columns // lanes
    wide = rows + 8
    row_index = lax.axis_index("rows")
    last_row = lax.axis_size("rows") - 1
    odd = row_index % 2 == 1
    blank = jnp.zeros((wide, lanes), jnp.float32)
    half[0] = blank
    half[tiles + 1] = blank
    for array in (clean, fine):
        array[0] = blank
        array[tiles + 1] = blank
    place = lax.broadcasted_iota(jnp.int32, (wide, lanes), 0)
    inside = ((place >= 4) | (row_index > 0)) & ((place < rows + 4) | (row_index < last_row))

    def load_step(t, carry):
        outer = [array[:, tile_of(t)] for array in (from_odd, own_odd)]
        inner = [array[:, tile_of(t)] for array in (own_even, from_even)]
        rows_in[t, 0:8, :] = jnp.where(odd, inner[1], outer[0])
        rows_in[t, 8:16, :] = jnp.where(odd, inner[0], outer[1])
        rows_in[t, 16:24, :] = jnp.where(odd, outer[1], inner[0])
        rows_in[t, 24:32, :] = jnp.where(odd, outer[0], inner[1])
        for f in range(count):
            detail[t, f] = frames[f, :, tile_of(t)] - smoothed[f, :, tile_of(t)]
        return carry

    def vertical_step(t, carry):
        half[t + 1] = vertical(lambda s: rows_in[t, pl.ds(s, wide), :])
        return carry

    def horizontal_step(t, carry):
        smooth = jnp.where(inside, horizontal(half[t], half[t + 1], half[t + 2]), 0.0)
        clean[t + 1] = smooth
        fine[t + 1] = rows_in[t, pl.ds(4, wide), :] - smooth
        return carry

    by_tiles(load_step, tiles, 8)
    by_tiles(vertical_step, tiles, 8)
    by_tiles(horizontal_step, tiles, 8)
    shift_columns(fine, shifted, base[0, 1], tiles)
    first_row = 1 + base[0, 0]
    zero = jnp.zeros((8, lanes), jnp.float32)

    def fold(product):
        return jnp.sum(product.reshape(rows // 8, 8, lanes), axis=0)

    def per_offset(j, carry):
        def step(t, totals):
            parts = [detail[t, f] for f in range(count)]
            result = []
            for i in range(reach):
                window = shifted[j, t, pl.ds(first_row + i, rows), :]
                for f in range(count):
                    result.append(totals[i * count + f] + fold(parts[f] * window))
            return tuple(result)

        totals = by_tiles(step, tiles, 8, (zero,) * (reach * count))
        for i in range(reach * count):
            sums[j * reach * count + i] = totals[i]
        return carry

    sums[...] = jnp.zeros(sums.shape, jnp.float32)
    lax.fori_loop(0, reach, per_offset, 0)

    def power_step(t, totals):
        own = fine[t + 1, pl.ds(4, rows), :]
        values = [detail[t, f] for f in range(count)] + [own]
        return tuple(total + fold(value * value) for total, value in zip(totals, values))

    powers = by_tiles(power_step, tiles, 8, (zero,) * (count + 1))
    for f in range(count + 1):
        sums[reach * reach * count + f] = powers[f]
    part[...] = lanes_from(jnp.sum(sums[...], axis=1), part.shape[0])


def lanes_from(columns_in, copies):
    ones = jnp.ones((copies, lanes), jnp.float32)
    return lax.dot_general(
        ones,
        columns_in,
        (((1,), (1,)), ((), ())),
        precision=lax.Precision.HIGHEST,
        preferred_element_type=jnp.float32,
    )


def blend_weights(totals, count):
    entry = lax.broadcasted_iota(jnp.int32, totals.shape, 1)
    used = reach * reach * count

    def pick(index):
        return jnp.sum(jnp.where(entry == index, totals, 0.0), axis=1, keepdims=True)

    ref_power = pick(used + count)
    weights = jnp.zeros_like(totals)
    middle = (reach * reach // 2) * count
    for f in range(count):
        member = (entry < used) & (lax.rem(entry, count) == f)
        norm_product = jnp.sqrt((pick(used + f) + 1e-06) * (ref_power + 1e-06))
        rho = jnp.where(member, totals, 0.0) / norm_product
        squared = rho * rho
        scale = 1.0 / (0.05 + jnp.sum(squared, axis=1, keepdims=True))
        weights = weights + (squared + jnp.where(entry == middle + f, 0.05, 0.0)) * scale
    return weights


def pressure_kernel(base, parts, clean, smoothed, pressure, moments, part, shifted, splat, sums):
    count, rows, columns = smoothed.shape
    tiles = columns // lanes
    weights = blend_weights(parts[0:1, :], count)
    square = (lanes, lanes)
    diagonal = lax.broadcasted_iota(jnp.int32, square, 0) == lax.broadcasted_iota(jnp.int32, square, 1)
    spread = jnp.where(diagonal, jnp.broadcast_to(weights, square), 0.0)
    spread = jnp.broadcast_to(jnp.sum(spread, axis=1, keepdims=True), square)
    for k in range(reach * reach * count):
        splat[k] = jnp.broadcast_to(spread[k : k + 1, :], (8, lanes))
    shift_columns(clean, shifted, base[0, 1], tiles)
    first_row = 1 + base[0, 0]
    zero = jnp.zeros((8, lanes), jnp.float32)
    groups = rows // 8
    pair = 2

    def step(t, totals):
        values = [[[zero] * groups for f in range(count)] for p in range(pair)]
        for j in range(reach):
            for i in range(reach):
                factor = [splat[(j * reach + i) * count + f] for f in range(count)]
                for p in range(pair):
                    for g in range(groups):
                        window = shifted[j, t * pair + p, pl.ds(first_row + i + 8 * g, 8), :]
                        for f in range(count):
                            values[p][f][g] = values[p][f][g] + factor[f] * window
        totals = list(totals)
        for p in range(pair):
            where = tile_of(t * pair + p)
            for g in range(groups):
                band = slice(8 * g, 8 * g + 8)
                first = zero
                second = zero
                for f in range(count):
                    ratio = values[p][f][g] / smoothed[f, band, where]
                    value = calib_zero + ratio * (calib_linear + calib_square * ratio)
                    squared = value * value
                    pressure[f, band, where] = value
                    first = first + value
                    second = second + squared
                    totals[f] = totals[f] + value
                    totals[count + f] = totals[count + f] + squared
                moments[0, band, where] = first
                moments[1, band, where] = second
        return tuple(totals)

    totals = lax.fori_loop(0, tiles // pair, step, (zero,) * (2 * count))
    sums[...] = jnp.zeros(sums.shape, jnp.float32)
    for k in range(2 * count):
        sums[k] = totals[k]
    part[...] = lanes_from(jnp.sum(sums[...], axis=1), part.shape[0])


def paired(value, axis, first):
    size = lax.axis_size(axis)
    pairs = [(i, i + 1) for i in range(first, size - 1, 2)]
    return lax.ppermute(value, axis, pairs + [(j, i) for i, j in pairs])


def by_parity(odd, array, height, dim):
    length = array.shape[dim]
    low = lax.slice_in_dim(array, 0, height, axis=dim)
    high = lax.slice_in_dim(array, length - height, length, axis=dim)
    return jnp.where(odd, high, low), jnp.where(odd, low, high)


def from_owner(shard, odd, axis, root):
    mine = lax.axis_index(axis) == root
    if lax.axis_size(axis) == 2:
        halves = by_parity(odd, shard, shard.shape[0] // 2, 0)
        return [jnp.where(mine, half, paired(half, axis, 0)) for half in halves]
    whole = lax.psum(jnp.where(mine, shard, jnp.zeros_like(shard)), axis)
    return by_parity(odd, whole, shard.shape[0] // 2, 0)


def total_over(value, axis):
    size = lax.axis_size(axis)
    if size & (size - 1):
        return lax.psum(value, axis)
    step = 1
    while step < size:
        value = value + lax.ppermute(value, axis, [(i, i ^ step) for i in range(size)])
        step *= 2
    return value


def shards(frames_raw, wind_off, run_owner, search_base):
    count, rows, columns = frames_raw.shape
    tiles = columns // lanes
    wide = rows + 8
    size = lax.axis_size("rows")
    f32 = jnp.float32
    struct = functools.partial(jax.ShapeDtypeStruct, dtype=f32)
    odd = lax.axis_index("rows") % 2 == 1
    own_odd, own_even = from_owner(wind_off[0], odd, "frames", run_owner[0])
    frames_odd, frames_even = by_parity(odd, frames_raw, 4, 1)
    frames_odd = paired(frames_odd, "rows", 1)
    frames_even = paired(frames_even, "rows", 0)
    from_odd = paired(own_odd, "rows", 1)
    from_even = paired(own_even, "rows", 0)
    smoothed = pl.pallas_call(
        smooth_kernel,
        out_shape=struct((count, rows, columns)),
        in_specs=[vmem] * 3,
        out_specs=vmem,
        scratch_shapes=[
            pltpu.VMEM((count, tiles, rows + 16, lanes), f32),
            pltpu.VMEM((count, tiles + 2, rows, lanes), f32),
        ],
        compiler_params=params,
        name="smooth",
    )(frames_raw, frames_odd, frames_even)
    clean, part = pl.pallas_call(
        match_kernel,
        out_shape=(struct((tiles + 2, wide, lanes)), struct((8, lanes))),
        in_specs=[smem] + [vmem] * 6,
        out_specs=(vmem, vmem),
        scratch_shapes=[
            pltpu.VMEM((tiles, rows + 16, lanes), f32),
            pltpu.VMEM((tiles + 2, wide, lanes), f32),
            pltpu.VMEM((tiles + 2, wide, lanes), f32),
            pltpu.VMEM((reach, tiles, wide, lanes), f32),
            pltpu.VMEM((tiles, count, rows, lanes), f32),
            pltpu.VMEM((lanes, 8, lanes), f32),
        ],
        compiler_params=params,
        name="match",
    )(search_base, own_odd, own_even, from_odd, from_even, frames_raw, smoothed)
    parts = total_over(part, "rows")
    pressure, moments, part = pl.pallas_call(
        pressure_kernel,
        out_shape=(struct((count, rows, columns)), struct((2, rows, columns)), struct((8, lanes))),
        in_specs=[smem] + [vmem] * 3,
        out_specs=(vmem, vmem, vmem),
        scratch_shapes=[
            pltpu.VMEM((reach, tiles, wide, lanes), f32),
            pltpu.VMEM((reach * reach * count, 8, lanes), f32),
            pltpu.VMEM((lanes, 8, lanes), f32),
        ],
        compiler_params=params,
        name="pressure",
    )(search_base, parts, clean, smoothed)
    whole = total_over(moments, "frames")
    spatial = jnp.sum(lax.all_gather(part[0], "rows"), axis=0)
    cell_count = rows * columns * size
    frame_mean = spatial[:count] / cell_count
    frame_rms = jnp.sqrt(spatial[count : 2 * count] / cell_count - frame_mean * frame_mean)
    total_frames = count * lax.axis_size("frames")
    time_mean = whole[0] / total_frames
    time_rms = jnp.sqrt(jnp.maximum(whole[1] / total_frames - time_mean * time_mean, 0.0))
    return (pressure, frame_mean, frame_rms, time_mean, time_rms)


def solution(mesh):
    placed = (P("frames", "rows", None), P("frames", "rows", None), P("rows"), P("frames", None))
    return jax.shard_map(
        shards,
        mesh=mesh,
        in_specs=placed,
        out_specs=(
            P("frames", "rows", None),
            P("frames"),
            P("frames"),
            P("rows", None),
            P("rows", None),
        ),
        check_vma=False,
    )
```

```python
import functools

import jax
import jax.numpy as jnp
from jax import lax
from jax.experimental import pallas as pl
from jax.experimental.pallas import tpu as pltpu
from jax.sharding import PartitionSpec as P

taps = (1.0 / 256, 8.0 / 256, 28.0 / 256, 56.0 / 256, 70.0 / 256)
calib_zero = -0.25
calib_linear = 1.0
calib_square = 0.15
lanes = 128
reach = 7
slot = 32
params = pltpu.CompilerParams(vmem_limit_bytes=24 * 1024 * 1024)
vmem = pl.BlockSpec(memory_space=pltpu.VMEM)
smem = pl.BlockSpec(memory_space=pltpu.SMEM)


def tile_of(index):
    return pl.ds(pl.multiple_of(index * lanes, lanes), lanes)


def by_tiles(step, tiles, group, init=()):
    def body(index, carry):
        for inner in range(group):
            carry = step(index * group + inner, carry)
        return carry

    return lax.fori_loop(0, tiles // group, body, init)


def lane_of(shape):
    return lax.broadcasted_iota(jnp.int32, shape, len(shape) - 1)


def fold(product):
    return jnp.sum(product.reshape(product.shape[0] // 8, 8, lanes), axis=0)


def vertical(load):
    total = taps[4] * load(4)
    for step in range(4):
        total = total + taps[step] * (load(step) + load(8 - step))
    return total


def moved(before, here, after, step):
    if step > 0:
        return pltpu.roll(jnp.where(lane_of(here.shape) < step, after, here), lanes - step, 1)
    if step < 0:
        return pltpu.roll(jnp.where(lane_of(here.shape) >= lanes + step, before, here), -step, 1)
    return here


def horizontal(before, here, after):
    total = taps[4] * here
    for step in range(1, 5):
        pair = moved(before, here, after, step) + moved(before, here, after, -step)
        total = total + taps[4 - step] * pair
    return total


def halves(value):
    high = value.astype(jnp.bfloat16)
    low = (value - high.astype(jnp.float32)).astype(jnp.bfloat16)
    return high, low


def by_row_shift(value, rows, direction):
    place = lax.broadcasted_iota(jnp.int32, value.shape, 0) % rows
    step = 1
    while step < rows:
        turned = pltpu.roll(value, step if direction > 0 else lanes - step, 1)
        value = jnp.where((place & step) != 0, turned, value)
        step *= 2
    return value


def smooth_kernel(frames, from_odd, from_even, inverse, stack, power, rows_in, half, fine):
    count, rows, columns = frames.shape
    tiles = columns // lanes
    ring = tiles + 2
    odd = lax.axis_index("rows") % 2 == 1
    zero = jnp.zeros((rows, lanes), jnp.float32)
    for f in range(count):
        half[f, 0] = zero
        half[f, tiles + 1] = zero
    blank = jnp.zeros((count * rows, lanes), jnp.float32)
    fine[0] = blank
    fine[tiles + 1] = blank
    fine[tiles + 2] = blank

    def load_step(t, carry):
        for f in range(count):
            outer = from_odd[f, :, tile_of(t)]
            inner = from_even[f, :, tile_of(t)]
            rows_in[f, t, 4:8, :] = jnp.where(odd, inner, outer)
            rows_in[f, t, 8 : 8 + rows, :] = frames[f, :, tile_of(t)]
            rows_in[f, t, 8 + rows : 12 + rows, :] = jnp.where(odd, outer, inner)
        return carry

    def vertical_step(t, carry):
        for f in range(count):
            half[f, t + 1] = vertical(lambda s: rows_in[f, t, pl.ds(4 + s, rows), :])
        return carry

    def horizontal_step(t, totals):
        result = []
        for f in range(count):
            smooth = horizontal(half[f, t], half[f, t + 1], half[f, t + 2])
            inverse[f, :, tile_of(t)] = 1.0 / smooth
            detail = frames[f, :, tile_of(t)] - smooth
            fine[t + 1, f * rows : (f + 1) * rows, :] = detail
            result.append(totals[f] + fold(detail * detail))
        return tuple(result)

    def stack_step(t, carry):
        before, here, after = fine[t], fine[t + 1], fine[t + 2]
        for j in range(reach):
            high, low = halves(moved(before, here, after, 3 - j))
            size = count * rows
            stack[j * size : (j + 1) * size, tile_of(t)] = high
            stack[(reach + j) * size : (reach + j + 1) * size, tile_of(t)] = low
        return carry

    by_tiles(load_step, tiles, 8)
    by_tiles(vertical_step, tiles, 8)
    powers = by_tiles(horizontal_step, tiles, 8, (jnp.zeros((8, lanes), jnp.float32),) * count)
    for f in range(count):
        power[f * 8 : f * 8 + 8, :] = powers[f]
    fine[tiles + 3] = fine[1]
    by_tiles(stack_step, ring, ring // 2)


def column_shift(offset):
    negative = offset < 0
    first = jnp.where(negative, 0, 1)
    amount = jnp.where(negative, offset + lanes, offset)
    back = lax.rem(lanes - amount, lanes)

    def shift(source, t):
        here = source[t + first]
        after = source[t + first + 1]
        value = pltpu.roll(jnp.where(lane_of(here.shape) < amount, after, here), back, 1)
        spare = jnp.zeros((slot - value.shape[0], lanes), jnp.float32)
        return jnp.concatenate([value, spare], axis=0)

    return shift


def match_kernel(
    base, own_odd, own_even, from_odd, from_even, stack, power, clean, part, rows_in, half, fine, stream
):
    rows = own_odd.shape[0] * 2
    tiles = own_odd.shape[1] // lanes
    count = power.shape[0] // 8
    ring = tiles + 2
    wide = rows + 8
    row_index = lax.axis_index("rows")
    last_row = lax.axis_size("rows") - 1
    odd = row_index % 2 == 1
    blank = jnp.zeros((wide, lanes), jnp.float32)
    half[0] = blank
    half[tiles + 1] = blank
    clean[0] = blank
    clean[tiles + 1] = blank
    fine[0] = blank
    fine[tiles + 1] = blank
    fine[tiles + 2] = blank
    place = lax.broadcasted_iota(jnp.int32, (wide, lanes), 0)
    inside = ((place >= 4) | (row_index > 0)) & ((place < rows + 4) | (row_index < last_row))

    def load_step(t, carry):
        outer = [array[:, tile_of(t)] for array in (from_odd, own_odd)]
        inner = [array[:, tile_of(t)] for array in (own_even, from_even)]
        rows_in[t, 0:8, :] = jnp.where(odd, inner[1], outer[0])
        rows_in[t, 8:16, :] = jnp.where(odd, inner[0], outer[1])
        rows_in[t, 16:24, :] = jnp.where(odd, outer[1], inner[0])
        rows_in[t, 24:32, :] = jnp.where(odd, outer[0], inner[1])
        return carry

    def vertical_step(t, carry):
        half[t + 1] = vertical(lambda s: rows_in[t, pl.ds(s, wide), :])
        return carry

    def horizontal_step(t, total):
        smooth = jnp.where(inside, horizontal(half[t], half[t + 1], half[t + 2]), 0.0)
        clean[t + 1] = smooth
        detail = rows_in[t, pl.ds(4, wide), :] - smooth
        fine[t + 1] = detail
        own = jnp.where((place >= 4) & (place < rows + 4), detail, 0.0)
        return total + fold(own * own)

    by_tiles(load_step, tiles, 8)
    by_tiles(vertical_step, tiles, 8)
    ref_power = by_tiles(horizontal_step, tiles, 8, jnp.zeros((8, lanes), jnp.float32))
    fine[tiles + 3] = fine[1]
    shift = column_shift(base[0, 1])
    stream[2 * slot : 4 * slot, :] = jnp.zeros((2 * slot, ring * lanes), jnp.bfloat16)

    def stream_step(t, carry):
        high, low = halves(shift(fine, t))
        stream[0:slot, tile_of(t)] = high
        stream[slot : 2 * slot, tile_of(t)] = low
        return carry

    by_tiles(stream_step, ring, ring // 2)
    product = lax.dot_general(
        stack[...], stream[...], (((1,), (1,)), ((), ())), preferred_element_type=jnp.float32
    )
    size = reach * count * rows
    product = product[:size] + product[size:]
    product = product + pltpu.roll(product, lanes - slot, 1)
    product = by_row_shift(product, rows, -1)
    part[...] = jnp.zeros(part.shape, jnp.float32)
    for j in range(reach):
        for f in range(count):
            start = (j * count + f) * rows
            part[f * 8 + j : f * 8 + j + 1, :] = jnp.sum(product[start : start + rows], axis=0, keepdims=True)
    lags = pltpu.roll(part[0 : 8 * count, :], lax.rem(lanes - 1 - base[0, 0], lanes), 1)
    part[0 : 8 * count, :] = jnp.where(lane_of(lags.shape) < reach, lags, 0.0)
    start = 8 * count
    for f in range(count):
        part[start + f : start + f + 1, :] = jnp.sum(power[f * 8 : f * 8 + 8, :], axis=0, keepdims=True)
    part[start + count : start + count + 1, :] = jnp.sum(ref_power, axis=0, keepdims=True)
    powers = part[start : start + 8, :]
    part[start : start + 8, :] = jnp.broadcast_to(jnp.sum(powers, axis=1, keepdims=True), powers.shape)


def spread_kernel(base, clean, spread):
    tiles = clean.shape[0] - 2
    full = spread.shape[0] // 2
    spare = jnp.zeros((full - reach * slot, tiles * lanes), jnp.bfloat16)
    spread[reach * slot : full, :] = spare
    spread[full + reach * slot : 2 * full, :] = spare

    def per_offset(j, carry):
        shift = column_shift(base[0, 1] + j - 3)
        at = pl.multiple_of(j * slot, slot)

        def step(t, inner):
            high, low = halves(shift(clean, t))
            spread[pl.ds(at, slot), tile_of(t)] = high
            spread[pl.ds(full + at, slot), tile_of(t)] = low
            return inner

        by_tiles(step, tiles, 32)
        return carry

    lax.fori_loop(0, reach, per_offset, 0)


def blend_weights(matches, frame_power, ref_power):
    norm_product = jnp.sqrt((frame_power + 1e-06) * (ref_power + 1e-06))
    rho = matches / norm_product
    squared = rho * rho
    total = jnp.sum(jnp.sum(squared, axis=0, keepdims=True), axis=1, keepdims=True)
    across = lax.broadcasted_iota(jnp.int32, matches.shape, 0)
    middle = (across == reach // 2) & (lane_of(matches.shape) == reach // 2)
    return (squared + jnp.where(middle, 0.05, 0.0)) / (0.05 + total)


def banded(weights, rows, first_row):
    across = lax.broadcasted_iota(jnp.int32, weights.shape, 0)
    spaced = weights
    for step in (1, 2):
        spaced = jnp.where((across & step) != 0, pltpu.roll(spaced, step * slot, 1), spaced)
    tiles = []
    for member in (across < 4, across >= 4):
        line = jnp.sum(jnp.where(member, spaced, 0.0), axis=0, keepdims=True)
        block = by_row_shift(jnp.broadcast_to(line, (rows, lanes)), rows, 1)
        tiles.append(pltpu.roll(block, first_row, 1))
    return jnp.concatenate(tiles, axis=1)


def pressure_kernel(base, parts, spread, inverse, pressure, moments, part):
    count, rows, columns = inverse.shape
    start = 8 * count
    full = spread.shape[0] // 2
    first_row = 1 + base[0, 0]
    ref_power = parts[start + count : start + count + 1, :]
    bands = []
    for f in range(count):
        weights = blend_weights(parts[f * 8 : f * 8 + 8, :], parts[start + f : start + f + 1, :], ref_power)
        bands.append(banded(weights, rows, first_row))
    mixing = jnp.concatenate(halves(jnp.concatenate(bands, axis=0)), axis=0)
    chunk = 2 * lanes
    zero = jnp.zeros((8, lanes), jnp.float32)
    size = count * rows

    def step(t, totals):
        where = pl.ds(pl.multiple_of(t * chunk, chunk), chunk)
        product = jnp.dot(mixing, spread[0:full, where], preferred_element_type=jnp.float32)
        product = product + jnp.dot(mixing, spread[full : 2 * full, where], preferred_element_type=jnp.float32)
        registered = product[:size] + product[size:]
        first = second = None
        totals = list(totals)
        for f in range(count):
            ratio = registered[f * rows : (f + 1) * rows] * inverse[f, :, where]
            value = calib_zero + ratio * (calib_linear + calib_square * ratio)
            squared = value * value
            pressure[f, :, where] = value
            first = value if first is None else first + value
            second = squared if second is None else second + squared
            for total, array in ((f, value), (count + f, squared)):
                for c in range(chunk // lanes):
                    totals[total] = totals[total] + fold(array[:, c * lanes : (c + 1) * lanes])
        moments[0, :, where] = first
        moments[1, :, where] = second
        return tuple(totals)

    totals = by_tiles(step, columns // chunk, 4, (zero,) * (2 * count))
    part[...] = jnp.zeros(part.shape, jnp.float32)
    for k in range(2 * count):
        part[k : k + 1, :] = jnp.sum(totals[k], axis=0, keepdims=True)


def paired(value, axis, first):
    size = lax.axis_size(axis)
    pairs = [(i, i + 1) for i in range(first, size - 1, 2)]
    return lax.ppermute(value, axis, pairs + [(j, i) for i, j in pairs])


def by_parity(odd, array, height, dim):
    length = array.shape[dim]
    low = lax.slice_in_dim(array, 0, height, axis=dim)
    high = lax.slice_in_dim(array, length - height, length, axis=dim)
    return jnp.where(odd, high, low), jnp.where(odd, low, high)


def from_owner(shard, axis, root):
    mine = lax.axis_index(axis) == root
    if lax.axis_size(axis) == 2:
        return jnp.where(mine, shard, paired(shard, axis, 0))
    return lax.psum(jnp.where(mine, shard, jnp.zeros_like(shard)), axis)


def total_over(value, axis):
    size = lax.axis_size(axis)
    if size & (size - 1):
        return lax.psum(value, axis)
    step = 1
    while step < size:
        value = value + lax.ppermute(value, axis, [(i, i ^ step) for i in range(size)])
        step *= 2
    return value


def shards(frames_raw, wind_off, run_owner, search_base):
    count, rows, columns = frames_raw.shape
    tiles = columns // lanes
    ring = tiles + 2
    wide = rows + 8
    depth = reach * count * rows
    f32 = jnp.float32
    bf16 = jnp.bfloat16
    struct = functools.partial(jax.ShapeDtypeStruct, dtype=f32)
    odd = lax.axis_index("rows") % 2 == 1
    reference = from_owner(wind_off[0], "frames", run_owner[0])
    frames_odd, frames_even = by_parity(odd, frames_raw, 4, 1)
    frames_even = paired(frames_even, "rows", 0)
    frames_odd = paired(frames_odd, "rows", 1)
    own_odd, own_even = by_parity(odd, reference, rows // 2, 0)
    from_even = paired(own_even, "rows", 0)
    from_odd = paired(own_odd, "rows", 1)
    inverse, stack, power = pl.pallas_call(
        smooth_kernel,
        out_shape=(
            struct((count, rows, columns)),
            jax.ShapeDtypeStruct((2 * depth, ring * lanes), bf16),
            struct((8 * count, lanes)),
        ),
        in_specs=[vmem] * 3,
        out_specs=(vmem,) * 3,
        scratch_shapes=[
            pltpu.VMEM((count, tiles, rows + 16, lanes), f32),
            pltpu.VMEM((count, tiles + 2, rows, lanes), f32),
            pltpu.VMEM((ring + 2, count * rows, lanes), f32),
        ],
        compiler_params=params,
        name="smooth",
    )(frames_raw, frames_odd, frames_even)
    clean, part = pl.pallas_call(
        match_kernel,
        out_shape=(struct((tiles + 2, wide, lanes)), struct((8 * count + 8, lanes))),
        in_specs=[smem] + [vmem] * 6,
        out_specs=(vmem, vmem),
        scratch_shapes=[
            pltpu.VMEM((tiles, rows + 16, lanes), f32),
            pltpu.VMEM((tiles + 2, wide, lanes), f32),
            pltpu.VMEM((ring + 2, wide, lanes), f32),
            pltpu.VMEM((4 * slot, ring * lanes), bf16),
        ],
        compiler_params=params,
        name="match",
    )(search_base, own_odd, own_even, from_odd, from_even, stack, power)
    parts = total_over(part, "rows")
    spread = pl.pallas_call(
        spread_kernel,
        out_shape=jax.ShapeDtypeStruct((2 * 8 * slot, columns), bf16),
        in_specs=[smem, vmem],
        out_specs=vmem,
        compiler_params=params,
        name="spread",
    )(search_base, clean)
    pressure, moments, part = pl.pallas_call(
        pressure_kernel,
        out_shape=(struct((count, rows, columns)), struct((2, rows, columns)), struct((8, lanes))),
        in_specs=[smem] + [vmem] * 3,
        out_specs=(vmem, vmem, vmem),
        compiler_params=params,
        name="pressure",
    )(search_base, parts, spread, inverse)
    whole = total_over(moments, "frames")
    spatial = jnp.sum(total_over(part, "rows"), axis=1)
    cell_count = rows * columns * lax.axis_size("rows")
    frame_mean = spatial[:count] / cell_count
    frame_rms = jnp.sqrt(spatial[count : 2 * count] / cell_count - frame_mean * frame_mean)
    total_frames = count * lax.axis_size("frames")
    time_mean = whole[0] / total_frames
    time_rms = jnp.sqrt(jnp.maximum(whole[1] / total_frames - time_mean * time_mean, 0.0))
    return (pressure, frame_mean, frame_rms, time_mean, time_rms)


def solution(mesh):
    placed = (P("frames", "rows", None), P("frames", "rows", None), P("rows"), P("frames", None))
    return jax.shard_map(
        shards,
        mesh=mesh,
        in_specs=placed,
        out_specs=(
            P("frames", "rows", None),
            P("frames"),
            P("frames"),
            P("rows", None),
            P("rows", None),
        ),
        check_vma=False,
    )
```

```python
import functools

import jax
import jax.numpy as jnp
from jax import lax
from jax.experimental import pallas as pl
from jax.experimental.pallas import tpu as pltpu
from jax.sharding import PartitionSpec as P

taps = (1.0 / 256, 8.0 / 256, 28.0 / 256, 56.0 / 256, 70.0 / 256)
calib_zero = -0.25
calib_linear = 1.0
calib_square = 0.15
lanes = 128
reach = 7
slot = 32
params = pltpu.CompilerParams(vmem_limit_bytes=24 * 1024 * 1024)
vmem = pl.BlockSpec(memory_space=pltpu.VMEM)
smem = pl.BlockSpec(memory_space=pltpu.SMEM)


def tile_of(index):
    return pl.ds(pl.multiple_of(index * lanes, lanes), lanes)


def by_tiles(step, tiles, group, init=()):
    def body(index, carry):
        for inner in range(group):
            carry = step(index * group + inner, carry)
        return carry

    return lax.fori_loop(0, tiles // group, body, init)


def lane_of(shape):
    return lax.broadcasted_iota(jnp.int32, shape, len(shape) - 1)


def fold(product):
    return jnp.sum(product.reshape(product.shape[0] // 8, 8, lanes), axis=0)


def vertical(load):
    total = taps[4] * load(4)
    for step in range(4):
        total = total + taps[step] * (load(step) + load(8 - step))
    return total


def moved(before, here, after, step):
    if step > 0:
        return pltpu.roll(jnp.where(lane_of(here.shape) < step, after, here), lanes - step, 1)
    if step < 0:
        return pltpu.roll(jnp.where(lane_of(here.shape) >= lanes + step, before, here), -step, 1)
    return here


def horizontal(before, here, after):
    total = taps[4] * here
    for step in range(1, 5):
        pair = moved(before, here, after, step) + moved(before, here, after, -step)
        total = total + taps[4 - step] * pair
    return total


def halves(value):
    high = value.astype(jnp.bfloat16)
    low = (value - high.astype(jnp.float32)).astype(jnp.bfloat16)
    return high, low


def by_row_shift(value, rows, direction):
    place = lax.broadcasted_iota(jnp.int32, value.shape, 0) % rows
    unit = 1
    while unit < rows:
        digit = (place // unit) % 4
        result = value
        for times in range(1, 4):
            amount = times * unit
            turned = pltpu.roll(value, amount if direction > 0 else lanes - amount, 1)
            result = jnp.where(digit == times, turned, result)
        value = result
        unit *= 4
    return value


def cut_kernel(
    base, frames, wind, raw, across, frames_odd, frames_even, wind_odd, wind_even, offsets, wind_here, arrived
):
    count, rows, columns = raw.shape
    tiles = columns // lanes
    odd = lax.axis_index("rows") % 2 == 1
    copies = [pltpu.make_async_copy(frames.at[f], raw.at[f], arrived.at[f]) for f in range(count)]
    copies.append(pltpu.make_async_copy(wind.at[0], wind_here, arrived.at[count]))
    copies.append(pltpu.make_async_copy(base, offsets, arrived.at[count + 1]))
    for copy in copies:
        copy.start()

    for f in range(count):
        copies[f].wait()

        def step(t, carry):
            at = tile_of(t)
            before = jnp.where(t > 0, raw[f, :, tile_of(jnp.maximum(t - 1, 0))], 0.0)
            after = jnp.where(t < tiles - 1, raw[f, :, tile_of(jnp.minimum(t + 1, tiles - 1))], 0.0)
            value = horizontal(before, raw[f, :, at], after)
            across[f, t] = value
            low = value[0:4]
            high = value[rows - 4 : rows]
            frames_odd[f, :, at] = jnp.where(odd, high, low)
            frames_even[f, :, at] = jnp.where(odd, low, high)
            return carry

        by_tiles(step, tiles, 16)

    for copy in copies[count:]:
        copy.wait()

    def wind_step(t, carry):
        at = tile_of(t)
        low = wind_here[0 : rows // 2, at]
        high = wind_here[rows // 2 : rows, at]
        wind_odd[:, at] = jnp.where(odd, high, low)
        wind_even[:, at] = jnp.where(odd, low, high)
        return carry

    by_tiles(wind_step, tiles, 16)


def smooth_kernel(frames, across, from_odd, from_even, inverse, stack, power, rows_in, fine):
    count, rows, columns = frames.shape
    tiles = columns // lanes
    ring = tiles + 2
    odd = lax.axis_index("rows") % 2 == 1
    blank = jnp.zeros((count * rows, lanes), jnp.float32)
    fine[0] = blank
    fine[tiles + 1] = blank
    fine[tiles + 2] = blank

    def load_step(t, carry):
        for f in range(count):
            outer = from_odd[f, :, tile_of(t)]
            inner = from_even[f, :, tile_of(t)]
            rows_in[f, t, 4:8, :] = jnp.where(odd, inner, outer)
            rows_in[f, t, 8 : 8 + rows, :] = across[f, t]
            rows_in[f, t, 8 + rows : 12 + rows, :] = jnp.where(odd, outer, inner)
        return carry

    def vertical_step(t, totals):
        result = []
        for f in range(count):
            smooth = vertical(lambda s: rows_in[f, t, pl.ds(4 + s, rows), :])
            inverse[f, :, tile_of(t)] = 1.0 / smooth
            detail = frames[f, :, tile_of(t)] - smooth
            fine[t + 1, f * rows : (f + 1) * rows, :] = detail
            result.append(totals[f] + fold(detail * detail))
        return tuple(result)

    def stack_step(t, carry):
        before, here, after = fine[t], fine[t + 1], fine[t + 2]
        for j in range(reach):
            high, low = halves(moved(before, here, after, 3 - j))
            size = count * rows
            stack[j * size : (j + 1) * size, tile_of(t)] = high
            stack[(reach + j) * size : (reach + j + 1) * size, tile_of(t)] = low
        return carry

    by_tiles(load_step, tiles, 8)
    powers = by_tiles(vertical_step, tiles, 8, (jnp.zeros((8, lanes), jnp.float32),) * count)
    for f in range(count):
        power[f * 8 : f * 8 + 8, :] = powers[f]
    fine[tiles + 3] = fine[1]
    by_tiles(stack_step, ring, ring // 2)


def column_shift(offset):
    negative = offset < 0
    first = jnp.where(negative, 0, 1)
    amount = jnp.where(negative, offset + lanes, offset)
    back = lax.rem(lanes - amount, lanes)

    def shift(source, t):
        here = source[t + first]
        after = source[t + first + 1]
        value = pltpu.roll(jnp.where(lane_of(here.shape) < amount, after, here), back, 1)
        spare = jnp.zeros((slot - value.shape[0], lanes), jnp.float32)
        return jnp.concatenate([value, spare], axis=0)

    return shift


def match_kernel(
    base, own_odd, own_even, from_odd, from_even, stack, power, clean, part, rows_in, half, fine, stream
):
    rows = own_odd.shape[0] * 2
    tiles = own_odd.shape[1] // lanes
    count = power.shape[0] // 8
    ring = tiles + 2
    wide = rows + 8
    row_index = lax.axis_index("rows")
    last_row = lax.axis_size("rows") - 1
    odd = row_index % 2 == 1
    blank = jnp.zeros((wide, lanes), jnp.float32)
    half[0] = blank
    half[tiles + 1] = blank
    clean[0] = blank
    clean[tiles + 1] = blank
    fine[0] = blank
    fine[tiles + 1] = blank
    fine[tiles + 2] = blank
    place = lax.broadcasted_iota(jnp.int32, (wide, lanes), 0)
    inside = ((place >= 4) | (row_index > 0)) & ((place < rows + 4) | (row_index < last_row))

    def load_step(t, carry):
        outer = [array[:, tile_of(t)] for array in (from_odd, own_odd)]
        inner = [array[:, tile_of(t)] for array in (own_even, from_even)]
        rows_in[t, 0:8, :] = jnp.where(odd, inner[1], outer[0])
        rows_in[t, 8:16, :] = jnp.where(odd, inner[0], outer[1])
        rows_in[t, 16:24, :] = jnp.where(odd, outer[1], inner[0])
        rows_in[t, 24:32, :] = jnp.where(odd, outer[0], inner[1])
        return carry

    def vertical_step(t, carry):
        half[t + 1] = vertical(lambda s: rows_in[t, pl.ds(s, wide), :])
        return carry

    def horizontal_step(t, total):
        smooth = jnp.where(inside, horizontal(half[t], half[t + 1], half[t + 2]), 0.0)
        clean[t + 1] = smooth
        detail = rows_in[t, pl.ds(4, wide), :] - smooth
        fine[t + 1] = detail
        own = jnp.where((place >= 4) & (place < rows + 4), detail, 0.0)
        return total + fold(own * own)

    by_tiles(load_step, tiles, 8)
    by_tiles(vertical_step, tiles, 8)
    ref_power = by_tiles(horizontal_step, tiles, 8, jnp.zeros((8, lanes), jnp.float32))
    fine[tiles + 3] = fine[1]
    shift = column_shift(base[0, 1])
    stream[2 * slot : 4 * slot, :] = jnp.zeros((2 * slot, ring * lanes), jnp.bfloat16)

    def stream_step(t, carry):
        high, low = halves(shift(fine, t))
        stream[0:slot, tile_of(t)] = high
        stream[slot : 2 * slot, tile_of(t)] = low
        return carry

    by_tiles(stream_step, ring, ring // 2)
    product = lax.dot_general(
        stack[...], stream[...], (((1,), (1,)), ((), ())), preferred_element_type=jnp.float32
    )
    size = reach * count * rows
    product = product[:size] + product[size:]
    product = by_row_shift(product, rows, -1)
    part[...] = jnp.zeros(part.shape, jnp.float32)
    for j in range(reach):
        for f in range(count):
            start = (j * count + f) * rows
            part[f * 8 + j : f * 8 + j + 1, :] = jnp.sum(product[start : start + rows], axis=0, keepdims=True)
    lags = part[0 : 8 * count, :]
    back = lanes - 1 - base[0, 0]
    lags = pltpu.roll(lags, lax.rem(back, lanes), 1) + pltpu.roll(lags, lax.rem(back + lanes - slot, lanes), 1)
    part[0 : 8 * count, :] = jnp.where(lane_of(lags.shape) < reach, lags, 0.0)
    start = 8 * count
    for f in range(count):
        part[start + f : start + f + 1, :] = jnp.sum(power[f * 8 : f * 8 + 8, :], axis=0, keepdims=True)
    part[start + count : start + count + 1, :] = jnp.sum(ref_power, axis=0, keepdims=True)
    powers = part[start : start + 8, :]
    part[start : start + 8, :] = jnp.broadcast_to(jnp.sum(powers, axis=1, keepdims=True), powers.shape)


def spread_kernel(base, clean, spread):
    tiles = clean.shape[0] - 2
    full = spread.shape[0] // 2
    spare = jnp.zeros((full - reach * slot, tiles * lanes), jnp.bfloat16)
    spread[reach * slot : full, :] = spare
    spread[full + reach * slot : 2 * full, :] = spare

    def per_offset(j, carry):
        shift = column_shift(base[0, 1] + j - 3)
        at = pl.multiple_of(j * slot, slot)

        def step(t, inner):
            high, low = halves(shift(clean, t))
            spread[pl.ds(at, slot), tile_of(t)] = high
            spread[pl.ds(full + at, slot), tile_of(t)] = low
            return inner

        by_tiles(step, tiles, 32)
        return carry

    lax.fori_loop(0, reach, per_offset, 0)


def blend_weights(matches, frame_power, ref_power):
    norm_product = jnp.sqrt((frame_power + 1e-06) * (ref_power + 1e-06))
    rho = matches / norm_product
    squared = rho * rho
    total = jnp.sum(jnp.sum(squared, axis=0, keepdims=True), axis=1, keepdims=True)
    across = lax.broadcasted_iota(jnp.int32, matches.shape, 0)
    middle = (across == reach // 2) & (lane_of(matches.shape) == reach // 2)
    return (squared + jnp.where(middle, 0.05, 0.0)) / (0.05 + total)


def banded(weights, rows, first_row):
    across = lax.broadcasted_iota(jnp.int32, weights.shape, 0)
    spaced = jnp.zeros_like(weights)
    for times in range(4):
        turned = pltpu.roll(weights, first_row + times * slot, 1)
        spaced = jnp.where(across % 4 == times, turned, spaced)
    tiles = []
    for member in (across < 4, across >= 4):
        line = jnp.sum(jnp.where(member, spaced, 0.0), axis=0, keepdims=True)
        tiles.append(by_row_shift(jnp.broadcast_to(line, (rows, lanes)), rows, 1))
    return jnp.concatenate(tiles, axis=1)


def pressure_kernel(base, parts, spread, inverse, pressure, moments, part):
    count, rows, columns = inverse.shape
    start = 8 * count
    full = spread.shape[0] // 2
    first_row = 1 + base[0, 0]
    ref_power = parts[start + count : start + count + 1, :]
    bands = []
    for f in range(count):
        weights = blend_weights(parts[f * 8 : f * 8 + 8, :], parts[start + f : start + f + 1, :], ref_power)
        bands.append(banded(weights, rows, first_row))
    mixing = jnp.concatenate(halves(jnp.concatenate(bands, axis=0)), axis=0)
    chunk = 2 * lanes
    zero = jnp.zeros((8, lanes), jnp.float32)
    size = count * rows

    def step(t, totals):
        where = pl.ds(pl.multiple_of(t * chunk, chunk), chunk)
        product = jnp.dot(mixing, spread[0:full, where], preferred_element_type=jnp.float32)
        product = product + jnp.dot(mixing, spread[full : 2 * full, where], preferred_element_type=jnp.float32)
        registered = product[:size] + product[size:]
        first = second = None
        totals = list(totals)
        for f in range(count):
            ratio = registered[f * rows : (f + 1) * rows] * inverse[f, :, where]
            value = calib_zero + ratio * (calib_linear + calib_square * ratio)
            squared = value * value
            pressure[f, :, where] = value
            first = value if first is None else first + value
            second = squared if second is None else second + squared
            for total, array in ((f, value), (count + f, squared)):
                for c in range(chunk // lanes):
                    totals[total] = totals[total] + fold(array[:, c * lanes : (c + 1) * lanes])
        moments[0, :, where] = first
        moments[1, :, where] = second
        return tuple(totals)

    totals = by_tiles(step, columns // chunk, 8, (zero,) * (2 * count))
    part[...] = jnp.zeros(part.shape, jnp.float32)
    for k in range(2 * count):
        part[k : k + 1, :] = jnp.sum(totals[k], axis=0, keepdims=True)


def paired(value, axis, first):
    size = lax.axis_size(axis)
    pairs = [(i, i + 1) for i in range(first, size - 1, 2)]
    return lax.ppermute(value, axis, pairs + [(j, i) for i, j in pairs])


def by_parity(odd, array, height, dim):
    length = array.shape[dim]
    low = lax.slice_in_dim(array, 0, height, axis=dim)
    high = lax.slice_in_dim(array, length - height, length, axis=dim)
    return jnp.where(odd, high, low), jnp.where(odd, low, high)


def from_owner(shard, cut, odd, axis, root):
    mine = lax.axis_index(axis) == root
    if lax.axis_size(axis) == 2:
        received = by_parity(odd, paired(shard, axis, 0), shard.shape[0] // 2, 0)
        return [jnp.where(mine, own, other) for own, other in zip(cut, received)]
    whole = lax.psum(jnp.where(mine, shard, jnp.zeros_like(shard)), axis)
    return by_parity(odd, whole, shard.shape[0] // 2, 0)


def total_over_rows(value, odd):
    size = lax.axis_size("rows")
    if size & (size - 1) or size < 2:
        return lax.psum(value, "rows")
    value = value + lax.ppermute(value, "rows", [(i, i + 1) for i in range(0, size, 2)])
    step = 2
    while step < size:
        value = value + lax.ppermute(value, "rows", [(i, i ^ step) for i in range(1, size, 2)])
        step *= 2
    back = lax.ppermute(value, "rows", [(i, i - 1) for i in range(1, size, 2)])
    return jnp.where(odd, value, back)


def total_over(value, axis):
    size = lax.axis_size(axis)
    if size & (size - 1):
        return lax.psum(value, axis)
    step = 1
    while step < size:
        value = value + lax.ppermute(value, axis, [(i, i ^ step) for i in range(size)])
        step *= 2
    return value


def shards(frames_raw, wind_off, run_owner, search_base):
    count, rows, columns = frames_raw.shape
    tiles = columns // lanes
    ring = tiles + 2
    wide = rows + 8
    depth = reach * count * rows
    f32 = jnp.float32
    bf16 = jnp.bfloat16
    struct = functools.partial(jax.ShapeDtypeStruct, dtype=f32)
    odd = lax.axis_index("rows") % 2 == 1
    edge = struct((count, 4, columns))
    side = struct((rows // 2, columns))
    raw, across, frames_odd, frames_even, wind_odd, wind_even, offsets = pl.pallas_call(
        cut_kernel,
        out_shape=(
            struct((count, rows, columns)),
            struct((count, tiles, rows, lanes)),
            edge,
            edge,
            side,
            side,
            jax.ShapeDtypeStruct((1, 2), jnp.int32),
        ),
        in_specs=[pl.BlockSpec(memory_space=pl.ANY)] * 3,
        out_specs=(vmem,) * 6 + (smem,),
        scratch_shapes=[pltpu.VMEM((rows, columns), f32), pltpu.SemaphoreType.DMA((count + 2,))],
        compiler_params=params,
        name="cut",
    )(search_base, frames_raw, wind_off)
    own_odd, own_even = from_owner(wind_off[0], (wind_odd, wind_even), odd, "frames", run_owner[0])
    frames_odd = paired(frames_odd, "rows", 1)
    frames_even = paired(frames_even, "rows", 0)
    from_even = paired(own_even, "rows", 0)
    from_odd = paired(own_odd, "rows", 1)
    inverse, stack, power = pl.pallas_call(
        smooth_kernel,
        out_shape=(
            struct((count, rows, columns)),
            jax.ShapeDtypeStruct((2 * depth, ring * lanes), bf16),
            struct((8 * count, lanes)),
        ),
        in_specs=[vmem] * 4,
        out_specs=(vmem,) * 3,
        scratch_shapes=[
            pltpu.VMEM((count, tiles, rows + 16, lanes), f32),
            pltpu.VMEM((ring + 2, count * rows, lanes), f32),
        ],
        compiler_params=params,
        name="smooth",
    )(raw, across, frames_odd, frames_even)
    clean, part = pl.pallas_call(
        match_kernel,
        out_shape=(struct((tiles + 2, wide, lanes)), struct((8 * count + 8, lanes))),
        in_specs=[smem] + [vmem] * 6,
        out_specs=(vmem, vmem),
        scratch_shapes=[
            pltpu.VMEM((tiles, rows + 16, lanes), f32),
            pltpu.VMEM((tiles + 2, wide, lanes), f32),
            pltpu.VMEM((ring + 2, wide, lanes), f32),
            pltpu.VMEM((4 * slot, ring * lanes), bf16),
        ],
        compiler_params=params,
        name="match",
    )(offsets, own_odd, own_even, from_odd, from_even, stack, power)
    parts = total_over_rows(part, odd)
    spread = pl.pallas_call(
        spread_kernel,
        out_shape=jax.ShapeDtypeStruct((2 * 8 * slot, columns), bf16),
        in_specs=[smem, vmem],
        out_specs=vmem,
        compiler_params=params,
        name="spread",
    )(offsets, clean)
    pressure, moments, part = pl.pallas_call(
        pressure_kernel,
        out_shape=(struct((count, rows, columns)), struct((2, rows, columns)), struct((8, lanes))),
        in_specs=[smem] + [vmem] * 3,
        out_specs=(vmem, vmem, vmem),
        compiler_params=params,
        name="pressure",
    )(offsets, parts, spread, inverse)
    whole = total_over(moments, "frames")
    spatial = jnp.sum(total_over_rows(part, odd), axis=1)
    cell_count = rows * columns * lax.axis_size("rows")
    frame_mean = spatial[:count] / cell_count
    frame_rms = jnp.sqrt(spatial[count : 2 * count] / cell_count - frame_mean * frame_mean)
    total_frames = count * lax.axis_size("frames")
    time_mean = whole[0] / total_frames
    time_rms = jnp.sqrt(jnp.maximum(whole[1] / total_frames - time_mean * time_mean, 0.0))
    return (pressure, frame_mean, frame_rms, time_mean, time_rms)


def solution(mesh):
    placed = (P("frames", "rows", None), P("frames", "rows", None), P("rows"), P("frames", None))
    return jax.shard_map(
        shards,
        mesh=mesh,
        in_specs=placed,
        out_specs=(
            P("frames", "rows", None),
            P("frames"),
            P("frames"),
            P("rows", None),
            P("rows", None),
        ),
        check_vma=False,
    )
```

```python
import functools

import jax
import jax.numpy as jnp
from jax import lax
from jax.experimental import pallas as pl
from jax.experimental.pallas import tpu as pltpu
from jax.sharding import PartitionSpec as P

taps = (1.0 / 256, 8.0 / 256, 28.0 / 256, 56.0 / 256, 70.0 / 256)
calib_zero = -0.25
calib_linear = 1.0
calib_square = 0.15
lanes = 128
reach = 7
slot = 32
params = pltpu.CompilerParams(vmem_limit_bytes=24 * 1024 * 1024)
vmem = pl.BlockSpec(memory_space=pltpu.VMEM)
smem = pl.BlockSpec(memory_space=pltpu.SMEM)


def tile_of(index):
    return pl.ds(pl.multiple_of(index * lanes, lanes), lanes)


def by_tiles(step, tiles, group, init=()):
    def body(index, carry):
        for inner in range(group):
            carry = step(index * group + inner, carry)
        return carry

    return lax.fori_loop(0, tiles // group, body, init)


def lane_of(shape):
    return lax.broadcasted_iota(jnp.int32, shape, len(shape) - 1)


def fold(product):
    return jnp.sum(product.reshape(product.shape[0] // 8, 8, lanes), axis=0)


def vertical(load):
    total = taps[4] * load(4)
    for step in range(4):
        total = total + taps[step] * (load(step) + load(8 - step))
    return total


def moved(before, here, after, step):
    if step > 0:
        return pltpu.roll(jnp.where(lane_of(here.shape) < step, after, here), lanes - step, 1)
    if step < 0:
        return pltpu.roll(jnp.where(lane_of(here.shape) >= lanes + step, before, here), -step, 1)
    return here


def horizontal(before, here, after):
    total = taps[4] * here
    for step in range(1, 5):
        pair = moved(before, here, after, step) + moved(before, here, after, -step)
        total = total + taps[4 - step] * pair
    return total


def halves(value):
    high = value.astype(jnp.bfloat16)
    low = (value - high.astype(jnp.float32)).astype(jnp.bfloat16)
    return high, low


def by_row_shift(value, rows, direction):
    place = lax.broadcasted_iota(jnp.int32, value.shape, 0) % rows
    unit = 1
    while unit < rows:
        digit = (place // unit) % 4
        result = value
        for times in range(1, 4):
            amount = times * unit
            turned = pltpu.roll(value, amount if direction > 0 else lanes - amount, 1)
            result = jnp.where(digit == times, turned, result)
        value = result
        unit *= 4
    return value


def at_edge():
    index = lax.axis_index("rows")
    return (index == 0) | (index == lax.axis_size("rows") - 1)


def cut_kernel(base, frames, raw, frames_odd, frames_even, offsets, arrived):
    count, rows, columns = raw.shape
    tiles = columns // lanes
    odd = lax.axis_index("rows") % 2 == 1
    copies = [pltpu.make_async_copy(frames.at[f], raw.at[f], arrived.at[f]) for f in range(count)]
    copies.append(pltpu.make_async_copy(base, offsets, arrived.at[count]))
    for copy in copies:
        copy.start()
    for copy in copies:
        copy.wait()

    def step(t, carry):
        at = tile_of(t)
        for f in range(count):
            low = raw[f, 0:4, at]
            high = raw[f, rows - 4 : rows, at]
            frames_odd[f, :, at] = jnp.where(odd, high, low)
            frames_even[f, :, at] = jnp.where(odd, low, high)
        return carry

    by_tiles(step, tiles, 16)


def smooth_kernel(frames, from_odd, from_even, inverse, stack, power, rows_in, half, fine):
    count, rows, columns = frames.shape
    tiles = columns // lanes
    ring = tiles + 2
    odd = lax.axis_index("rows") % 2 == 1
    edge = at_edge()
    zero = jnp.zeros((rows, lanes), jnp.float32)
    for f in range(count):
        half[f, 0] = zero
        half[f, tiles + 1] = zero
    blank = jnp.zeros((count * rows, lanes), jnp.float32)
    fine[0] = blank
    fine[tiles + 1] = blank
    fine[tiles + 2] = blank

    def load_step(t, carry):
        for f in range(count):
            outer = jnp.where(edge, 0.0, from_odd[f, :, tile_of(t)])
            inner = from_even[f, :, tile_of(t)]
            rows_in[f, t, 4:8, :] = jnp.where(odd, inner, outer)
            rows_in[f, t, 8 : 8 + rows, :] = frames[f, :, tile_of(t)]
            rows_in[f, t, 8 + rows : 12 + rows, :] = jnp.where(odd, outer, inner)
        return carry

    def vertical_step(t, carry):
        for f in range(count):
            half[f, t + 1] = vertical(lambda s: rows_in[f, t, pl.ds(4 + s, rows), :])
        return carry

    def horizontal_step(t, totals):
        result = []
        for f in range(count):
            smooth = horizontal(half[f, t], half[f, t + 1], half[f, t + 2])
            inverse[f, :, tile_of(t)] = 1.0 / smooth
            detail = frames[f, :, tile_of(t)] - smooth
            fine[t + 1, f * rows : (f + 1) * rows, :] = detail
            result.append(totals[f] + fold(detail * detail))
        return tuple(result)

    def stack_step(t, carry):
        before, here, after = fine[t], fine[t + 1], fine[t + 2]
        for j in range(reach):
            high, low = halves(moved(before, here, after, 3 - j))
            size = count * rows
            stack[j * size : (j + 1) * size, tile_of(t)] = high
            stack[(reach + j) * size : (reach + j + 1) * size, tile_of(t)] = low
        return carry

    by_tiles(load_step, tiles, 8)
    by_tiles(vertical_step, tiles, 8)
    powers = by_tiles(horizontal_step, tiles, 8, (jnp.zeros((8, lanes), jnp.float32),) * count)
    for f in range(count):
        power[f * 8 : f * 8 + 8, :] = powers[f]
    fine[tiles + 3] = fine[1]
    by_tiles(stack_step, ring, ring // 2)


def column_shift(offset):
    negative = offset < 0
    first = jnp.where(negative, 0, 1)
    amount = jnp.where(negative, offset + lanes, offset)
    back = lax.rem(lanes - amount, lanes)

    def shift(source, t):
        here = source[t + first]
        after = source[t + first + 1]
        value = pltpu.roll(jnp.where(lane_of(here.shape) < amount, after, here), back, 1)
        spare = jnp.zeros((slot - value.shape[0], lanes), jnp.float32)
        return jnp.concatenate([value, spare], axis=0)

    return shift


def match_kernel(
    base, own_odd, own_even, from_odd, from_even, stack, power, clean, part, rows_in, half, fine, stream
):
    rows = own_odd.shape[0] * 2
    tiles = own_odd.shape[1] // lanes
    count = power.shape[0] // 8
    ring = tiles + 2
    wide = rows + 8
    row_index = lax.axis_index("rows")
    last_row = lax.axis_size("rows") - 1
    odd = row_index % 2 == 1
    edge = at_edge()
    blank = jnp.zeros((wide, lanes), jnp.float32)
    half[0] = blank
    half[tiles + 1] = blank
    clean[0] = blank
    clean[tiles + 1] = blank
    fine[0] = blank
    fine[tiles + 1] = blank
    fine[tiles + 2] = blank
    place = lax.broadcasted_iota(jnp.int32, (wide, lanes), 0)
    inside = ((place >= 4) | (row_index > 0)) & ((place < rows + 4) | (row_index < last_row))

    def load_step(t, carry):
        outer = [jnp.where(edge, 0.0, from_odd[:, tile_of(t)]), own_odd[:, tile_of(t)]]
        inner = [array[:, tile_of(t)] for array in (own_even, from_even)]
        rows_in[t, 0:8, :] = jnp.where(odd, inner[1], outer[0])
        rows_in[t, 8:16, :] = jnp.where(odd, inner[0], outer[1])
        rows_in[t, 16:24, :] = jnp.where(odd, outer[1], inner[0])
        rows_in[t, 24:32, :] = jnp.where(odd, outer[0], inner[1])
        return carry

    def vertical_step(t, carry):
        half[t + 1] = vertical(lambda s: rows_in[t, pl.ds(s, wide), :])
        return carry

    def horizontal_step(t, total):
        smooth = jnp.where(inside, horizontal(half[t], half[t + 1], half[t + 2]), 0.0)
        clean[t + 1] = smooth
        detail = rows_in[t, pl.ds(4, wide), :] - smooth
        fine[t + 1] = detail
        own = jnp.where((place >= 4) & (place < rows + 4), detail, 0.0)
        return total + fold(own * own)

    by_tiles(load_step, tiles, 8)
    by_tiles(vertical_step, tiles, 8)
    ref_power = by_tiles(horizontal_step, tiles, 8, jnp.zeros((8, lanes), jnp.float32))
    fine[tiles + 3] = fine[1]
    shift = column_shift(base[0, 1])
    stream[2 * slot : 4 * slot, :] = jnp.zeros((2 * slot, ring * lanes), jnp.bfloat16)

    def stream_step(t, carry):
        high, low = halves(shift(fine, t))
        stream[0:slot, tile_of(t)] = high
        stream[slot : 2 * slot, tile_of(t)] = low
        return carry

    by_tiles(stream_step, ring, ring // 2)
    product = lax.dot_general(
        stack[...], stream[...], (((1,), (1,)), ((), ())), preferred_element_type=jnp.float32
    )
    size = reach * count * rows
    product = product[:size] + product[size:]
    product = by_row_shift(product, rows, -1)
    part[...] = jnp.zeros(part.shape, jnp.float32)
    for j in range(reach):
        for f in range(count):
            start = (j * count + f) * rows
            part[f * 8 + j : f * 8 + j + 1, :] = jnp.sum(product[start : start + rows], axis=0, keepdims=True)
    lags = part[0 : 8 * count, :]
    back = lanes - 1 - base[0, 0]
    lags = pltpu.roll(lags, lax.rem(back, lanes), 1) + pltpu.roll(lags, lax.rem(back + lanes - slot, lanes), 1)
    part[0 : 8 * count, :] = jnp.where(lane_of(lags.shape) < reach, lags, 0.0)
    start = 8 * count
    for f in range(count):
        part[start + f : start + f + 1, :] = jnp.sum(power[f * 8 : f * 8 + 8, :], axis=0, keepdims=True)
    part[start + count : start + count + 1, :] = jnp.sum(ref_power, axis=0, keepdims=True)
    powers = part[start : start + 8, :]
    part[start : start + 8, :] = jnp.broadcast_to(jnp.sum(powers, axis=1, keepdims=True), powers.shape)


def spread_kernel(base, clean, spread):
    tiles = clean.shape[0] - 2
    full = spread.shape[0] // 2
    spare = jnp.zeros((full - reach * slot, tiles * lanes), jnp.bfloat16)
    spread[reach * slot : full, :] = spare
    spread[full + reach * slot : 2 * full, :] = spare

    def per_offset(j, carry):
        shift = column_shift(base[0, 1] + j - 3)
        at = pl.multiple_of(j * slot, slot)

        def step(t, inner):
            high, low = halves(shift(clean, t))
            spread[pl.ds(at, slot), tile_of(t)] = high
            spread[pl.ds(full + at, slot), tile_of(t)] = low
            return inner

        by_tiles(step, tiles, 32)
        return carry

    lax.fori_loop(0, reach, per_offset, 0)


def blend_weights(matches, frame_power, ref_power):
    norm_product = jnp.sqrt((frame_power + 1e-06) * (ref_power + 1e-06))
    rho = matches / norm_product
    squared = rho * rho
    total = jnp.sum(jnp.sum(squared, axis=0, keepdims=True), axis=1, keepdims=True)
    across = lax.broadcasted_iota(jnp.int32, matches.shape, 0)
    middle = (across == reach // 2) & (lane_of(matches.shape) == reach // 2)
    return (squared + jnp.where(middle, 0.05, 0.0)) / (0.05 + total)


def banded(weights, rows, first_row):
    across = lax.broadcasted_iota(jnp.int32, weights.shape, 0)
    spaced = jnp.zeros_like(weights)
    for times in range(4):
        turned = pltpu.roll(weights, first_row + times * slot, 1)
        spaced = jnp.where(across % 4 == times, turned, spaced)
    tiles = []
    for member in (across < 4, across >= 4):
        line = jnp.sum(jnp.where(member, spaced, 0.0), axis=0, keepdims=True)
        tiles.append(by_row_shift(jnp.broadcast_to(line, (rows, lanes)), rows, 1))
    return jnp.concatenate(tiles, axis=1)


def pressure_kernel(base, parts, spread, inverse, pressure, moments, part):
    count, rows, columns = inverse.shape
    start = 8 * count
    full = spread.shape[0] // 2
    first_row = 1 + base[0, 0]
    ref_power = parts[start + count : start + count + 1, :]
    bands = []
    for f in range(count):
        weights = blend_weights(parts[f * 8 : f * 8 + 8, :], parts[start + f : start + f + 1, :], ref_power)
        bands.append(banded(weights, rows, first_row))
    mixing = jnp.concatenate(halves(jnp.concatenate(bands, axis=0)), axis=0)
    chunk = 2 * lanes
    zero = jnp.zeros((8, lanes), jnp.float32)
    size = count * rows

    def step(t, totals):
        where = pl.ds(pl.multiple_of(t * chunk, chunk), chunk)
        product = jnp.dot(mixing, spread[0:full, where], preferred_element_type=jnp.float32)
        product = product + jnp.dot(mixing, spread[full : 2 * full, where], preferred_element_type=jnp.float32)
        registered = product[:size] + product[size:]
        first = second = None
        totals = list(totals)
        for f in range(count):
            ratio = registered[f * rows : (f + 1) * rows] * inverse[f, :, where]
            value = calib_zero + ratio * (calib_linear + calib_square * ratio)
            squared = value * value
            pressure[f, :, where] = value
            first = value if first is None else first + value
            second = squared if second is None else second + squared
            for total, array in ((f, value), (count + f, squared)):
                for c in range(chunk // lanes):
                    totals[total] = totals[total] + fold(array[:, c * lanes : (c + 1) * lanes])
        moments[0, :, where] = first
        moments[1, :, where] = second
        return tuple(totals)

    totals = by_tiles(step, columns // chunk, 8, (zero,) * (2 * count))
    part[...] = jnp.zeros(part.shape, jnp.float32)
    for k in range(2 * count):
        part[k : k + 1, :] = jnp.sum(totals[k], axis=0, keepdims=True)


def paired(value, axis, first):
    size = lax.axis_size(axis)
    partner = list(range(size))
    for i in range(first, size - 1, 2):
        partner[i], partner[i + 1] = i + 1, i
    return lax.ppermute(value, axis, list(enumerate(partner)))


def by_parity(odd, array, height, dim):
    length = array.shape[dim]
    low = lax.slice_in_dim(array, 0, height, axis=dim)
    high = lax.slice_in_dim(array, length - height, length, axis=dim)
    return jnp.where(odd, high, low), jnp.where(odd, low, high)


def from_owner(shard, odd, axis, root):
    mine = lax.axis_index(axis) == root
    if lax.axis_size(axis) == 2:
        halves_here = lax.optimization_barrier(by_parity(odd, shard, shard.shape[0] // 2, 0))
        received = by_parity(odd, paired(shard, axis, 0), shard.shape[0] // 2, 0)
        return [jnp.where(mine, own, other) for own, other in zip(halves_here, received)]
    whole = lax.psum(jnp.where(mine, shard, jnp.zeros_like(shard)), axis)
    return by_parity(odd, whole, shard.shape[0] // 2, 0)


def total_over_rows(value, odd):
    size = lax.axis_size("rows")
    if size & (size - 1) or size < 2:
        return lax.psum(value, "rows")
    value = value + paired(value, "rows", 0)
    step = 2
    while step < size:
        pairs = [(i, i ^ step if i % 2 else i) for i in range(size)]
        value = value + lax.ppermute(value, "rows", pairs)
        step *= 2
    return jnp.where(odd, value, paired(value, "rows", 0))


def total_over(value, axis):
    size = lax.axis_size(axis)
    if size & (size - 1):
        return lax.psum(value, axis)
    step = 1
    while step < size:
        value = value + lax.ppermute(value, axis, [(i, i ^ step) for i in range(size)])
        step *= 2
    return value


def shards(frames_raw, wind_off, run_owner, search_base):
    count, rows, columns = frames_raw.shape
    tiles = columns // lanes
    ring = tiles + 2
    wide = rows + 8
    depth = reach * count * rows
    f32 = jnp.float32
    bf16 = jnp.bfloat16
    struct = functools.partial(jax.ShapeDtypeStruct, dtype=f32)
    odd = lax.axis_index("rows") % 2 == 1
    own_odd, own_even = from_owner(wind_off[0], odd, "frames", run_owner[0])
    raw, frames_odd, frames_even, offsets = pl.pallas_call(
        cut_kernel,
        out_shape=(
            struct((count, rows, columns)),
            struct((count, 4, columns)),
            struct((count, 4, columns)),
            jax.ShapeDtypeStruct((1, 2), jnp.int32),
        ),
        in_specs=[pl.BlockSpec(memory_space=pl.ANY)] * 2,
        out_specs=(vmem,) * 3 + (smem,),
        scratch_shapes=[pltpu.SemaphoreType.DMA((count + 1,))],
        compiler_params=params,
        name="cut",
    )(search_base, frames_raw)
    frames_odd = paired(frames_odd, "rows", 1)
    frames_even = paired(frames_even, "rows", 0)
    from_even = paired(own_even, "rows", 0)
    from_odd = paired(own_odd, "rows", 1)
    inverse, stack, power = pl.pallas_call(
        smooth_kernel,
        out_shape=(
            struct((count, rows, columns)),
            jax.ShapeDtypeStruct((2 * depth, ring * lanes), bf16),
            struct((8 * count, lanes)),
        ),
        in_specs=[vmem] * 3,
        out_specs=(vmem,) * 3,
        scratch_shapes=[
            pltpu.VMEM((count, tiles, rows + 16, lanes), f32),
            pltpu.VMEM((count, tiles + 2, rows, lanes), f32),
            pltpu.VMEM((ring + 2, count * rows, lanes), f32),
        ],
        compiler_params=params,
        name="smooth",
    )(raw, frames_odd, frames_even)
    clean, part = pl.pallas_call(
        match_kernel,
        out_shape=(struct((tiles + 2, wide, lanes)), struct((8 * count + 8, lanes))),
        in_specs=[smem] + [vmem] * 6,
        out_specs=(vmem, vmem),
        scratch_shapes=[
            pltpu.VMEM((tiles, rows + 16, lanes), f32),
            pltpu.VMEM((tiles + 2, wide, lanes), f32),
            pltpu.VMEM((ring + 2, wide, lanes), f32),
            pltpu.VMEM((4 * slot, ring * lanes), bf16),
        ],
        compiler_params=params,
        name="match",
    )(offsets, own_odd, own_even, from_odd, from_even, stack, power)
    parts = total_over_rows(part, odd)
    spread = pl.pallas_call(
        spread_kernel,
        out_shape=jax.ShapeDtypeStruct((2 * 8 * slot, columns), bf16),
        in_specs=[smem, vmem],
        out_specs=vmem,
        compiler_params=params,
        name="spread",
    )(offsets, clean)
    pressure, moments, part = pl.pallas_call(
        pressure_kernel,
        out_shape=(struct((count, rows, columns)), struct((2, rows, columns)), struct((8, lanes))),
        in_specs=[smem] + [vmem] * 3,
        out_specs=(vmem, vmem, vmem),
        compiler_params=params,
        name="pressure",
    )(offsets, parts, spread, inverse)
    whole = total_over(moments, "frames")
    spatial = jnp.sum(total_over_rows(part, odd), axis=1)
    cell_count = rows * columns * lax.axis_size("rows")
    frame_mean = spatial[:count] / cell_count
    frame_rms = jnp.sqrt(spatial[count : 2 * count] / cell_count - frame_mean * frame_mean)
    total_frames = count * lax.axis_size("frames")
    time_mean = whole[0] / total_frames
    time_rms = jnp.sqrt(jnp.maximum(whole[1] / total_frames - time_mean * time_mean, 0.0))
    return (pressure, frame_mean, frame_rms, time_mean, time_rms)


def solution(mesh):
    placed = (P("frames", "rows", None), P("frames", "rows", None), P("rows"), P("frames", None))
    return jax.shard_map(
        shards,
        mesh=mesh,
        in_specs=placed,
        out_specs=(
            P("frames", "rows", None),
            P("frames"),
            P("frames"),
            P("rows", None),
            P("rows", None),
        ),
        check_vma=False,
    )
```

```python
import functools

import jax
import jax.numpy as jnp
from jax import lax
from jax.experimental import pallas as pl
from jax.experimental.pallas import tpu as pltpu
from jax.sharding import PartitionSpec as P

taps = (1.0 / 256, 8.0 / 256, 28.0 / 256, 56.0 / 256, 70.0 / 256)
calib_zero = -0.25
calib_linear = 1.0
calib_square = 0.15
lanes = 128
reach = 7
slot = 32
params = pltpu.CompilerParams(vmem_limit_bytes=24 * 1024 * 1024)
vmem = pl.BlockSpec(memory_space=pltpu.VMEM)
smem = pl.BlockSpec(memory_space=pltpu.SMEM)


def tile_of(index):
    return pl.ds(pl.multiple_of(index * lanes, lanes), lanes)


def by_tiles(step, tiles, group, init=()):
    def body(index, carry):
        for inner in range(group):
            carry = step(index * group + inner, carry)
        return carry

    return lax.fori_loop(0, tiles // group, body, init)


def lane_of(shape):
    return lax.broadcasted_iota(jnp.int32, shape, len(shape) - 1)


def fold(product):
    return jnp.sum(product.reshape(product.shape[0] // 8, 8, lanes), axis=0)


def vertical(load):
    total = taps[4] * load(4)
    for step in range(4):
        total = total + taps[step] * (load(step) + load(8 - step))
    return total


def moved(before, here, after, step):
    if step > 0:
        return pltpu.roll(jnp.where(lane_of(here.shape) < step, after, here), lanes - step, 1)
    if step < 0:
        return pltpu.roll(jnp.where(lane_of(here.shape) >= lanes + step, before, here), -step, 1)
    return here


def horizontal(before, here, after):
    total = taps[4] * here
    for step in range(1, 5):
        pair = moved(before, here, after, step) + moved(before, here, after, -step)
        total = total + taps[4 - step] * pair
    return total


def halves(value):
    high = value.astype(jnp.bfloat16)
    low = (value - high.astype(jnp.float32)).astype(jnp.bfloat16)
    return high, low


def by_row_shift(value, rows, direction):
    place = lax.broadcasted_iota(jnp.int32, value.shape, 0) % rows
    unit = 1
    while unit < rows:
        digit = (place // unit) % 4
        result = value
        for times in range(1, 4):
            amount = times * unit
            turned = pltpu.roll(value, amount if direction > 0 else lanes - amount, 1)
            result = jnp.where(digit == times, turned, result)
        value = result
        unit *= 4
    return value


def at_edge():
    index = lax.axis_index("rows")
    return (index == 0) | (index == lax.axis_size("rows") - 1)


def smooth_kernel(frames, from_odd, from_even, inverse, stack, power, rows_in, half, fine):
    count, rows, columns = frames.shape
    tiles = columns // lanes
    ring = tiles + 2
    odd = lax.axis_index("rows") % 2 == 1
    edge = at_edge()
    zero = jnp.zeros((rows, lanes), jnp.float32)
    for f in range(count):
        half[f, 0] = zero
        half[f, tiles + 1] = zero
    blank = jnp.zeros((count * rows, lanes), jnp.float32)
    fine[0] = blank
    fine[tiles + 1] = blank
    fine[tiles + 2] = blank

    def load_step(t, carry):
        for f in range(count):
            outer = jnp.where(edge, 0.0, from_odd[f, :, tile_of(t)])
            inner = from_even[f, :, tile_of(t)]
            rows_in[f, t, 4:8, :] = jnp.where(odd, inner, outer)
            rows_in[f, t, 8 : 8 + rows, :] = frames[f, :, tile_of(t)]
            rows_in[f, t, 8 + rows : 12 + rows, :] = jnp.where(odd, outer, inner)
        return carry

    def vertical_step(t, carry):
        for f in range(count):
            half[f, t + 1] = vertical(lambda s: rows_in[f, t, pl.ds(4 + s, rows), :])
        return carry

    def horizontal_step(t, totals):
        result = []
        for f in range(count):
            smooth = horizontal(half[f, t], half[f, t + 1], half[f, t + 2])
            inverse[f, :, tile_of(t)] = 1.0 / smooth
            detail = frames[f, :, tile_of(t)] - smooth
            fine[t + 1, f * rows : (f + 1) * rows, :] = detail
            result.append(totals[f] + fold(detail * detail))
        return tuple(result)

    def stack_step(t, carry):
        before, here, after = fine[t], fine[t + 1], fine[t + 2]
        for j in range(reach):
            high, low = halves(moved(before, here, after, 3 - j))
            size = count * rows
            stack[j * size : (j + 1) * size, tile_of(t)] = high
            stack[(reach + j) * size : (reach + j + 1) * size, tile_of(t)] = low
        return carry

    by_tiles(load_step, tiles, 8)
    by_tiles(vertical_step, tiles, 8)
    powers = by_tiles(horizontal_step, tiles, 8, (jnp.zeros((8, lanes), jnp.float32),) * count)
    for f in range(count):
        power[f * 8 : f * 8 + 8, :] = powers[f]
    fine[tiles + 3] = fine[1]
    by_tiles(stack_step, ring, ring // 2)


def column_shift(offset):
    negative = offset < 0
    first = jnp.where(negative, 0, 1)
    amount = jnp.where(negative, offset + lanes, offset)
    back = lax.rem(lanes - amount, lanes)

    def shift(source, t):
        here = source[t + first]
        after = source[t + first + 1]
        value = pltpu.roll(jnp.where(lane_of(here.shape) < amount, after, here), back, 1)
        spare = jnp.zeros((slot - value.shape[0], lanes), jnp.float32)
        return jnp.concatenate([value, spare], axis=0)

    return shift


def match_kernel(
    base, own_odd, own_even, from_odd, from_even, stack, power, clean, part, rows_in, half, fine, stream, lags
):
    rows = own_odd.shape[0] * 2
    tiles = own_odd.shape[1] // lanes
    count = power.shape[0] // 8
    ring = tiles + 2
    wide = rows + 8
    row_index = lax.axis_index("rows")
    last_row = lax.axis_size("rows") - 1
    odd = row_index % 2 == 1
    edge = at_edge()
    blank = jnp.zeros((wide, lanes), jnp.float32)
    half[0] = blank
    half[tiles + 1] = blank
    clean[0] = blank
    clean[tiles + 1] = blank
    fine[0] = blank
    fine[tiles + 1] = blank
    fine[tiles + 2] = blank
    place = lax.broadcasted_iota(jnp.int32, (wide, lanes), 0)
    inside = ((place >= 4) | (row_index > 0)) & ((place < rows + 4) | (row_index < last_row))

    def load_step(t, carry):
        outer = [jnp.where(edge, 0.0, from_odd[:, tile_of(t)]), own_odd[:, tile_of(t)]]
        inner = [array[:, tile_of(t)] for array in (own_even, from_even)]
        rows_in[t, 0:8, :] = jnp.where(odd, inner[1], outer[0])
        rows_in[t, 8:16, :] = jnp.where(odd, inner[0], outer[1])
        rows_in[t, 16:24, :] = jnp.where(odd, outer[1], inner[0])
        rows_in[t, 24:32, :] = jnp.where(odd, outer[0], inner[1])
        return carry

    def vertical_step(t, carry):
        half[t + 1] = vertical(lambda s: rows_in[t, pl.ds(s, wide), :])
        return carry

    def horizontal_step(t, total):
        smooth = jnp.where(inside, horizontal(half[t], half[t + 1], half[t + 2]), 0.0)
        clean[t + 1] = smooth
        detail = rows_in[t, pl.ds(4, wide), :] - smooth
        fine[t + 1] = detail
        own = jnp.where((place >= 4) & (place < rows + 4), detail, 0.0)
        return total + fold(own * own)

    by_tiles(load_step, tiles, 8)
    by_tiles(vertical_step, tiles, 8)
    ref_power = by_tiles(horizontal_step, tiles, 8, jnp.zeros((8, lanes), jnp.float32))
    fine[tiles + 3] = fine[1]
    shift = column_shift(base[0, 1])
    stream[2 * slot : 4 * slot, :] = jnp.zeros((2 * slot, ring * lanes), jnp.bfloat16)

    def stream_step(t, carry):
        high, low = halves(shift(fine, t))
        stream[0:slot, tile_of(t)] = high
        stream[slot : 2 * slot, tile_of(t)] = low
        return carry

    by_tiles(stream_step, ring, ring // 2)
    product = lax.dot_general(
        stack[...], stream[...], (((1,), (1,)), ((), ())), preferred_element_type=jnp.float32
    )
    size = reach * count * rows
    product = product[:size] + product[size:]
    product = by_row_shift(product, rows, -1)
    lags[...] = jnp.zeros(lags.shape, jnp.float32)
    for j in range(reach):
        for f in range(count):
            start = (j * count + f) * rows
            lags[f * 8 + j : f * 8 + j + 1, :] = jnp.sum(product[start : start + rows], axis=0, keepdims=True)
    back = 2 * lanes - 1 - base[0, 0]
    across = lax.broadcasted_iota(jnp.int32, (8, lanes), 0)
    lane = lane_of((8, lanes))
    packed = jnp.zeros((8, lanes), jnp.float32)
    for f in range(count):
        block = lags[f * 8 : f * 8 + 8, :]
        for j in range(reach):
            at = (f * reach + j) * reach
            high = pltpu.roll(block, lax.rem(back + at, lanes), 1)
            low = pltpu.roll(block, lax.rem(back + at + lanes - slot, lanes), 1)
            packed = packed + jnp.where((across == j) & (lane >= at) & (lane < at + reach), high + low, 0.0)
    lags[0:8, :] = jnp.zeros((8, lanes), jnp.float32)
    for f in range(count):
        lags[f : f + 1, :] = jnp.sum(power[f * 8 : f * 8 + 8, :], axis=0, keepdims=True)
    lags[count : count + 1, :] = jnp.sum(ref_power, axis=0, keepdims=True)
    powers = jnp.sum(lags[0:8, :], axis=1, keepdims=True)
    packed = packed + jnp.where(lane == count * reach * reach + across, powers, 0.0)
    part[...] = jnp.broadcast_to(jnp.sum(packed, axis=0, keepdims=True), part.shape)


def spread_kernel(base, clean, spread):
    tiles = clean.shape[0] - 2
    full = spread.shape[0] // 2
    spare = jnp.zeros((full - reach * slot, tiles * lanes), jnp.bfloat16)
    spread[reach * slot : full, :] = spare
    spread[full + reach * slot : 2 * full, :] = spare

    def per_offset(j, carry):
        shift = column_shift(base[0, 1] + j - 3)
        at = pl.multiple_of(j * slot, slot)

        def step(t, inner):
            high, low = halves(shift(clean, t))
            spread[pl.ds(at, slot), tile_of(t)] = high
            spread[pl.ds(full + at, slot), tile_of(t)] = low
            return inner

        by_tiles(step, tiles, 32)
        return carry

    lax.fori_loop(0, reach, per_offset, 0)


def blend_weights(totals, count):
    lane = lane_of(totals.shape)
    block = reach * reach

    def pick(index):
        return jnp.sum(jnp.where(lane == index, totals, 0.0), axis=1, keepdims=True)

    ref_power = pick(count * block + count)
    weights = []
    for f in range(count):
        norm_product = jnp.sqrt((pick(count * block + f) + 1e-06) * (ref_power + 1e-06))
        member = (lane >= f * block) & (lane < (f + 1) * block)
        rho = jnp.where(member, totals, 0.0) / norm_product
        squared = rho * rho
        middle = jnp.where(lane == f * block + block // 2, 0.05, 0.0)
        weights.append((squared + middle) / (0.05 + jnp.sum(squared, axis=1, keepdims=True)))
    return weights


def banded(weights, f, rows, first_row):
    lane = lane_of(weights.shape)
    tiles = []
    for group in (range(4), range(4, reach)):
        line = jnp.zeros_like(weights)
        for j in group:
            at = first_row + (j % 4) * slot
            turned = pltpu.roll(weights, lax.rem(at + 2 * lanes - (f * reach + j) * reach, lanes), 1)
            line = jnp.where((lane >= at) & (lane < at + reach), turned, line)
        line = jnp.broadcast_to(line[0:1], (rows, lanes))
        tiles.append(by_row_shift(line, rows, 1))
    return jnp.concatenate(tiles, axis=1)


def pressure_kernel(base, parts, spread, inverse, pressure, moments, part):
    count, rows, columns = inverse.shape
    full = spread.shape[0] // 2
    first_row = 1 + base[0, 0]
    totals = jnp.broadcast_to(jnp.sum(parts[...], axis=0, keepdims=True), (8, lanes))
    weights = blend_weights(totals, count)
    bands = [banded(weights[f], f, rows, first_row) for f in range(count)]
    mixing = jnp.concatenate(halves(jnp.concatenate(bands, axis=0)), axis=0)
    chunk = 2 * lanes
    zero = jnp.zeros((8, lanes), jnp.float32)
    size = count * rows

    def step(t, totals):
        where = pl.ds(pl.multiple_of(t * chunk, chunk), chunk)
        product = jnp.dot(mixing, spread[0:full, where], preferred_element_type=jnp.float32)
        product = product + jnp.dot(mixing, spread[full : 2 * full, where], preferred_element_type=jnp.float32)
        registered = product[:size] + product[size:]
        first = second = None
        totals = list(totals)
        for f in range(count):
            ratio = registered[f * rows : (f + 1) * rows] * inverse[f, :, where]
            value = calib_zero + ratio * (calib_linear + calib_square * ratio)
            squared = value * value
            pressure[f, :, where] = value
            first = value if first is None else first + value
            second = squared if second is None else second + squared
            for total, array in ((f, value), (count + f, squared)):
                for c in range(chunk // lanes):
                    totals[total] = totals[total] + fold(array[:, c * lanes : (c + 1) * lanes])
        moments[0, :, where] = first
        moments[1, :, where] = second
        return tuple(totals)

    totals = by_tiles(step, columns // chunk, 8, (zero,) * (2 * count))
    line = jnp.zeros((8, lanes), jnp.float32)
    for k in range(2 * count):
        value = jnp.sum(jnp.sum(totals[k], axis=0, keepdims=True), axis=1, keepdims=True)
        line = line + jnp.where(lane_of(line.shape) == k, value, 0.0)
    part[...] = jnp.broadcast_to(line[0:1], part.shape)


def paired(value, axis, first):
    size = lax.axis_size(axis)
    partner = list(range(size))
    for i in range(first, size - 1, 2):
        partner[i], partner[i + 1] = i + 1, i
    return lax.ppermute(value, axis, list(enumerate(partner)))


def by_parity(odd, array, height, dim):
    length = array.shape[dim]
    low = lax.slice_in_dim(array, 0, height, axis=dim)
    high = lax.slice_in_dim(array, length - height, length, axis=dim)
    return jnp.where(odd, high, low), jnp.where(odd, low, high)


def from_owner(shard, odd, axis, root):
    mine = lax.axis_index(axis) == root
    height = shard.shape[0] // 2
    if lax.axis_size(axis) != 2:
        whole = lax.psum(jnp.where(mine, shard, jnp.zeros_like(shard)), axis)
        return by_parity(odd, whole, height, 0)
    here = lax.optimization_barrier(jnp.maximum(shard, 0.0))
    odd_here, even_here = by_parity(odd, here, height, 0)
    odd_there = paired(odd_here, axis, 0)
    even_here, odd_there = lax.optimization_barrier((even_here, odd_there))
    even_there = paired(even_here, axis, 0)
    return jnp.where(mine, odd_here, odd_there), jnp.where(mine, even_here, even_there)


def total_over(value, axis):
    size = lax.axis_size(axis)
    if size & (size - 1):
        return lax.psum(value, axis)
    step = 1
    while step < size:
        value = value + lax.ppermute(value, axis, [(i, i ^ step) for i in range(size)])
        step *= 2
    return value


def shards(frames_raw, wind_off, run_owner, search_base):
    count, rows, columns = frames_raw.shape
    tiles = columns // lanes
    ring = tiles + 2
    wide = rows + 8
    depth = reach * count * rows
    size = lax.axis_size("rows")
    f32 = jnp.float32
    bf16 = jnp.bfloat16
    struct = functools.partial(jax.ShapeDtypeStruct, dtype=f32)
    odd = lax.axis_index("rows") % 2 == 1
    own_odd, own_even = from_owner(wind_off[0], odd, "frames", run_owner[0])
    raw = lax.optimization_barrier(jnp.maximum(frames_raw, 0.0))
    offsets = jnp.clip(search_base, -8, 8)
    frames_odd, frames_even = by_parity(odd, raw, 4, 1)
    frames_odd = paired(frames_odd, "rows", 1)
    frames_even = paired(frames_even, "rows", 0)
    from_even = paired(own_even, "rows", 0)
    from_odd = paired(own_odd, "rows", 1)
    inverse, stack, power = pl.pallas_call(
        smooth_kernel,
        out_shape=(
            struct((count, rows, columns)),
            jax.ShapeDtypeStruct((2 * depth, ring * lanes), bf16),
            struct((8 * count, lanes)),
        ),
        in_specs=[vmem] * 3,
        out_specs=(vmem,) * 3,
        scratch_shapes=[
            pltpu.VMEM((count, tiles, rows + 16, lanes), f32),
            pltpu.VMEM((count, tiles + 2, rows, lanes), f32),
            pltpu.VMEM((ring + 2, count * rows, lanes), f32),
        ],
        compiler_params=params,
        name="smooth",
    )(raw, frames_odd, frames_even)
    clean, part = pl.pallas_call(
        match_kernel,
        out_shape=(struct((tiles + 2, wide, lanes)), struct((size, lanes))),
        in_specs=[smem] + [vmem] * 6,
        out_specs=(vmem, vmem),
        scratch_shapes=[
            pltpu.VMEM((tiles, rows + 16, lanes), f32),
            pltpu.VMEM((tiles + 2, wide, lanes), f32),
            pltpu.VMEM((ring + 2, wide, lanes), f32),
            pltpu.VMEM((4 * slot, ring * lanes), bf16),
            pltpu.VMEM((8 * count, lanes), f32),
        ],
        compiler_params=params,
        name="match",
    )(offsets, own_odd, own_even, from_odd, from_even, stack, power)
    parts = lax.all_to_all(part, "rows", 0, 0, tiled=True)
    spread = pl.pallas_call(
        spread_kernel,
        out_shape=jax.ShapeDtypeStruct((2 * 8 * slot, columns), bf16),
        in_specs=[smem, vmem],
        out_specs=vmem,
        compiler_params=params,
        name="spread",
    )(offsets, clean)
    pressure, moments, part = pl.pallas_call(
        pressure_kernel,
        out_shape=(struct((count, rows, columns)), struct((2, rows, columns)), struct((size, lanes))),
        in_specs=[smem] + [vmem] * 3,
        out_specs=(vmem, vmem, vmem),
        compiler_params=params,
        name="pressure",
    )(offsets, parts, spread, inverse)
    whole = total_over(moments, "frames")
    spatial = jnp.sum(lax.all_to_all(part, "rows", 0, 0, tiled=True), axis=0)
    cell_count = rows * columns * size
    frame_mean = spatial[:count] / cell_count
    frame_rms = jnp.sqrt(spatial[count : 2 * count] / cell_count - frame_mean * frame_mean)
    total_frames = count * lax.axis_size("frames")
    time_mean = whole[0] / total_frames
    time_rms = jnp.sqrt(jnp.maximum(whole[1] / total_frames - time_mean * time_mean, 0.0))
    return (pressure, frame_mean, frame_rms, time_mean, time_rms)


def solution(mesh):
    placed = (P("frames", "rows", None), P("frames", "rows", None), P("rows"), P("frames", None))
    return jax.shard_map(
        shards,
        mesh=mesh,
        in_specs=placed,
        out_specs=(
            P("frames", "rows", None),
            P("frames"),
            P("frames"),
            P("rows", None),
            P("rows", None),
        ),
        check_vma=False,
    )
```

```python
import functools

import jax
import jax.numpy as jnp
from jax import lax
from jax.experimental import pallas as pl
from jax.experimental.pallas import tpu as pltpu
from jax.sharding import PartitionSpec as P

taps = (1.0 / 256, 8.0 / 256, 28.0 / 256, 56.0 / 256, 70.0 / 256)
calib_zero = -0.25
calib_linear = 1.0
calib_square = 0.15
lanes = 128
reach = 7
slot = 32
params = pltpu.CompilerParams(vmem_limit_bytes=14 * 1024 * 1024)
vmem = pl.BlockSpec(memory_space=pltpu.VMEM)
smem = pl.BlockSpec(memory_space=pltpu.SMEM)


def tile_of(index):
    return pl.ds(pl.multiple_of(index * lanes, lanes), lanes)


def by_tiles(step, tiles, group, init=()):
    def body(index, carry):
        for inner in range(group):
            carry = step(index * group + inner, carry)
        return carry

    return lax.fori_loop(0, tiles // group, body, init)


def lane_of(shape):
    return lax.broadcasted_iota(jnp.int32, shape, len(shape) - 1)


def fold(product):
    return jnp.sum(product.reshape(product.shape[0] // 8, 8, lanes), axis=0)


def vertical(load):
    total = taps[4] * load(4)
    for step in range(4):
        total = total + taps[step] * (load(step) + load(8 - step))
    return total


def moved(before, here, after, step):
    if step > 0:
        return pltpu.roll(jnp.where(lane_of(here.shape) < step, after, here), lanes - step, 1)
    if step < 0:
        return pltpu.roll(jnp.where(lane_of(here.shape) >= lanes + step, before, here), -step, 1)
    return here


def horizontal(before, here, after):
    total = taps[4] * here
    for step in range(1, 5):
        pair = moved(before, here, after, step) + moved(before, here, after, -step)
        total = total + taps[4 - step] * pair
    return total


def halves(value):
    high = value.astype(jnp.bfloat16)
    low = (value - high.astype(jnp.float32)).astype(jnp.bfloat16)
    return high, low


def by_row_shift(value, rows, direction):
    place = lax.broadcasted_iota(jnp.int32, value.shape, 0) % rows
    unit = 1
    while unit < rows:
        digit = (place // unit) % 4
        result = value
        for times in range(1, 4):
            amount = times * unit
            turned = pltpu.roll(value, amount if direction > 0 else lanes - amount, 1)
            result = jnp.where(digit == times, turned, result)
        value = result
        unit *= 4
    return value


def at_edge():
    index = lax.axis_index("rows")
    return (index == 0) | (index == lax.axis_size("rows") - 1)


def smooth_kernel(frames, from_odd, from_even, inverse, stack, power, rows_in, half, fine):
    count, rows, columns = frames.shape
    tiles = columns // lanes
    ring = tiles + 2
    odd = lax.axis_index("rows") % 2 == 1
    edge = at_edge()
    zero = jnp.zeros((rows, lanes), jnp.float32)
    for f in range(count):
        half[f, 0] = zero
        half[f, tiles + 1] = zero
    blank = jnp.zeros((count * rows, lanes), jnp.float32)
    fine[0] = blank
    fine[tiles + 1] = blank
    fine[tiles + 2] = blank

    def load_step(t, carry):
        for f in range(count):
            outer = jnp.where(edge, 0.0, from_odd[f, :, tile_of(t)])
            inner = from_even[f, :, tile_of(t)]
            rows_in[f, t, 4:8, :] = jnp.where(odd, inner, outer)
            rows_in[f, t, 8 : 8 + rows, :] = frames[f, :, tile_of(t)]
            rows_in[f, t, 8 + rows : 12 + rows, :] = jnp.where(odd, outer, inner)
        return carry

    def vertical_step(t, carry):
        for f in range(count):
            half[f, t + 1] = vertical(lambda s: rows_in[f, t, pl.ds(4 + s, rows), :])
        return carry

    def horizontal_step(t, totals):
        result = []
        for f in range(count):
            smooth = horizontal(half[f, t], half[f, t + 1], half[f, t + 2])
            inverse[f, :, tile_of(t)] = 1.0 / smooth
            detail = frames[f, :, tile_of(t)] - smooth
            fine[t + 1, f * rows : (f + 1) * rows, :] = detail
            result.append(totals[f] + fold(detail * detail))
        return tuple(result)

    def stack_step(t, carry):
        before, here, after = fine[t], fine[t + 1], fine[t + 2]
        for j in range(reach):
            high, low = halves(moved(before, here, after, 3 - j))
            size = count * rows
            stack[j * size : (j + 1) * size, tile_of(t)] = high
            stack[(reach + j) * size : (reach + j + 1) * size, tile_of(t)] = low
        return carry

    by_tiles(load_step, tiles, 8)
    by_tiles(vertical_step, tiles, 8)
    powers = by_tiles(horizontal_step, tiles, 8, (jnp.zeros((8, lanes), jnp.float32),) * count)
    for f in range(count):
        power[f * 8 : f * 8 + 8, :] = powers[f]
    fine[tiles + 3] = fine[1]
    by_tiles(stack_step, ring, ring // 2)


def column_shift(offset):
    negative = offset < 0
    first = jnp.where(negative, 0, 1)
    amount = jnp.where(negative, offset + lanes, offset)
    back = (lanes - amount) & (lanes - 1)

    def shift(source, t):
        here = source[t + first]
        after = source[t + first + 1]
        value = pltpu.roll(jnp.where(lane_of(here.shape) < amount, after, here), back, 1)
        spare = jnp.zeros((slot - value.shape[0], lanes), jnp.float32)
        return jnp.concatenate([value, spare], axis=0)

    return shift


def match_kernel(
    base, own_odd, own_even, from_odd, from_even, stack, power, clean, part, rows_in, half, fine, stream, lags
):
    rows = own_odd.shape[0] * 2
    tiles = own_odd.shape[1] // lanes
    count = power.shape[0] // 8
    ring = tiles + 2
    wide = rows + 8
    row_index = lax.axis_index("rows")
    last_row = lax.axis_size("rows") - 1
    odd = row_index % 2 == 1
    edge = at_edge()
    blank = jnp.zeros((wide, lanes), jnp.float32)
    half[0] = blank
    half[tiles + 1] = blank
    clean[0] = blank
    clean[tiles + 1] = blank
    fine[0] = blank
    fine[tiles + 1] = blank
    fine[tiles + 2] = blank
    place = lax.broadcasted_iota(jnp.int32, (wide, lanes), 0)
    inside = ((place >= 4) | (row_index > 0)) & ((place < rows + 4) | (row_index < last_row))

    def load_step(t, carry):
        outer = [jnp.where(edge, 0.0, from_odd[:, tile_of(t)]), own_odd[:, tile_of(t)]]
        inner = [array[:, tile_of(t)] for array in (own_even, from_even)]
        rows_in[t, 0:8, :] = jnp.where(odd, inner[1], outer[0])
        rows_in[t, 8:16, :] = jnp.where(odd, inner[0], outer[1])
        rows_in[t, 16:24, :] = jnp.where(odd, outer[1], inner[0])
        rows_in[t, 24:32, :] = jnp.where(odd, outer[0], inner[1])
        return carry

    def vertical_step(t, carry):
        half[t + 1] = vertical(lambda s: rows_in[t, pl.ds(s, wide), :])
        return carry

    def horizontal_step(t, total):
        smooth = jnp.where(inside, horizontal(half[t], half[t + 1], half[t + 2]), 0.0)
        clean[t + 1] = smooth
        detail = rows_in[t, pl.ds(4, wide), :] - smooth
        fine[t + 1] = detail
        own = jnp.where((place >= 4) & (place < rows + 4), detail, 0.0)
        return total + fold(own * own)

    by_tiles(load_step, tiles, 8)
    by_tiles(vertical_step, tiles, 8)
    ref_power = by_tiles(horizontal_step, tiles, 8, jnp.zeros((8, lanes), jnp.float32))
    fine[tiles + 3] = fine[1]
    shift = column_shift(base[0, 1])
    stream[2 * slot : 4 * slot, :] = jnp.zeros((2 * slot, ring * lanes), jnp.bfloat16)

    def stream_step(t, carry):
        high, low = halves(shift(fine, t))
        stream[0:slot, tile_of(t)] = high
        stream[slot : 2 * slot, tile_of(t)] = low
        return carry

    by_tiles(stream_step, ring, ring // 2)
    product = lax.dot_general(
        stack[...], stream[...], (((1,), (1,)), ((), ())), preferred_element_type=jnp.float32
    )
    size = reach * count * rows
    product = product[:size] + product[size:]
    product = by_row_shift(product, rows, -1)
    lags[...] = jnp.zeros(lags.shape, jnp.float32)
    for j in range(reach):
        for f in range(count):
            start = (j * count + f) * rows
            lags[f * 8 + j : f * 8 + j + 1, :] = jnp.sum(product[start : start + rows], axis=0, keepdims=True)
    back = 2 * lanes - 1 - base[0, 0]
    across = lax.broadcasted_iota(jnp.int32, (8, lanes), 0)
    lane = lane_of((8, lanes))
    packed = jnp.zeros((8, lanes), jnp.float32)
    for f in range(count):
        block = lags[f * 8 : f * 8 + 8, :]
        for j in range(reach):
            at = (f * reach + j) * reach
            high = pltpu.roll(block, (back + at) & (lanes - 1), 1)
            low = pltpu.roll(block, (back + at - slot) & (lanes - 1), 1)
            packed = packed + jnp.where((across == j) & (lane >= at) & (lane < at + reach), high + low, 0.0)
    lags[0:8, :] = jnp.zeros((8, lanes), jnp.float32)
    for f in range(count):
        lags[f : f + 1, :] = jnp.sum(power[f * 8 : f * 8 + 8, :], axis=0, keepdims=True)
    lags[count : count + 1, :] = jnp.sum(ref_power, axis=0, keepdims=True)
    powers = jnp.sum(lags[0:8, :], axis=1, keepdims=True)
    packed = packed + jnp.where(lane == count * reach * reach + across, powers, 0.0)
    part[...] = jnp.broadcast_to(jnp.sum(packed, axis=0, keepdims=True), part.shape)


def spread_kernel(base, clean, spread):
    tiles = clean.shape[0] - 2
    full = spread.shape[0] // 2
    spare = jnp.zeros((full - reach * slot, tiles * lanes), jnp.bfloat16)
    spread[reach * slot : full, :] = spare
    spread[full + reach * slot : 2 * full, :] = spare

    def per_offset(j, carry):
        shift = column_shift(base[0, 1] + j - 3)
        at = pl.multiple_of(j * slot, slot)

        def step(t, inner):
            high, low = halves(shift(clean, t))
            spread[pl.ds(at, slot), tile_of(t)] = high
            spread[pl.ds(full + at, slot), tile_of(t)] = low
            return inner

        by_tiles(step, tiles, 32)
        return carry

    lax.fori_loop(0, reach, per_offset, 0)


def blend_weights(totals, count):
    lane = lane_of(totals.shape)
    block = reach * reach

    def pick(index):
        return jnp.sum(jnp.where(lane == index, totals, 0.0), axis=1, keepdims=True)

    ref_power = pick(count * block + count)
    weights = []
    for f in range(count):
        norm_product = jnp.sqrt((pick(count * block + f) + 1e-06) * (ref_power + 1e-06))
        member = (lane >= f * block) & (lane < (f + 1) * block)
        rho = jnp.where(member, totals, 0.0) / norm_product
        squared = rho * rho
        middle = jnp.where(lane == f * block + block // 2, 0.05, 0.0)
        weights.append((squared + middle) / (0.05 + jnp.sum(squared, axis=1, keepdims=True)))
    return weights


def banded(weights, f, rows, first_row):
    lane = lane_of(weights.shape)
    tiles = []
    for group in (range(4), range(4, reach)):
        line = jnp.zeros_like(weights)
        for j in group:
            at = first_row + (j % 4) * slot
            turned = pltpu.roll(weights, (at + 2 * lanes - (f * reach + j) * reach) & (lanes - 1), 1)
            line = jnp.where((lane >= at) & (lane < at + reach), turned, line)
        line = jnp.broadcast_to(line[0:1], (rows, lanes))
        tiles.append(by_row_shift(line, rows, 1))
    return jnp.concatenate(tiles, axis=1)


def pressure_kernel(base, parts, spread, inverse, pressure, moments, part):
    count, rows, columns = inverse.shape
    full = spread.shape[0] // 2
    first_row = 1 + base[0, 0]
    totals = jnp.broadcast_to(jnp.sum(parts[...], axis=0, keepdims=True), (8, lanes))
    weights = blend_weights(totals, count)
    bands = [banded(weights[f], f, rows, first_row) for f in range(count)]
    mixing = jnp.concatenate(halves(jnp.concatenate(bands, axis=0)), axis=0)
    chunk = 2 * lanes
    zero = jnp.zeros((8, lanes), jnp.float32)
    size = count * rows

    def step(t, totals):
        where = pl.ds(pl.multiple_of(t * chunk, chunk), chunk)
        product = jnp.dot(mixing, spread[0:full, where], preferred_element_type=jnp.float32)
        product = product + jnp.dot(mixing, spread[full : 2 * full, where], preferred_element_type=jnp.float32)
        registered = product[:size] + product[size:]
        first = second = None
        totals = list(totals)
        for f in range(count):
            ratio = registered[f * rows : (f + 1) * rows] * inverse[f, :, where]
            value = calib_zero + ratio * (calib_linear + calib_square * ratio)
            squared = value * value
            pressure[f, :, where] = value
            first = value if first is None else first + value
            second = squared if second is None else second + squared
            for total, array in ((f, value), (count + f, squared)):
                for c in range(chunk // lanes):
                    totals[total] = totals[total] + fold(array[:, c * lanes : (c + 1) * lanes])
        moments[0, :, where] = first
        moments[1, :, where] = second
        return tuple(totals)

    totals = by_tiles(step, columns // chunk, 8, (zero,) * (2 * count))
    line = jnp.zeros((8, lanes), jnp.float32)
    for k in range(2 * count):
        value = jnp.sum(jnp.sum(totals[k], axis=0, keepdims=True), axis=1, keepdims=True)
        line = line + jnp.where(lane_of(line.shape) == k, value, 0.0)
    part[...] = jnp.broadcast_to(line[0:1], part.shape)


def paired(value, axis, first):
    size = lax.axis_size(axis)
    partner = list(range(size))
    for i in range(first, size - 1, 2):
        partner[i], partner[i + 1] = i + 1, i
    return lax.ppermute(value, axis, list(enumerate(partner)))


def by_parity(odd, array, height, dim):
    length = array.shape[dim]
    low = lax.slice_in_dim(array, 0, height, axis=dim)
    high = lax.slice_in_dim(array, length - height, length, axis=dim)
    return jnp.where(odd, high, low), jnp.where(odd, low, high)


def from_owner(shard, odd, axis, root):
    mine = lax.axis_index(axis) == root
    height = shard.shape[0] // 2
    if lax.axis_size(axis) != 2:
        whole = lax.psum(jnp.where(mine, shard, jnp.zeros_like(shard)), axis)
        return by_parity(odd, whole, height, 0)
    here = lax.optimization_barrier(jnp.maximum(shard, 0.0))
    odd_here, even_here = by_parity(odd, here, height, 0)
    odd_there = paired(odd_here, axis, 0)
    even_here, odd_there = lax.optimization_barrier((even_here, odd_there))
    even_there = paired(even_here, axis, 0)
    return jnp.where(mine, odd_here, odd_there), jnp.where(mine, even_here, even_there)


def total_over(value, axis):
    size = lax.axis_size(axis)
    if size & (size - 1):
        return lax.psum(value, axis)
    step = 1
    while step < size:
        value = value + lax.ppermute(value, axis, [(i, i ^ step) for i in range(size)])
        step *= 2
    return value


def shards(frames_raw, wind_off, run_owner, search_base):
    count, rows, columns = frames_raw.shape
    tiles = columns // lanes
    ring = tiles + 2
    wide = rows + 8
    depth = reach * count * rows
    size = lax.axis_size("rows")
    f32 = jnp.float32
    bf16 = jnp.bfloat16
    struct = functools.partial(jax.ShapeDtypeStruct, dtype=f32)
    odd = lax.axis_index("rows") % 2 == 1
    raw = lax.optimization_barrier(jnp.maximum(frames_raw, 0.0))
    offsets = jnp.clip(search_base, -8, 8)
    frames_odd, frames_even = by_parity(odd, raw, 4, 1)
    frames_odd, run = lax.optimization_barrier((frames_odd, wind_off[0]))
    frames_odd = paired(frames_odd, "rows", 1)
    frames_even = paired(frames_even, "rows", 0)
    own_odd, own_even = from_owner(run, odd, "frames", run_owner[0])
    from_odd = paired(own_odd, "rows", 1)
    inverse, stack, power = pl.pallas_call(
        smooth_kernel,
        out_shape=(
            struct((count, rows, columns)),
            jax.ShapeDtypeStruct((2 * depth, ring * lanes), bf16),
            struct((8 * count, lanes)),
        ),
        in_specs=[vmem] * 3,
        out_specs=(vmem,) * 3,
        scratch_shapes=[
            pltpu.VMEM((count, tiles, rows + 16, lanes), f32),
            pltpu.VMEM((count, tiles + 2, rows, lanes), f32),
            pltpu.VMEM((ring + 2, count * rows, lanes), f32),
        ],
        compiler_params=params,
        name="smooth",
    )(raw, frames_odd, frames_even)
    own_even, power = lax.optimization_barrier((own_even, power))
    from_even = paired(own_even, "rows", 0)
    clean, part = pl.pallas_call(
        match_kernel,
        out_shape=(struct((tiles + 2, wide, lanes)), struct((size, lanes))),
        in_specs=[smem] + [vmem] * 6,
        out_specs=(vmem, vmem),
        scratch_shapes=[
            pltpu.VMEM((tiles, rows + 16, lanes), f32),
            pltpu.VMEM((tiles + 2, wide, lanes), f32),
            pltpu.VMEM((ring + 2, wide, lanes), f32),
            pltpu.VMEM((4 * slot, ring * lanes), bf16),
            pltpu.VMEM((8 * count, lanes), f32),
        ],
        compiler_params=params,
        name="match",
    )(offsets, own_odd, own_even, from_odd, from_even, stack, power)
    parts = lax.all_to_all(part, "rows", 0, 0, tiled=True)
    spread = pl.pallas_call(
        spread_kernel,
        out_shape=jax.ShapeDtypeStruct((2 * 8 * slot, columns), bf16),
        in_specs=[smem, vmem],
        out_specs=vmem,
        compiler_params=params,
        name="spread",
    )(offsets, clean)
    pressure, moments, part = pl.pallas_call(
        pressure_kernel,
        out_shape=(struct((count, rows, columns)), struct((2, rows, columns)), struct((size, lanes))),
        in_specs=[smem] + [vmem] * 3,
        out_specs=(vmem, vmem, vmem),
        compiler_params=params,
        name="pressure",
    )(offsets, parts, spread, inverse)
    whole = total_over(moments, "frames")
    spatial = jnp.sum(lax.all_to_all(part, "rows", 0, 0, tiled=True), axis=0)
    cell_count = rows * columns * size
    frame_mean = spatial[:count] / cell_count
    frame_rms = jnp.sqrt(spatial[count : 2 * count] / cell_count - frame_mean * frame_mean)
    total_frames = count * lax.axis_size("frames")
    time_mean = whole[0] / total_frames
    time_rms = jnp.sqrt(jnp.maximum(whole[1] / total_frames - time_mean * time_mean, 0.0))
    return (pressure, frame_mean, frame_rms, time_mean, time_rms)


def solution(mesh):
    placed = (P("frames", "rows", None), P("frames", "rows", None), P("rows"), P("frames", None))
    return jax.shard_map(
        shards,
        mesh=mesh,
        in_specs=placed,
        out_specs=(
            P("frames", "rows", None),
            P("frames"),
            P("frames"),
            P("rows", None),
            P("rows", None),
        ),
        check_vma=False,
    )
```

```python
import functools

import jax
import jax.numpy as jnp
from jax import lax
from jax.experimental import pallas as pl
from jax.experimental.pallas import tpu as pltpu
from jax.sharding import PartitionSpec as P

taps = (1.0 / 256, 8.0 / 256, 28.0 / 256, 56.0 / 256, 70.0 / 256)
calib_zero = -0.25
calib_linear = 1.0
calib_square = 0.15
lanes = 128
reach = 7
slot = 32
params = pltpu.CompilerParams(vmem_limit_bytes=14 * 1024 * 1024)
vmem = pl.BlockSpec(memory_space=pltpu.VMEM)
smem = pl.BlockSpec(memory_space=pltpu.SMEM)


def tile_of(index):
    return pl.ds(pl.multiple_of(index * lanes, lanes), lanes)


def by_tiles(step, tiles, group, init=()):
    def body(index, carry):
        for inner in range(group):
            carry = step(index * group + inner, carry)
        return carry

    return lax.fori_loop(0, tiles // group, body, init)


def lane_of(shape):
    return lax.broadcasted_iota(jnp.int32, shape, len(shape) - 1)


def fold(product):
    return jnp.sum(product.reshape(product.shape[0] // 8, 8, lanes), axis=0)


def vertical(load):
    total = taps[4] * load(4)
    for step in range(4):
        total = total + taps[step] * (load(step) + load(8 - step))
    return total


def moved(before, here, after, step):
    if step > 0:
        return pltpu.roll(jnp.where(lane_of(here.shape) < step, after, here), lanes - step, 1)
    if step < 0:
        return pltpu.roll(jnp.where(lane_of(here.shape) >= lanes + step, before, here), -step, 1)
    return here


def horizontal(before, here, after):
    total = taps[4] * here
    for step in range(1, 5):
        pair = moved(before, here, after, step) + moved(before, here, after, -step)
        total = total + taps[4 - step] * pair
    return total


def halves(value):
    high = value.astype(jnp.bfloat16)
    low = (value - high.astype(jnp.float32)).astype(jnp.bfloat16)
    return high, low


def by_row_shift(value, rows, direction):
    place = lax.broadcasted_iota(jnp.int32, value.shape, 0) % rows
    unit = 1
    while unit < rows:
        digit = (place // unit) % 4
        result = value
        for times in range(1, 4):
            amount = times * unit
            turned = pltpu.roll(value, amount if direction > 0 else lanes - amount, 1)
            result = jnp.where(digit == times, turned, result)
        value = result
        unit *= 4
    return value


def at_edge():
    index = lax.axis_index("rows")
    return (index == 0) | (index == lax.axis_size("rows") - 1)


def smooth_kernel(frames, from_odd, from_even, inverse, stack, power, rows_in, half, pieces):
    count, rows, columns = frames.shape
    tiles = columns // lanes
    ring = tiles + 2
    odd = lax.axis_index("rows") % 2 == 1
    edge = at_edge()
    zero = jnp.zeros((rows, lanes), jnp.float32)
    for f in range(count):
        half[f, 0] = zero
        half[f, tiles + 1] = zero
    blank = jnp.zeros((2 * count * rows, lanes), jnp.bfloat16)
    pieces[0] = blank
    pieces[tiles + 1] = blank
    pieces[tiles + 2] = blank

    def load_step(t, carry):
        for f in range(count):
            outer = jnp.where(edge, 0.0, from_odd[f, :, tile_of(t)])
            inner = from_even[f, :, tile_of(t)]
            rows_in[f, t, 4:8, :] = jnp.where(odd, inner, outer)
            rows_in[f, t, 8 : 8 + rows, :] = frames[f, :, tile_of(t)]
            rows_in[f, t, 8 + rows : 12 + rows, :] = jnp.where(odd, outer, inner)
        return carry

    def vertical_step(t, carry):
        for f in range(count):
            half[f, t + 1] = vertical(lambda s: rows_in[f, t, pl.ds(4 + s, rows), :])
        return carry

    def horizontal_step(t, totals):
        result = []
        details = []
        for f in range(count):
            smooth = horizontal(half[f, t], half[f, t + 1], half[f, t + 2])
            inverse[f, :, tile_of(t)] = 1.0 / smooth
            details.append(frames[f, :, tile_of(t)] - smooth)
            result.append(totals[f] + fold(details[f] * details[f]))
        pieces[t + 1] = jnp.concatenate(halves(jnp.concatenate(details, axis=0)), axis=0)
        return tuple(result)

    def stack_step(t, carry):
        before, here, after = pieces[t], pieces[t + 1], pieces[t + 2]
        size = count * rows
        for j in range(reach):
            turned = moved(before, here, after, 3 - j)
            stack[j * size : (j + 1) * size, tile_of(t)] = turned[:size]
            stack[(reach + j) * size : (reach + j + 1) * size, tile_of(t)] = turned[size:]
        return carry

    by_tiles(load_step, tiles, 8)
    by_tiles(vertical_step, tiles, 8)
    powers = by_tiles(horizontal_step, tiles, 8, (jnp.zeros((8, lanes), jnp.float32),) * count)
    for f in range(count):
        power[f * 8 : f * 8 + 8, :] = powers[f]
    pieces[tiles + 3] = pieces[1]
    by_tiles(stack_step, ring, ring // 2)


def column_shift(offset):
    negative = offset < 0
    first = jnp.where(negative, 0, 1)
    amount = jnp.where(negative, offset + lanes, offset)
    back = (lanes - amount) & (lanes - 1)

    def shift(source, t):
        here = source[t + first]
        after = source[t + first + 1]
        return pltpu.roll(jnp.where(lane_of(here.shape) < amount, after, here), back, 1)

    return shift


def match_kernel(
    base, own_odd, own_even, from_odd, from_even, stack, power, clean, part, rows_in, half, fine, stream, lags
):
    rows = own_odd.shape[0] * 2
    tiles = own_odd.shape[1] // lanes
    count = power.shape[0] // 8
    ring = tiles + 2
    wide = rows + 8
    row_index = lax.axis_index("rows")
    last_row = lax.axis_size("rows") - 1
    odd = row_index % 2 == 1
    edge = at_edge()
    blank = jnp.zeros((wide, lanes), jnp.float32)
    half[0] = blank
    half[tiles + 1] = blank
    empty = jnp.zeros((2 * slot, lanes), jnp.bfloat16)
    for array in (clean, fine):
        array[0] = empty
        array[tiles + 1] = empty
    fine[tiles + 2] = empty
    spare = jnp.zeros((slot - wide, lanes), jnp.float32)

    def cut(value):
        return jnp.concatenate(halves(jnp.concatenate([value, spare], axis=0)), axis=0)

    place = lax.broadcasted_iota(jnp.int32, (wide, lanes), 0)
    inside = ((place >= 4) | (row_index > 0)) & ((place < rows + 4) | (row_index < last_row))

    def load_step(t, carry):
        outer = [jnp.where(edge, 0.0, from_odd[:, tile_of(t)]), own_odd[:, tile_of(t)]]
        inner = [array[:, tile_of(t)] for array in (own_even, from_even)]
        rows_in[t, 0:8, :] = jnp.where(odd, inner[1], outer[0])
        rows_in[t, 8:16, :] = jnp.where(odd, inner[0], outer[1])
        rows_in[t, 16:24, :] = jnp.where(odd, outer[1], inner[0])
        rows_in[t, 24:32, :] = jnp.where(odd, outer[0], inner[1])
        return carry

    def vertical_step(t, carry):
        half[t + 1] = vertical(lambda s: rows_in[t, pl.ds(s, wide), :])
        return carry

    def horizontal_step(t, total):
        smooth = jnp.where(inside, horizontal(half[t], half[t + 1], half[t + 2]), 0.0)
        clean[t + 1] = cut(smooth)
        detail = rows_in[t, pl.ds(4, wide), :] - smooth
        fine[t + 1] = cut(detail)
        own = jnp.where((place >= 4) & (place < rows + 4), detail, 0.0)
        return total + fold(own * own)

    by_tiles(load_step, tiles, 8)
    by_tiles(vertical_step, tiles, 8)
    ref_power = by_tiles(horizontal_step, tiles, 8, jnp.zeros((8, lanes), jnp.float32))
    fine[tiles + 3] = fine[1]
    shift = column_shift(base[0, 1])
    stream[2 * slot : 4 * slot, :] = jnp.zeros((2 * slot, ring * lanes), jnp.bfloat16)

    def stream_step(t, carry):
        stream[0 : 2 * slot, tile_of(t)] = shift(fine, t)
        return carry

    by_tiles(stream_step, ring, ring // 2)
    product = lax.dot_general(
        stack[...], stream[...], (((1,), (1,)), ((), ())), preferred_element_type=jnp.float32
    )
    size = reach * count * rows
    product = product[:size] + product[size:]
    product = by_row_shift(product, rows, -1)
    lags[...] = jnp.zeros(lags.shape, jnp.float32)
    for j in range(reach):
        for f in range(count):
            start = (j * count + f) * rows
            lags[f * 8 + j : f * 8 + j + 1, :] = jnp.sum(product[start : start + rows], axis=0, keepdims=True)
    back = 2 * lanes - 1 - base[0, 0]
    across = lax.broadcasted_iota(jnp.int32, (8, lanes), 0)
    lane = lane_of((8, lanes))
    packed = jnp.zeros((8, lanes), jnp.float32)
    for f in range(count):
        block = lags[f * 8 : f * 8 + 8, :]
        for j in range(reach):
            at = (f * reach + j) * reach
            high = pltpu.roll(block, (back + at) & (lanes - 1), 1)
            low = pltpu.roll(block, (back + at - slot) & (lanes - 1), 1)
            packed = packed + jnp.where((across == j) & (lane >= at) & (lane < at + reach), high + low, 0.0)
    lags[0:8, :] = jnp.zeros((8, lanes), jnp.float32)
    for f in range(count):
        lags[f : f + 1, :] = jnp.sum(power[f * 8 : f * 8 + 8, :], axis=0, keepdims=True)
    lags[count : count + 1, :] = jnp.sum(ref_power, axis=0, keepdims=True)
    powers = jnp.sum(lags[0:8, :], axis=1, keepdims=True)
    packed = packed + jnp.where(lane == count * reach * reach + across, powers, 0.0)
    part[...] = jnp.broadcast_to(jnp.sum(packed, axis=0, keepdims=True), part.shape)


def spread_columns(clean, spread, base_col):
    tiles = clean.shape[0] - 2
    full = spread.shape[0] // 2
    spare = jnp.zeros((full - reach * slot, tiles * lanes), jnp.bfloat16)
    spread[reach * slot : full, :] = spare
    spread[full + reach * slot : 2 * full, :] = spare

    def per_offset(j, carry):
        shift = column_shift(base_col + j - 3)
        at = pl.multiple_of(j * slot, slot)

        def step(t, inner):
            turned = shift(clean, t)
            spread[pl.ds(at, slot), tile_of(t)] = turned[:slot]
            spread[pl.ds(full + at, slot), tile_of(t)] = turned[slot:]
            return inner

        by_tiles(step, tiles, 32)
        return carry

    lax.fori_loop(0, reach, per_offset, 0)


def blend_weights(totals, count):
    lane = lane_of(totals.shape)
    block = reach * reach

    def pick(index):
        return jnp.sum(jnp.where(lane == index, totals, 0.0), axis=1, keepdims=True)

    ref_power = pick(count * block + count)
    weights = []
    for f in range(count):
        norm_product = jnp.sqrt((pick(count * block + f) + 1e-06) * (ref_power + 1e-06))
        member = (lane >= f * block) & (lane < (f + 1) * block)
        rho = jnp.where(member, totals, 0.0) / norm_product
        squared = rho * rho
        middle = jnp.where(lane == f * block + block // 2, 0.05, 0.0)
        weights.append((squared + middle) / (0.05 + jnp.sum(squared, axis=1, keepdims=True)))
    return weights


def banded(weights, f, rows, first_row):
    lane = lane_of(weights.shape)
    tiles = []
    for group in (range(4), range(4, reach)):
        line = jnp.zeros_like(weights)
        for j in group:
            at = first_row + (j % 4) * slot
            turned = pltpu.roll(weights, (at + 2 * lanes - (f * reach + j) * reach) & (lanes - 1), 1)
            line = jnp.where((lane >= at) & (lane < at + reach), turned, line)
        line = jnp.broadcast_to(line[0:1], (rows, lanes))
        tiles.append(by_row_shift(line, rows, 1))
    return jnp.concatenate(tiles, axis=1)


def pressures(base, totals, clean, spread, inverse):
    count, rows, columns = inverse.shape
    full = spread.shape[0] // 2
    weights = blend_weights(jnp.broadcast_to(totals[0:1, :], (8, lanes)), count)
    bands = [banded(weights[f], f, rows, 1 + base[0, 0]) for f in range(count)]
    mixing = jnp.concatenate(halves(jnp.concatenate(bands, axis=0)), axis=0)
    spread_columns(clean, spread, base[0, 1])

    def chunk_values(where):
        product = jnp.dot(mixing, spread[0:full, where], preferred_element_type=jnp.float32)
        product = product + jnp.dot(mixing, spread[full : 2 * full, where], preferred_element_type=jnp.float32)
        registered = product[: count * rows] + product[count * rows :]
        values = []
        for f in range(count):
            ratio = registered[f * rows : (f + 1) * rows] * inverse[f, :, where]
            values.append(calib_zero + ratio * (calib_linear + calib_square * ratio))
        return values

    return chunk_values


def chunk_of(t):
    return pl.ds(pl.multiple_of(t * 2 * lanes, 2 * lanes), 2 * lanes)


def pressure_kernel(base, totals, clean, inverse, pressure, moments, part, spread):
    count, rows, columns = inverse.shape
    chunk_values = pressures(base, totals, clean, spread, inverse)

    def step(t, sums):
        where = chunk_of(t)
        values = chunk_values(where)
        squares = [value * value for value in values]
        for f in range(count):
            pressure[f, :, where] = values[f]
        moments[0, :, where] = sum(values[1:], values[0])
        moments[1, :, where] = sum(squares[1:], squares[0])
        result = []
        for total, array in zip(sums, values + squares):
            result.append(total + fold(array[:, :lanes]) + fold(array[:, lanes:]))
        return tuple(result)

    zero = jnp.zeros((8, lanes), jnp.float32)
    sums = by_tiles(step, columns // (2 * lanes), 8, (zero,) * (2 * count))
    line = zero
    for k in range(2 * count):
        value = jnp.sum(jnp.sum(sums[k], axis=0, keepdims=True), axis=1, keepdims=True)
        line = line + jnp.where(lane_of(line.shape) == k, value, 0.0)
    part[...] = jnp.broadcast_to(line[0:1], part.shape)


def time_kernel(base, totals, clean, inverse, moments, time_mean, time_rms, spread):
    count, rows, columns = inverse.shape
    chunk_values = pressures(base, totals, clean, spread, inverse)
    frames = 2 * count

    def step(t, carry):
        where = chunk_of(t)
        first = moments[0, :, where]
        second = moments[1, :, where]
        for value in chunk_values(where):
            first = first + value
            second = second + value * value
        mean = first * (1.0 / frames)
        time_mean[:, where] = mean
        time_rms[:, where] = jnp.sqrt(jnp.maximum(second * (1.0 / frames) - mean * mean, 0.0))
        return carry

    by_tiles(step, columns // (2 * lanes), 8)


def paired(value, axis, first):
    size = lax.axis_size(axis)
    partner = list(range(size))
    for i in range(first, size - 1, 2):
        partner[i], partner[i + 1] = i + 1, i
    return lax.ppermute(value, axis, list(enumerate(partner)))


def by_parity(odd, array, height, dim):
    length = array.shape[dim]
    low = lax.slice_in_dim(array, 0, height, axis=dim)
    high = lax.slice_in_dim(array, length - height, length, axis=dim)
    return jnp.where(odd, high, low), jnp.where(odd, low, high)


def from_owner(shard, odd, axis, root):
    mine = lax.axis_index(axis) == root
    height = shard.shape[0] // 2
    if lax.axis_size(axis) != 2:
        whole = lax.psum(jnp.where(mine, shard, jnp.zeros_like(shard)), axis)
        return by_parity(odd, whole, height, 0)
    here = lax.optimization_barrier(jnp.maximum(shard, 0.0))
    odd_here, even_here = by_parity(odd, here, height, 0)
    odd_there = paired(odd_here, axis, 0)
    even_here, odd_there = lax.optimization_barrier((even_here, odd_there))
    even_there = paired(even_here, axis, 0)
    return jnp.where(mine, odd_here, odd_there), jnp.where(mine, even_here, even_there)


def total_over(value, axis):
    size = lax.axis_size(axis)
    if size & (size - 1):
        return lax.psum(value, axis)
    step = 1
    while step < size:
        value = value + lax.ppermute(value, axis, [(i, i ^ step) for i in range(size)])
        step *= 2
    return value


def shards(frames_raw, wind_off, run_owner, search_base):
    count, rows, columns = frames_raw.shape
    tiles = columns // lanes
    ring = tiles + 2
    wide = rows + 8
    depth = reach * count * rows
    size = lax.axis_size("rows")
    f32 = jnp.float32
    bf16 = jnp.bfloat16
    struct = functools.partial(jax.ShapeDtypeStruct, dtype=f32)
    odd = lax.axis_index("rows") % 2 == 1
    raw = lax.optimization_barrier(jnp.maximum(frames_raw, 0.0))
    offsets = jnp.clip(search_base, -8, 8)
    frames_odd, frames_even = by_parity(odd, raw, 4, 1)
    frames_odd, run = lax.optimization_barrier((frames_odd, wind_off[0]))
    frames_odd = paired(frames_odd, "rows", 1)
    frames_even = paired(frames_even, "rows", 0)
    own_odd, own_even = from_owner(run, odd, "frames", run_owner[0])
    from_odd = paired(own_odd, "rows", 1)
    inverse, stack, power = pl.pallas_call(
        smooth_kernel,
        out_shape=(
            struct((count, rows, columns)),
            jax.ShapeDtypeStruct((2 * depth, ring * lanes), bf16),
            struct((8 * count, lanes)),
        ),
        in_specs=[vmem] * 3,
        out_specs=(vmem,) * 3,
        scratch_shapes=[
            pltpu.VMEM((count, tiles, rows + 16, lanes), f32),
            pltpu.VMEM((count, tiles + 2, rows, lanes), f32),
            pltpu.VMEM((ring + 2, 2 * count * rows, lanes), bf16),
        ],
        compiler_params=params,
        name="smooth",
    )(raw, frames_odd, frames_even)
    own_even, power = lax.optimization_barrier((own_even, power))
    from_even = paired(own_even, "rows", 0)
    blocks = lax.axis_size("frames")
    if blocks == 2:
        inverse_out, from_even = lax.optimization_barrier((inverse, from_even))
        other_inverse = paired(inverse_out, "frames", 0)
    clean, part = pl.pallas_call(
        match_kernel,
        out_shape=(jax.ShapeDtypeStruct((tiles + 2, 2 * slot, lanes), bf16), struct((size, lanes))),
        in_specs=[smem] + [vmem] * 6,
        out_specs=(vmem, vmem),
        scratch_shapes=[
            pltpu.VMEM((tiles, rows + 16, lanes), f32),
            pltpu.VMEM((tiles + 2, wide, lanes), f32),
            pltpu.VMEM((ring + 2, 2 * slot, lanes), bf16),
            pltpu.VMEM((4 * slot, ring * lanes), bf16),
            pltpu.VMEM((8 * count, lanes), f32),
        ],
        compiler_params=params,
        name="match",
    )(offsets, own_odd, own_even, from_odd, from_even, stack, power)
    parts = lax.all_to_all(part, "rows", 0, 0, tiled=True)
    totals = jnp.sum(parts, axis=0, keepdims=True)
    spread = pltpu.VMEM((2 * 8 * slot, columns), bf16)
    pressure, moments, part = pl.pallas_call(
        pressure_kernel,
        out_shape=(struct((count, rows, columns)), struct((2, rows, columns)), struct((size, lanes))),
        in_specs=[smem] + [vmem] * 3,
        out_specs=(vmem, vmem, vmem),
        scratch_shapes=[spread],
        compiler_params=params,
        name="pressure",
    )(offsets, totals, clean, inverse)
    if blocks == 2:
        row = jnp.concatenate([totals[:, : lanes - 2], offsets.astype(f32)], axis=1)
        row, part = lax.optimization_barrier((row, part))
        row = paired(row, "frames", 0)
        time_mean, time_rms = pl.pallas_call(
            time_kernel,
            out_shape=(struct((rows, columns)), struct((rows, columns))),
            in_specs=[smem] + [vmem] * 4,
            out_specs=(vmem, vmem),
            scratch_shapes=[spread],
            compiler_params=params,
            name="time",
        )(row[:, lanes - 2 :].astype(jnp.int32), row, clean, other_inverse, moments)
    else:
        whole = total_over(moments, "frames")
        total_frames = count * blocks
        time_mean = whole[0] / total_frames
        time_rms = jnp.sqrt(jnp.maximum(whole[1] / total_frames - time_mean * time_mean, 0.0))
    spatial = jnp.sum(lax.all_to_all(part, "rows", 0, 0, tiled=True), axis=0)
    cell_count = rows * columns * size
    frame_mean = spatial[:count] / cell_count
    frame_rms = jnp.sqrt(spatial[count : 2 * count] / cell_count - frame_mean * frame_mean)
    return (pressure, frame_mean, frame_rms, time_mean, time_rms)


def solution(mesh):
    placed = (P("frames", "rows", None), P("frames", "rows", None), P("rows"), P("frames", None))
    return jax.shard_map(
        shards,
        mesh=mesh,
        in_specs=placed,
        out_specs=(
            P("frames", "rows", None),
            P("frames"),
            P("frames"),
            P("rows", None),
            P("rows", None),
        ),
        check_vma=False,
    )
```

```python
import functools

import jax
import jax.numpy as jnp
from jax import lax
from jax.experimental import pallas as pl
from jax.experimental.pallas import tpu as pltpu
from jax.sharding import PartitionSpec as P

taps = (1.0 / 256, 8.0 / 256, 28.0 / 256, 56.0 / 256, 70.0 / 256)
calib_zero = -0.25
calib_linear = 1.0
calib_square = 0.15
lanes = 128
reach = 7
slot = 32
params = pltpu.CompilerParams(vmem_limit_bytes=14 * 1024 * 1024)
vmem = pl.BlockSpec(memory_space=pltpu.VMEM)
smem = pl.BlockSpec(memory_space=pltpu.SMEM)


def cost(mebibytes):
    return pl.CostEstimate(flops=0, bytes_accessed=mebibytes * 2**20, transcendentals=0)


def tile_of(index):
    return pl.ds(pl.multiple_of(index * lanes, lanes), lanes)


def by_tiles(step, tiles, group, init=()):
    def body(index, carry):
        for inner in range(group):
            carry = step(index * group + inner, carry)
        return carry

    return lax.fori_loop(0, tiles // group, body, init)


def lane_of(shape):
    return lax.broadcasted_iota(jnp.int32, shape, len(shape) - 1)


def fold(product):
    return jnp.sum(product.reshape(product.shape[0] // 8, 8, lanes), axis=0)


def vertical(load):
    total = taps[4] * load(4)
    for step in range(4):
        total = total + taps[step] * (load(step) + load(8 - step))
    return total


def moved(before, here, after, step):
    if step > 0:
        return pltpu.roll(jnp.where(lane_of(here.shape) < step, after, here), lanes - step, 1)
    if step < 0:
        return pltpu.roll(jnp.where(lane_of(here.shape) >= lanes + step, before, here), -step, 1)
    return here


def halves(value):
    high = value.astype(jnp.bfloat16)
    low = (value - high.astype(jnp.float32)).astype(jnp.bfloat16)
    return high, low


def cut(value):
    return jnp.concatenate(halves(value), axis=0)


def fill_band(band):
    shape = (lanes, lanes)
    apart = lax.broadcasted_iota(jnp.int32, shape, 0) - lax.broadcasted_iota(jnp.int32, shape, 1)

    def block(offset):
        distance = jnp.abs(apart + offset)
        value = jnp.zeros(shape, jnp.float32)
        for step in range(5):
            value = jnp.where(distance == step, taps[4 - step], value)
        return value.astype(jnp.bfloat16)

    none = jnp.zeros(shape, jnp.bfloat16)
    before, here, after = block(-lanes), block(0), block(lanes)
    for index, pair in enumerate(((before, none), (here, before), (after, here), (none, after))):
        band[index * lanes : (index + 1) * lanes, :] = jnp.concatenate(pair, axis=1)


def chunk_of(t):
    return pl.ds(pl.multiple_of(t * 2 * lanes, 2 * lanes), 2 * lanes)


def horizontal(wide, band, t):
    window = wide[:, pl.ds(pl.multiple_of(t * 2 * lanes, 2 * lanes), 4 * lanes)]
    product = jnp.dot(window, band[...], preferred_element_type=jnp.float32)
    half = product.shape[0] // 2
    return product[:half] + product[half:]


def by_row_shift(value, rows, direction):
    place = lax.broadcasted_iota(jnp.int32, value.shape, 0) % rows
    unit = 1
    while unit < rows:
        digit = (place // unit) % 4
        result = value
        for times in range(1, 4):
            amount = times * unit
            turned = pltpu.roll(value, amount if direction > 0 else lanes - amount, 1)
            result = jnp.where(digit == times, turned, result)
        value = result
        unit *= 4
    return value


def at_edge():
    index = lax.axis_index("rows")
    return (index == 0) | (index == lax.axis_size("rows") - 1)


def smooth_kernel(frames, from_odd, from_even, inverse, stack, power, rows_in, wide, band, pieces):
    count, rows, columns = frames.shape
    tiles = columns // lanes
    ring = tiles + 2
    odd = lax.axis_index("rows") % 2 == 1
    edge = at_edge()
    blank = jnp.zeros((2 * count * rows, lanes), jnp.bfloat16)
    wide[:, tile_of(0)] = blank
    wide[:, tile_of(tiles + 1)] = blank
    fill_band(band)
    pieces[0] = blank
    pieces[tiles + 1] = blank
    pieces[tiles + 2] = blank

    def load_step(t, carry):
        for f in range(count):
            outer = jnp.where(edge, 0.0, from_odd[f, :, tile_of(t)])
            inner = from_even[f, :, tile_of(t)]
            rows_in[f, t, 4:8, :] = jnp.where(odd, inner, outer)
            rows_in[f, t, 8 : 8 + rows, :] = frames[f, :, tile_of(t)]
            rows_in[f, t, 8 + rows : 12 + rows, :] = jnp.where(odd, outer, inner)
        return carry

    def vertical_step(t, carry):
        parts = [vertical(lambda s: rows_in[f, t, pl.ds(4 + s, rows), :]) for f in range(count)]
        wide[:, tile_of(t + 1)] = cut(jnp.concatenate(parts, axis=0))
        return carry

    def horizontal_step(t, totals):
        smooth = horizontal(wide, band, t)
        result = []
        details = []
        for f in range(count):
            part = smooth[f * rows : (f + 1) * rows]
            inverse[f, :, chunk_of(t)] = 1.0 / part
            details.append(frames[f, :, chunk_of(t)] - part)
            square = details[f] * details[f]
            result.append(totals[f] + fold(square[:, :lanes]) + fold(square[:, lanes:]))
        detail = cut(jnp.concatenate(details, axis=0))
        pieces[2 * t + 1] = detail[:, :lanes]
        pieces[2 * t + 2] = detail[:, lanes:]
        return tuple(result)

    def stack_step(t, carry):
        before, here, after = pieces[t], pieces[t + 1], pieces[t + 2]
        size = count * rows
        for j in range(reach):
            turned = moved(before, here, after, 3 - j)
            stack[j * size : (j + 1) * size, tile_of(t)] = turned[:size]
            stack[(reach + j) * size : (reach + j + 1) * size, tile_of(t)] = turned[size:]
        return carry

    by_tiles(load_step, tiles, 8)
    by_tiles(vertical_step, tiles, 8)
    powers = by_tiles(horizontal_step, tiles // 2, 8, (jnp.zeros((8, lanes), jnp.float32),) * count)
    for f in range(count):
        power[f * 8 : f * 8 + 8, :] = powers[f]
    pieces[tiles + 3] = pieces[1]
    by_tiles(stack_step, ring, ring // 2)


def column_shift(offset):
    negative = offset < 0
    first = jnp.where(negative, 0, 1)
    amount = jnp.where(negative, offset + lanes, offset)
    back = (lanes - amount) & (lanes - 1)

    def shift(source, t):
        here = source[t + first]
        after = source[t + first + 1]
        return pltpu.roll(jnp.where(lane_of(here.shape) < amount, after, here), back, 1)

    return shift


def match_kernel(
    base, own_odd, own_even, from_odd, from_even, stack, power, clean, part, rows_in, padded, band, fine, stream, lags
):
    rows = own_odd.shape[0] * 2
    tiles = own_odd.shape[1] // lanes
    count = power.shape[0] // 8
    ring = tiles + 2
    wide = rows + 8
    row_index = lax.axis_index("rows")
    last_row = lax.axis_size("rows") - 1
    odd = row_index % 2 == 1
    edge = at_edge()
    empty = jnp.zeros((2 * slot, lanes), jnp.bfloat16)
    padded[:, tile_of(0)] = empty
    padded[:, tile_of(tiles + 1)] = empty
    fill_band(band)
    for array in (clean, fine):
        array[0] = empty
        array[tiles + 1] = empty
    fine[tiles + 2] = empty
    spare = jnp.zeros((slot - wide, lanes), jnp.float32)
    place = lax.broadcasted_iota(jnp.int32, (slot, 2 * lanes), 0)
    own = (place >= 4) & (place < rows + 4)
    inside = ((place >= 4) | (row_index > 0)) & ((place < rows + 4) | (row_index < last_row)) & (place < wide)

    def load_step(t, carry):
        outer = [jnp.where(edge, 0.0, from_odd[:, tile_of(t)]), own_odd[:, tile_of(t)]]
        inner = [array[:, tile_of(t)] for array in (own_even, from_even)]
        rows_in[t, 0:8, :] = jnp.where(odd, inner[1], outer[0])
        rows_in[t, 8:16, :] = jnp.where(odd, inner[0], outer[1])
        rows_in[t, 16:24, :] = jnp.where(odd, outer[1], inner[0])
        rows_in[t, 24:32, :] = jnp.where(odd, outer[0], inner[1])
        return carry

    def vertical_step(t, carry):
        value = vertical(lambda s: rows_in[t, pl.ds(s, wide), :])
        padded[:, tile_of(t + 1)] = cut(jnp.concatenate([value, spare], axis=0))
        return carry

    def horizontal_step(t, total):
        smooth = jnp.where(inside, horizontal(padded, band, t), 0.0)
        raw = [jnp.concatenate([rows_in[2 * t + c, pl.ds(4, wide), :], spare], axis=0) for c in range(2)]
        detail = jnp.concatenate(raw, axis=1) - smooth
        square = jnp.where(own, detail * detail, 0.0)
        for array, value in ((clean, cut(smooth)), (fine, cut(detail))):
            array[2 * t + 1] = value[:, :lanes]
            array[2 * t + 2] = value[:, lanes:]
        return total + fold(square[:, :lanes]) + fold(square[:, lanes:])

    by_tiles(load_step, tiles, 8)
    by_tiles(vertical_step, tiles, 8)
    ref_power = by_tiles(horizontal_step, tiles // 2, 8, jnp.zeros((8, lanes), jnp.float32))
    fine[tiles + 3] = fine[1]
    shift = column_shift(base[0, 1])
    stream[2 * slot : 4 * slot, :] = jnp.zeros((2 * slot, ring * lanes), jnp.bfloat16)

    def stream_step(t, carry):
        stream[0 : 2 * slot, tile_of(t)] = shift(fine, t)
        return carry

    by_tiles(stream_step, ring, ring // 2)
    product = lax.dot_general(
        stack[...], stream[...], (((1,), (1,)), ((), ())), preferred_element_type=jnp.float32
    )
    size = reach * count * rows
    product = product[:size] + product[size:]
    product = by_row_shift(product, rows, -1)
    lags[...] = jnp.zeros(lags.shape, jnp.float32)
    for j in range(reach):
        for f in range(count):
            start = (j * count + f) * rows
            lags[f * 8 + j : f * 8 + j + 1, :] = jnp.sum(product[start : start + rows], axis=0, keepdims=True)
    back = 2 * lanes - 1 - base[0, 0]
    across = lax.broadcasted_iota(jnp.int32, (8, lanes), 0)
    lane = lane_of((8, lanes))
    packed = jnp.zeros((8, lanes), jnp.float32)
    for f in range(count):
        block = lags[f * 8 : f * 8 + 8, :]
        for j in range(reach):
            at = (f * reach + j) * reach
            high = pltpu.roll(block, (back + at) & (lanes - 1), 1)
            low = pltpu.roll(block, (back + at - slot) & (lanes - 1), 1)
            packed = packed + jnp.where((across == j) & (lane >= at) & (lane < at + reach), high + low, 0.0)
    lags[0:8, :] = jnp.zeros((8, lanes), jnp.float32)
    for f in range(count):
        lags[f : f + 1, :] = jnp.sum(power[f * 8 : f * 8 + 8, :], axis=0, keepdims=True)
    lags[count : count + 1, :] = jnp.sum(ref_power, axis=0, keepdims=True)
    powers = jnp.sum(lags[0:8, :], axis=1, keepdims=True)
    packed = packed + jnp.where(lane == count * reach * reach + across, powers, 0.0)
    part[...] = jnp.broadcast_to(jnp.sum(packed, axis=0, keepdims=True), part.shape)


def spread_columns(clean, spread, base_col):
    tiles = clean.shape[0] - 2
    full = spread.shape[0] // 2
    spare = jnp.zeros((full - reach * slot, tiles * lanes), jnp.bfloat16)
    spread[reach * slot : full, :] = spare
    spread[full + reach * slot : 2 * full, :] = spare

    def per_offset(j, carry):
        shift = column_shift(base_col + j - 3)
        at = pl.multiple_of(j * slot, slot)

        def step(t, inner):
            turned = shift(clean, t)
            spread[pl.ds(at, slot), tile_of(t)] = turned[:slot]
            spread[pl.ds(full + at, slot), tile_of(t)] = turned[slot:]
            return inner

        by_tiles(step, tiles, 32)
        return carry

    lax.fori_loop(0, reach, per_offset, 0)


def blend_weights(totals, count):
    lane = lane_of(totals.shape)
    block = reach * reach

    def pick(index):
        return jnp.sum(jnp.where(lane == index, totals, 0.0), axis=1, keepdims=True)

    ref_power = pick(count * block + count)
    weights = []
    for f in range(count):
        norm_product = jnp.sqrt((pick(count * block + f) + 1e-06) * (ref_power + 1e-06))
        member = (lane >= f * block) & (lane < (f + 1) * block)
        rho = jnp.where(member, totals, 0.0) / norm_product
        squared = rho * rho
        middle = jnp.where(lane == f * block + block // 2, 0.05, 0.0)
        weights.append((squared + middle) / (0.05 + jnp.sum(squared, axis=1, keepdims=True)))
    return weights


def banded(weights, f, rows, first_row):
    lane = lane_of(weights.shape)
    tiles = []
    for group in (range(4), range(4, reach)):
        line = jnp.zeros_like(weights)
        for j in group:
            at = first_row + (j % 4) * slot
            turned = pltpu.roll(weights, (at + 2 * lanes - (f * reach + j) * reach) & (lanes - 1), 1)
            line = jnp.where((lane >= at) & (lane < at + reach), turned, line)
        line = jnp.broadcast_to(line[0:1], (rows, lanes))
        tiles.append(by_row_shift(line, rows, 1))
    return jnp.concatenate(tiles, axis=1)


def pressures(base, totals, clean, spread, inverse):
    count, rows, columns = inverse.shape
    full = spread.shape[0] // 2
    weights = blend_weights(jnp.broadcast_to(totals[0:1, :], (8, lanes)), count)
    bands = [banded(weights[f], f, rows, 1 + base[0, 0]) for f in range(count)]
    mixing = jnp.concatenate(halves(jnp.concatenate(bands, axis=0)), axis=0)
    spread_columns(clean, spread, base[0, 1])

    def chunk_values(where):
        product = jnp.dot(mixing, spread[0:full, where], preferred_element_type=jnp.float32)
        product = product + jnp.dot(mixing, spread[full : 2 * full, where], preferred_element_type=jnp.float32)
        registered = product[: count * rows] + product[count * rows :]
        values = []
        for f in range(count):
            ratio = registered[f * rows : (f + 1) * rows] * inverse[f, :, where]
            values.append(calib_zero + ratio * (calib_linear + calib_square * ratio))
        return values

    return chunk_values


def pressure_kernel(base, totals, clean, inverse, pressure, moments, part, spread):
    count, rows, columns = inverse.shape
    chunk_values = pressures(base, totals, clean, spread, inverse)

    def step(t, sums):
        where = chunk_of(t)
        values = chunk_values(where)
        squares = [value * value for value in values]
        for f in range(count):
            pressure[f, :, where] = values[f]
        moments[0, :, where] = sum(values[1:], values[0])
        moments[1, :, where] = sum(squares[1:], squares[0])
        result = []
        for total, array in zip(sums, values + squares):
            result.append(total + fold(array[:, :lanes]) + fold(array[:, lanes:]))
        return tuple(result)

    zero = jnp.zeros((8, lanes), jnp.float32)
    sums = by_tiles(step, columns // (2 * lanes), 8, (zero,) * (2 * count))
    line = zero
    for k in range(2 * count):
        value = jnp.sum(jnp.sum(sums[k], axis=0, keepdims=True), axis=1, keepdims=True)
        line = line + jnp.where(lane_of(line.shape) == k, value, 0.0)
    part[...] = jnp.broadcast_to(line[0:1], part.shape)


def time_kernel(base, totals, clean, inverse, moments, time_mean, time_rms, spread):
    count, rows, columns = inverse.shape
    chunk_values = pressures(base, totals, clean, spread, inverse)
    frames = 2 * count

    def step(t, carry):
        where = chunk_of(t)
        first = moments[0, :, where]
        second = moments[1, :, where]
        for value in chunk_values(where):
            first = first + value
            second = second + value * value
        mean = first * (1.0 / frames)
        time_mean[:, where] = mean
        time_rms[:, where] = jnp.sqrt(jnp.maximum(second * (1.0 / frames) - mean * mean, 0.0))
        return carry

    by_tiles(step, columns // (2 * lanes), 8)


def paired(value, axis, first):
    size = lax.axis_size(axis)
    partner = list(range(size))
    for i in range(first, size - 1, 2):
        partner[i], partner[i + 1] = i + 1, i
    return lax.ppermute(value, axis, list(enumerate(partner)))


def by_parity(odd, array, height, dim):
    length = array.shape[dim]
    low = lax.slice_in_dim(array, 0, height, axis=dim)
    high = lax.slice_in_dim(array, length - height, length, axis=dim)
    return jnp.where(odd, high, low), jnp.where(odd, low, high)


def from_owner(shard, odd, axis, root):
    mine = lax.axis_index(axis) == root
    height = shard.shape[0] // 2
    if lax.axis_size(axis) != 2:
        whole = lax.psum(jnp.where(mine, shard, jnp.zeros_like(shard)), axis)
        return by_parity(odd, whole, height, 0)
    here = lax.optimization_barrier(jnp.maximum(shard, 0.0))
    odd_here, even_here = by_parity(odd, here, height, 0)
    odd_there = paired(odd_here, axis, 0)
    even_here, odd_there = lax.optimization_barrier((even_here, odd_there))
    even_there = paired(even_here, axis, 0)
    return jnp.where(mine, odd_here, odd_there), jnp.where(mine, even_here, even_there)


def total_over(value, axis):
    size = lax.axis_size(axis)
    if size & (size - 1):
        return lax.psum(value, axis)
    step = 1
    while step < size:
        value = value + lax.ppermute(value, axis, [(i, i ^ step) for i in range(size)])
        step *= 2
    return value


def shards(frames_raw, wind_off, run_owner, search_base):
    count, rows, columns = frames_raw.shape
    tiles = columns // lanes
    ring = tiles + 2
    wide = rows + 8
    depth = reach * count * rows
    size = lax.axis_size("rows")
    f32 = jnp.float32
    bf16 = jnp.bfloat16
    struct = functools.partial(jax.ShapeDtypeStruct, dtype=f32)
    odd = lax.axis_index("rows") % 2 == 1
    raw = lax.optimization_barrier(jnp.maximum(frames_raw, 0.0))
    offsets = jnp.clip(search_base, -8, 8)
    frames_odd, frames_even = by_parity(odd, raw, 4, 1)
    frames_odd, run = lax.optimization_barrier((frames_odd, wind_off[0]))
    frames_odd = paired(frames_odd, "rows", 1)
    frames_even = paired(frames_even, "rows", 0)
    own_odd, own_even = from_owner(run, odd, "frames", run_owner[0])
    from_odd = paired(own_odd, "rows", 1)
    inverse, stack, power = pl.pallas_call(
        smooth_kernel,
        out_shape=(
            struct((count, rows, columns)),
            jax.ShapeDtypeStruct((2 * depth, ring * lanes), bf16),
            struct((8 * count, lanes)),
        ),
        in_specs=[vmem] * 3,
        out_specs=(vmem,) * 3,
        scratch_shapes=[
            pltpu.VMEM((count, tiles, rows + 16, lanes), f32),
            pltpu.VMEM((2 * count * rows, (tiles + 2) * lanes), bf16),
            pltpu.VMEM((4 * lanes, 2 * lanes), bf16),
            pltpu.VMEM((ring + 2, 2 * count * rows, lanes), bf16),
        ],
        compiler_params=params,
        cost_estimate=cost(8),
        name="smooth",
    )(raw, frames_odd, frames_even)
    own_even, power = lax.optimization_barrier((own_even, power))
    from_even = paired(own_even, "rows", 0)
    blocks = lax.axis_size("frames")
    clean, part = pl.pallas_call(
        match_kernel,
        out_shape=(jax.ShapeDtypeStruct((tiles + 2, 2 * slot, lanes), bf16), struct((size, lanes))),
        in_specs=[smem] + [vmem] * 6,
        out_specs=(vmem, vmem),
        scratch_shapes=[
            pltpu.VMEM((tiles, rows + 16, lanes), f32),
            pltpu.VMEM((2 * slot, (tiles + 2) * lanes), bf16),
            pltpu.VMEM((4 * lanes, 2 * lanes), bf16),
            pltpu.VMEM((ring + 2, 2 * slot, lanes), bf16),
            pltpu.VMEM((4 * slot, ring * lanes), bf16),
            pltpu.VMEM((8 * count, lanes), f32),
        ],
        compiler_params=params,
        cost_estimate=cost(12),
        name="match",
    )(offsets, own_odd, own_even, from_odd, from_even, stack, power)
    if blocks == 2:
        inverse_out, part = lax.optimization_barrier((inverse, part))
        other_inverse = paired(inverse_out, "frames", 0)
    parts = lax.all_to_all(part, "rows", 0, 0, tiled=True)
    totals = jnp.sum(parts, axis=0, keepdims=True)
    spread = pltpu.VMEM((2 * 8 * slot, columns), bf16)
    pressure, moments, part = pl.pallas_call(
        pressure_kernel,
        out_shape=(struct((count, rows, columns)), struct((2, rows, columns)), struct((size, lanes))),
        in_specs=[smem] + [vmem] * 3,
        out_specs=(vmem, vmem, vmem),
        scratch_shapes=[spread],
        compiler_params=params,
        cost_estimate=cost(12),
        name="pressure",
    )(offsets, totals, clean, inverse)
    if blocks == 2:
        row = jnp.concatenate([totals[:, : lanes - 2], offsets.astype(f32)], axis=1)
        row, part = lax.optimization_barrier((row, part))
        row = paired(row, "frames", 0)
        time_mean, time_rms = pl.pallas_call(
            time_kernel,
            out_shape=(struct((rows, columns)), struct((rows, columns))),
            in_specs=[smem] + [vmem] * 4,
            out_specs=(vmem, vmem),
            scratch_shapes=[spread],
            compiler_params=params,
            cost_estimate=cost(12),
            name="time",
        )(row[:, lanes - 2 :].astype(jnp.int32), row, clean, other_inverse, moments)
    else:
        whole = total_over(moments, "frames")
        total_frames = count * blocks
        time_mean = whole[0] / total_frames
        time_rms = jnp.sqrt(jnp.maximum(whole[1] / total_frames - time_mean * time_mean, 0.0))
    sums = lax.all_to_all(part, "rows", 0, 0, tiled=True)
    sums, time_mean, time_rms = lax.optimization_barrier((sums, time_mean, time_rms))
    spatial = jnp.sum(sums, axis=0)
    cell_count = rows * columns * size
    frame_mean = spatial[:count] / cell_count
    frame_rms = jnp.sqrt(spatial[count : 2 * count] / cell_count - frame_mean * frame_mean)
    return (pressure, frame_mean, frame_rms, time_mean, time_rms)


def solution(mesh):
    placed = (P("frames", "rows", None), P("frames", "rows", None), P("rows"), P("frames", None))
    return jax.shard_map(
        shards,
        mesh=mesh,
        in_specs=placed,
        out_specs=(
            P("frames", "rows", None),
            P("frames"),
            P("frames"),
            P("rows", None),
            P("rows", None),
        ),
        check_vma=False,
    )
```

```python
import functools

import jax
import jax.numpy as jnp
from jax import lax
from jax.experimental import pallas as pl
from jax.experimental.pallas import tpu as pltpu
from jax.sharding import PartitionSpec as P

taps = (1.0 / 256, 8.0 / 256, 28.0 / 256, 56.0 / 256, 70.0 / 256)
calib_zero = -0.25
calib_linear = 1.0
calib_square = 0.15
lanes = 128
reach = 7
slot = 32
params = pltpu.CompilerParams(vmem_limit_bytes=14 * 1024 * 1024)
vmem = pl.BlockSpec(memory_space=pltpu.VMEM)
smem = pl.BlockSpec(memory_space=pltpu.SMEM)


def cost(mebibytes):
    return pl.CostEstimate(flops=0, bytes_accessed=mebibytes * 2**20, transcendentals=0)


def tile_of(index):
    return pl.ds(pl.multiple_of(index * lanes, lanes), lanes)


def by_tiles(step, tiles, group, init=()):
    def body(index, carry):
        for inner in range(group):
            carry = step(index * group + inner, carry)
        return carry

    return lax.fori_loop(0, tiles // group, body, init)


def lane_of(shape):
    return lax.broadcasted_iota(jnp.int32, shape, len(shape) - 1)


def fold(product):
    return jnp.sum(product.reshape(product.shape[0] // 8, 8, lanes), axis=0)


def vertical(load):
    total = taps[4] * load(4)
    for step in range(4):
        total = total + taps[step] * (load(step) + load(8 - step))
    return total


def moved(before, here, after, step):
    if step > 0:
        return pltpu.roll(jnp.where(lane_of(here.shape) < step, after, here), lanes - step, 1)
    if step < 0:
        return pltpu.roll(jnp.where(lane_of(here.shape) >= lanes + step, before, here), -step, 1)
    return here


def halves(value):
    high = value.astype(jnp.bfloat16)
    low = (value - high.astype(jnp.float32)).astype(jnp.bfloat16)
    return high, low


def cut(value):
    return jnp.concatenate(halves(value), axis=0)


def fill_band(band):
    shape = (lanes, lanes)
    apart = lax.broadcasted_iota(jnp.int32, shape, 0) - lax.broadcasted_iota(jnp.int32, shape, 1)

    def block(offset):
        distance = jnp.abs(apart + offset)
        value = jnp.zeros(shape, jnp.float32)
        for step in range(5):
            value = jnp.where(distance == step, taps[4 - step], value)
        return value.astype(jnp.bfloat16)

    none = jnp.zeros(shape, jnp.bfloat16)
    before, here, after = block(-lanes), block(0), block(lanes)
    for index, pair in enumerate(((before, none), (here, before), (after, here), (none, after))):
        band[index * lanes : (index + 1) * lanes, :] = jnp.concatenate(pair, axis=1)


def chunk_of(t):
    return pl.ds(pl.multiple_of(t * 2 * lanes, 2 * lanes), 2 * lanes)


def horizontal(wide, band, t):
    window = wide[:, pl.ds(pl.multiple_of(t * 2 * lanes, 2 * lanes), 4 * lanes)]
    product = jnp.dot(window, band[...], preferred_element_type=jnp.float32)
    half = product.shape[0] // 2
    return product[:half] + product[half:]


def by_row_shift(value, rows, direction):
    place = lax.broadcasted_iota(jnp.int32, value.shape, 0) % rows
    unit = 1
    while unit < rows:
        digit = (place // unit) % 4
        result = value
        for times in range(1, 4):
            amount = times * unit
            turned = pltpu.roll(value, amount if direction > 0 else lanes - amount, 1)
            result = jnp.where(digit == times, turned, result)
        value = result
        unit *= 4
    return value


def at_edge():
    index = lax.axis_index("rows")
    return (index == 0) | (index == lax.axis_size("rows") - 1)


def smooth_kernel(frames, from_odd, from_even, inverse, stack, power, band, rows_in, wide, pieces):
    count, rows, columns = frames.shape
    tiles = columns // lanes
    ring = tiles + 2
    odd = lax.axis_index("rows") % 2 == 1
    edge = at_edge()
    blank = jnp.zeros((2 * count * rows, lanes), jnp.bfloat16)
    wide[:, tile_of(0)] = blank
    wide[:, tile_of(tiles + 1)] = blank
    fill_band(band)
    pieces[0] = blank
    pieces[tiles + 1] = blank
    pieces[tiles + 2] = blank

    def load_step(t, carry):
        for f in range(count):
            outer = jnp.where(edge, 0.0, from_odd[f, :, tile_of(t)])
            inner = from_even[f, :, tile_of(t)]
            rows_in[f, t, 4:8, :] = jnp.where(odd, inner, outer)
            rows_in[f, t, 8 : 8 + rows, :] = frames[f, :, tile_of(t)]
            rows_in[f, t, 8 + rows : 12 + rows, :] = jnp.where(odd, outer, inner)
        return carry

    def vertical_step(t, carry):
        parts = [vertical(lambda s: rows_in[f, t, pl.ds(4 + s, rows), :]) for f in range(count)]
        wide[:, tile_of(t + 1)] = cut(jnp.concatenate(parts, axis=0))
        return carry

    def horizontal_step(t, totals):
        smooth = horizontal(wide, band, t)
        result = []
        details = []
        for f in range(count):
            part = smooth[f * rows : (f + 1) * rows]
            inverse[f, :, chunk_of(t)] = 1.0 / part
            details.append(frames[f, :, chunk_of(t)] - part)
            square = details[f] * details[f]
            result.append(totals[f] + fold(square[:, :lanes]) + fold(square[:, lanes:]))
        detail = cut(jnp.concatenate(details, axis=0))
        pieces[2 * t + 1] = detail[:, :lanes]
        pieces[2 * t + 2] = detail[:, lanes:]
        return tuple(result)

    def stack_step(t, carry):
        before, here, after = pieces[t], pieces[t + 1], pieces[t + 2]
        size = count * rows
        for j in range(reach):
            turned = moved(before, here, after, 3 - j)
            stack[j * size : (j + 1) * size, tile_of(t)] = turned[:size]
            stack[(reach + j) * size : (reach + j + 1) * size, tile_of(t)] = turned[size:]
        return carry

    by_tiles(load_step, tiles, 8)
    by_tiles(vertical_step, tiles, 8)
    powers = by_tiles(horizontal_step, tiles // 2, 8, (jnp.zeros((8, lanes), jnp.float32),) * count)
    for f in range(count):
        power[f * 8 : f * 8 + 8, :] = powers[f]
    pieces[tiles + 3] = pieces[1]
    by_tiles(stack_step, ring, ring // 2)


def column_shift(offset):
    negative = offset < 0
    first = jnp.where(negative, 0, 1)
    amount = jnp.where(negative, offset + lanes, offset)
    back = (lanes - amount) & (lanes - 1)

    def shift(source, t):
        here = source[t + first]
        after = source[t + first + 1]
        return pltpu.roll(jnp.where(lane_of(here.shape) < amount, after, here), back, 1)

    return shift


def match_kernel(
    base, own_odd, own_even, from_odd, from_even, stack, power, band, clean, part, rows_in, padded, fine, stream, lags
):
    rows = own_odd.shape[0] * 2
    tiles = own_odd.shape[1] // lanes
    count = power.shape[0] // 8
    ring = tiles + 2
    wide = rows + 8
    row_index = lax.axis_index("rows")
    last_row = lax.axis_size("rows") - 1
    odd = row_index % 2 == 1
    edge = at_edge()
    empty = jnp.zeros((2 * slot, lanes), jnp.bfloat16)
    padded[:, tile_of(0)] = empty
    padded[:, tile_of(tiles + 1)] = empty
    for array in (clean, fine):
        array[0] = empty
        array[tiles + 1] = empty
    fine[tiles + 2] = empty
    spare = jnp.zeros((slot - wide, lanes), jnp.float32)
    place = lax.broadcasted_iota(jnp.int32, (slot, 2 * lanes), 0)
    own = (place >= 4) & (place < rows + 4)
    inside = ((place >= 4) | (row_index > 0)) & ((place < rows + 4) | (row_index < last_row)) & (place < wide)

    def load_step(t, carry):
        outer = [jnp.where(edge, 0.0, from_odd[:, tile_of(t)]), own_odd[:, tile_of(t)]]
        inner = [array[:, tile_of(t)] for array in (own_even, from_even)]
        rows_in[t, 0:8, :] = jnp.where(odd, inner[1], outer[0])
        rows_in[t, 8:16, :] = jnp.where(odd, inner[0], outer[1])
        rows_in[t, 16:24, :] = jnp.where(odd, outer[1], inner[0])
        rows_in[t, 24:32, :] = jnp.where(odd, outer[0], inner[1])
        return carry

    def vertical_step(t, carry):
        value = vertical(lambda s: rows_in[t, pl.ds(s, wide), :])
        padded[:, tile_of(t + 1)] = cut(jnp.concatenate([value, spare], axis=0))
        return carry

    def horizontal_step(t, total):
        smooth = jnp.where(inside, horizontal(padded, band, t), 0.0)
        raw = [jnp.concatenate([rows_in[2 * t + c, pl.ds(4, wide), :], spare], axis=0) for c in range(2)]
        detail = jnp.concatenate(raw, axis=1) - smooth
        square = jnp.where(own, detail * detail, 0.0)
        for array, value in ((clean, cut(smooth)), (fine, cut(detail))):
            array[2 * t + 1] = value[:, :lanes]
            array[2 * t + 2] = value[:, lanes:]
        return total + fold(square[:, :lanes]) + fold(square[:, lanes:])

    by_tiles(load_step, tiles, 8)
    by_tiles(vertical_step, tiles, 8)
    ref_power = by_tiles(horizontal_step, tiles // 2, 8, jnp.zeros((8, lanes), jnp.float32))
    fine[tiles + 3] = fine[1]
    shift = column_shift(base[0, 1])
    stream[2 * slot : 4 * slot, :] = jnp.zeros((2 * slot, ring * lanes), jnp.bfloat16)

    def stream_step(t, carry):
        stream[0 : 2 * slot, tile_of(t)] = shift(fine, t)
        return carry

    by_tiles(stream_step, ring, ring // 2)
    product = lax.dot_general(
        stack[...], stream[...], (((1,), (1,)), ((), ())), preferred_element_type=jnp.float32
    )
    size = reach * count * rows
    product = product[:size] + product[size:]
    product = by_row_shift(product, rows, -1)
    lags[...] = jnp.zeros(lags.shape, jnp.float32)
    for j in range(reach):
        for f in range(count):
            start = (j * count + f) * rows
            lags[f * 8 + j : f * 8 + j + 1, :] = jnp.sum(product[start : start + rows], axis=0, keepdims=True)
    back = 2 * lanes - 1 - base[0, 0]
    across = lax.broadcasted_iota(jnp.int32, (8, lanes), 0)
    lane = lane_of((8, lanes))
    packed = jnp.zeros((8, lanes), jnp.float32)
    for f in range(count):
        block = lags[f * 8 : f * 8 + 8, :]
        for j in range(reach):
            at = (f * reach + j) * reach
            high = pltpu.roll(block, (back + at) & (lanes - 1), 1)
            low = pltpu.roll(block, (back + at - slot) & (lanes - 1), 1)
            packed = packed + jnp.where((across == j) & (lane >= at) & (lane < at + reach), high + low, 0.0)
    lags[0:8, :] = jnp.zeros((8, lanes), jnp.float32)
    for f in range(count):
        lags[f : f + 1, :] = jnp.sum(power[f * 8 : f * 8 + 8, :], axis=0, keepdims=True)
    lags[count : count + 1, :] = jnp.sum(ref_power, axis=0, keepdims=True)
    powers = jnp.sum(lags[0:8, :], axis=1, keepdims=True)
    packed = packed + jnp.where(lane == count * reach * reach + across, powers, 0.0)
    part[...] = jnp.sum(packed, axis=0, keepdims=True)


def spread_columns(clean, spread, base_col):
    tiles = clean.shape[0] - 2
    full = spread.shape[0] // 2
    spare = jnp.zeros((full - reach * slot, tiles * lanes), jnp.bfloat16)
    spread[reach * slot : full, :] = spare
    spread[full + reach * slot : 2 * full, :] = spare

    def per_offset(j, carry):
        shift = column_shift(base_col + j - 3)
        at = pl.multiple_of(j * slot, slot)

        def step(t, inner):
            turned = shift(clean, t)
            spread[pl.ds(at, slot), tile_of(t)] = turned[:slot]
            spread[pl.ds(full + at, slot), tile_of(t)] = turned[slot:]
            return inner

        by_tiles(step, tiles, 32)
        return carry

    lax.fori_loop(0, reach, per_offset, 0)


def blend_weights(totals, count):
    lane = lane_of(totals.shape)
    block = reach * reach

    def pick(index):
        return jnp.sum(jnp.where(lane == index, totals, 0.0), axis=1, keepdims=True)

    ref_power = pick(count * block + count)
    weights = []
    for f in range(count):
        norm_product = jnp.sqrt((pick(count * block + f) + 1e-06) * (ref_power + 1e-06))
        member = (lane >= f * block) & (lane < (f + 1) * block)
        rho = jnp.where(member, totals, 0.0) / norm_product
        squared = rho * rho
        middle = jnp.where(lane == f * block + block // 2, 0.05, 0.0)
        weights.append((squared + middle) / (0.05 + jnp.sum(squared, axis=1, keepdims=True)))
    return weights


def banded(weights, f, rows, first_row):
    lane = lane_of(weights.shape)
    tiles = []
    for group in (range(4), range(4, reach)):
        line = jnp.zeros_like(weights)
        for j in group:
            at = first_row + (j % 4) * slot
            turned = pltpu.roll(weights, (at + 2 * lanes - (f * reach + j) * reach) & (lanes - 1), 1)
            line = jnp.where((lane >= at) & (lane < at + reach), turned, line)
        line = jnp.broadcast_to(line[0:1], (rows, lanes))
        tiles.append(by_row_shift(line, rows, 1))
    return jnp.concatenate(tiles, axis=1)


def pressures(base, totals, clean, spread, inverse):
    count, rows, columns = inverse.shape
    full = spread.shape[0] // 2
    weights = blend_weights(jnp.broadcast_to(totals[0:1, :], (8, lanes)), count)
    bands = [banded(weights[f], f, rows, 1 + base[0, 0]) for f in range(count)]
    mixing = jnp.concatenate(halves(jnp.concatenate(bands, axis=0)), axis=0)
    spread_columns(clean, spread, base[0, 1])

    def chunk_values(where):
        product = jnp.dot(mixing, spread[0:full, where], preferred_element_type=jnp.float32)
        product = product + jnp.dot(mixing, spread[full : 2 * full, where], preferred_element_type=jnp.float32)
        registered = product[: count * rows] + product[count * rows :]
        values = []
        for f in range(count):
            ratio = registered[f * rows : (f + 1) * rows] * inverse[f, :, where]
            values.append(calib_zero + ratio * (calib_linear + calib_square * ratio))
        return values

    return chunk_values


def pressure_kernel(base, totals, clean, inverse, pressure, moments, part, spread):
    count, rows, columns = inverse.shape
    chunk_values = pressures(base, totals, clean, spread, inverse)

    def step(t, sums):
        where = chunk_of(t)
        values = chunk_values(where)
        squares = [value * value for value in values]
        for f in range(count):
            pressure[f, :, where] = values[f]
        moments[0, :, where] = sum(values[1:], values[0])
        moments[1, :, where] = sum(squares[1:], squares[0])
        result = []
        for total, array in zip(sums, values + squares):
            result.append(total + fold(array[:, :lanes]) + fold(array[:, lanes:]))
        return tuple(result)

    zero = jnp.zeros((8, lanes), jnp.float32)
    sums = by_tiles(step, columns // (2 * lanes), 8, (zero,) * (2 * count))
    line = zero
    for k in range(2 * count):
        value = jnp.sum(jnp.sum(sums[k], axis=0, keepdims=True), axis=1, keepdims=True)
        line = line + jnp.where(lane_of(line.shape) == k, value, 0.0)
    part[...] = line[0:1]


def time_kernel(base, totals, clean, inverse, moments, time_mean, time_rms, spread):
    count, rows, columns = inverse.shape
    chunk_values = pressures(base, totals, clean, spread, inverse)
    frames = 2 * count

    def step(t, carry):
        where = chunk_of(t)
        first = moments[0, :, where]
        second = moments[1, :, where]
        for value in chunk_values(where):
            first = first + value
            second = second + value * value
        mean = first * (1.0 / frames)
        time_mean[:, where] = mean
        time_rms[:, where] = jnp.sqrt(jnp.maximum(second * (1.0 / frames) - mean * mean, 0.0))
        return carry

    by_tiles(step, columns // (2 * lanes), 8)


def paired(value, axis, first):
    size = lax.axis_size(axis)
    partner = list(range(size))
    for i in range(first, size - 1, 2):
        partner[i], partner[i + 1] = i + 1, i
    return lax.ppermute(value, axis, list(enumerate(partner)))


def by_parity(odd, array, height, dim):
    length = array.shape[dim]
    low = lax.slice_in_dim(array, 0, height, axis=dim)
    high = lax.slice_in_dim(array, length - height, length, axis=dim)
    return jnp.where(odd, high, low), jnp.where(odd, low, high)


def from_owner(shard, here, odd, axis, root):
    mine = lax.axis_index(axis) == root
    height = shard.shape[0] // 2
    if lax.axis_size(axis) != 2:
        whole = lax.psum(jnp.where(mine, shard, jnp.zeros_like(shard)), axis)
        return by_parity(odd, whole, height, 0)
    there = by_parity(odd, paired(shard, axis, 0), height, 0)
    here = by_parity(odd, here, height, 0)
    return [jnp.where(mine, own, other) for own, other in zip(here, there)]


def total_over_rows(row):
    size = lax.axis_size("rows")
    row = row + paired(row, "rows", 0)
    groups = [list(range(core, size, 2)) for core in range(2)]
    rows = jnp.broadcast_to(row, (size // 2, lanes))
    return lax.all_to_all(rows, "rows", 0, 0, axis_index_groups=groups, tiled=True)


def total_over(value, axis):
    size = lax.axis_size(axis)
    if size & (size - 1):
        return lax.psum(value, axis)
    step = 1
    while step < size:
        value = value + lax.ppermute(value, axis, [(i, i ^ step) for i in range(size)])
        step *= 2
    return value


def shards(frames_raw, wind_off, run_owner, search_base):
    count, rows, columns = frames_raw.shape
    tiles = columns // lanes
    ring = tiles + 2
    wide = rows + 8
    depth = reach * count * rows
    size = lax.axis_size("rows")
    f32 = jnp.float32
    bf16 = jnp.bfloat16
    struct = functools.partial(jax.ShapeDtypeStruct, dtype=f32)
    odd = lax.axis_index("rows") % 2 == 1
    raw, run = lax.optimization_barrier((jnp.maximum(frames_raw, 0.0), jnp.maximum(wind_off[0], 0.0)))
    own_odd, own_even = from_owner(wind_off[0], run, odd, "frames", run_owner[0])
    from_odd = paired(own_odd, "rows", 1)
    from_even = paired(own_even, "rows", 0)
    offsets = jnp.clip(search_base, -8, 8)
    frames_odd, frames_even = by_parity(odd, raw, 4, 1)
    frames_odd = paired(frames_odd, "rows", 1)
    frames_even = paired(frames_even, "rows", 0)
    inverse, stack, power, band = pl.pallas_call(
        smooth_kernel,
        out_shape=(
            struct((count, rows, columns)),
            jax.ShapeDtypeStruct((2 * depth, ring * lanes), bf16),
            struct((8 * count, lanes)),
            jax.ShapeDtypeStruct((4 * lanes, 2 * lanes), bf16),
        ),
        in_specs=[vmem] * 3,
        out_specs=(vmem,) * 4,
        scratch_shapes=[
            pltpu.VMEM((count, tiles, rows + 16, lanes), f32),
            pltpu.VMEM((2 * count * rows, (tiles + 2) * lanes), bf16),
            pltpu.VMEM((ring + 2, 2 * count * rows, lanes), bf16),
        ],
        compiler_params=params,
        cost_estimate=cost(8),
        name="smooth",
    )(raw, frames_odd, frames_even)
    blocks = lax.axis_size("frames")
    clean, part = pl.pallas_call(
        match_kernel,
        out_shape=(jax.ShapeDtypeStruct((tiles + 2, 2 * slot, lanes), bf16), struct((1, lanes))),
        in_specs=[smem] + [vmem] * 7,
        out_specs=(vmem, vmem),
        scratch_shapes=[
            pltpu.VMEM((tiles, rows + 16, lanes), f32),
            pltpu.VMEM((2 * slot, (tiles + 2) * lanes), bf16),
            pltpu.VMEM((ring + 2, 2 * slot, lanes), bf16),
            pltpu.VMEM((4 * slot, ring * lanes), bf16),
            pltpu.VMEM((8 * count, lanes), f32),
        ],
        compiler_params=params,
        cost_estimate=cost(12),
        name="match",
    )(offsets, own_odd, own_even, from_odd, from_even, stack, power, band)
    if blocks == 2:
        inverse_out, part = lax.optimization_barrier((inverse, part))
        other_inverse = paired(inverse_out, "frames", 0)
    parts = total_over_rows(part)
    totals = jnp.sum(parts, axis=0, keepdims=True)
    spread = pltpu.VMEM((2 * 8 * slot, columns), bf16)
    pressure, moments, part = pl.pallas_call(
        pressure_kernel,
        out_shape=(struct((count, rows, columns)), struct((2, rows, columns)), struct((1, lanes))),
        in_specs=[smem] + [vmem] * 3,
        out_specs=(vmem, vmem, vmem),
        scratch_shapes=[spread],
        compiler_params=params,
        cost_estimate=cost(12),
        name="pressure",
    )(offsets, totals, clean, inverse)
    if blocks == 2:
        row = jnp.concatenate([totals[:, : lanes - 2], offsets.astype(f32)], axis=1)
        row, part = lax.optimization_barrier((row, part))
        row = paired(row, "frames", 0)
        time_mean, time_rms = pl.pallas_call(
            time_kernel,
            out_shape=(struct((rows, columns)), struct((rows, columns))),
            in_specs=[smem] + [vmem] * 4,
            out_specs=(vmem, vmem),
            scratch_shapes=[spread],
            compiler_params=params,
            cost_estimate=cost(12),
            name="time",
        )(row[:, lanes - 2 :].astype(jnp.int32), row, clean, other_inverse, moments)
    else:
        whole = total_over(moments, "frames")
        total_frames = count * blocks
        time_mean = whole[0] / total_frames
        time_rms = jnp.sqrt(jnp.maximum(whole[1] / total_frames - time_mean * time_mean, 0.0))
    sums = total_over_rows(part)
    sums, time_mean, time_rms = lax.optimization_barrier((sums, time_mean, time_rms))
    spatial = jnp.sum(sums, axis=0)
    cell_count = rows * columns * size
    frame_mean = spatial[:count] / cell_count
    frame_rms = jnp.sqrt(spatial[count : 2 * count] / cell_count - frame_mean * frame_mean)
    return (pressure, frame_mean, frame_rms, time_mean, time_rms)


def solution(mesh):
    placed = (P("frames", "rows", None), P("frames", "rows", None), P("rows"), P("frames", None))
    return jax.shard_map(
        shards,
        mesh=mesh,
        in_specs=placed,
        out_specs=(
            P("frames", "rows", None),
            P("frames"),
            P("frames"),
            P("rows", None),
            P("rows", None),
        ),
        check_vma=False,
    )
```

```python
import functools

import jax
import jax.numpy as jnp
from jax import lax
from jax.experimental import pallas as pl
from jax.experimental.pallas import tpu as pltpu
from jax.sharding import PartitionSpec as P

taps = (1.0 / 256, 8.0 / 256, 28.0 / 256, 56.0 / 256, 70.0 / 256)
calib_zero = -0.25
calib_linear = 1.0
calib_square = 0.15
lanes = 128
reach = 7
slot = 32
params = pltpu.CompilerParams(vmem_limit_bytes=14 * 1024 * 1024)
vmem = pl.BlockSpec(memory_space=pltpu.VMEM)
smem = pl.BlockSpec(memory_space=pltpu.SMEM)


def cost(mebibytes):
    return pl.CostEstimate(flops=0, bytes_accessed=mebibytes * 2**20, transcendentals=0)


def tile_of(index):
    return pl.ds(pl.multiple_of(index * lanes, lanes), lanes)


def by_tiles(step, tiles, group, init=()):
    def body(index, carry):
        for inner in range(group):
            carry = step(index * group + inner, carry)
        return carry

    return lax.fori_loop(0, tiles // group, body, init)


def lane_of(shape):
    return lax.broadcasted_iota(jnp.int32, shape, len(shape) - 1)


def fold(product):
    return jnp.sum(product.reshape(product.shape[0] // 8, 8, lanes), axis=0)


def vertical(load):
    total = taps[4] * load(4)
    for step in range(4):
        total = total + taps[step] * (load(step) + load(8 - step))
    return total


def moved(before, here, after, step):
    if step > 0:
        return pltpu.roll(jnp.where(lane_of(here.shape) < step, after, here), lanes - step, 1)
    if step < 0:
        return pltpu.roll(jnp.where(lane_of(here.shape) >= lanes + step, before, here), -step, 1)
    return here


def halves(value):
    high = value.astype(jnp.bfloat16)
    low = (value - high.astype(jnp.float32)).astype(jnp.bfloat16)
    return high, low


def cut(value):
    return jnp.concatenate(halves(value), axis=0)


def fill_band(band):
    shape = (lanes, lanes)
    apart = lax.broadcasted_iota(jnp.int32, shape, 0) - lax.broadcasted_iota(jnp.int32, shape, 1)

    def block(offset):
        distance = jnp.abs(apart + offset)
        value = jnp.zeros(shape, jnp.float32)
        for step in range(5):
            value = jnp.where(distance == step, taps[4 - step], value)
        return value.astype(jnp.bfloat16)

    none = jnp.zeros(shape, jnp.bfloat16)
    before, here, after = block(-lanes), block(0), block(lanes)
    for index, pair in enumerate(((before, none), (here, before), (after, here), (none, after))):
        band[index * lanes : (index + 1) * lanes, :] = jnp.concatenate(pair, axis=1)


def chunk_of(t):
    return pl.ds(pl.multiple_of(t * 2 * lanes, 2 * lanes), 2 * lanes)


def horizontal(wide, band, t):
    window = wide[:, pl.ds(pl.multiple_of(t * 2 * lanes, 2 * lanes), 4 * lanes)]
    product = jnp.dot(window, band[...], preferred_element_type=jnp.float32)
    half = product.shape[0] // 2
    return product[:half] + product[half:]


def by_row_shift(value, rows, direction):
    place = lax.broadcasted_iota(jnp.int32, value.shape, 0) % rows
    unit = 1
    while unit < rows:
        digit = (place // unit) % 4
        result = value
        for times in range(1, 4):
            amount = times * unit
            turned = pltpu.roll(value, amount if direction > 0 else lanes - amount, 1)
            result = jnp.where(digit == times, turned, result)
        value = result
        unit *= 4
    return value


def at_edge():
    index = lax.axis_index("rows")
    return (index == 0) | (index == lax.axis_size("rows") - 1)


def smooth_kernel(frames, from_odd, from_even, inverse, stack, power, band, rows_in, wide, pieces):
    count, rows, columns = frames.shape
    tiles = columns // lanes
    ring = tiles + 2
    odd = lax.axis_index("rows") % 2 == 1
    edge = at_edge()
    blank = jnp.zeros((2 * count * rows, lanes), jnp.bfloat16)
    wide[:, tile_of(0)] = blank
    wide[:, tile_of(tiles + 1)] = blank
    fill_band(band)
    pieces[0] = blank
    pieces[tiles + 1] = blank
    pieces[tiles + 2] = blank

    def load_step(t, carry):
        for f in range(count):
            outer = jnp.where(edge, 0.0, from_odd[f, :, tile_of(t)])
            inner = from_even[f, :, tile_of(t)]
            rows_in[f, t, 4:8, :] = jnp.where(odd, inner, outer)
            rows_in[f, t, 8 : 8 + rows, :] = frames[f, :, tile_of(t)]
            rows_in[f, t, 8 + rows : 12 + rows, :] = jnp.where(odd, outer, inner)
        return carry

    def vertical_step(t, carry):
        parts = [vertical(lambda s: rows_in[f, t, pl.ds(4 + s, rows), :]) for f in range(count)]
        wide[:, tile_of(t + 1)] = cut(jnp.concatenate(parts, axis=0))
        return carry

    def horizontal_step(t, totals):
        smooth = horizontal(wide, band, t)
        result = []
        details = []
        for f in range(count):
            part = smooth[f * rows : (f + 1) * rows]
            inverse[f, :, chunk_of(t)] = 1.0 / part
            details.append(frames[f, :, chunk_of(t)] - part)
            square = details[f] * details[f]
            result.append(totals[f] + fold(square[:, :lanes]) + fold(square[:, lanes:]))
        detail = cut(jnp.concatenate(details, axis=0))
        pieces[2 * t + 1] = detail[:, :lanes]
        pieces[2 * t + 2] = detail[:, lanes:]
        return tuple(result)

    def stack_step(t, carry):
        before, here, after = pieces[t], pieces[t + 1], pieces[t + 2]
        size = count * rows
        for j in range(reach):
            turned = moved(before, here, after, 3 - j)
            stack[j * size : (j + 1) * size, tile_of(t)] = turned[:size]
            stack[(reach + j) * size : (reach + j + 1) * size, tile_of(t)] = turned[size:]
        return carry

    by_tiles(load_step, tiles, 8)
    by_tiles(vertical_step, tiles, 8)
    powers = by_tiles(horizontal_step, tiles // 2, 8, (jnp.zeros((8, lanes), jnp.float32),) * count)
    for f in range(count):
        power[f * 8 : f * 8 + 8, :] = powers[f]
    pieces[tiles + 3] = pieces[1]
    by_tiles(stack_step, ring, ring // 2)


def column_shift(offset):
    negative = offset < 0
    first = jnp.where(negative, 0, 1)
    amount = jnp.where(negative, offset + lanes, offset)
    back = (lanes - amount) & (lanes - 1)

    def shift(source, t):
        here = source[t + first]
        after = source[t + first + 1]
        return pltpu.roll(jnp.where(lane_of(here.shape) < amount, after, here), back, 1)

    return shift


def match_kernel(
    base, own_odd, own_even, from_odd, from_even, stack, power, band, clean, part, rows_in, padded, fine, stream, lags
):
    rows = own_odd.shape[0] * 2
    tiles = own_odd.shape[1] // lanes
    count = power.shape[0] // 8
    ring = tiles + 2
    wide = rows + 8
    row_index = lax.axis_index("rows")
    last_row = lax.axis_size("rows") - 1
    odd = row_index % 2 == 1
    edge = at_edge()
    empty = jnp.zeros((2 * slot, lanes), jnp.bfloat16)
    padded[:, tile_of(0)] = empty
    padded[:, tile_of(tiles + 1)] = empty
    for array in (clean, fine):
        array[0] = empty
        array[tiles + 1] = empty
    fine[tiles + 2] = empty
    spare = jnp.zeros((slot - wide, lanes), jnp.float32)
    place = lax.broadcasted_iota(jnp.int32, (slot, 2 * lanes), 0)
    own = (place >= 4) & (place < rows + 4)
    inside = ((place >= 4) | (row_index > 0)) & ((place < rows + 4) | (row_index < last_row)) & (place < wide)

    def load_step(t, carry):
        outer = [jnp.where(edge, 0.0, from_odd[:, tile_of(t)]), own_odd[:, tile_of(t)]]
        inner = [array[:, tile_of(t)] for array in (own_even, from_even)]
        rows_in[t, 0:8, :] = jnp.where(odd, inner[1], outer[0])
        rows_in[t, 8:16, :] = jnp.where(odd, inner[0], outer[1])
        rows_in[t, 16:24, :] = jnp.where(odd, outer[1], inner[0])
        rows_in[t, 24:32, :] = jnp.where(odd, outer[0], inner[1])
        return carry

    def vertical_step(t, carry):
        value = vertical(lambda s: rows_in[t, pl.ds(s, wide), :])
        padded[:, tile_of(t + 1)] = cut(jnp.concatenate([value, spare], axis=0))
        return carry

    def horizontal_step(t, total):
        smooth = jnp.where(inside, horizontal(padded, band, t), 0.0)
        raw = [jnp.concatenate([rows_in[2 * t + c, pl.ds(4, wide), :], spare], axis=0) for c in range(2)]
        detail = jnp.concatenate(raw, axis=1) - smooth
        square = jnp.where(own, detail * detail, 0.0)
        for array, value in ((clean, cut(smooth)), (fine, cut(detail))):
            array[2 * t + 1] = value[:, :lanes]
            array[2 * t + 2] = value[:, lanes:]
        return total + fold(square[:, :lanes]) + fold(square[:, lanes:])

    by_tiles(load_step, tiles, 8)
    by_tiles(vertical_step, tiles, 8)
    ref_power = by_tiles(horizontal_step, tiles // 2, 8, jnp.zeros((8, lanes), jnp.float32))
    fine[tiles + 3] = fine[1]
    shift = column_shift(base[0, 1])
    stream[2 * slot : 4 * slot, :] = jnp.zeros((2 * slot, ring * lanes), jnp.bfloat16)

    def stream_step(t, carry):
        stream[0 : 2 * slot, tile_of(t)] = shift(fine, t)
        return carry

    by_tiles(stream_step, ring, ring // 2)
    product = lax.dot_general(
        stack[...], stream[...], (((1,), (1,)), ((), ())), preferred_element_type=jnp.float32
    )
    size = reach * count * rows
    product = product[:size] + product[size:]
    product = by_row_shift(product, rows, -1)
    lags[...] = jnp.zeros(lags.shape, jnp.float32)
    for j in range(reach):
        for f in range(count):
            start = (j * count + f) * rows
            lags[f * 8 + j : f * 8 + j + 1, :] = jnp.sum(product[start : start + rows], axis=0, keepdims=True)
    back = 2 * lanes - 1 - base[0, 0]
    across = lax.broadcasted_iota(jnp.int32, (8, lanes), 0)
    lane = lane_of((8, lanes))
    packed = jnp.zeros((8, lanes), jnp.float32)
    for f in range(count):
        block = lags[f * 8 : f * 8 + 8, :]
        for j in range(reach):
            at = (f * reach + j) * reach
            high = pltpu.roll(block, (back + at) & (lanes - 1), 1)
            low = pltpu.roll(block, (back + at - slot) & (lanes - 1), 1)
            packed = packed + jnp.where((across == j) & (lane >= at) & (lane < at + reach), high + low, 0.0)
    lags[0:8, :] = jnp.zeros((8, lanes), jnp.float32)
    for f in range(count):
        lags[f : f + 1, :] = jnp.sum(power[f * 8 : f * 8 + 8, :], axis=0, keepdims=True)
    lags[count : count + 1, :] = jnp.sum(ref_power, axis=0, keepdims=True)
    powers = jnp.sum(lags[0:8, :], axis=1, keepdims=True)
    packed = packed + jnp.where(lane == count * reach * reach + across, powers, 0.0)
    part[...] = jnp.broadcast_to(jnp.sum(packed, axis=0, keepdims=True), part.shape)


def spread_columns(clean, high, low, base_col):
    tiles = clean.shape[0] - 2
    full = high.shape[0]
    spare = jnp.zeros((full - reach * slot, tiles * lanes), jnp.bfloat16)
    high[reach * slot : full, :] = spare
    low[reach * slot : full, :] = spare

    def per_offset(j, carry):
        shift = column_shift(base_col + j - 3)
        at = pl.multiple_of(j * slot, slot)

        def step(t, inner):
            turned = shift(clean, t)
            high[pl.ds(at, slot), tile_of(t)] = turned[:slot]
            low[pl.ds(at, slot), tile_of(t)] = turned[slot:]
            return inner

        by_tiles(step, tiles, 32)
        return carry

    lax.fori_loop(0, reach, per_offset, 0)


def spread_kernel(base, clean, high, low):
    spread_columns(clean, high, low, base[0, 1])


def blend_weights(totals, count):
    lane = lane_of(totals.shape)
    block = reach * reach

    def pick(index):
        return jnp.sum(jnp.where(lane == index, totals, 0.0), axis=1, keepdims=True)

    ref_power = pick(count * block + count)
    weights = []
    for f in range(count):
        norm_product = jnp.sqrt((pick(count * block + f) + 1e-06) * (ref_power + 1e-06))
        member = (lane >= f * block) & (lane < (f + 1) * block)
        rho = jnp.where(member, totals, 0.0) / norm_product
        squared = rho * rho
        middle = jnp.where(lane == f * block + block // 2, 0.05, 0.0)
        weights.append((squared + middle) / (0.05 + jnp.sum(squared, axis=1, keepdims=True)))
    return weights


def banded(weights, f, rows, first_row):
    lane = lane_of(weights.shape)
    tiles = []
    for group in (range(4), range(4, reach)):
        line = jnp.zeros_like(weights)
        for j in group:
            at = first_row + (j % 4) * slot
            turned = pltpu.roll(weights, (at + 2 * lanes - (f * reach + j) * reach) & (lanes - 1), 1)
            line = jnp.where((lane >= at) & (lane < at + reach), turned, line)
        line = jnp.broadcast_to(line[0:1], (rows, lanes))
        tiles.append(by_row_shift(line, rows, 1))
    return jnp.concatenate(tiles, axis=1)


def pressures(base, totals, high, low, inverse):
    count, rows, columns = inverse.shape
    weights = blend_weights(jnp.broadcast_to(totals[0:1, :], (8, lanes)), count)
    bands = [banded(weights[f], f, rows, 1 + base[0, 0]) for f in range(count)]
    mixing = jnp.concatenate(halves(jnp.concatenate(bands, axis=0)), axis=0)
    def chunk_values(where):
        product = jnp.dot(mixing, high[:, where], preferred_element_type=jnp.float32)
        product = product + jnp.dot(mixing, low[:, where], preferred_element_type=jnp.float32)
        registered = product[: count * rows] + product[count * rows :]
        values = []
        for f in range(count):
            ratio = registered[f * rows : (f + 1) * rows] * inverse[f, :, where]
            values.append(calib_zero + ratio * (calib_linear + calib_square * ratio))
        return values

    return chunk_values


def pressure_kernel(base, totals, high, low, inverse, pressure, moments, part):
    count, rows, columns = inverse.shape
    chunk_values = pressures(base, totals, high, low, inverse)

    def step(t, sums):
        where = chunk_of(t)
        values = chunk_values(where)
        squares = [value * value for value in values]
        for f in range(count):
            pressure[f, :, where] = values[f]
        moments[0, :, where] = sum(values[1:], values[0])
        moments[1, :, where] = sum(squares[1:], squares[0])
        result = []
        for total, array in zip(sums, values + squares):
            result.append(total + fold(array[:, :lanes]) + fold(array[:, lanes:]))
        return tuple(result)

    zero = jnp.zeros((8, lanes), jnp.float32)
    sums = by_tiles(step, columns // (2 * lanes), 8, (zero,) * (2 * count))
    line = zero
    for k in range(2 * count):
        value = jnp.sum(jnp.sum(sums[k], axis=0, keepdims=True), axis=1, keepdims=True)
        line = line + jnp.where(lane_of(line.shape) == k, value, 0.0)
    part[...] = jnp.broadcast_to(line[0:1], part.shape)


def time_kernel(base, totals, clean, inverse, moments, time_mean, time_rms, high, low):
    count, rows, columns = inverse.shape
    spread_columns(clean, high, low, base[0, 1])
    chunk_values = pressures(base, totals, high, low, inverse)
    frames = 2 * count

    def step(t, carry):
        where = chunk_of(t)
        first = moments[0, :, where]
        second = moments[1, :, where]
        for value in chunk_values(where):
            first = first + value
            second = second + value * value
        mean = first * (1.0 / frames)
        time_mean[:, where] = mean
        time_rms[:, where] = jnp.sqrt(jnp.maximum(second * (1.0 / frames) - mean * mean, 0.0))
        return carry

    by_tiles(step, columns // (2 * lanes), 8)


def paired(value, axis, first):
    size = lax.axis_size(axis)
    partner = list(range(size))
    for i in range(first, size - 1, 2):
        partner[i], partner[i + 1] = i + 1, i
    return lax.ppermute(value, axis, list(enumerate(partner)))


def by_parity(odd, array, height, dim):
    length = array.shape[dim]
    low = lax.slice_in_dim(array, 0, height, axis=dim)
    high = lax.slice_in_dim(array, length - height, length, axis=dim)
    return jnp.where(odd, high, low), jnp.where(odd, low, high)


def from_owner(shard, here, odd, axis, root):
    mine = lax.axis_index(axis) == root
    height = shard.shape[0] // 2
    if lax.axis_size(axis) != 2:
        whole = lax.psum(jnp.where(mine, shard, jnp.zeros_like(shard)), axis)
        return by_parity(odd, whole, height, 0)
    there = by_parity(odd, paired(shard, axis, 0), height, 0)
    here = by_parity(odd, here, height, 0)
    return [jnp.where(mine, own, other) for own, other in zip(here, there)]


def total_over(value, axis):
    size = lax.axis_size(axis)
    if size & (size - 1):
        return lax.psum(value, axis)
    step = 1
    while step < size:
        value = value + lax.ppermute(value, axis, [(i, i ^ step) for i in range(size)])
        step *= 2
    return value


def shards(frames_raw, wind_off, run_owner, search_base):
    count, rows, columns = frames_raw.shape
    tiles = columns // lanes
    ring = tiles + 2
    wide = rows + 8
    depth = reach * count * rows
    size = lax.axis_size("rows")
    f32 = jnp.float32
    bf16 = jnp.bfloat16
    struct = functools.partial(jax.ShapeDtypeStruct, dtype=f32)
    odd = lax.axis_index("rows") % 2 == 1
    raw, run = lax.optimization_barrier((jnp.maximum(frames_raw, 0.0), jnp.maximum(wind_off[0], 0.0)))
    own_odd, own_even = from_owner(wind_off[0], run, odd, "frames", run_owner[0])
    from_odd = paired(own_odd, "rows", 1)
    from_even = paired(own_even, "rows", 0)
    frames_odd, frames_even = by_parity(odd, raw, 4, 1)
    frames_odd = paired(frames_odd, "rows", 1)
    frames_even = paired(frames_even, "rows", 0)
    inverse, stack, power, band = pl.pallas_call(
        smooth_kernel,
        out_shape=(
            struct((count, rows, columns)),
            jax.ShapeDtypeStruct((2 * depth, ring * lanes), bf16),
            struct((8 * count, lanes)),
            jax.ShapeDtypeStruct((4 * lanes, 2 * lanes), bf16),
        ),
        in_specs=[vmem] * 3,
        out_specs=(vmem,) * 4,
        scratch_shapes=[
            pltpu.VMEM((count, tiles, rows + 16, lanes), f32),
            pltpu.VMEM((2 * count * rows, (tiles + 2) * lanes), bf16),
            pltpu.VMEM((ring + 2, 2 * count * rows, lanes), bf16),
        ],
        compiler_params=params,
        cost_estimate=cost(8),
        name="smooth",
    )(raw, frames_odd, frames_even)
    offsets = jnp.clip(search_base, -8, 8)
    blocks = lax.axis_size("frames")
    clean, part = pl.pallas_call(
        match_kernel,
        out_shape=(jax.ShapeDtypeStruct((tiles + 2, 2 * slot, lanes), bf16), struct((size, lanes))),
        in_specs=[smem] + [vmem] * 7,
        out_specs=(vmem, vmem),
        scratch_shapes=[
            pltpu.VMEM((tiles, rows + 16, lanes), f32),
            pltpu.VMEM((2 * slot, (tiles + 2) * lanes), bf16),
            pltpu.VMEM((ring + 2, 2 * slot, lanes), bf16),
            pltpu.VMEM((4 * slot, ring * lanes), bf16),
            pltpu.VMEM((8 * count, lanes), f32),
        ],
        compiler_params=params,
        cost_estimate=cost(12),
        name="match",
    )(offsets, own_odd, own_even, from_odd, from_even, stack, power, band)
    if blocks == 2:
        inverse_out, part = lax.optimization_barrier((inverse, part))
        other_inverse = paired(inverse_out, "frames", 0)
    parts = lax.all_to_all(part, "rows", 0, 0, tiled=True)
    totals = jnp.sum(parts, axis=0, keepdims=True)
    spread = (8 * slot, columns)
    high, low = pl.pallas_call(
        spread_kernel,
        out_shape=(jax.ShapeDtypeStruct(spread, bf16),) * 2,
        in_specs=[smem, vmem],
        out_specs=(vmem,) * 2,
        compiler_params=params,
        cost_estimate=cost(4),
        name="spread",
    )(offsets, clean)
    pressure, moments, part = pl.pallas_call(
        pressure_kernel,
        out_shape=(struct((count, rows, columns)), struct((2, rows, columns)), struct((size, lanes))),
        in_specs=[smem] + [vmem] * 4,
        out_specs=(vmem, vmem, vmem),
        compiler_params=params,
        cost_estimate=cost(12),
        name="pressure",
    )(offsets, totals, high, low, inverse)
    if blocks == 2:
        row = jnp.concatenate([totals[:, : lanes - 2], offsets.astype(f32)], axis=1)
        row, part = lax.optimization_barrier((row, part))
        row = paired(row, "frames", 0)
        time_mean, time_rms = pl.pallas_call(
            time_kernel,
            out_shape=(struct((rows, columns)), struct((rows, columns))),
            in_specs=[smem] + [vmem] * 4,
            out_specs=(vmem, vmem),
            scratch_shapes=[pltpu.VMEM(spread, bf16)] * 2,
            compiler_params=params,
            cost_estimate=cost(12),
            name="time",
        )(row[:, lanes - 2 :].astype(jnp.int32), row, clean, other_inverse, moments)
    else:
        whole = total_over(moments, "frames")
        total_frames = count * blocks
        time_mean = whole[0] / total_frames
        time_rms = jnp.sqrt(jnp.maximum(whole[1] / total_frames - time_mean * time_mean, 0.0))
    sums = lax.all_to_all(part, "rows", 0, 0, tiled=True)
    sums, time_mean, time_rms = lax.optimization_barrier((sums, time_mean, time_rms))
    spatial = jnp.sum(sums, axis=0)
    cell_count = rows * columns * size
    frame_mean = spatial[:count] / cell_count
    frame_rms = jnp.sqrt(spatial[count : 2 * count] / cell_count - frame_mean * frame_mean)
    return (pressure, frame_mean, frame_rms, time_mean, time_rms)


def solution(mesh):
    placed = (P("frames", "rows", None), P("frames", "rows", None), P("rows"), P("frames", None))
    return jax.shard_map(
        shards,
        mesh=mesh,
        in_specs=placed,
        out_specs=(
            P("frames", "rows", None),
            P("frames"),
            P("frames"),
            P("rows", None),
            P("rows", None),
        ),
        check_vma=False,
    )
```

```python
import functools

import jax
import jax.numpy as jnp
from jax import lax
from jax.experimental import pallas as pl
from jax.experimental.pallas import tpu as pltpu
from jax.sharding import PartitionSpec as P

taps = (1.0 / 256, 8.0 / 256, 28.0 / 256, 56.0 / 256, 70.0 / 256)
calib_zero = -0.25
calib_linear = 1.0
calib_square = 0.15
lanes = 128
reach = 7
params = pltpu.CompilerParams(vmem_limit_bytes=14 * 1024 * 1024)
vmem = pl.BlockSpec(memory_space=pltpu.VMEM)
smem = pl.BlockSpec(memory_space=pltpu.SMEM)


def cost(mebibytes):
    return pl.CostEstimate(flops=0, bytes_accessed=mebibytes * 2**20, transcendentals=0)


def tile_of(index):
    return pl.ds(pl.multiple_of(index * lanes, lanes), lanes)


def by_tiles(step, tiles, group, init=()):
    def body(index, carry):
        for inner in range(group):
            carry = step(index * group + inner, carry)
        return carry

    return lax.fori_loop(0, tiles // group, body, init)


def lane_of(shape):
    return lax.broadcasted_iota(jnp.int32, shape, len(shape) - 1)


def fold(product):
    return jnp.sum(product.reshape(product.shape[0] // 8, 8, lanes), axis=0)


def vertical(load):
    total = taps[4] * load(4)
    for step in range(4):
        total = total + taps[step] * (load(step) + load(8 - step))
    return total


def moved(before, here, after, step):
    if step > 0:
        return pltpu.roll(jnp.where(lane_of(here.shape) < step, after, here), lanes - step, 1)
    if step < 0:
        return pltpu.roll(jnp.where(lane_of(here.shape) >= lanes + step, before, here), -step, 1)
    return here


def halves(value):
    high = value.astype(jnp.bfloat16)
    low = (value - high.astype(jnp.float32)).astype(jnp.bfloat16)
    return high, low


def cut(value):
    return jnp.concatenate(halves(value), axis=0)


def fill_band(band):
    shape = (lanes, lanes)
    apart = lax.broadcasted_iota(jnp.int32, shape, 0) - lax.broadcasted_iota(jnp.int32, shape, 1)

    def block(offset):
        distance = jnp.abs(apart + offset)
        value = jnp.zeros(shape, jnp.float32)
        for step in range(5):
            value = jnp.where(distance == step, taps[4 - step], value)
        return value.astype(jnp.bfloat16)

    none = jnp.zeros(shape, jnp.bfloat16)
    before, here, after = block(-lanes), block(0), block(lanes)
    for index, pair in enumerate(((before, none), (here, before), (after, here), (none, after))):
        band[index * lanes : (index + 1) * lanes, :] = jnp.concatenate(pair, axis=1)


def chunk_of(t):
    return pl.ds(pl.multiple_of(t * 2 * lanes, 2 * lanes), 2 * lanes)


def horizontal(wide, band, t):
    window = wide[:, pl.ds(pl.multiple_of(t * 2 * lanes, 2 * lanes), 4 * lanes)]
    product = jnp.dot(window, band[...], preferred_element_type=jnp.float32)
    half = product.shape[0] // 2
    return product[:half] + product[half:]


def by_row_shift(value, rows, direction):
    place = lax.broadcasted_iota(jnp.int32, value.shape, 0) % rows
    unit = 1
    while unit < rows:
        digit = (place // unit) % 4
        result = value
        for times in range(1, 4):
            amount = times * unit
            turned = pltpu.roll(value, amount if direction > 0 else value.shape[1] - amount, 1)
            result = jnp.where(digit == times, turned, result)
        value = result
        unit *= 4
    return value


def at_edge():
    index = lax.axis_index("rows")
    return (index == 0) | (index == lax.axis_size("rows") - 1)


def smooth_kernel(frames, from_odd, from_even, inverse, stack, power, band, rows_in, wide, pieces):
    count, rows, columns = frames.shape
    tiles = columns // lanes
    ring = tiles + 2
    odd = lax.axis_index("rows") % 2 == 1
    edge = at_edge()
    blank = jnp.zeros((2 * count * rows, lanes), jnp.bfloat16)
    wide[:, tile_of(0)] = blank
    wide[:, tile_of(tiles + 1)] = blank
    fill_band(band)
    pieces[0] = blank
    pieces[tiles + 1] = blank
    pieces[tiles + 2] = blank

    def load_step(t, carry):
        for f in range(count):
            outer = jnp.where(edge, 0.0, from_odd[f, :, tile_of(t)])
            inner = from_even[f, :, tile_of(t)]
            rows_in[f, t, 4:8, :] = jnp.where(odd, inner, outer)
            rows_in[f, t, 8 : 8 + rows, :] = frames[f, :, tile_of(t)]
            rows_in[f, t, 8 + rows : 12 + rows, :] = jnp.where(odd, outer, inner)
        return carry

    def vertical_step(t, carry):
        parts = [vertical(lambda s: rows_in[f, t, pl.ds(4 + s, rows), :]) for f in range(count)]
        wide[:, tile_of(t + 1)] = cut(jnp.concatenate(parts, axis=0))
        return carry

    def horizontal_step(t, totals):
        smooth = horizontal(wide, band, t)
        result = []
        details = []
        for f in range(count):
            part = smooth[f * rows : (f + 1) * rows]
            inverse[f, :, chunk_of(t)] = 1.0 / part
            details.append(frames[f, :, chunk_of(t)] - part)
            square = details[f] * details[f]
            result.append(totals[f] + fold(square[:, :lanes]) + fold(square[:, lanes:]))
        detail = cut(jnp.concatenate(details, axis=0))
        pieces[2 * t + 1] = detail[:, :lanes]
        pieces[2 * t + 2] = detail[:, lanes:]
        return tuple(result)

    def stack_step(t, carry):
        before, here, after = pieces[t], pieces[t + 1], pieces[t + 2]
        size = count * rows
        for j in range(reach):
            turned = moved(before, here, after, 3 - j)
            stack[j * size : (j + 1) * size, tile_of(t)] = turned[:size]
            stack[(reach + j) * size : (reach + j + 1) * size, tile_of(t)] = turned[size:]
        return carry

    by_tiles(load_step, tiles, 8)
    by_tiles(vertical_step, tiles, 8)
    powers = by_tiles(horizontal_step, tiles // 2, 8, (jnp.zeros((8, lanes), jnp.float32),) * count)
    for f in range(count):
        power[f * 8 : f * 8 + 8, :] = powers[f]
    pieces[tiles + 3] = pieces[1]
    by_tiles(stack_step, ring, ring // 2)


def column_shift(offset):
    negative = offset < 0
    first = jnp.where(negative, 0, 1)
    amount = jnp.where(negative, offset + lanes, offset)
    back = (lanes - amount) & (lanes - 1)

    def shift(source, t):
        here = source[t + first]
        after = source[t + first + 1]
        return pltpu.roll(jnp.where(lane_of(here.shape) < amount, after, here), back, 1)

    return shift


def match_kernel(
    base, own_odd, own_even, from_odd, from_even, stack, power, band, clean, part, rows_in, padded, fine, stream, folded, lags
):
    rows = own_odd.shape[0] * 2
    tiles = own_odd.shape[1] // lanes
    count = power.shape[0] // 8
    ring = tiles + 2
    wide = rows + 8
    row_index = lax.axis_index("rows")
    last_row = lax.axis_size("rows") - 1
    odd = row_index % 2 == 1
    edge = at_edge()
    empty = jnp.zeros((2 * wide, lanes), jnp.bfloat16)
    padded[:, tile_of(0)] = empty
    padded[:, tile_of(tiles + 1)] = empty
    for array in (clean, fine):
        array[0] = empty
        array[tiles + 1] = empty
    fine[tiles + 2] = empty
    place = lax.broadcasted_iota(jnp.int32, (wide, 2 * lanes), 0)
    own = (place >= 4) & (place < rows + 4)
    inside = ((place >= 4) | (row_index > 0)) & ((place < rows + 4) | (row_index < last_row))

    def load_step(t, carry):
        outer = [jnp.where(edge, 0.0, from_odd[:, tile_of(t)]), own_odd[:, tile_of(t)]]
        inner = [array[:, tile_of(t)] for array in (own_even, from_even)]
        rows_in[t, 0:8, :] = jnp.where(odd, inner[1], outer[0])
        rows_in[t, 8:16, :] = jnp.where(odd, inner[0], outer[1])
        rows_in[t, 16:24, :] = jnp.where(odd, outer[1], inner[0])
        rows_in[t, 24:32, :] = jnp.where(odd, outer[0], inner[1])
        return carry

    def vertical_step(t, carry):
        padded[:, tile_of(t + 1)] = cut(vertical(lambda s: rows_in[t, pl.ds(s, wide), :]))
        return carry

    def horizontal_step(t, total):
        smooth = jnp.where(inside, horizontal(padded, band, t), 0.0)
        raw = [rows_in[2 * t + c, pl.ds(4, wide), :] for c in range(2)]
        detail = jnp.concatenate(raw, axis=1) - smooth
        square = jnp.where(own, detail * detail, 0.0)
        for array, value in ((clean, cut(smooth)), (fine, cut(detail))):
            array[2 * t + 1] = value[:, :lanes]
            array[2 * t + 2] = value[:, lanes:]
        return total + fold(square[:, :lanes]) + fold(square[:, lanes:])

    by_tiles(load_step, tiles, 8)
    by_tiles(vertical_step, tiles, 8)
    ref_power = by_tiles(horizontal_step, tiles // 2, 8, jnp.zeros((8, lanes), jnp.float32))
    fine[tiles + 3] = fine[1]
    shift = column_shift(base[0, 1])

    def stream_step(t, carry):
        stream[:, tile_of(t)] = shift(fine, t)
        return carry

    by_tiles(stream_step, ring, ring // 2)
    product = lax.dot_general(
        stack[...], stream[...], (((1,), (1,)), ((), ())), preferred_element_type=jnp.float32
    )
    size = reach * count * rows
    folded[...] = jnp.zeros(folded.shape, jnp.float32)
    folded[:, 0 : 2 * wide] = product[:size] + product[size:]
    product = by_row_shift(folded[...], rows, -1)
    lags[...] = jnp.zeros(lags.shape, jnp.float32)
    for j in range(reach):
        for f in range(count):
            start = (j * count + f) * rows
            lags[f * 8 + j : f * 8 + j + 1, :] = jnp.sum(product[start : start + rows], axis=0, keepdims=True)
    back = 2 * lanes - 1 - base[0, 0]
    across = lax.broadcasted_iota(jnp.int32, (8, lanes), 0)
    lane = lane_of((8, lanes))
    packed = jnp.zeros((8, lanes), jnp.float32)
    for f in range(count):
        block = lags[f * 8 : f * 8 + 8, :]
        for j in range(reach):
            at = (f * reach + j) * reach
            high = pltpu.roll(block, (back + at) & (lanes - 1), 1)
            low = pltpu.roll(block, (back + at - wide) & (lanes - 1), 1)
            packed = packed + jnp.where((across == j) & (lane >= at) & (lane < at + reach), high + low, 0.0)
    lags[0:8, :] = jnp.zeros((8, lanes), jnp.float32)
    for f in range(count):
        lags[f : f + 1, :] = jnp.sum(power[f * 8 : f * 8 + 8, :], axis=0, keepdims=True)
    lags[count : count + 1, :] = jnp.sum(ref_power, axis=0, keepdims=True)
    powers = jnp.sum(lags[0:8, :], axis=1, keepdims=True)
    packed = packed + jnp.where(lane == count * reach * reach + across, powers, 0.0)
    part[...] = jnp.broadcast_to(jnp.sum(packed, axis=0, keepdims=True), part.shape)


def spread_columns(clean, spread, base_col):
    tiles = clean.shape[0] - 2
    size = clean.shape[1]
    spare = spread.shape[0] - reach * size
    spread[reach * size :, :] = jnp.zeros((spare, tiles * lanes), jnp.bfloat16)

    def per_offset(j, carry):
        shift = column_shift(base_col + j - 3)
        at = pl.multiple_of(j * size, size)

        def step(t, inner):
            spread[pl.ds(at, size), tile_of(t)] = shift(clean, t)
            return inner

        by_tiles(step, tiles, 32)
        return carry

    lax.fori_loop(0, reach, per_offset, 0)


def blend_weights(totals, count):
    lane = lane_of(totals.shape)
    block = reach * reach

    def pick(index):
        return jnp.sum(jnp.where(lane == index, totals, 0.0), axis=1, keepdims=True)

    ref_power = pick(count * block + count)
    weights = []
    for f in range(count):
        norm_product = jnp.sqrt((pick(count * block + f) + 1e-06) * (ref_power + 1e-06))
        member = (lane >= f * block) & (lane < (f + 1) * block)
        rho = jnp.where(member, totals, 0.0) / norm_product
        squared = rho * rho
        middle = jnp.where(lane == f * block + block // 2, 0.05, 0.0)
        weights.append((squared + middle) / (0.05 + jnp.sum(squared, axis=1, keepdims=True)))
    return weights


def banded(weights, f, rows, first_row, depth):
    wide = rows + 8
    blank = jnp.zeros((weights.shape[0], depth - lanes), jnp.float32)
    weights = jnp.concatenate([weights, blank], axis=1)
    lane = lane_of(weights.shape)
    line = jnp.zeros_like(weights)
    for j in range(reach):
        at = first_row + j * 2 * wide
        amount = at - (f * reach + j) * reach
        amount = jnp.where(amount < 0, amount + depth, amount)
        line = jnp.where((lane >= at) & (lane < at + reach), pltpu.roll(weights, amount, 1), line)
    line = line + pltpu.roll(line, wide, 1)
    return by_row_shift(jnp.broadcast_to(line[0:1], (rows, depth)), rows, 1)


def pressures(base, totals, clean, spread, inverse):
    count, rows, columns = inverse.shape
    depth = spread.shape[0]
    weights = blend_weights(jnp.broadcast_to(totals[0:1, :], (8, lanes)), count)
    bands = [banded(weights[f], f, rows, 1 + base[0, 0], depth) for f in range(count)]
    mixing = cut(jnp.concatenate(bands, axis=0))
    spread_columns(clean, spread, base[0, 1])

    def chunk_values(where):
        product = jnp.dot(mixing, spread[:, where], preferred_element_type=jnp.float32)
        registered = product[: count * rows] + product[count * rows :]
        values = []
        for f in range(count):
            ratio = registered[f * rows : (f + 1) * rows] * inverse[f, :, where]
            values.append(calib_zero + ratio * (calib_linear + calib_square * ratio))
        return values

    return chunk_values


def pressure_kernel(base, totals, clean, inverse, pressure, moments, part, spread, held, sent):
    count, rows, columns = inverse.shape
    chunk_values = pressures(base, totals, clean, spread, inverse)

    def step(t, sums):
        where = chunk_of(t)
        values = chunk_values(where)
        squares = [value * value for value in values]
        for f in range(count):
            held[f, :, where] = values[f]
        moments[0, :, where] = sum(values[1:], values[0])
        moments[1, :, where] = sum(squares[1:], squares[0])
        result = []
        for total, array in zip(sums, values + squares):
            result.append(total + fold(array[:, :lanes]) + fold(array[:, lanes:]))
        return tuple(result)

    zero = jnp.zeros((8, lanes), jnp.float32)
    sums = by_tiles(step, columns // (2 * lanes), 8, (zero,) * (2 * count))
    copy = pltpu.make_async_copy(held, pressure, sent)
    copy.start()
    line = zero
    for k in range(2 * count):
        value = jnp.sum(jnp.sum(sums[k], axis=0, keepdims=True), axis=1, keepdims=True)
        line = line + jnp.where(lane_of(line.shape) == k, value, 0.0)
    part[...] = jnp.broadcast_to(line[0:1], part.shape)
    copy.wait()


def time_kernel(base, totals, clean, inverse, moments, time_mean, time_rms, spread):
    count, rows, columns = inverse.shape
    chunk_values = pressures(base, totals, clean, spread, inverse)
    frames = 2 * count

    def step(t, carry):
        where = chunk_of(t)
        first = moments[0, :, where]
        second = moments[1, :, where]
        for value in chunk_values(where):
            first = first + value
            second = second + value * value
        mean = first * (1.0 / frames)
        time_mean[:, where] = mean
        time_rms[:, where] = jnp.sqrt(jnp.maximum(second * (1.0 / frames) - mean * mean, 0.0))
        return carry

    by_tiles(step, columns // (2 * lanes), 8)


def paired(value, axis, first):
    size = lax.axis_size(axis)
    partner = list(range(size))
    for i in range(first, size - 1, 2):
        partner[i], partner[i + 1] = i + 1, i
    return lax.ppermute(value, axis, list(enumerate(partner)))


def by_parity(odd, array, height, dim):
    length = array.shape[dim]
    low = lax.slice_in_dim(array, 0, height, axis=dim)
    high = lax.slice_in_dim(array, length - height, length, axis=dim)
    return jnp.where(odd, high, low), jnp.where(odd, low, high)


def from_owner(shard, here, odd, axis, root):
    mine = lax.axis_index(axis) == root
    height = shard.shape[0] // 2
    if lax.axis_size(axis) != 2:
        whole = lax.psum(jnp.where(mine, shard, jnp.zeros_like(shard)), axis)
        return by_parity(odd, whole, height, 0)
    there = by_parity(odd, paired(shard, axis, 0), height, 0)
    here = by_parity(odd, here, height, 0)
    return [jnp.where(mine, own, other) for own, other in zip(here, there)]


def total_over(value, axis):
    size = lax.axis_size(axis)
    if size & (size - 1):
        return lax.psum(value, axis)
    step = 1
    while step < size:
        value = value + lax.ppermute(value, axis, [(i, i ^ step) for i in range(size)])
        step *= 2
    return value


def shards(frames_raw, wind_off, run_owner, search_base):
    count, rows, columns = frames_raw.shape
    tiles = columns // lanes
    ring = tiles + 2
    wide = rows + 8
    depth = reach * count * rows
    size = lax.axis_size("rows")
    f32 = jnp.float32
    bf16 = jnp.bfloat16
    struct = functools.partial(jax.ShapeDtypeStruct, dtype=f32)
    odd = lax.axis_index("rows") % 2 == 1
    raw, run = lax.optimization_barrier((jnp.maximum(frames_raw, 0.0), jnp.maximum(wind_off[0], 0.0)))
    own_odd, own_even = from_owner(wind_off[0], run, odd, "frames", run_owner[0])
    from_odd = paired(own_odd, "rows", 1)
    from_even = paired(own_even, "rows", 0)
    frames_odd, frames_even = by_parity(odd, raw, 4, 1)
    frames_odd = paired(frames_odd, "rows", 1)
    frames_even = paired(frames_even, "rows", 0)
    inverse, stack, power, band = pl.pallas_call(
        smooth_kernel,
        out_shape=(
            struct((count, rows, columns)),
            jax.ShapeDtypeStruct((2 * depth, ring * lanes), bf16),
            struct((8 * count, lanes)),
            jax.ShapeDtypeStruct((4 * lanes, 2 * lanes), bf16),
        ),
        in_specs=[vmem] * 3,
        out_specs=(vmem,) * 4,
        scratch_shapes=[
            pltpu.VMEM((count, tiles, rows + 16, lanes), f32),
            pltpu.VMEM((2 * count * rows, (tiles + 2) * lanes), bf16),
            pltpu.VMEM((ring + 2, 2 * count * rows, lanes), bf16),
        ],
        compiler_params=params,
        cost_estimate=cost(8),
        name="smooth",
    )(raw, frames_odd, frames_even)
    offsets = jnp.clip(search_base, -8, 8)
    blocks = lax.axis_size("frames")
    clean, part = pl.pallas_call(
        match_kernel,
        out_shape=(jax.ShapeDtypeStruct((tiles + 2, 2 * wide, lanes), bf16), struct((size, lanes))),
        in_specs=[smem] + [vmem] * 7,
        out_specs=(vmem, vmem),
        scratch_shapes=[
            pltpu.VMEM((tiles, rows + 16, lanes), f32),
            pltpu.VMEM((2 * wide, (tiles + 2) * lanes), bf16),
            pltpu.VMEM((ring + 2, 2 * wide, lanes), bf16),
            pltpu.VMEM((2 * wide, ring * lanes), bf16),
            pltpu.VMEM((depth, lanes), f32),
            pltpu.VMEM((8 * count, lanes), f32),
        ],
        compiler_params=params,
        cost_estimate=cost(12),
        name="match",
    )(offsets, own_odd, own_even, from_odd, from_even, stack, power, band)
    if blocks == 2:
        inverse_out, part = lax.optimization_barrier((inverse, part))
        other_inverse = paired(inverse_out, "frames", 0)
    parts = lax.all_to_all(part, "rows", 0, 0, tiled=True)
    totals = jnp.sum(parts, axis=0, keepdims=True)
    depth = -(-reach * 2 * wide // lanes) * lanes
    spread = pltpu.VMEM((depth, columns), bf16)
    pressure, moments, part = pl.pallas_call(
        pressure_kernel,
        out_shape=(struct((count, rows, columns)), struct((2, rows, columns)), struct((size, lanes))),
        in_specs=[smem] + [vmem] * 3,
        out_specs=(pl.BlockSpec(memory_space=pl.ANY), vmem, vmem),
        scratch_shapes=[spread, pltpu.VMEM((count, rows, columns), f32), pltpu.SemaphoreType.DMA],
        compiler_params=params,
        cost_estimate=cost(12),
        name="pressure",
    )(offsets, totals, clean, inverse)
    if blocks == 2:
        row = jnp.concatenate([totals[:, : lanes - 2], offsets.astype(f32)], axis=1)
        row, part = lax.optimization_barrier((row, part))
        row = paired(row, "frames", 0)
        time_mean, time_rms = pl.pallas_call(
            time_kernel,
            out_shape=(struct((rows, columns)), struct((rows, columns))),
            in_specs=[smem] + [vmem] * 4,
            out_specs=(vmem, vmem),
            scratch_shapes=[spread],
            compiler_params=params,
            cost_estimate=cost(12),
            name="time",
        )(row[:, lanes - 2 :].astype(jnp.int32), row, clean, other_inverse, moments)
    else:
        whole = total_over(moments, "frames")
        total_frames = count * blocks
        time_mean = whole[0] / total_frames
        time_rms = jnp.sqrt(jnp.maximum(whole[1] / total_frames - time_mean * time_mean, 0.0))
    sums = lax.all_to_all(part, "rows", 0, 0, tiled=True)
    sums, time_mean, time_rms = lax.optimization_barrier((sums, time_mean, time_rms))
    spatial = jnp.sum(sums, axis=0)
    cell_count = rows * columns * size
    frame_mean = spatial[:count] / cell_count
    frame_rms = jnp.sqrt(spatial[count : 2 * count] / cell_count - frame_mean * frame_mean)
    return (pressure, frame_mean, frame_rms, time_mean, time_rms)


def solution(mesh):
    placed = (P("frames", "rows", None), P("frames", "rows", None), P("rows"), P("frames", None))
    return jax.shard_map(
        shards,
        mesh=mesh,
        in_specs=placed,
        out_specs=(
            P("frames", "rows", None),
            P("frames"),
            P("frames"),
            P("rows", None),
            P("rows", None),
        ),
        check_vma=False,
    )
```

```python
import functools

import jax
import jax.numpy as jnp
from jax import lax
from jax.experimental import pallas as pl
from jax.experimental.pallas import tpu as pltpu
from jax.sharding import PartitionSpec as P

taps = (1.0 / 256, 8.0 / 256, 28.0 / 256, 56.0 / 256, 70.0 / 256)
calib_zero = -0.25
calib_linear = 1.0
calib_square = 0.15
lanes = 128
reach = 7
params = pltpu.CompilerParams(vmem_limit_bytes=14 * 1024 * 1024)
vmem = pl.BlockSpec(memory_space=pltpu.VMEM)
smem = pl.BlockSpec(memory_space=pltpu.SMEM)


def cost(mebibytes):
    return pl.CostEstimate(flops=0, bytes_accessed=mebibytes * 2**20, transcendentals=0)


def tile_of(index):
    return pl.ds(pl.multiple_of(index * lanes, lanes), lanes)


def by_tiles(step, tiles, group, init=()):
    def body(index, carry):
        for inner in range(group):
            carry = step(index * group + inner, carry)
        return carry

    return lax.fori_loop(0, tiles // group, body, init)


def lane_of(shape):
    return lax.broadcasted_iota(jnp.int32, shape, len(shape) - 1)


def fold(product):
    return jnp.sum(product.reshape(product.shape[0] // 8, 8, lanes), axis=0)


def vertical(load):
    total = taps[4] * load(4)
    for step in range(4):
        total = total + taps[step] * (load(step) + load(8 - step))
    return total


def moved(before, here, after, step):
    if step > 0:
        return pltpu.roll(jnp.where(lane_of(here.shape) < step, after, here), lanes - step, 1)
    if step < 0:
        return pltpu.roll(jnp.where(lane_of(here.shape) >= lanes + step, before, here), -step, 1)
    return here


def halves(value):
    high = value.astype(jnp.bfloat16)
    low = (value - high.astype(jnp.float32)).astype(jnp.bfloat16)
    return high, low


def cut(value):
    return jnp.concatenate(halves(value), axis=0)


def fill_band(band):
    shape = (lanes, lanes)
    apart = lax.broadcasted_iota(jnp.int32, shape, 0) - lax.broadcasted_iota(jnp.int32, shape, 1)

    def block(offset):
        distance = jnp.abs(apart + offset)
        value = jnp.zeros(shape, jnp.float32)
        for step in range(5):
            value = jnp.where(distance == step, taps[4 - step], value)
        return value.astype(jnp.bfloat16)

    none = jnp.zeros(shape, jnp.bfloat16)
    before, here, after = block(-lanes), block(0), block(lanes)
    for index, pair in enumerate(((before, none), (here, before), (after, here), (none, after))):
        band[index * lanes : (index + 1) * lanes, :] = jnp.concatenate(pair, axis=1)


def chunk_of(t):
    return pl.ds(pl.multiple_of(t * 2 * lanes, 2 * lanes), 2 * lanes)


def horizontal(wide, band, t):
    window = wide[:, pl.ds(pl.multiple_of(t * 2 * lanes, 2 * lanes), 4 * lanes)]
    product = jnp.dot(window, band[...], preferred_element_type=jnp.float32)
    half = product.shape[0] // 2
    return product[:half] + product[half:]


def by_row_shift(value, rows, direction):
    place = lax.broadcasted_iota(jnp.int32, value.shape, 0) % rows
    unit = 1
    while unit < rows:
        digit = (place // unit) % 4
        result = value
        for times in range(1, 4):
            amount = times * unit
            turned = pltpu.roll(value, amount if direction > 0 else value.shape[1] - amount, 1)
            result = jnp.where(digit == times, turned, result)
        value = result
        unit *= 4
    return value


def at_edge():
    index = lax.axis_index("rows")
    return (index == 0) | (index == lax.axis_size("rows") - 1)


def smooth_kernel(frames, from_odd, from_even, inverse, stack, power, band, rows_in, wide, pieces):
    count, rows, columns = frames.shape
    tiles = columns // lanes
    ring = tiles + 2
    odd = lax.axis_index("rows") % 2 == 1
    edge = at_edge()
    blank = jnp.zeros((2 * count * rows, lanes), jnp.bfloat16)
    wide[:, tile_of(0)] = blank
    wide[:, tile_of(tiles + 1)] = blank
    fill_band(band)
    pieces[0] = blank
    pieces[tiles + 1] = blank
    pieces[tiles + 2] = blank

    def load_step(t, carry):
        for f in range(count):
            outer = jnp.where(edge, 0.0, from_odd[f, :, tile_of(t)])
            inner = from_even[f, :, tile_of(t)]
            rows_in[f, t, 4:8, :] = jnp.where(odd, inner, outer)
            rows_in[f, t, 8 : 8 + rows, :] = frames[f, :, tile_of(t)]
            rows_in[f, t, 8 + rows : 12 + rows, :] = jnp.where(odd, outer, inner)
        return carry

    def vertical_step(t, carry):
        parts = [vertical(lambda s: rows_in[f, t, pl.ds(4 + s, rows), :]) for f in range(count)]
        wide[:, tile_of(t + 1)] = cut(jnp.concatenate(parts, axis=0))
        return carry

    def horizontal_step(t, totals):
        smooth = horizontal(wide, band, t)
        result = []
        details = []
        for f in range(count):
            part = smooth[f * rows : (f + 1) * rows]
            inverse[f, :, chunk_of(t)] = 1.0 / part
            details.append(frames[f, :, chunk_of(t)] - part)
            square = details[f] * details[f]
            result.append(totals[f] + fold(square[:, :lanes]) + fold(square[:, lanes:]))
        detail = cut(jnp.concatenate(details, axis=0))
        pieces[2 * t + 1] = detail[:, :lanes]
        pieces[2 * t + 2] = detail[:, lanes:]
        return tuple(result)

    def stack_step(t, carry):
        before, here, after = pieces[t], pieces[t + 1], pieces[t + 2]
        size = count * rows
        for j in range(reach):
            turned = moved(before, here, after, 3 - j)
            stack[j * size : (j + 1) * size, tile_of(t)] = turned[:size]
            stack[(reach + j) * size : (reach + j + 1) * size, tile_of(t)] = turned[size:]
        return carry

    by_tiles(load_step, tiles, 8)
    by_tiles(vertical_step, tiles, 8)
    powers = by_tiles(horizontal_step, tiles // 2, 8, (jnp.zeros((8, lanes), jnp.float32),) * count)
    for f in range(count):
        power[f * 8 : f * 8 + 8, :] = powers[f]
    pieces[tiles + 3] = pieces[1]
    by_tiles(stack_step, ring, ring // 2)


def column_shift(offset):
    negative = offset < 0
    first = jnp.where(negative, 0, 1)
    amount = jnp.where(negative, offset + lanes, offset)
    back = (lanes - amount) & (lanes - 1)

    def shift(source, t):
        here = source[t + first]
        after = source[t + first + 1]
        return pltpu.roll(jnp.where(lane_of(here.shape) < amount, after, here), back, 1)

    return shift


def match_kernel(
    base, own_odd, own_even, from_odd, from_even, stack, power, band, clean, part, rows_in, padded, fine, stream, folded, lags
):
    rows = own_odd.shape[0] * 2
    tiles = own_odd.shape[1] // lanes
    count = power.shape[0] // 8
    ring = tiles + 2
    wide = rows + 8
    row_index = lax.axis_index("rows")
    last_row = lax.axis_size("rows") - 1
    odd = row_index % 2 == 1
    edge = at_edge()
    empty = jnp.zeros((2 * wide, lanes), jnp.bfloat16)
    padded[:, tile_of(0)] = empty
    padded[:, tile_of(tiles + 1)] = empty
    for array in (clean, fine):
        array[0] = empty
        array[tiles + 1] = empty
    fine[tiles + 2] = empty
    place = lax.broadcasted_iota(jnp.int32, (wide, 2 * lanes), 0)
    own = (place >= 4) & (place < rows + 4)
    inside = ((place >= 4) | (row_index > 0)) & ((place < rows + 4) | (row_index < last_row))

    def load_step(t, carry):
        outer = [jnp.where(edge, 0.0, from_odd[:, tile_of(t)]), own_odd[:, tile_of(t)]]
        inner = [array[:, tile_of(t)] for array in (own_even, from_even)]
        rows_in[t, 0:8, :] = jnp.where(odd, inner[1], outer[0])
        rows_in[t, 8:16, :] = jnp.where(odd, inner[0], outer[1])
        rows_in[t, 16:24, :] = jnp.where(odd, outer[1], inner[0])
        rows_in[t, 24:32, :] = jnp.where(odd, outer[0], inner[1])
        return carry

    def vertical_step(t, carry):
        padded[:, tile_of(t + 1)] = cut(vertical(lambda s: rows_in[t, pl.ds(s, wide), :]))
        return carry

    def horizontal_step(t, total):
        smooth = jnp.where(inside, horizontal(padded, band, t), 0.0)
        raw = [rows_in[2 * t + c, pl.ds(4, wide), :] for c in range(2)]
        detail = jnp.concatenate(raw, axis=1) - smooth
        square = jnp.where(own, detail * detail, 0.0)
        for array, value in ((clean, cut(smooth)), (fine, cut(detail))):
            array[2 * t + 1] = value[:, :lanes]
            array[2 * t + 2] = value[:, lanes:]
        return total + fold(square[:, :lanes]) + fold(square[:, lanes:])

    by_tiles(load_step, tiles, 8)
    by_tiles(vertical_step, tiles, 8)
    ref_power = by_tiles(horizontal_step, tiles // 2, 8, jnp.zeros((8, lanes), jnp.float32))
    fine[tiles + 3] = fine[1]
    shift = column_shift(base[0, 1])

    def stream_step(t, carry):
        stream[:, tile_of(t)] = shift(fine, t)
        return carry

    by_tiles(stream_step, ring, ring // 2)
    product = lax.dot_general(
        stack[...], stream[...], (((1,), (1,)), ((), ())), preferred_element_type=jnp.float32
    )
    size = reach * count * rows
    folded[...] = jnp.zeros(folded.shape, jnp.float32)
    folded[:, 0 : 2 * wide] = product[:size] + product[size:]
    product = by_row_shift(folded[...], rows, -1)
    lags[...] = jnp.zeros(lags.shape, jnp.float32)
    for j in range(reach):
        for f in range(count):
            start = (j * count + f) * rows
            lags[f * 8 + j : f * 8 + j + 1, :] = jnp.sum(product[start : start + rows], axis=0, keepdims=True)
    back = 2 * lanes - 1 - base[0, 0]
    across = lax.broadcasted_iota(jnp.int32, (8, lanes), 0)
    lane = lane_of((8, lanes))
    packed = jnp.zeros((8, lanes), jnp.float32)
    for f in range(count):
        block = lags[f * 8 : f * 8 + 8, :]
        for j in range(reach):
            at = (f * reach + j) * reach
            high = pltpu.roll(block, (back + at) & (lanes - 1), 1)
            low = pltpu.roll(block, (back + at - wide) & (lanes - 1), 1)
            packed = packed + jnp.where((across == j) & (lane >= at) & (lane < at + reach), high + low, 0.0)
    lags[0:8, :] = jnp.zeros((8, lanes), jnp.float32)
    for f in range(count):
        lags[f : f + 1, :] = jnp.sum(power[f * 8 : f * 8 + 8, :], axis=0, keepdims=True)
    lags[count : count + 1, :] = jnp.sum(ref_power, axis=0, keepdims=True)
    powers = jnp.sum(lags[0:8, :], axis=1, keepdims=True)
    packed = packed + jnp.where(lane == count * reach * reach + across, powers, 0.0)
    part[...] = jnp.broadcast_to(jnp.sum(packed, axis=0, keepdims=True), part.shape)


def spread_columns(clean, spread, base_col):
    tiles = clean.shape[0] - 2
    size = clean.shape[1]
    spare = spread.shape[0] - reach * size
    spread[reach * size :, :] = jnp.zeros((spare, tiles * lanes), jnp.bfloat16)

    def per_offset(j, carry):
        shift = column_shift(base_col + j - 3)
        at = pl.multiple_of(j * size, size)

        def step(t, inner):
            spread[pl.ds(at, size), tile_of(t)] = shift(clean, t)
            return inner

        by_tiles(step, tiles, 32)
        return carry

    lax.fori_loop(0, reach, per_offset, 0)


def blend_weights(totals, count):
    lane = lane_of(totals.shape)
    block = reach * reach

    def pick(index):
        return jnp.sum(jnp.where(lane == index, totals, 0.0), axis=1, keepdims=True)

    ref_power = pick(count * block + count)
    weights = []
    for f in range(count):
        norm_product = jnp.sqrt((pick(count * block + f) + 1e-06) * (ref_power + 1e-06))
        member = (lane >= f * block) & (lane < (f + 1) * block)
        rho = jnp.where(member, totals, 0.0) / norm_product
        squared = rho * rho
        middle = jnp.where(lane == f * block + block // 2, 0.05, 0.0)
        weights.append((squared + middle) / (0.05 + jnp.sum(squared, axis=1, keepdims=True)))
    return weights


def banded(weights, f, rows, first_row, depth):
    wide = rows + 8
    blank = jnp.zeros((weights.shape[0], depth - lanes), jnp.float32)
    weights = jnp.concatenate([weights, blank], axis=1)
    lane = lane_of(weights.shape)
    line = jnp.zeros_like(weights)
    for j in range(reach):
        at = first_row + j * 2 * wide
        amount = at - (f * reach + j) * reach
        amount = jnp.where(amount < 0, amount + depth, amount)
        line = jnp.where((lane >= at) & (lane < at + reach), pltpu.roll(weights, amount, 1), line)
    line = line + pltpu.roll(line, wide, 1)
    return by_row_shift(jnp.broadcast_to(line[0:1], (rows, depth)), rows, 1)


def pressures(base, totals, clean, spread, inverse):
    count, rows, columns = inverse.shape
    depth = spread.shape[0]
    weights = blend_weights(jnp.broadcast_to(totals[0:1, :], (8, lanes)), count)
    bands = [banded(weights[f], f, rows, 1 + base[0, 0], depth) for f in range(count)]
    mixing = cut(jnp.concatenate(bands, axis=0))
    spread_columns(clean, spread, base[0, 1])

    def chunk_values(where):
        product = jnp.dot(mixing, spread[:, where], preferred_element_type=jnp.float32)
        registered = product[: count * rows] + product[count * rows :]
        values = []
        for f in range(count):
            ratio = registered[f * rows : (f + 1) * rows] * inverse[f, :, where]
            values.append(calib_zero + ratio * (calib_linear + calib_square * ratio))
        return values

    return chunk_values


def pressure_kernel(base, totals, clean, inverse, pressure, moments, part, spread):
    count, rows, columns = inverse.shape
    chunk_values = pressures(base, totals, clean, spread, inverse)

    def step(t, sums):
        where = chunk_of(t)
        values = chunk_values(where)
        squares = [value * value for value in values]
        for f in range(count):
            pressure[f, :, where] = values[f]
        moments[0, :, where] = sum(values[1:], values[0])
        moments[1, :, where] = sum(squares[1:], squares[0])
        result = []
        for total, array in zip(sums, values + squares):
            result.append(total + fold(array[:, :lanes]) + fold(array[:, lanes:]))
        return tuple(result)

    zero = jnp.zeros((8, lanes), jnp.float32)
    sums = by_tiles(step, columns // (2 * lanes), 8, (zero,) * (2 * count))
    line = zero
    for k in range(2 * count):
        value = jnp.sum(jnp.sum(sums[k], axis=0, keepdims=True), axis=1, keepdims=True)
        line = line + jnp.where(lane_of(line.shape) == k, value, 0.0)
    part[...] = jnp.broadcast_to(line[0:1], part.shape)


def time_kernel(base, totals, clean, inverse, moments, time_mean, time_rms, spread):
    count, rows, columns = inverse.shape
    chunk_values = pressures(base, totals, clean, spread, inverse)
    frames = 2 * count

    def step(t, carry):
        where = chunk_of(t)
        first = moments[0, :, where]
        second = moments[1, :, where]
        for value in chunk_values(where):
            first = first + value
            second = second + value * value
        mean = first * (1.0 / frames)
        time_mean[:, where] = mean
        time_rms[:, where] = jnp.sqrt(jnp.maximum(second * (1.0 / frames) - mean * mean, 0.0))
        return carry

    by_tiles(step, columns // (2 * lanes), 8)


def paired(value, axis, first):
    size = lax.axis_size(axis)
    partner = list(range(size))
    for i in range(first, size - 1, 2):
        partner[i], partner[i + 1] = i + 1, i
    return lax.ppermute(value, axis, list(enumerate(partner)))


def by_parity(odd, array, height, dim):
    length = array.shape[dim]
    low = lax.slice_in_dim(array, 0, height, axis=dim)
    high = lax.slice_in_dim(array, length - height, length, axis=dim)
    return jnp.where(odd, high, low), jnp.where(odd, low, high)


def from_owner(shard, here, odd, axis, root):
    mine = lax.axis_index(axis) == root
    height = shard.shape[0] // 2
    if lax.axis_size(axis) != 2:
        whole = lax.psum(jnp.where(mine, shard, jnp.zeros_like(shard)), axis)
        return by_parity(odd, whole, height, 0)
    there = by_parity(odd, paired(shard, axis, 0), height, 0)
    here = by_parity(odd, here, height, 0)
    return [jnp.where(mine, own, other) for own, other in zip(here, there)]


def total_over(value, axis):
    size = lax.axis_size(axis)
    if size & (size - 1):
        return lax.psum(value, axis)
    step = 1
    while step < size:
        value = value + lax.ppermute(value, axis, [(i, i ^ step) for i in range(size)])
        step *= 2
    return value


def shards(frames_raw, wind_off, run_owner, search_base):
    count, rows, columns = frames_raw.shape
    tiles = columns // lanes
    ring = tiles + 2
    wide = rows + 8
    depth = reach * count * rows
    size = lax.axis_size("rows")
    f32 = jnp.float32
    bf16 = jnp.bfloat16
    struct = functools.partial(jax.ShapeDtypeStruct, dtype=f32)
    odd = lax.axis_index("rows") % 2 == 1
    raw, run = lax.optimization_barrier((jnp.maximum(frames_raw, 0.0), jnp.maximum(wind_off[0], 0.0)))
    own_odd, own_even = from_owner(wind_off[0], run, odd, "frames", run_owner[0])
    from_odd = paired(own_odd, "rows", 1)
    from_even = paired(own_even, "rows", 0)
    frames_odd, frames_even = by_parity(odd, raw, 4, 1)
    frames_odd = paired(frames_odd, "rows", 1)
    frames_even = paired(frames_even, "rows", 0)
    frames_odd, own_odd = lax.optimization_barrier((frames_odd, own_odd))
    inverse, stack, power, band = pl.pallas_call(
        smooth_kernel,
        out_shape=(
            struct((count, rows, columns)),
            jax.ShapeDtypeStruct((2 * depth, ring * lanes), bf16),
            struct((8 * count, lanes)),
            jax.ShapeDtypeStruct((4 * lanes, 2 * lanes), bf16),
        ),
        in_specs=[vmem] * 3,
        out_specs=(vmem,) * 4,
        scratch_shapes=[
            pltpu.VMEM((count, tiles, rows + 16, lanes), f32),
            pltpu.VMEM((2 * count * rows, (tiles + 2) * lanes), bf16),
            pltpu.VMEM((ring + 2, 2 * count * rows, lanes), bf16),
        ],
        compiler_params=params,
        cost_estimate=cost(8),
        name="smooth",
    )(raw, frames_odd, frames_even)
    offsets = jnp.clip(search_base, -8, 8)
    blocks = lax.axis_size("frames")
    if blocks == 2:
        other_inverse = paired(inverse, "frames", 0)
    clean, part = pl.pallas_call(
        match_kernel,
        out_shape=(jax.ShapeDtypeStruct((tiles + 2, 2 * wide, lanes), bf16), struct((size, lanes))),
        in_specs=[smem] + [vmem] * 7,
        out_specs=(vmem, vmem),
        scratch_shapes=[
            pltpu.VMEM((tiles, rows + 16, lanes), f32),
            pltpu.VMEM((2 * wide, (tiles + 2) * lanes), bf16),
            pltpu.VMEM((ring + 2, 2 * wide, lanes), bf16),
            pltpu.VMEM((2 * wide, ring * lanes), bf16),
            pltpu.VMEM((depth, lanes), f32),
            pltpu.VMEM((8 * count, lanes), f32),
        ],
        compiler_params=params,
        cost_estimate=cost(12),
        name="match",
    )(offsets, own_odd, own_even, from_odd, from_even, stack, power, band)
    parts = lax.all_to_all(part, "rows", 0, 0, tiled=True)
    totals = jnp.sum(parts, axis=0, keepdims=True)
    depth = -(-reach * 2 * wide // lanes) * lanes
    spread = pltpu.VMEM((depth, columns), bf16)
    pressure, moments, part = pl.pallas_call(
        pressure_kernel,
        out_shape=(struct((count, rows, columns)), struct((2, rows, columns)), struct((size, lanes))),
        in_specs=[smem] + [vmem] * 3,
        out_specs=(vmem, vmem, vmem),
        scratch_shapes=[spread],
        compiler_params=params,
        cost_estimate=cost(12),
        name="pressure",
    )(offsets, totals, clean, inverse)
    if blocks == 2:
        row = jnp.concatenate([totals[:, : lanes - 2], offsets.astype(f32)], axis=1)
        row, part = lax.optimization_barrier((row, part))
        row = paired(row, "frames", 0)
        time_mean, time_rms = pl.pallas_call(
            time_kernel,
            out_shape=(struct((rows, columns)), struct((rows, columns))),
            in_specs=[smem] + [vmem] * 4,
            out_specs=(vmem, vmem),
            scratch_shapes=[spread],
            compiler_params=params,
            cost_estimate=cost(12),
            name="time",
        )(row[:, lanes - 2 :].astype(jnp.int32), row, clean, other_inverse, moments)
    else:
        whole = total_over(moments, "frames")
        total_frames = count * blocks
        time_mean = whole[0] / total_frames
        time_rms = jnp.sqrt(jnp.maximum(whole[1] / total_frames - time_mean * time_mean, 0.0))
    sums = lax.all_to_all(part, "rows", 0, 0, tiled=True)
    sums, time_mean, time_rms = lax.optimization_barrier((sums, time_mean, time_rms))
    spatial = jnp.sum(sums, axis=0)
    cell_count = rows * columns * size
    frame_mean = spatial[:count] / cell_count
    frame_rms = jnp.sqrt(spatial[count : 2 * count] / cell_count - frame_mean * frame_mean)
    return (pressure, frame_mean, frame_rms, time_mean, time_rms)


def solution(mesh):
    placed = (P("frames", "rows", None), P("frames", "rows", None), P("rows"), P("frames", None))
    return jax.shard_map(
        shards,
        mesh=mesh,
        in_specs=placed,
        out_specs=(
            P("frames", "rows", None),
            P("frames"),
            P("frames"),
            P("rows", None),
            P("rows", None),
        ),
        check_vma=False,
    )
```

```python
import functools

import jax
import jax.numpy as jnp
from jax import lax
from jax.experimental import pallas as pl
from jax.experimental.pallas import tpu as pltpu
from jax.sharding import PartitionSpec as P

taps = (1.0 / 256, 8.0 / 256, 28.0 / 256, 56.0 / 256, 70.0 / 256)
calib_zero = -0.25
calib_linear = 1.0
calib_square = 0.15
lanes = 128
reach = 7
near = 4
far = 2
params = pltpu.CompilerParams(vmem_limit_bytes=14 * 1024 * 1024)
vmem = pl.BlockSpec(memory_space=pltpu.VMEM)
smem = pl.BlockSpec(memory_space=pltpu.SMEM)


def cost(mebibytes):
    return pl.CostEstimate(flops=0, bytes_accessed=mebibytes * 2**20, transcendentals=0)


def tile_of(index):
    return pl.ds(pl.multiple_of(index * lanes, lanes), lanes)


def by_tiles(step, tiles, group, init=()):
    def body(index, carry):
        for inner in range(group):
            carry = step(index * group + inner, carry)
        return carry

    return lax.fori_loop(0, tiles // group, body, init)


def lane_of(shape):
    return lax.broadcasted_iota(jnp.int32, shape, len(shape) - 1)


def fold(product):
    return jnp.sum(product.reshape(product.shape[0] // 8, 8, lanes), axis=0)


def vertical(load):
    total = taps[4] * load(4)
    for step in range(4):
        total = total + taps[step] * (load(step) + load(8 - step))
    return total


def moved(before, here, after, step):
    if step > 0:
        return pltpu.roll(jnp.where(lane_of(here.shape) < step, after, here), lanes - step, 1)
    if step < 0:
        return pltpu.roll(jnp.where(lane_of(here.shape) >= lanes + step, before, here), -step, 1)
    return here


def halves(value):
    high = value.astype(jnp.bfloat16)
    low = (value - high.astype(jnp.float32)).astype(jnp.bfloat16)
    return high, low


def cut(value):
    return jnp.concatenate(halves(value), axis=0)


def fill_band(band):
    shape = (lanes, lanes)
    apart = lax.broadcasted_iota(jnp.int32, shape, 0) - lax.broadcasted_iota(jnp.int32, shape, 1)

    def block(offset):
        distance = jnp.abs(apart + offset)
        value = jnp.zeros(shape, jnp.float32)
        for step in range(5):
            value = jnp.where(distance == step, taps[4 - step], value)
        return value.astype(jnp.bfloat16)

    none = jnp.zeros(shape, jnp.bfloat16)
    before, here, after = block(-lanes), block(0), block(lanes)
    for index, pair in enumerate(((before, none), (here, before), (after, here), (none, after))):
        band[index * lanes : (index + 1) * lanes, :] = jnp.concatenate(pair, axis=1)


def chunk_of(t):
    return pl.ds(pl.multiple_of(t * 2 * lanes, 2 * lanes), 2 * lanes)


def horizontal(wide, band, t):
    window = wide[:, pl.ds(pl.multiple_of(t * 2 * lanes, 2 * lanes), 4 * lanes)]
    product = jnp.dot(window, band[...], preferred_element_type=jnp.float32)
    half = product.shape[0] // 2
    return product[:half] + product[half:]


def by_row_shift(value, rows, direction):
    place = lax.broadcasted_iota(jnp.int32, value.shape, 0) % rows
    unit = 1
    while unit < rows:
        digit = (place // unit) % 4
        result = value
        for times in range(1, 4):
            amount = times * unit
            turned = pltpu.roll(value, amount if direction > 0 else value.shape[1] - amount, 1)
            result = jnp.where(digit == times, turned, result)
        value = result
        unit *= 4
    return value


def at_edge():
    index = lax.axis_index("rows")
    return (index == 0) | (index == lax.axis_size("rows") - 1)


def smooth_kernel(frames, from_odd, from_even, inverse, stack, power, band, rows_in, wide, pieces):
    count, rows, columns = frames.shape
    tiles = columns // lanes
    ring = tiles + 2
    odd = lax.axis_index("rows") % 2 == 1
    edge = at_edge()
    blank = jnp.zeros((2 * count * rows, lanes), jnp.bfloat16)
    wide[:, tile_of(0)] = blank
    wide[:, tile_of(tiles + 1)] = blank
    fill_band(band)
    pieces[0] = blank
    pieces[tiles + 1] = blank
    pieces[tiles + 2] = blank

    def load_step(t, carry):
        for f in range(count):
            outer = jnp.where(edge, 0.0, from_odd[f, :, tile_of(t)])
            inner = from_even[f, :, tile_of(t)]
            rows_in[f, t, 4:8, :] = jnp.where(odd, inner, outer)
            rows_in[f, t, 8 : 8 + rows, :] = frames[f, :, tile_of(t)]
            rows_in[f, t, 8 + rows : 12 + rows, :] = jnp.where(odd, outer, inner)
        return carry

    def vertical_step(t, carry):
        parts = [vertical(lambda s: rows_in[f, t, pl.ds(4 + s, rows), :]) for f in range(count)]
        wide[:, tile_of(t + 1)] = cut(jnp.concatenate(parts, axis=0))
        return carry

    def horizontal_step(t, totals):
        smooth = horizontal(wide, band, t)
        result = []
        details = []
        for f in range(count):
            part = smooth[f * rows : (f + 1) * rows]
            inverse[f, :, chunk_of(t)] = 1.0 / part
            details.append(frames[f, :, chunk_of(t)] - part)
            square = details[f] * details[f]
            result.append(totals[f] + fold(square[:, :lanes]) + fold(square[:, lanes:]))
        detail = cut(jnp.concatenate(details, axis=0))
        pieces[2 * t + 1] = detail[:, :lanes]
        pieces[2 * t + 2] = detail[:, lanes:]
        return tuple(result)

    def stack_step(t, carry):
        before, here, after = pieces[t], pieces[t + 1], pieces[t + 2]
        size = count * rows
        for a in range(near):
            turned = moved(before, here, after, 1 - a)
            stack[a * size : (a + 1) * size, tile_of(t)] = turned[:size]
            stack[(near + a) * size : (near + a + 1) * size, tile_of(t)] = turned[size:]
        return carry

    by_tiles(load_step, tiles, 8)
    by_tiles(vertical_step, tiles, 8)
    powers = by_tiles(horizontal_step, tiles // 2, 8, (jnp.zeros((8, lanes), jnp.float32),) * count)
    for f in range(count):
        power[f * 8 : f * 8 + 8, :] = powers[f]
    pieces[tiles + 3] = pieces[1]
    by_tiles(stack_step, ring, ring // 2)


def column_shift(offset):
    negative = offset < 0
    first = jnp.where(negative, 0, 1)
    amount = jnp.where(negative, offset + lanes, offset)
    back = (lanes - amount) & (lanes - 1)

    def shift(source, t):
        here = source[t + first]
        after = source[t + first + 1]
        return pltpu.roll(jnp.where(lane_of(here.shape) < amount, after, here), back, 1)

    return shift


def match_kernel(
    base, own_odd, own_even, from_odd, from_even, stack, power, band, clean, part, rows_in, padded, fine, stream, folded, lags
):
    rows = own_odd.shape[0] * 2
    tiles = own_odd.shape[1] // lanes
    count = power.shape[0] // 8
    ring = tiles + 2
    wide = rows + 8
    row_index = lax.axis_index("rows")
    last_row = lax.axis_size("rows") - 1
    odd = row_index % 2 == 1
    edge = at_edge()
    empty = jnp.zeros((2 * wide, lanes), jnp.bfloat16)
    padded[:, tile_of(0)] = empty
    padded[:, tile_of(tiles + 1)] = empty
    for array in (clean, fine):
        array[0] = empty
        array[tiles + 1] = empty
    fine[tiles + 2] = empty
    place = lax.broadcasted_iota(jnp.int32, (wide, 2 * lanes), 0)
    own = (place >= 4) & (place < rows + 4)
    inside = ((place >= 4) | (row_index > 0)) & ((place < rows + 4) | (row_index < last_row))

    def load_step(t, carry):
        outer = [jnp.where(edge, 0.0, from_odd[:, tile_of(t)]), own_odd[:, tile_of(t)]]
        inner = [array[:, tile_of(t)] for array in (own_even, from_even)]
        rows_in[t, 0:8, :] = jnp.where(odd, inner[1], outer[0])
        rows_in[t, 8:16, :] = jnp.where(odd, inner[0], outer[1])
        rows_in[t, 16:24, :] = jnp.where(odd, outer[1], inner[0])
        rows_in[t, 24:32, :] = jnp.where(odd, outer[0], inner[1])
        return carry

    def vertical_step(t, carry):
        padded[:, tile_of(t + 1)] = cut(vertical(lambda s: rows_in[t, pl.ds(s, wide), :]))
        return carry

    def horizontal_step(t, total):
        smooth = jnp.where(inside, horizontal(padded, band, t), 0.0)
        raw = [rows_in[2 * t + c, pl.ds(4, wide), :] for c in range(2)]
        detail = jnp.concatenate(raw, axis=1) - smooth
        square = jnp.where(own, detail * detail, 0.0)
        for array, value in ((clean, cut(smooth)), (fine, cut(detail))):
            array[2 * t + 1] = value[:, :lanes]
            array[2 * t + 2] = value[:, lanes:]
        return total + fold(square[:, :lanes]) + fold(square[:, lanes:])

    by_tiles(load_step, tiles, 8)
    by_tiles(vertical_step, tiles, 8)
    ref_power = by_tiles(horizontal_step, tiles // 2, 8, jnp.zeros((8, lanes), jnp.float32))
    fine[tiles + 3] = fine[1]
    shifts = [column_shift(base[0, 1] + near * b - 2) for b in range(far)]

    def stream_step(t, carry):
        for b, shift in enumerate(shifts):
            stream[b * 2 * wide : (b + 1) * 2 * wide, tile_of(t)] = shift(fine, t)
        return carry

    by_tiles(stream_step, ring, ring // 2)
    product = lax.dot_general(
        stack[...], stream[...], (((1,), (1,)), ((), ())), preferred_element_type=jnp.float32
    )
    size = near * count * rows
    folded[...] = jnp.zeros(folded.shape, jnp.float32)
    folded[:, 0 : far * 2 * wide] = product[:size] + product[size:]
    product = by_row_shift(folded[...], rows, -1)
    lags[...] = jnp.zeros(lags.shape, jnp.float32)
    for a in range(near):
        for f in range(count):
            start = (a * count + f) * rows
            lags[f * 8 + a : f * 8 + a + 1, :] = jnp.sum(product[start : start + rows], axis=0, keepdims=True)
    back = 4 * lanes - 1 - base[0, 0]
    across = lax.broadcasted_iota(jnp.int32, (8, lanes), 0)
    lane = lane_of((8, lanes))
    packed = jnp.zeros((8, lanes), jnp.float32)
    for f in range(count):
        block = lags[f * 8 : f * 8 + 8, :]
        for j in range(reach):
            at = (f * reach + j) * reach
            there = back + at - (j // near) * 2 * wide
            high = pltpu.roll(block, there & (lanes - 1), 1)
            low = pltpu.roll(block, (there - wide) & (lanes - 1), 1)
            member = (across == j % near) & (lane >= at) & (lane < at + reach)
            packed = packed + jnp.where(member, high + low, 0.0)
    lags[0:8, :] = jnp.zeros((8, lanes), jnp.float32)
    for f in range(count):
        lags[f : f + 1, :] = jnp.sum(power[f * 8 : f * 8 + 8, :], axis=0, keepdims=True)
    lags[count : count + 1, :] = jnp.sum(ref_power, axis=0, keepdims=True)
    powers = jnp.sum(lags[0:8, :], axis=1, keepdims=True)
    packed = packed + jnp.where(lane == count * reach * reach + across, powers, 0.0)
    part[...] = jnp.broadcast_to(jnp.sum(packed, axis=0, keepdims=True), part.shape)


def spread_columns(clean, spread, base_col):
    tiles = clean.shape[0] - 2
    size = clean.shape[1]
    spare = spread.shape[0] - reach * size
    spread[reach * size :, :] = jnp.zeros((spare, tiles * lanes), jnp.bfloat16)

    def per_offset(j, carry):
        shift = column_shift(base_col + j - 3)
        at = pl.multiple_of(j * size, size)

        def step(t, inner):
            spread[pl.ds(at, size), tile_of(t)] = shift(clean, t)
            return inner

        by_tiles(step, tiles, 32)
        return carry

    lax.fori_loop(0, reach, per_offset, 0)


def blend_weights(totals, count):
    lane = lane_of(totals.shape)
    block = reach * reach

    def pick(index):
        return jnp.sum(jnp.where(lane == index, totals, 0.0), axis=1, keepdims=True)

    ref_power = pick(count * block + count)
    weights = []
    for f in range(count):
        norm_product = jnp.sqrt((pick(count * block + f) + 1e-06) * (ref_power + 1e-06))
        member = (lane >= f * block) & (lane < (f + 1) * block)
        rho = jnp.where(member, totals, 0.0) / norm_product
        squared = rho * rho
        middle = jnp.where(lane == f * block + block // 2, 0.05, 0.0)
        weights.append((squared + middle) / (0.05 + jnp.sum(squared, axis=1, keepdims=True)))
    return weights


def banded(weights, f, rows, first_row, depth):
    wide = rows + 8
    blank = jnp.zeros((weights.shape[0], depth - lanes), jnp.float32)
    weights = jnp.concatenate([weights, blank], axis=1)
    lane = lane_of(weights.shape)
    line = jnp.zeros_like(weights)
    for j in range(reach):
        at = first_row + j * 2 * wide
        amount = at - (f * reach + j) * reach
        amount = jnp.where(amount < 0, amount + depth, amount)
        line = jnp.where((lane >= at) & (lane < at + reach), pltpu.roll(weights, amount, 1), line)
    line = line + pltpu.roll(line, wide, 1)
    return by_row_shift(jnp.broadcast_to(line[0:1], (rows, depth)), rows, 1)


def pressures(base, totals, clean, spread, inverse):
    count, rows, columns = inverse.shape
    depth = spread.shape[0]
    weights = blend_weights(jnp.broadcast_to(totals[0:1, :], (8, lanes)), count)
    bands = [banded(weights[f], f, rows, 1 + base[0, 0], depth) for f in range(count)]
    mixing = cut(jnp.concatenate(bands, axis=0))
    spread_columns(clean, spread, base[0, 1])

    def chunk_values(where):
        product = jnp.dot(mixing, spread[:, where], preferred_element_type=jnp.float32)
        registered = product[: count * rows] + product[count * rows :]
        values = []
        for f in range(count):
            ratio = registered[f * rows : (f + 1) * rows] * inverse[f, :, where]
            values.append(calib_zero + ratio * (calib_linear + calib_square * ratio))
        return values

    return chunk_values


def pressure_kernel(base, totals, clean, inverse, pressure, moments, part, spread):
    count, rows, columns = inverse.shape
    chunk_values = pressures(base, totals, clean, spread, inverse)

    def step(t, sums):
        where = chunk_of(t)
        values = chunk_values(where)
        squares = [value * value for value in values]
        for f in range(count):
            pressure[f, :, where] = values[f]
        moments[0, :, where] = sum(values[1:], values[0])
        moments[1, :, where] = sum(squares[1:], squares[0])
        result = []
        for total, array in zip(sums, values + squares):
            result.append(total + fold(array[:, :lanes]) + fold(array[:, lanes:]))
        return tuple(result)

    zero = jnp.zeros((8, lanes), jnp.float32)
    sums = by_tiles(step, columns // (2 * lanes), 8, (zero,) * (2 * count))
    line = zero
    for k in range(2 * count):
        value = jnp.sum(jnp.sum(sums[k], axis=0, keepdims=True), axis=1, keepdims=True)
        line = line + jnp.where(lane_of(line.shape) == k, value, 0.0)
    part[...] = jnp.broadcast_to(line[0:1], part.shape)


def time_kernel(base, totals, clean, inverse, moments, time_mean, time_rms, spread):
    count, rows, columns = inverse.shape
    chunk_values = pressures(base, totals, clean, spread, inverse)
    frames = 2 * count

    def step(t, carry):
        where = chunk_of(t)
        first = moments[0, :, where]
        second = moments[1, :, where]
        for value in chunk_values(where):
            first = first + value
            second = second + value * value
        mean = first * (1.0 / frames)
        time_mean[:, where] = mean
        time_rms[:, where] = jnp.sqrt(jnp.maximum(second * (1.0 / frames) - mean * mean, 0.0))
        return carry

    by_tiles(step, columns // (2 * lanes), 8)


def paired(value, axis, first):
    size = lax.axis_size(axis)
    partner = list(range(size))
    for i in range(first, size - 1, 2):
        partner[i], partner[i + 1] = i + 1, i
    return lax.ppermute(value, axis, list(enumerate(partner)))


def by_parity(odd, array, height, dim):
    length = array.shape[dim]
    low = lax.slice_in_dim(array, 0, height, axis=dim)
    high = lax.slice_in_dim(array, length - height, length, axis=dim)
    return jnp.where(odd, high, low), jnp.where(odd, low, high)


def from_owner(shard, here, odd, axis, root):
    mine = lax.axis_index(axis) == root
    height = shard.shape[0] // 2
    if lax.axis_size(axis) != 2:
        whole = lax.psum(jnp.where(mine, shard, jnp.zeros_like(shard)), axis)
        return by_parity(odd, whole, height, 0)
    there = by_parity(odd, paired(shard, axis, 0), height, 0)
    here = by_parity(odd, here, height, 0)
    return [jnp.where(mine, own, other) for own, other in zip(here, there)]


def total_over(value, axis):
    size = lax.axis_size(axis)
    if size & (size - 1):
        return lax.psum(value, axis)
    step = 1
    while step < size:
        value = value + lax.ppermute(value, axis, [(i, i ^ step) for i in range(size)])
        step *= 2
    return value


def shards(frames_raw, wind_off, run_owner, search_base):
    count, rows, columns = frames_raw.shape
    tiles = columns // lanes
    ring = tiles + 2
    wide = rows + 8
    depth = near * count * rows
    size = lax.axis_size("rows")
    f32 = jnp.float32
    bf16 = jnp.bfloat16
    struct = functools.partial(jax.ShapeDtypeStruct, dtype=f32)
    odd = lax.axis_index("rows") % 2 == 1
    raw, run = lax.optimization_barrier((jnp.maximum(frames_raw, 0.0), jnp.maximum(wind_off[0], 0.0)))
    owner, offsets = lax.optimization_barrier((run_owner, jnp.clip(search_base, -8, 8)))
    own_odd, own_even = from_owner(wind_off[0], run, odd, "frames", owner[0])
    from_odd = paired(own_odd, "rows", 1)
    from_even = paired(own_even, "rows", 0)
    frames_odd, frames_even = by_parity(odd, raw, 4, 1)
    frames_odd = paired(frames_odd, "rows", 1)
    frames_even = paired(frames_even, "rows", 0)
    frames_odd, own_odd = lax.optimization_barrier((frames_odd, own_odd))
    inverse, stack, power, band = pl.pallas_call(
        smooth_kernel,
        out_shape=(
            struct((count, rows, columns)),
            jax.ShapeDtypeStruct((2 * depth, ring * lanes), bf16),
            struct((8 * count, lanes)),
            jax.ShapeDtypeStruct((4 * lanes, 2 * lanes), bf16),
        ),
        in_specs=[vmem] * 3,
        out_specs=(vmem,) * 4,
        scratch_shapes=[
            pltpu.VMEM((count, tiles, rows + 16, lanes), f32),
            pltpu.VMEM((2 * count * rows, (tiles + 2) * lanes), bf16),
            pltpu.VMEM((ring + 2, 2 * count * rows, lanes), bf16),
        ],
        compiler_params=params,
        cost_estimate=cost(8),
        name="smooth",
    )(raw, frames_odd, frames_even)
    blocks = lax.axis_size("frames")
    if blocks == 2:
        other_inverse = paired(inverse, "frames", 0)
    clean, part = pl.pallas_call(
        match_kernel,
        out_shape=(jax.ShapeDtypeStruct((tiles + 2, 2 * wide, lanes), bf16), struct((size, lanes))),
        in_specs=[smem] + [vmem] * 7,
        out_specs=(vmem, vmem),
        scratch_shapes=[
            pltpu.VMEM((tiles, rows + 16, lanes), f32),
            pltpu.VMEM((2 * wide, (tiles + 2) * lanes), bf16),
            pltpu.VMEM((ring + 2, 2 * wide, lanes), bf16),
            pltpu.VMEM((far * 2 * wide, ring * lanes), bf16),
            pltpu.VMEM((depth, lanes), f32),
            pltpu.VMEM((8 * count, lanes), f32),
        ],
        compiler_params=params,
        cost_estimate=cost(12),
        name="match",
    )(offsets, own_odd, own_even, from_odd, from_even, stack, power, band)
    parts = lax.all_to_all(part, "rows", 0, 0, tiled=True)
    totals = jnp.sum(parts, axis=0, keepdims=True)
    depth = -(-reach * 2 * wide // lanes) * lanes
    spread = pltpu.VMEM((depth, columns), bf16)
    pressure, moments, part = pl.pallas_call(
        pressure_kernel,
        out_shape=(struct((count, rows, columns)), struct((2, rows, columns)), struct((size, lanes))),
        in_specs=[smem] + [vmem] * 3,
        out_specs=(vmem, vmem, vmem),
        scratch_shapes=[spread],
        compiler_params=params,
        cost_estimate=cost(12),
        name="pressure",
    )(offsets, totals, clean, inverse)
    if blocks == 2:
        row = jnp.concatenate([totals[:, : lanes - 2], offsets.astype(f32)], axis=1)
        row, part = lax.optimization_barrier((row, part))
        row = paired(row, "frames", 0)
        time_mean, time_rms = pl.pallas_call(
            time_kernel,
            out_shape=(struct((rows, columns)), struct((rows, columns))),
            in_specs=[smem] + [vmem] * 4,
            out_specs=(vmem, vmem),
            scratch_shapes=[spread],
            compiler_params=params,
            cost_estimate=cost(12),
            name="time",
        )(row[:, lanes - 2 :].astype(jnp.int32), row, clean, other_inverse, moments)
    else:
        whole = total_over(moments, "frames")
        total_frames = count * blocks
        time_mean = whole[0] / total_frames
        time_rms = jnp.sqrt(jnp.maximum(whole[1] / total_frames - time_mean * time_mean, 0.0))
    sums = lax.all_to_all(part, "rows", 0, 0, tiled=True)
    sums, time_mean, time_rms = lax.optimization_barrier((sums, time_mean, time_rms))
    spatial = jnp.sum(sums, axis=0)
    cell_count = rows * columns * size
    frame_mean = spatial[:count] / cell_count
    frame_rms = jnp.sqrt(spatial[count : 2 * count] / cell_count - frame_mean * frame_mean)
    return (pressure, frame_mean, frame_rms, time_mean, time_rms)


def solution(mesh):
    placed = (P("frames", "rows", None), P("frames", "rows", None), P("rows"), P("frames", None))
    return jax.shard_map(
        shards,
        mesh=mesh,
        in_specs=placed,
        out_specs=(
            P("frames", "rows", None),
            P("frames"),
            P("frames"),
            P("rows", None),
            P("rows", None),
        ),
        check_vma=False,
    )
```

```python
import functools

import jax
import jax.numpy as jnp
from jax import lax
from jax.experimental import pallas as pl
from jax.experimental.pallas import tpu as pltpu
from jax.sharding import PartitionSpec as P

taps = (1.0 / 256, 8.0 / 256, 28.0 / 256, 56.0 / 256, 70.0 / 256)
calib_zero = -0.25
calib_linear = 1.0
calib_square = 0.15
lanes = 128
reach = 7
near = 4
far = 2
params = pltpu.CompilerParams(vmem_limit_bytes=14 * 1024 * 1024)
vmem = pl.BlockSpec(memory_space=pltpu.VMEM)
smem = pl.BlockSpec(memory_space=pltpu.SMEM)


def cost(mebibytes):
    return pl.CostEstimate(flops=0, bytes_accessed=mebibytes * 2**20, transcendentals=0)


def tile_of(index):
    return pl.ds(pl.multiple_of(index * lanes, lanes), lanes)


def by_tiles(step, tiles, group, init=()):
    def body(index, carry):
        for inner in range(group):
            carry = step(index * group + inner, carry)
        return carry

    return lax.fori_loop(0, tiles // group, body, init)


def lane_of(shape):
    return lax.broadcasted_iota(jnp.int32, shape, len(shape) - 1)


def fold(product):
    return jnp.sum(product.reshape(product.shape[0] // 8, 8, lanes), axis=0)


def vertical(load):
    total = taps[4] * load(4)
    for step in range(4):
        total = total + taps[step] * (load(step) + load(8 - step))
    return total


def moved(before, here, after, step):
    if step > 0:
        return pltpu.roll(jnp.where(lane_of(here.shape) < step, after, here), lanes - step, 1)
    if step < 0:
        return pltpu.roll(jnp.where(lane_of(here.shape) >= lanes + step, before, here), -step, 1)
    return here


def halves(value):
    high = value.astype(jnp.bfloat16)
    low = (value - high.astype(jnp.float32)).astype(jnp.bfloat16)
    return high, low


def cut(value):
    return jnp.concatenate(halves(value), axis=0)


def fill_band(band):
    shape = (lanes, lanes)
    apart = lax.broadcasted_iota(jnp.int32, shape, 0) - lax.broadcasted_iota(jnp.int32, shape, 1)

    def block(offset):
        distance = jnp.abs(apart + offset)
        value = jnp.zeros(shape, jnp.float32)
        for step in range(5):
            value = jnp.where(distance == step, taps[4 - step], value)
        return value.astype(jnp.bfloat16)

    none = jnp.zeros(shape, jnp.bfloat16)
    before, here, after = block(-lanes), block(0), block(lanes)
    for index, pair in enumerate(((before, none), (here, before), (after, here), (none, after))):
        band[index * lanes : (index + 1) * lanes, :] = jnp.concatenate(pair, axis=1)


def chunk_of(t):
    return pl.ds(pl.multiple_of(t * 2 * lanes, 2 * lanes), 2 * lanes)


def horizontal(wide, band, t):
    window = wide[:, pl.ds(pl.multiple_of(t * 2 * lanes, 2 * lanes), 4 * lanes)]
    product = jnp.dot(window, band[...], preferred_element_type=jnp.float32)
    half = product.shape[0] // 2
    return product[:half] + product[half:]


def by_row_shift(value, rows, direction):
    place = lax.broadcasted_iota(jnp.int32, value.shape, 0) % rows
    unit = 1
    while unit < rows:
        digit = (place // unit) % 4
        result = value
        for times in range(1, 4):
            amount = times * unit
            turned = pltpu.roll(value, amount if direction > 0 else value.shape[1] - amount, 1)
            result = jnp.where(digit == times, turned, result)
        value = result
        unit *= 4
    return value


def at_edge():
    index = lax.axis_index("rows")
    return (index == 0) | (index == lax.axis_size("rows") - 1)


def smooth_kernel(frames, from_odd, from_even, inverse, stack, power, band, rows_in, wide, pieces):
    count, rows, columns = frames.shape
    tiles = columns // lanes
    ring = tiles + 2
    odd = lax.axis_index("rows") % 2 == 1
    edge = at_edge()
    blank = jnp.zeros((2 * count * rows, lanes), jnp.bfloat16)
    wide[:, tile_of(0)] = blank
    wide[:, tile_of(tiles + 1)] = blank
    fill_band(band)
    pieces[0] = blank
    pieces[tiles + 1] = blank
    pieces[tiles + 2] = blank

    def load_step(t, carry):
        for f in range(count):
            outer = jnp.where(edge, 0.0, from_odd[f, :, tile_of(t)])
            inner = from_even[f, :, tile_of(t)]
            rows_in[f, t, 4:8, :] = jnp.where(odd, inner, outer)
            rows_in[f, t, 8 : 8 + rows, :] = frames[f, :, tile_of(t)]
            rows_in[f, t, 8 + rows : 12 + rows, :] = jnp.where(odd, outer, inner)
        return carry

    def vertical_step(t, carry):
        parts = [vertical(lambda s: rows_in[f, t, pl.ds(4 + s, rows), :]) for f in range(count)]
        wide[:, tile_of(t + 1)] = cut(jnp.concatenate(parts, axis=0))
        return carry

    def horizontal_step(t, totals):
        smooth = horizontal(wide, band, t)
        result = []
        details = []
        for f in range(count):
            part = smooth[f * rows : (f + 1) * rows]
            inverse[f, :, chunk_of(t)] = 1.0 / part
            details.append(frames[f, :, chunk_of(t)] - part)
            square = details[f] * details[f]
            result.append(totals[f] + fold(square[:, :lanes]) + fold(square[:, lanes:]))
        detail = cut(jnp.concatenate(details, axis=0))
        pieces[2 * t + 1] = detail[:, :lanes]
        pieces[2 * t + 2] = detail[:, lanes:]
        return tuple(result)

    def stack_step(t, carry):
        before, here, after = pieces[t], pieces[t + 1], pieces[t + 2]
        size = count * rows
        for a in range(near):
            turned = moved(before, here, after, 1 - a)
            stack[a * size : (a + 1) * size, tile_of(t)] = turned[:size]
            stack[(near + a) * size : (near + a + 1) * size, tile_of(t)] = turned[size:]
        return carry

    by_tiles(load_step, tiles, 8)
    by_tiles(vertical_step, tiles, 8)
    powers = by_tiles(horizontal_step, tiles // 2, 8, (jnp.zeros((8, lanes), jnp.float32),) * count)
    for f in range(count):
        power[f * 8 : f * 8 + 8, :] = powers[f]
    pieces[tiles + 3] = pieces[1]
    by_tiles(stack_step, ring, ring // 2)


def column_shift(offset):
    negative = offset < 0
    first = jnp.where(negative, 0, 1)
    amount = jnp.where(negative, offset + lanes, offset)
    back = (lanes - amount) & (lanes - 1)

    def shift(source, t):
        here = source[t + first]
        after = source[t + first + 1]
        return pltpu.roll(jnp.where(lane_of(here.shape) < amount, after, here), back, 1)

    return shift


def match_kernel(
    base, own_odd, own_even, from_odd, from_even, stack, power, band, clean, part, rows_in, padded, fine, stream, folded, lags
):
    rows = own_odd.shape[0] * 2
    tiles = own_odd.shape[1] // lanes
    count = power.shape[0] // 8
    ring = tiles + 2
    wide = rows + 8
    row_index = lax.axis_index("rows")
    last_row = lax.axis_size("rows") - 1
    odd = row_index % 2 == 1
    edge = at_edge()
    empty = jnp.zeros((2 * wide, lanes), jnp.bfloat16)
    padded[:, tile_of(0)] = empty
    padded[:, tile_of(tiles + 1)] = empty
    for array in (clean, fine):
        array[0] = empty
        array[tiles + 1] = empty
    fine[tiles + 2] = empty
    place = lax.broadcasted_iota(jnp.int32, (wide, 2 * lanes), 0)
    own = (place >= 4) & (place < rows + 4)
    inside = ((place >= 4) | (row_index > 0)) & ((place < rows + 4) | (row_index < last_row))

    def load_step(t, carry):
        outer = [jnp.where(edge, 0.0, from_odd[:, tile_of(t)]), own_odd[:, tile_of(t)]]
        inner = [array[:, tile_of(t)] for array in (own_even, from_even)]
        rows_in[t, 0:8, :] = jnp.where(odd, inner[1], outer[0])
        rows_in[t, 8:16, :] = jnp.where(odd, inner[0], outer[1])
        rows_in[t, 16:24, :] = jnp.where(odd, outer[1], inner[0])
        rows_in[t, 24:32, :] = jnp.where(odd, outer[0], inner[1])
        return carry

    def vertical_step(t, carry):
        padded[:, tile_of(t + 1)] = cut(vertical(lambda s: rows_in[t, pl.ds(s, wide), :]))
        return carry

    def horizontal_step(t, total):
        smooth = jnp.where(inside, horizontal(padded, band, t), 0.0)
        raw = [rows_in[2 * t + c, pl.ds(4, wide), :] for c in range(2)]
        detail = jnp.concatenate(raw, axis=1) - smooth
        square = jnp.where(own, detail * detail, 0.0)
        for array, value in ((clean, cut(smooth)), (fine, cut(detail))):
            array[2 * t + 1] = value[:, :lanes]
            array[2 * t + 2] = value[:, lanes:]
        return total + fold(square[:, :lanes]) + fold(square[:, lanes:])

    by_tiles(load_step, tiles, 8)
    by_tiles(vertical_step, tiles, 8)
    ref_power = by_tiles(horizontal_step, tiles // 2, 8, jnp.zeros((8, lanes), jnp.float32))
    fine[tiles + 3] = fine[1]
    shifts = [column_shift(base[0, 1] + near * b - 2) for b in range(far)]

    def stream_step(t, carry):
        for b, shift in enumerate(shifts):
            stream[b * 2 * wide : (b + 1) * 2 * wide, tile_of(t)] = shift(fine, t)
        return carry

    by_tiles(stream_step, ring, ring // 2)
    product = lax.dot_general(
        stack[...], stream[...], (((1,), (1,)), ((), ())), preferred_element_type=jnp.float32
    )
    size = near * count * rows
    folded[...] = jnp.zeros(folded.shape, jnp.float32)
    folded[:, 0 : far * 2 * wide] = product[:size] + product[size:]
    product = by_row_shift(folded[...], rows, -1)
    lags[...] = jnp.zeros(lags.shape, jnp.float32)
    for a in range(near):
        for f in range(count):
            start = (a * count + f) * rows
            lags[f * 8 + a : f * 8 + a + 1, :] = jnp.sum(product[start : start + rows], axis=0, keepdims=True)
    back = 4 * lanes - 1 - base[0, 0]
    across = lax.broadcasted_iota(jnp.int32, (8, lanes), 0)
    lane = lane_of((8, lanes))
    packed = jnp.zeros((8, lanes), jnp.float32)
    for f in range(count):
        block = lags[f * 8 : f * 8 + 8, :]
        for j in range(reach):
            at = (f * reach + j) * reach
            there = back + at - (j // near) * 2 * wide
            high = pltpu.roll(block, there & (lanes - 1), 1)
            low = pltpu.roll(block, (there - wide) & (lanes - 1), 1)
            member = (across == j % near) & (lane >= at) & (lane < at + reach)
            packed = packed + jnp.where(member, high + low, 0.0)
    lags[0:8, :] = jnp.zeros((8, lanes), jnp.float32)
    for f in range(count):
        lags[f : f + 1, :] = jnp.sum(power[f * 8 : f * 8 + 8, :], axis=0, keepdims=True)
    lags[count : count + 1, :] = jnp.sum(ref_power, axis=0, keepdims=True)
    powers = jnp.sum(lags[0:8, :], axis=1, keepdims=True)
    packed = packed + jnp.where(lane == count * reach * reach + across, powers, 0.0)
    packed = jnp.sum(packed, axis=0, keepdims=True)
    for place in range(2):
        offset = base[0, place].astype(jnp.float32)
        packed = jnp.where(lane[0:1] == lanes - 2 + place, offset, packed)
    part[...] = jnp.broadcast_to(packed, part.shape)


def spread_columns(clean, spread, base_col):
    tiles = clean.shape[0] - 2
    size = clean.shape[1]
    spare = spread.shape[0] - reach * size
    spread[reach * size :, :] = jnp.zeros((spare, tiles * lanes), jnp.bfloat16)

    for j in range(reach):
        shift = column_shift(base_col + j - 3)
        for t in range(tiles):
            spread[j * size : (j + 1) * size, t * lanes : (t + 1) * lanes] = shift(clean, t)


def blend_weights(totals, count):
    lane = lane_of(totals.shape)
    block = reach * reach

    def pick(index):
        return jnp.sum(jnp.where(lane == index, totals, 0.0), axis=1, keepdims=True)

    ref_power = pick(count * block + count)
    weights = []
    for f in range(count):
        norm_product = jnp.sqrt((pick(count * block + f) + 1e-06) * (ref_power + 1e-06))
        member = (lane >= f * block) & (lane < (f + 1) * block)
        rho = jnp.where(member, totals, 0.0) / norm_product
        squared = rho * rho
        middle = jnp.where(lane == f * block + block // 2, 0.05, 0.0)
        weights.append((squared + middle) / (0.05 + jnp.sum(squared, axis=1, keepdims=True)))
    return weights


def banded(weights, f, rows, first_row, depth):
    wide = rows + 8
    blank = jnp.zeros((weights.shape[0], depth - lanes), jnp.float32)
    weights = jnp.concatenate([weights, blank], axis=1)
    lane = lane_of(weights.shape)
    line = jnp.zeros_like(weights)
    for j in range(reach):
        at = first_row + j * 2 * wide
        amount = at - (f * reach + j) * reach
        amount = jnp.where(amount < 0, amount + depth, amount)
        line = jnp.where((lane >= at) & (lane < at + reach), pltpu.roll(weights, amount, 1), line)
    line = line + pltpu.roll(line, wide, 1)
    return by_row_shift(jnp.broadcast_to(line[0:1], (rows, depth)), rows, 1)


def pressures(base, totals, clean, spread, inverse):
    count, rows, columns = inverse.shape
    depth = spread.shape[0]
    weights = blend_weights(jnp.broadcast_to(totals[0:1, :], (8, lanes)), count)
    bands = [banded(weights[f], f, rows, 1 + base[0, 0], depth) for f in range(count)]
    mixing = cut(jnp.concatenate(bands, axis=0))
    spread_columns(clean, spread, base[0, 1])

    def chunk_values(where):
        product = jnp.dot(mixing, spread[:, where], preferred_element_type=jnp.float32)
        registered = product[: count * rows] + product[count * rows :]
        values = []
        for f in range(count):
            ratio = registered[f * rows : (f + 1) * rows] * inverse[f, :, where]
            values.append(calib_zero + ratio * (calib_linear + calib_square * ratio))
        return values

    return chunk_values


def pressure_kernel(base, totals, clean, inverse, pressure, moments, part, spread):
    count, rows, columns = inverse.shape
    chunk_values = pressures(base, totals, clean, spread, inverse)

    def step(t, sums):
        where = chunk_of(t)
        values = chunk_values(where)
        squares = [value * value for value in values]
        for f in range(count):
            pressure[f, :, where] = values[f]
        moments[0, :, where] = sum(values[1:], values[0])
        moments[1, :, where] = sum(squares[1:], squares[0])
        result = []
        for total, array in zip(sums, values + squares):
            result.append(total + fold(array[:, :lanes]) + fold(array[:, lanes:]))
        return tuple(result)

    zero = jnp.zeros((8, lanes), jnp.float32)
    sums = by_tiles(step, columns // (2 * lanes), 8, (zero,) * (2 * count))
    line = zero
    for k in range(2 * count):
        value = jnp.sum(jnp.sum(sums[k], axis=0, keepdims=True), axis=1, keepdims=True)
        line = line + jnp.where(lane_of(line.shape) == k, value, 0.0)
    part[...] = jnp.broadcast_to(line[0:1], part.shape)


def time_kernel(base, totals, clean, inverse, moments, time_mean, time_rms, spread):
    count, rows, columns = inverse.shape
    chunk_values = pressures(base, totals, clean, spread, inverse)
    frames = 2 * count

    def step(t, carry):
        where = chunk_of(t)
        first = moments[0, :, where]
        second = moments[1, :, where]
        for value in chunk_values(where):
            first = first + value
            second = second + value * value
        mean = first * (1.0 / frames)
        time_mean[:, where] = mean
        time_rms[:, where] = jnp.sqrt(jnp.maximum(second * (1.0 / frames) - mean * mean, 0.0))
        return carry

    by_tiles(step, columns // (2 * lanes), 8)


def paired(value, axis, first):
    size = lax.axis_size(axis)
    partner = list(range(size))
    for i in range(first, size - 1, 2):
        partner[i], partner[i + 1] = i + 1, i
    return lax.ppermute(value, axis, list(enumerate(partner)))


def by_parity(odd, array, height, dim):
    length = array.shape[dim]
    low = lax.slice_in_dim(array, 0, height, axis=dim)
    high = lax.slice_in_dim(array, length - height, length, axis=dim)
    return jnp.where(odd, high, low), jnp.where(odd, low, high)


def from_owner(shard, here, odd, axis, root):
    mine = lax.axis_index(axis) == root
    height = shard.shape[0] // 2
    if lax.axis_size(axis) != 2:
        whole = lax.psum(jnp.where(mine, shard, jnp.zeros_like(shard)), axis)
        return by_parity(odd, whole, height, 0)
    there = by_parity(odd, paired(shard, axis, 0), height, 0)
    here = by_parity(odd, here, height, 0)
    return [jnp.where(mine, own, other) for own, other in zip(here, there)]


def total_over(value, axis):
    size = lax.axis_size(axis)
    if size & (size - 1):
        return lax.psum(value, axis)
    step = 1
    while step < size:
        value = value + lax.ppermute(value, axis, [(i, i ^ step) for i in range(size)])
        step *= 2
    return value


def shards(frames_raw, wind_off, run_owner, search_base):
    count, rows, columns = frames_raw.shape
    tiles = columns // lanes
    ring = tiles + 2
    wide = rows + 8
    depth = near * count * rows
    size = lax.axis_size("rows")
    f32 = jnp.float32
    bf16 = jnp.bfloat16
    struct = functools.partial(jax.ShapeDtypeStruct, dtype=f32)
    odd = lax.axis_index("rows") % 2 == 1
    raw, run = lax.optimization_barrier((jnp.maximum(frames_raw, 0.0), jnp.maximum(wind_off[0], 0.0)))
    owner, offsets = lax.optimization_barrier((run_owner, jnp.clip(search_base, -8, 8)))
    own_odd, own_even = from_owner(wind_off[0], run, odd, "frames", owner[0])
    from_odd = paired(own_odd, "rows", 1)
    from_even = paired(own_even, "rows", 0)
    frames_odd, frames_even = by_parity(odd, raw, 4, 1)
    frames_odd = paired(frames_odd, "rows", 1)
    frames_even = paired(frames_even, "rows", 0)
    frames_odd, own_odd = lax.optimization_barrier((frames_odd, own_odd))
    inverse, stack, power, band = pl.pallas_call(
        smooth_kernel,
        out_shape=(
            struct((count, rows, columns)),
            jax.ShapeDtypeStruct((2 * depth, ring * lanes), bf16),
            struct((8 * count, lanes)),
            jax.ShapeDtypeStruct((4 * lanes, 2 * lanes), bf16),
        ),
        in_specs=[vmem] * 3,
        out_specs=(vmem,) * 4,
        scratch_shapes=[
            pltpu.VMEM((count, tiles, rows + 16, lanes), f32),
            pltpu.VMEM((2 * count * rows, (tiles + 2) * lanes), bf16),
            pltpu.VMEM((ring + 2, 2 * count * rows, lanes), bf16),
        ],
        compiler_params=params,
        cost_estimate=cost(8),
        name="smooth",
    )(raw, frames_odd, frames_even)
    blocks = lax.axis_size("frames")
    peers = size * blocks if blocks == 2 else size
    if blocks == 2:
        other_inverse = paired(inverse, "frames", 0)
    clean, part = pl.pallas_call(
        match_kernel,
        out_shape=(jax.ShapeDtypeStruct((tiles + 2, 2 * wide, lanes), bf16), struct((peers, lanes))),
        in_specs=[smem] + [vmem] * 7,
        out_specs=(vmem, vmem),
        scratch_shapes=[
            pltpu.VMEM((tiles, rows + 16, lanes), f32),
            pltpu.VMEM((2 * wide, (tiles + 2) * lanes), bf16),
            pltpu.VMEM((ring + 2, 2 * wide, lanes), bf16),
            pltpu.VMEM((far * 2 * wide, ring * lanes), bf16),
            pltpu.VMEM((depth, lanes), f32),
            pltpu.VMEM((8 * count, lanes), f32),
        ],
        compiler_params=params,
        cost_estimate=cost(12),
        name="match",
    )(offsets, own_odd, own_even, from_odd, from_even, stack, power, band)
    if blocks == 2:
        parts = lax.all_to_all(part, ("rows", "frames"), 0, 0, tiled=True).reshape(size, blocks, lanes)
        mine = lax.axis_index("frames") == 0
        both = jnp.sum(parts, axis=0)
        totals = jnp.where(mine, both[0:1], both[1:2])
        row = jnp.where(mine, both[1:2], both[0:1])
        place = jnp.where(mine, parts[0, 1:2], parts[0, 0:1])[:, lanes - 2 :].astype(jnp.int32)
    else:
        totals = jnp.sum(lax.all_to_all(part, "rows", 0, 0, tiled=True), axis=0, keepdims=True)
    depth = -(-reach * 2 * wide // lanes) * lanes
    spread = pltpu.VMEM((depth, columns), bf16)
    pressure, moments, part = pl.pallas_call(
        pressure_kernel,
        out_shape=(struct((count, rows, columns)), struct((2, rows, columns)), struct((size, lanes))),
        in_specs=[smem] + [vmem] * 3,
        out_specs=(vmem, vmem, vmem),
        scratch_shapes=[spread],
        compiler_params=params,
        cost_estimate=cost(12),
        name="pressure",
    )(offsets, totals, clean, inverse)
    if blocks == 2:
        time_mean, time_rms = pl.pallas_call(
            time_kernel,
            out_shape=(struct((rows, columns)), struct((rows, columns))),
            in_specs=[smem] + [vmem] * 4,
            out_specs=(vmem, vmem),
            scratch_shapes=[spread],
            compiler_params=params,
            cost_estimate=cost(12),
            name="time",
        )(place, row, clean, other_inverse, moments)
    else:
        whole = total_over(moments, "frames")
        total_frames = count * blocks
        time_mean = whole[0] / total_frames
        time_rms = jnp.sqrt(jnp.maximum(whole[1] / total_frames - time_mean * time_mean, 0.0))
    sums = lax.all_to_all(part, "rows", 0, 0, tiled=True)
    sums, time_mean, time_rms = lax.optimization_barrier((sums, time_mean, time_rms))
    spatial = jnp.sum(sums, axis=0)
    cell_count = rows * columns * size
    frame_mean = spatial[:count] / cell_count
    frame_rms = jnp.sqrt(spatial[count : 2 * count] / cell_count - frame_mean * frame_mean)
    return (pressure, frame_mean, frame_rms, time_mean, time_rms)


def solution(mesh):
    placed = (P("frames", "rows", None), P("frames", "rows", None), P("rows"), P("frames", None))
    return jax.shard_map(
        shards,
        mesh=mesh,
        in_specs=placed,
        out_specs=(
            P("frames", "rows", None),
            P("frames"),
            P("frames"),
            P("rows", None),
            P("rows", None),
        ),
        check_vma=False,
    )
```

```python
import functools

import jax
import jax.numpy as jnp
from jax import lax
from jax.experimental import pallas as pl
from jax.experimental.pallas import tpu as pltpu
from jax.sharding import PartitionSpec as P

taps = (1.0 / 256, 8.0 / 256, 28.0 / 256, 56.0 / 256, 70.0 / 256)
calib_zero = -0.25
calib_linear = 1.0
calib_square = 0.15
lanes = 128
reach = 7
near = 4
far = 2
params = pltpu.CompilerParams(vmem_limit_bytes=14 * 1024 * 1024)
vmem = pl.BlockSpec(memory_space=pltpu.VMEM)
smem = pl.BlockSpec(memory_space=pltpu.SMEM)


def cost(mebibytes):
    return pl.CostEstimate(flops=0, bytes_accessed=mebibytes * 2**20, transcendentals=0)


def tile_of(index):
    if isinstance(index, int):
        return slice(index * lanes, (index + 1) * lanes)
    return pl.ds(pl.multiple_of(index * lanes, lanes), lanes)


def by_tiles(step, tiles, group, init=()):
    if group == tiles:
        for index in range(tiles):
            init = step(index, init)
        return init

    def body(index, carry):
        for inner in range(group):
            carry = step(index * group + inner, carry)
        return carry

    return lax.fori_loop(0, tiles // group, body, init)


def lane_of(shape):
    return lax.broadcasted_iota(jnp.int32, shape, len(shape) - 1)


def fold(product):
    return jnp.sum(product.reshape(product.shape[0] // 8, 8, lanes), axis=0)


def vertical(load):
    total = taps[4] * load(4)
    for step in range(4):
        total = total + taps[step] * (load(step) + load(8 - step))
    return total


def moved(before, here, after, step):
    if step > 0:
        return pltpu.roll(jnp.where(lane_of(here.shape) < step, after, here), lanes - step, 1)
    if step < 0:
        return pltpu.roll(jnp.where(lane_of(here.shape) >= lanes + step, before, here), -step, 1)
    return here


def halves(value):
    high = value.astype(jnp.bfloat16)
    low = (value - high.astype(jnp.float32)).astype(jnp.bfloat16)
    return high, low


def cut(value):
    return jnp.concatenate(halves(value), axis=0)


def fill_band(band):
    shape = (lanes, lanes)
    apart = lax.broadcasted_iota(jnp.int32, shape, 0) - lax.broadcasted_iota(jnp.int32, shape, 1)

    def block(offset):
        distance = jnp.abs(apart + offset)
        value = jnp.zeros(shape, jnp.float32)
        for step in range(5):
            value = jnp.where(distance == step, taps[4 - step], value)
        return value.astype(jnp.bfloat16)

    none = jnp.zeros(shape, jnp.bfloat16)
    before, here, after = block(-lanes), block(0), block(lanes)
    for index, pair in enumerate(((before, none), (here, before), (after, here), (none, after))):
        band[index * lanes : (index + 1) * lanes, :] = jnp.concatenate(pair, axis=1)


def chunk_of(t):
    if isinstance(t, int):
        return slice(t * 2 * lanes, (t + 1) * 2 * lanes)
    return pl.ds(pl.multiple_of(t * 2 * lanes, 2 * lanes), 2 * lanes)


def horizontal(wide, band, t):
    window = wide[:, t * 2 * lanes : (t + 2) * 2 * lanes]
    product = jnp.dot(window, band[...], preferred_element_type=jnp.float32)
    half = product.shape[0] // 2
    return product[:half] + product[half:]


def by_row_shift(value, rows, direction):
    place = lax.broadcasted_iota(jnp.int32, value.shape, 0) % rows
    unit = 1
    while unit < rows:
        digit = (place // unit) % 4
        result = value
        for times in range(1, 4):
            amount = times * unit
            turned = pltpu.roll(value, amount if direction > 0 else value.shape[1] - amount, 1)
            result = jnp.where(digit == times, turned, result)
        value = result
        unit *= 4
    return value


def at_edge():
    index = lax.axis_index("rows")
    return (index == 0) | (index == lax.axis_size("rows") - 1)


def smooth_kernel(frames, from_odd, from_even, inverse, stack, power, band, rows_in, wide, pieces):
    count, rows, columns = frames.shape
    tiles = columns // lanes
    ring = tiles + 2
    odd = lax.axis_index("rows") % 2 == 1
    edge = at_edge()
    blank = jnp.zeros((2 * count * rows, lanes), jnp.bfloat16)
    wide[:, tile_of(0)] = blank
    wide[:, tile_of(tiles + 1)] = blank
    fill_band(band)
    pieces[0] = blank
    pieces[tiles + 1] = blank
    pieces[tiles + 2] = blank

    def load_step(t, carry):
        for f in range(count):
            outer = jnp.where(edge, 0.0, from_odd[f, :, tile_of(t)])
            inner = from_even[f, :, tile_of(t)]
            rows_in[f, t, 4:8, :] = jnp.where(odd, inner, outer)
            rows_in[f, t, 8 : 8 + rows, :] = frames[f, :, tile_of(t)]
            rows_in[f, t, 8 + rows : 12 + rows, :] = jnp.where(odd, outer, inner)
        return carry

    def vertical_step(t, carry):
        parts = [vertical(lambda s: rows_in[f, t, pl.ds(4 + s, rows), :]) for f in range(count)]
        wide[:, tile_of(t + 1)] = cut(jnp.concatenate(parts, axis=0))
        return carry

    def horizontal_step(t, totals):
        smooth = horizontal(wide, band, t)
        result = []
        details = []
        for f in range(count):
            part = smooth[f * rows : (f + 1) * rows]
            inverse[f, :, chunk_of(t)] = 1.0 / part
            details.append(frames[f, :, chunk_of(t)] - part)
            square = details[f] * details[f]
            result.append(totals[f] + fold(square[:, :lanes]) + fold(square[:, lanes:]))
        detail = cut(jnp.concatenate(details, axis=0))
        pieces[2 * t + 1] = detail[:, :lanes]
        pieces[2 * t + 2] = detail[:, lanes:]
        return tuple(result)

    def stack_step(t, carry):
        before, here, after = pieces[t], pieces[t + 1], pieces[t + 2]
        size = count * rows
        for a in range(near):
            turned = moved(before, here, after, 1 - a)
            stack[a * size : (a + 1) * size, tile_of(t)] = turned[:size]
            stack[(near + a) * size : (near + a + 1) * size, tile_of(t)] = turned[size:]
        return carry

    by_tiles(load_step, tiles, tiles)
    by_tiles(vertical_step, tiles, tiles)
    powers = by_tiles(horizontal_step, tiles // 2, tiles // 2, (jnp.zeros((8, lanes), jnp.float32),) * count)
    for f in range(count):
        power[f * 8 : f * 8 + 8, :] = powers[f]
    pieces[tiles + 3] = pieces[1]
    by_tiles(stack_step, ring, ring)


def column_shift(offset):
    negative = offset < 0
    first = jnp.where(negative, 0, 1)
    amount = jnp.where(negative, offset + lanes, offset)
    back = (lanes - amount) & (lanes - 1)

    def shift(source, t):
        here = source[t + first]
        after = source[t + first + 1]
        return pltpu.roll(jnp.where(lane_of(here.shape) < amount, after, here), back, 1)

    return shift


def match_kernel(
    base, own_odd, own_even, from_odd, from_even, stack, power, band, clean, part, rows_in, padded, fine, stream, folded, lags
):
    rows = own_odd.shape[0] * 2
    tiles = own_odd.shape[1] // lanes
    count = power.shape[0] // 8
    ring = tiles + 2
    wide = rows + 8
    row_index = lax.axis_index("rows")
    last_row = lax.axis_size("rows") - 1
    odd = row_index % 2 == 1
    edge = at_edge()
    empty = jnp.zeros((2 * wide, lanes), jnp.bfloat16)
    padded[:, tile_of(0)] = empty
    padded[:, tile_of(tiles + 1)] = empty
    for array in (clean, fine):
        array[0] = empty
        array[tiles + 1] = empty
    fine[tiles + 2] = empty
    place = lax.broadcasted_iota(jnp.int32, (wide, 2 * lanes), 0)
    own = (place >= 4) & (place < rows + 4)
    inside = ((place >= 4) | (row_index > 0)) & ((place < rows + 4) | (row_index < last_row))

    def load_step(t, carry):
        outer = [jnp.where(edge, 0.0, from_odd[:, tile_of(t)]), own_odd[:, tile_of(t)]]
        inner = [array[:, tile_of(t)] for array in (own_even, from_even)]
        rows_in[t, 0:8, :] = jnp.where(odd, inner[1], outer[0])
        rows_in[t, 8:16, :] = jnp.where(odd, inner[0], outer[1])
        rows_in[t, 16:24, :] = jnp.where(odd, outer[1], inner[0])
        rows_in[t, 24:32, :] = jnp.where(odd, outer[0], inner[1])
        return carry

    def vertical_step(t, carry):
        padded[:, tile_of(t + 1)] = cut(vertical(lambda s: rows_in[t, pl.ds(s, wide), :]))
        return carry

    def horizontal_step(t, total):
        smooth = jnp.where(inside, horizontal(padded, band, t), 0.0)
        raw = [rows_in[2 * t + c, pl.ds(4, wide), :] for c in range(2)]
        detail = jnp.concatenate(raw, axis=1) - smooth
        square = jnp.where(own, detail * detail, 0.0)
        for array, value in ((clean, cut(smooth)), (fine, cut(detail))):
            array[2 * t + 1] = value[:, :lanes]
            array[2 * t + 2] = value[:, lanes:]
        return total + fold(square[:, :lanes]) + fold(square[:, lanes:])

    by_tiles(load_step, tiles, tiles)
    by_tiles(vertical_step, tiles, tiles)
    ref_power = by_tiles(horizontal_step, tiles // 2, tiles // 2, jnp.zeros((8, lanes), jnp.float32))
    fine[tiles + 3] = fine[1]
    shifts = [column_shift(base[0, 1] + near * b - 2) for b in range(far)]

    def stream_step(t, carry):
        for b, shift in enumerate(shifts):
            stream[b * 2 * wide : (b + 1) * 2 * wide, tile_of(t)] = shift(fine, t)
        return carry

    by_tiles(stream_step, ring, ring)
    product = lax.dot_general(
        stack[...], stream[...], (((1,), (1,)), ((), ())), preferred_element_type=jnp.float32
    )
    size = near * count * rows
    folded[...] = jnp.zeros(folded.shape, jnp.float32)
    folded[:, 0 : far * 2 * wide] = product[:size] + product[size:]
    product = by_row_shift(folded[...], rows, -1)
    lags[...] = jnp.zeros(lags.shape, jnp.float32)
    for a in range(near):
        for f in range(count):
            start = (a * count + f) * rows
            lags[f * 8 + a : f * 8 + a + 1, :] = jnp.sum(product[start : start + rows], axis=0, keepdims=True)
    back = 4 * lanes - 1 - base[0, 0]
    across = lax.broadcasted_iota(jnp.int32, (8, lanes), 0)
    lane = lane_of((8, lanes))
    packed = jnp.zeros((8, lanes), jnp.float32)
    for f in range(count):
        block = lags[f * 8 : f * 8 + 8, :]
        for j in range(reach):
            at = (f * reach + j) * reach
            there = back + at - (j // near) * 2 * wide
            high = pltpu.roll(block, there & (lanes - 1), 1)
            low = pltpu.roll(block, (there - wide) & (lanes - 1), 1)
            member = (across == j % near) & (lane >= at) & (lane < at + reach)
            packed = packed + jnp.where(member, high + low, 0.0)
    lags[0:8, :] = jnp.zeros((8, lanes), jnp.float32)
    for f in range(count):
        lags[f : f + 1, :] = jnp.sum(power[f * 8 : f * 8 + 8, :], axis=0, keepdims=True)
    lags[count : count + 1, :] = jnp.sum(ref_power, axis=0, keepdims=True)
    powers = jnp.sum(lags[0:8, :], axis=1, keepdims=True)
    packed = packed + jnp.where(lane == count * reach * reach + across, powers, 0.0)
    packed = jnp.sum(packed, axis=0, keepdims=True)
    for place in range(2):
        offset = base[0, place].astype(jnp.float32)
        packed = jnp.where(lane[0:1] == lanes - 2 + place, offset, packed)
    part[...] = jnp.broadcast_to(packed, part.shape)


def spread_columns(clean, spread, base_col):
    tiles = clean.shape[0] - 2
    size = clean.shape[1]
    spare = spread.shape[0] - reach * size
    spread[reach * size :, :] = jnp.zeros((spare, tiles * lanes), jnp.bfloat16)

    for j in range(reach):
        shift = column_shift(base_col + j - 3)
        for t in range(tiles):
            spread[j * size : (j + 1) * size, t * lanes : (t + 1) * lanes] = shift(clean, t)


def blend_weights(totals, count):
    lane = lane_of(totals.shape)
    block = reach * reach

    def pick(index):
        return jnp.sum(jnp.where(lane == index, totals, 0.0), axis=1, keepdims=True)

    ref_power = pick(count * block + count)
    weights = []
    for f in range(count):
        norm_product = jnp.sqrt((pick(count * block + f) + 1e-06) * (ref_power + 1e-06))
        member = (lane >= f * block) & (lane < (f + 1) * block)
        rho = jnp.where(member, totals, 0.0) / norm_product
        squared = rho * rho
        middle = jnp.where(lane == f * block + block // 2, 0.05, 0.0)
        weights.append((squared + middle) / (0.05 + jnp.sum(squared, axis=1, keepdims=True)))
    return weights


def banded(weights, f, rows, first_row, depth):
    wide = rows + 8
    blank = jnp.zeros((weights.shape[0], depth - lanes), jnp.float32)
    weights = jnp.concatenate([weights, blank], axis=1)
    lane = lane_of(weights.shape)
    line = jnp.zeros_like(weights)
    for j in range(reach):
        at = first_row + j * 2 * wide
        amount = at - (f * reach + j) * reach
        amount = jnp.where(amount < 0, amount + depth, amount)
        line = jnp.where((lane >= at) & (lane < at + reach), pltpu.roll(weights, amount, 1), line)
    line = line + pltpu.roll(line, wide, 1)
    return by_row_shift(jnp.broadcast_to(line[0:1], (rows, depth)), rows, 1)


def pressures(base, totals, clean, spread, inverse):
    count, rows, columns = inverse.shape
    depth = spread.shape[0]
    weights = blend_weights(jnp.broadcast_to(totals[0:1, :], (8, lanes)), count)
    bands = [banded(weights[f], f, rows, 1 + base[0, 0], depth) for f in range(count)]
    mixing = cut(jnp.concatenate(bands, axis=0))
    spread_columns(clean, spread, base[0, 1])

    def chunk_values(where):
        product = jnp.dot(mixing, spread[:, where], preferred_element_type=jnp.float32)
        registered = product[: count * rows] + product[count * rows :]
        values = []
        for f in range(count):
            ratio = registered[f * rows : (f + 1) * rows] * inverse[f, :, where]
            values.append(calib_zero + ratio * (calib_linear + calib_square * ratio))
        return values

    return chunk_values


def pressure_kernel(base, totals, clean, inverse, pressure, moments, part, spread):
    count, rows, columns = inverse.shape
    chunk_values = pressures(base, totals, clean, spread, inverse)

    def step(t, sums):
        where = chunk_of(t)
        values = chunk_values(where)
        squares = [value * value for value in values]
        for f in range(count):
            pressure[f, :, where] = values[f]
        moments[0, :, where] = sum(values[1:], values[0])
        moments[1, :, where] = sum(squares[1:], squares[0])
        result = []
        for total, array in zip(sums, values + squares):
            result.append(total + fold(array[:, :lanes]) + fold(array[:, lanes:]))
        return tuple(result)

    zero = jnp.zeros((8, lanes), jnp.float32)
    sums = by_tiles(step, columns // (2 * lanes), columns // (2 * lanes), (zero,) * (2 * count))
    line = zero
    for k in range(2 * count):
        value = jnp.sum(jnp.sum(sums[k], axis=0, keepdims=True), axis=1, keepdims=True)
        line = line + jnp.where(lane_of(line.shape) == k, value, 0.0)
    part[...] = jnp.broadcast_to(line[0:1], part.shape)


def time_kernel(base, totals, clean, inverse, moments, time_mean, time_rms, spread):
    count, rows, columns = inverse.shape
    chunk_values = pressures(base, totals, clean, spread, inverse)
    frames = 2 * count

    def step(t, carry):
        where = chunk_of(t)
        first = moments[0, :, where]
        second = moments[1, :, where]
        for value in chunk_values(where):
            first = first + value
            second = second + value * value
        mean = first * (1.0 / frames)
        time_mean[:, where] = mean
        time_rms[:, where] = jnp.sqrt(jnp.maximum(second * (1.0 / frames) - mean * mean, 0.0))
        return carry

    by_tiles(step, columns // (2 * lanes), columns // (2 * lanes))


def paired(value, axis, first):
    size = lax.axis_size(axis)
    partner = list(range(size))
    for i in range(first, size - 1, 2):
        partner[i], partner[i + 1] = i + 1, i
    return lax.ppermute(value, axis, list(enumerate(partner)))


def by_parity(odd, array, height, dim):
    length = array.shape[dim]
    low = lax.slice_in_dim(array, 0, height, axis=dim)
    high = lax.slice_in_dim(array, length - height, length, axis=dim)
    return jnp.where(odd, high, low), jnp.where(odd, low, high)


def from_owner(shard, here, odd, axis, root):
    mine = lax.axis_index(axis) == root
    height = shard.shape[0] // 2
    if lax.axis_size(axis) != 2:
        whole = lax.psum(jnp.where(mine, shard, jnp.zeros_like(shard)), axis)
        return by_parity(odd, whole, height, 0)
    there = by_parity(odd, paired(shard, axis, 0), height, 0)
    here = by_parity(odd, here, height, 0)
    return [jnp.where(mine, own, other) for own, other in zip(here, there)]


def total_over(value, axis):
    size = lax.axis_size(axis)
    if size & (size - 1):
        return lax.psum(value, axis)
    step = 1
    while step < size:
        value = value + lax.ppermute(value, axis, [(i, i ^ step) for i in range(size)])
        step *= 2
    return value


def shards(frames_raw, wind_off, run_owner, search_base):
    count, rows, columns = frames_raw.shape
    tiles = columns // lanes
    ring = tiles + 2
    wide = rows + 8
    depth = near * count * rows
    size = lax.axis_size("rows")
    f32 = jnp.float32
    bf16 = jnp.bfloat16
    struct = functools.partial(jax.ShapeDtypeStruct, dtype=f32)
    odd = lax.axis_index("rows") % 2 == 1
    raw, run = lax.optimization_barrier((jnp.maximum(frames_raw, 0.0), jnp.maximum(wind_off[0], 0.0)))
    owner, offsets = lax.optimization_barrier((run_owner, jnp.clip(search_base, -8, 8)))
    own_odd, own_even = from_owner(wind_off[0], run, odd, "frames", owner[0])
    from_odd = paired(own_odd, "rows", 1)
    from_even = paired(own_even, "rows", 0)
    frames_odd, frames_even = by_parity(odd, raw, 4, 1)
    frames_odd = paired(frames_odd, "rows", 1)
    frames_even = paired(frames_even, "rows", 0)
    frames_odd, own_odd = lax.optimization_barrier((frames_odd, own_odd))
    inverse, stack, power, band = pl.pallas_call(
        smooth_kernel,
        out_shape=(
            struct((count, rows, columns)),
            jax.ShapeDtypeStruct((2 * depth, ring * lanes), bf16),
            struct((8 * count, lanes)),
            jax.ShapeDtypeStruct((4 * lanes, 2 * lanes), bf16),
        ),
        in_specs=[vmem] * 3,
        out_specs=(vmem,) * 4,
        scratch_shapes=[
            pltpu.VMEM((count, tiles, rows + 16, lanes), f32),
            pltpu.VMEM((2 * count * rows, (tiles + 2) * lanes), bf16),
            pltpu.VMEM((ring + 2, 2 * count * rows, lanes), bf16),
        ],
        compiler_params=params,
        cost_estimate=cost(8),
        name="smooth",
    )(raw, frames_odd, frames_even)
    blocks = lax.axis_size("frames")
    peers = size * blocks if blocks == 2 else size
    if blocks == 2:
        other_inverse = paired(inverse, "frames", 0)
    clean, part = pl.pallas_call(
        match_kernel,
        out_shape=(jax.ShapeDtypeStruct((tiles + 2, 2 * wide, lanes), bf16), struct((peers, lanes))),
        in_specs=[smem] + [vmem] * 7,
        out_specs=(vmem, vmem),
        scratch_shapes=[
            pltpu.VMEM((tiles, rows + 16, lanes), f32),
            pltpu.VMEM((2 * wide, (tiles + 2) * lanes), bf16),
            pltpu.VMEM((ring + 2, 2 * wide, lanes), bf16),
            pltpu.VMEM((far * 2 * wide, ring * lanes), bf16),
            pltpu.VMEM((depth, lanes), f32),
            pltpu.VMEM((8 * count, lanes), f32),
        ],
        compiler_params=params,
        cost_estimate=cost(12),
        name="match",
    )(offsets, own_odd, own_even, from_odd, from_even, stack, power, band)
    if blocks == 2:
        parts = lax.all_to_all(part, ("rows", "frames"), 0, 0, tiled=True).reshape(size, blocks, lanes)
        mine = lax.axis_index("frames") == 0
        both = jnp.sum(parts, axis=0)
        totals = jnp.where(mine, both[0:1], both[1:2])
        row = jnp.where(mine, both[1:2], both[0:1])
        place = jnp.where(mine, parts[0, 1:2], parts[0, 0:1])[:, lanes - 2 :].astype(jnp.int32)
    else:
        totals = jnp.sum(lax.all_to_all(part, "rows", 0, 0, tiled=True), axis=0, keepdims=True)
    depth = -(-reach * 2 * wide // lanes) * lanes
    spread = pltpu.VMEM((depth, columns), bf16)
    pressure, moments, part = pl.pallas_call(
        pressure_kernel,
        out_shape=(struct((count, rows, columns)), struct((2, rows, columns)), struct((size, lanes))),
        in_specs=[smem] + [vmem] * 3,
        out_specs=(vmem, vmem, vmem),
        scratch_shapes=[spread],
        compiler_params=params,
        cost_estimate=cost(12),
        name="pressure",
    )(offsets, totals, clean, inverse)
    if blocks == 2:
        time_mean, time_rms = pl.pallas_call(
            time_kernel,
            out_shape=(struct((rows, columns)), struct((rows, columns))),
            in_specs=[smem] + [vmem] * 4,
            out_specs=(vmem, vmem),
            scratch_shapes=[spread],
            compiler_params=params,
            cost_estimate=cost(12),
            name="time",
        )(place, row, clean, other_inverse, moments)
    else:
        whole = total_over(moments, "frames")
        total_frames = count * blocks
        time_mean = whole[0] / total_frames
        time_rms = jnp.sqrt(jnp.maximum(whole[1] / total_frames - time_mean * time_mean, 0.0))
    sums = lax.all_to_all(part, "rows", 0, 0, tiled=True)
    sums, time_mean, time_rms = lax.optimization_barrier((sums, time_mean, time_rms))
    spatial = jnp.sum(sums, axis=0)
    cell_count = rows * columns * size
    frame_mean = spatial[:count] / cell_count
    frame_rms = jnp.sqrt(spatial[count : 2 * count] / cell_count - frame_mean * frame_mean)
    return (pressure, frame_mean, frame_rms, time_mean, time_rms)


def solution(mesh):
    placed = (P("frames", "rows", None), P("frames", "rows", None), P("rows"), P("frames", None))
    return jax.shard_map(
        shards,
        mesh=mesh,
        in_specs=placed,
        out_specs=(
            P("frames", "rows", None),
            P("frames"),
            P("frames"),
            P("rows", None),
            P("rows", None),
        ),
        check_vma=False,
    )
```

```python
import functools

import jax
import jax.numpy as jnp
from jax import lax
from jax.experimental import pallas as pl
from jax.experimental.pallas import tpu as pltpu
from jax.sharding import PartitionSpec as P

taps = (1.0 / 256, 8.0 / 256, 28.0 / 256, 56.0 / 256, 70.0 / 256)
calib_zero = -0.25
calib_linear = 1.0
calib_square = 0.15
lanes = 128
reach = 7
near = 4
far = 2
params = pltpu.CompilerParams(vmem_limit_bytes=14 * 1024 * 1024)
vmem = pl.BlockSpec(memory_space=pltpu.VMEM)
smem = pl.BlockSpec(memory_space=pltpu.SMEM)


def cost(mebibytes):
    return pl.CostEstimate(flops=0, bytes_accessed=mebibytes * 2**20, transcendentals=0)


def tile_of(index):
    if isinstance(index, int):
        return slice(index * lanes, (index + 1) * lanes)
    return pl.ds(pl.multiple_of(index * lanes, lanes), lanes)


def by_tiles(step, tiles, group, init=()):
    if group == tiles:
        for index in range(tiles):
            init = step(index, init)
        return init

    def body(index, carry):
        for inner in range(group):
            carry = step(index * group + inner, carry)
        return carry

    return lax.fori_loop(0, tiles // group, body, init)


def lane_of(shape):
    return lax.broadcasted_iota(jnp.int32, shape, len(shape) - 1)


def fold(product):
    return jnp.sum(product.reshape(product.shape[0] // 8, 8, lanes), axis=0)


def vertical(load):
    total = taps[4] * load(4)
    for step in range(4):
        total = total + taps[step] * (load(step) + load(8 - step))
    return total


def moved(before, here, after, step):
    if step > 0:
        return pltpu.roll(jnp.where(lane_of(here.shape) < step, after, here), lanes - step, 1)
    if step < 0:
        return pltpu.roll(jnp.where(lane_of(here.shape) >= lanes + step, before, here), -step, 1)
    return here


def halves(value):
    high = value.astype(jnp.bfloat16)
    low = (value - high.astype(jnp.float32)).astype(jnp.bfloat16)
    return high, low


def cut(value):
    return jnp.concatenate(halves(value), axis=0)


def fill_band(band):
    shape = (lanes, lanes)
    apart = lax.broadcasted_iota(jnp.int32, shape, 0) - lax.broadcasted_iota(jnp.int32, shape, 1)

    def block(offset):
        distance = jnp.abs(apart + offset)
        value = jnp.zeros(shape, jnp.float32)
        for step in range(5):
            value = jnp.where(distance == step, taps[4 - step], value)
        return value.astype(jnp.bfloat16)

    none = jnp.zeros(shape, jnp.bfloat16)
    before, here, after = block(-lanes), block(0), block(lanes)
    for index, pair in enumerate(((before, none), (here, before), (after, here), (none, after))):
        band[index * lanes : (index + 1) * lanes, :] = jnp.concatenate(pair, axis=1)


def chunk_of(t):
    if isinstance(t, int):
        return slice(t * 2 * lanes, (t + 1) * 2 * lanes)
    return pl.ds(pl.multiple_of(t * 2 * lanes, 2 * lanes), 2 * lanes)


def horizontal(wide, band, t):
    window = wide[:, t * 2 * lanes : (t + 2) * 2 * lanes]
    product = jnp.dot(window, band[...], preferred_element_type=jnp.float32)
    half = product.shape[0] // 2
    return product[:half] + product[half:]


def by_row_shift(value, rows, direction):
    place = lax.broadcasted_iota(jnp.int32, value.shape, 0) % rows
    unit = 1
    while unit < rows:
        digit = (place // unit) % 4
        result = value
        for times in range(1, 4):
            amount = times * unit
            turned = pltpu.roll(value, amount if direction > 0 else value.shape[1] - amount, 1)
            result = jnp.where(digit == times, turned, result)
        value = result
        unit *= 4
    return value


def at_edge():
    index = lax.axis_index("rows")
    return (index == 0) | (index == lax.axis_size("rows") - 1)


def smooth_kernel(frames, from_odd, from_even, inverse, stack, power, band, rows_in, wide, pieces):
    count, rows, columns = frames.shape
    tiles = columns // lanes
    ring = tiles + 2
    odd = lax.axis_index("rows") % 2 == 1
    edge = at_edge()
    blank = jnp.zeros((2 * count * rows, lanes), jnp.bfloat16)
    wide[:, tile_of(0)] = blank
    wide[:, tile_of(tiles + 1)] = blank
    fill_band(band)
    pieces[0] = blank
    pieces[tiles + 1] = blank
    pieces[tiles + 2] = blank

    def load_step(t, carry):
        for f in range(count):
            outer = jnp.where(edge, 0.0, from_odd[f, :, tile_of(t)])
            inner = from_even[f, :, tile_of(t)]
            rows_in[f, t, 4:8, :] = jnp.where(odd, inner, outer)
            rows_in[f, t, 8 : 8 + rows, :] = frames[f, :, tile_of(t)]
            rows_in[f, t, 8 + rows : 12 + rows, :] = jnp.where(odd, outer, inner)
        return carry

    def vertical_step(t, carry):
        parts = [vertical(lambda s: rows_in[f, t, pl.ds(4 + s, rows), :]) for f in range(count)]
        wide[:, tile_of(t + 1)] = cut(jnp.concatenate(parts, axis=0))
        return carry

    def horizontal_step(t, totals):
        smooth = horizontal(wide, band, t)
        result = []
        details = []
        for f in range(count):
            part = smooth[f * rows : (f + 1) * rows]
            inverse[f, :, chunk_of(t)] = 1.0 / part
            details.append(frames[f, :, chunk_of(t)] - part)
            square = details[f] * details[f]
            result.append(totals[f] + fold(square[:, :lanes]) + fold(square[:, lanes:]))
        detail = cut(jnp.concatenate(details, axis=0))
        pieces[2 * t + 1] = detail[:, :lanes]
        pieces[2 * t + 2] = detail[:, lanes:]
        return tuple(result)

    def stack_step(t, carry):
        before, here, after = pieces[t], pieces[t + 1], pieces[t + 2]
        size = count * rows
        for a in range(near):
            turned = moved(before, here, after, 1 - a)
            stack[a * size : (a + 1) * size, tile_of(t)] = turned[:size]
            stack[(near + a) * size : (near + a + 1) * size, tile_of(t)] = turned[size:]
        return carry

    powers = (jnp.zeros((8, lanes), jnp.float32),) * count
    for t in range(tiles + 1):
        if t < tiles:
            load_step(t, 0)
            vertical_step(t, 0)
        if t % 2 == 0 and t > 0:
            powers = horizontal_step(t // 2 - 1, powers)
    for f in range(count):
        power[f * 8 : f * 8 + 8, :] = powers[f]
    pieces[tiles + 3] = pieces[1]
    by_tiles(stack_step, ring, ring)


def column_shift(offset):
    negative = offset < 0
    first = jnp.where(negative, 0, 1)
    amount = jnp.where(negative, offset + lanes, offset)
    back = (lanes - amount) & (lanes - 1)

    def shift(source, t):
        here = source[t + first]
        after = source[t + first + 1]
        return pltpu.roll(jnp.where(lane_of(here.shape) < amount, after, here), back, 1)

    return shift


def match_kernel(
    base, own_odd, own_even, from_odd, from_even, stack, power, band, clean, part, rows_in, padded, fine, stream, folded, lags
):
    rows = own_odd.shape[0] * 2
    tiles = own_odd.shape[1] // lanes
    count = power.shape[0] // 8
    ring = tiles + 2
    wide = rows + 8
    row_index = lax.axis_index("rows")
    last_row = lax.axis_size("rows") - 1
    odd = row_index % 2 == 1
    edge = at_edge()
    empty = jnp.zeros((2 * wide, lanes), jnp.bfloat16)
    padded[:, tile_of(0)] = empty
    padded[:, tile_of(tiles + 1)] = empty
    for array in (clean, fine):
        array[0] = empty
        array[tiles + 1] = empty
    fine[tiles + 2] = empty
    place = lax.broadcasted_iota(jnp.int32, (wide, 2 * lanes), 0)
    own = (place >= 4) & (place < rows + 4)
    inside = ((place >= 4) | (row_index > 0)) & ((place < rows + 4) | (row_index < last_row))

    def load_step(t, carry):
        outer = [jnp.where(edge, 0.0, from_odd[:, tile_of(t)]), own_odd[:, tile_of(t)]]
        inner = [array[:, tile_of(t)] for array in (own_even, from_even)]
        rows_in[t, 0:8, :] = jnp.where(odd, inner[1], outer[0])
        rows_in[t, 8:16, :] = jnp.where(odd, inner[0], outer[1])
        rows_in[t, 16:24, :] = jnp.where(odd, outer[1], inner[0])
        rows_in[t, 24:32, :] = jnp.where(odd, outer[0], inner[1])
        return carry

    def vertical_step(t, carry):
        padded[:, tile_of(t + 1)] = cut(vertical(lambda s: rows_in[t, pl.ds(s, wide), :]))
        return carry

    def horizontal_step(t, total):
        smooth = jnp.where(inside, horizontal(padded, band, t), 0.0)
        raw = [rows_in[2 * t + c, pl.ds(4, wide), :] for c in range(2)]
        detail = jnp.concatenate(raw, axis=1) - smooth
        square = jnp.where(own, detail * detail, 0.0)
        for array, value in ((clean, cut(smooth)), (fine, cut(detail))):
            array[2 * t + 1] = value[:, :lanes]
            array[2 * t + 2] = value[:, lanes:]
        return total + fold(square[:, :lanes]) + fold(square[:, lanes:])

    ref_power = jnp.zeros((8, lanes), jnp.float32)
    for t in range(tiles + 1):
        if t < tiles:
            load_step(t, 0)
            vertical_step(t, 0)
        if t % 2 == 0 and t > 0:
            ref_power = horizontal_step(t // 2 - 1, ref_power)
    fine[tiles + 3] = fine[1]
    shifts = [column_shift(base[0, 1] + near * b - 2) for b in range(far)]

    def stream_step(t, carry):
        for b, shift in enumerate(shifts):
            stream[b * 2 * wide : (b + 1) * 2 * wide, tile_of(t)] = shift(fine, t)
        return carry

    by_tiles(stream_step, ring, ring)
    product = None
    for half in range(2):
        at = slice(half * ring * lanes // 2, (half + 1) * ring * lanes // 2)
        term = lax.dot_general(
            stack[:, at], stream[:, at], (((1,), (1,)), ((), ())), preferred_element_type=jnp.float32
        )
        product = term if product is None else product + term
    size = near * count * rows
    folded[...] = jnp.zeros(folded.shape, jnp.float32)
    folded[:, 0 : far * 2 * wide] = product[:size] + product[size:]
    product = by_row_shift(folded[...], rows, -1)
    lags[...] = jnp.zeros(lags.shape, jnp.float32)
    for a in range(near):
        for f in range(count):
            start = (a * count + f) * rows
            lags[f * 8 + a : f * 8 + a + 1, :] = jnp.sum(product[start : start + rows], axis=0, keepdims=True)
    back = 4 * lanes - 1 - base[0, 0]
    across = lax.broadcasted_iota(jnp.int32, (8, lanes), 0)
    lane = lane_of((8, lanes))
    packed = jnp.zeros((8, lanes), jnp.float32)
    for f in range(count):
        block = lags[f * 8 : f * 8 + 8, :]
        for j in range(reach):
            at = (f * reach + j) * reach
            there = back + at - (j // near) * 2 * wide
            high = pltpu.roll(block, there & (lanes - 1), 1)
            low = pltpu.roll(block, (there - wide) & (lanes - 1), 1)
            member = (across == j % near) & (lane >= at) & (lane < at + reach)
            packed = packed + jnp.where(member, high + low, 0.0)
    lags[0:8, :] = jnp.zeros((8, lanes), jnp.float32)
    for f in range(count):
        lags[f : f + 1, :] = jnp.sum(power[f * 8 : f * 8 + 8, :], axis=0, keepdims=True)
    lags[count : count + 1, :] = jnp.sum(ref_power, axis=0, keepdims=True)
    powers = jnp.sum(lags[0:8, :], axis=1, keepdims=True)
    packed = packed + jnp.where(lane == count * reach * reach + across, powers, 0.0)
    packed = jnp.sum(packed, axis=0, keepdims=True)
    for place in range(2):
        offset = base[0, place].astype(jnp.float32)
        packed = jnp.where(lane[0:1] == lanes - 2 + place, offset, packed)
    part[...] = jnp.broadcast_to(packed, part.shape)


def spreader(clean, spread, base_col):
    size = clean.shape[1]
    spare = spread.shape[0] - reach * size
    shifts = [column_shift(base_col + j - 3) for j in range(reach)]

    def spread_tile(t):
        at = tile_of(t)
        for j, shift in enumerate(shifts):
            spread[j * size : (j + 1) * size, at] = shift(clean, t)
        spread[reach * size :, at] = jnp.zeros((spare, lanes), jnp.bfloat16)

    return spread_tile


def blend_weights(totals, count):
    lane = lane_of(totals.shape)
    block = reach * reach

    def pick(index):
        return jnp.sum(jnp.where(lane == index, totals, 0.0), axis=1, keepdims=True)

    ref_power = pick(count * block + count)
    weights = []
    for f in range(count):
        norm_product = jnp.sqrt((pick(count * block + f) + 1e-06) * (ref_power + 1e-06))
        member = (lane >= f * block) & (lane < (f + 1) * block)
        rho = jnp.where(member, totals, 0.0) / norm_product
        squared = rho * rho
        middle = jnp.where(lane == f * block + block // 2, 0.05, 0.0)
        weights.append((squared + middle) / (0.05 + jnp.sum(squared, axis=1, keepdims=True)))
    return weights


def banded(weights, f, rows, first_row, depth):
    wide = rows + 8
    blank = jnp.zeros((weights.shape[0], depth - lanes), jnp.float32)
    weights = jnp.concatenate([weights, blank], axis=1)
    lane = lane_of(weights.shape)
    line = jnp.zeros_like(weights)
    for j in range(reach):
        at = first_row + j * 2 * wide
        amount = at - (f * reach + j) * reach
        amount = jnp.where(amount < 0, amount + depth, amount)
        line = jnp.where((lane >= at) & (lane < at + reach), pltpu.roll(weights, amount, 1), line)
    line = line + pltpu.roll(line, wide, 1)
    return by_row_shift(jnp.broadcast_to(line[0:1], (rows, depth)), rows, 1)


def pressures(base, totals, clean, spread, inverse):
    count, rows, columns = inverse.shape
    depth = spread.shape[0]
    weights = blend_weights(jnp.broadcast_to(totals[0:1, :], (8, lanes)), count)
    bands = [banded(weights[f], f, rows, 1 + base[0, 0], depth) for f in range(count)]
    mixing = cut(jnp.concatenate(bands, axis=0))
    spread_tile = spreader(clean, spread, base[0, 1])

    def chunk_values(t):
        where = chunk_of(t)
        spread_tile(2 * t)
        spread_tile(2 * t + 1)
        product = jnp.dot(mixing, spread[:, where], preferred_element_type=jnp.float32)
        registered = product[: count * rows] + product[count * rows :]
        values = []
        for f in range(count):
            ratio = registered[f * rows : (f + 1) * rows] * inverse[f, :, where]
            values.append(calib_zero + ratio * (calib_linear + calib_square * ratio))
        return values

    return chunk_values


def pressure_kernel(base, totals, clean, inverse, pressure, moments, part, spread):
    count, rows, columns = inverse.shape
    chunk_values = pressures(base, totals, clean, spread, inverse)

    def step(t, sums):
        where = chunk_of(t)
        values = chunk_values(t)
        squares = [value * value for value in values]
        for f in range(count):
            pressure[f, :, where] = values[f]
        moments[0, :, where] = sum(values[1:], values[0])
        moments[1, :, where] = sum(squares[1:], squares[0])
        result = []
        for total, array in zip(sums, values + squares):
            result.append(total + fold(array[:, :lanes]) + fold(array[:, lanes:]))
        return tuple(result)

    zero = jnp.zeros((8, lanes), jnp.float32)
    sums = by_tiles(step, columns // (2 * lanes), columns // (2 * lanes), (zero,) * (2 * count))
    line = zero
    for k in range(2 * count):
        value = jnp.sum(jnp.sum(sums[k], axis=0, keepdims=True), axis=1, keepdims=True)
        line = line + jnp.where(lane_of(line.shape) == k, value, 0.0)
    part[...] = jnp.broadcast_to(line[0:1], part.shape)


def time_kernel(base, totals, clean, inverse, moments, time_mean, time_rms, spread):
    count, rows, columns = inverse.shape
    chunk_values = pressures(base, totals, clean, spread, inverse)
    frames = 2 * count

    def step(t, carry):
        where = chunk_of(t)
        first = moments[0, :, where]
        second = moments[1, :, where]
        for value in chunk_values(t):
            first = first + value
            second = second + value * value
        mean = first * (1.0 / frames)
        time_mean[:, where] = mean
        time_rms[:, where] = jnp.sqrt(jnp.maximum(second * (1.0 / frames) - mean * mean, 0.0))
        return carry

    by_tiles(step, columns // (2 * lanes), columns // (2 * lanes))


def paired(value, axis, first):
    size = lax.axis_size(axis)
    partner = list(range(size))
    for i in range(first, size - 1, 2):
        partner[i], partner[i + 1] = i + 1, i
    return lax.ppermute(value, axis, list(enumerate(partner)))


def by_parity(odd, array, height, dim):
    length = array.shape[dim]
    low = lax.slice_in_dim(array, 0, height, axis=dim)
    high = lax.slice_in_dim(array, length - height, length, axis=dim)
    return jnp.where(odd, high, low), jnp.where(odd, low, high)


def from_owner(shard, here, odd, axis, root):
    mine = lax.axis_index(axis) == root
    height = shard.shape[0] // 2
    if lax.axis_size(axis) != 2:
        whole = lax.psum(jnp.where(mine, shard, jnp.zeros_like(shard)), axis)
        return by_parity(odd, whole, height, 0)
    there = by_parity(odd, paired(shard, axis, 0), height, 0)
    here = by_parity(odd, here, height, 0)
    return [jnp.where(mine, own, other) for own, other in zip(here, there)]


def total_over(value, axis):
    size = lax.axis_size(axis)
    if size & (size - 1):
        return lax.psum(value, axis)
    step = 1
    while step < size:
        value = value + lax.ppermute(value, axis, [(i, i ^ step) for i in range(size)])
        step *= 2
    return value


def shards(frames_raw, wind_off, run_owner, search_base):
    count, rows, columns = frames_raw.shape
    tiles = columns // lanes
    ring = tiles + 2
    wide = rows + 8
    depth = near * count * rows
    size = lax.axis_size("rows")
    f32 = jnp.float32
    bf16 = jnp.bfloat16
    struct = functools.partial(jax.ShapeDtypeStruct, dtype=f32)
    odd = lax.axis_index("rows") % 2 == 1
    raw, run = lax.optimization_barrier((jnp.maximum(frames_raw, 0.0), jnp.maximum(wind_off[0], 0.0)))
    owner, offsets = lax.optimization_barrier((run_owner, jnp.clip(search_base, -8, 8)))
    own_odd, own_even = from_owner(wind_off[0], run, odd, "frames", owner[0])
    from_odd = paired(own_odd, "rows", 1)
    from_even = paired(own_even, "rows", 0)
    frames_odd, frames_even = by_parity(odd, raw, 4, 1)
    frames_odd = paired(frames_odd, "rows", 1)
    frames_even = paired(frames_even, "rows", 0)
    frames_odd, own_odd = lax.optimization_barrier((frames_odd, own_odd))
    inverse, stack, power, band = pl.pallas_call(
        smooth_kernel,
        out_shape=(
            struct((count, rows, columns)),
            jax.ShapeDtypeStruct((2 * depth, ring * lanes), bf16),
            struct((8 * count, lanes)),
            jax.ShapeDtypeStruct((4 * lanes, 2 * lanes), bf16),
        ),
        in_specs=[vmem] * 3,
        out_specs=(vmem,) * 4,
        scratch_shapes=[
            pltpu.VMEM((count, tiles, rows + 16, lanes), f32),
            pltpu.VMEM((2 * count * rows, (tiles + 2) * lanes), bf16),
            pltpu.VMEM((ring + 2, 2 * count * rows, lanes), bf16),
        ],
        compiler_params=params,
        cost_estimate=cost(8),
        name="smooth",
    )(raw, frames_odd, frames_even)
    blocks = lax.axis_size("frames")
    peers = size * blocks if blocks == 2 else size
    if blocks == 2:
        other_inverse = paired(inverse, "frames", 0)
    clean, part = pl.pallas_call(
        match_kernel,
        out_shape=(jax.ShapeDtypeStruct((tiles + 2, 2 * wide, lanes), bf16), struct((peers, lanes))),
        in_specs=[smem] + [vmem] * 7,
        out_specs=(vmem, vmem),
        scratch_shapes=[
            pltpu.VMEM((tiles, rows + 16, lanes), f32),
            pltpu.VMEM((2 * wide, (tiles + 2) * lanes), bf16),
            pltpu.VMEM((ring + 2, 2 * wide, lanes), bf16),
            pltpu.VMEM((far * 2 * wide, ring * lanes), bf16),
            pltpu.VMEM((depth, lanes), f32),
            pltpu.VMEM((8 * count, lanes), f32),
        ],
        compiler_params=params,
        cost_estimate=cost(12),
        name="match",
    )(offsets, own_odd, own_even, from_odd, from_even, stack, power, band)
    if blocks == 2:
        parts = lax.all_to_all(part, ("rows", "frames"), 0, 0, tiled=True).reshape(size, blocks, lanes)
        mine = lax.axis_index("frames") == 0
        both = jnp.sum(parts, axis=0)
        totals = jnp.where(mine, both[0:1], both[1:2])
        row = jnp.where(mine, both[1:2], both[0:1])
        place = jnp.where(mine, parts[0, 1:2], parts[0, 0:1])[:, lanes - 2 :].astype(jnp.int32)
    else:
        totals = jnp.sum(lax.all_to_all(part, "rows", 0, 0, tiled=True), axis=0, keepdims=True)
    depth = -(-reach * 2 * wide // lanes) * lanes
    spread = pltpu.VMEM((depth, columns), bf16)
    pressure, moments, part = pl.pallas_call(
        pressure_kernel,
        out_shape=(struct((count, rows, columns)), struct((2, rows, columns)), struct((size, lanes))),
        in_specs=[smem] + [vmem] * 3,
        out_specs=(vmem, vmem, vmem),
        scratch_shapes=[spread],
        compiler_params=params,
        cost_estimate=cost(12),
        name="pressure",
    )(offsets, totals, clean, inverse)
    if blocks == 2:
        time_mean, time_rms = pl.pallas_call(
            time_kernel,
            out_shape=(struct((rows, columns)), struct((rows, columns))),
            in_specs=[smem] + [vmem] * 4,
            out_specs=(vmem, vmem),
            scratch_shapes=[spread],
            compiler_params=params,
            cost_estimate=cost(12),
            name="time",
        )(place, row, clean, other_inverse, moments)
    else:
        whole = total_over(moments, "frames")
        total_frames = count * blocks
        time_mean = whole[0] / total_frames
        time_rms = jnp.sqrt(jnp.maximum(whole[1] / total_frames - time_mean * time_mean, 0.0))
    sums = lax.all_to_all(part, "rows", 0, 0, tiled=True)
    sums, time_mean, time_rms = lax.optimization_barrier((sums, time_mean, time_rms))
    spatial = jnp.sum(sums, axis=0)
    cell_count = rows * columns * size
    frame_mean = spatial[:count] / cell_count
    frame_rms = jnp.sqrt(spatial[count : 2 * count] / cell_count - frame_mean * frame_mean)
    return (pressure, frame_mean, frame_rms, time_mean, time_rms)


def solution(mesh):
    placed = (P("frames", "rows", None), P("frames", "rows", None), P("rows"), P("frames", None))
    return jax.shard_map(
        shards,
        mesh=mesh,
        in_specs=placed,
        out_specs=(
            P("frames", "rows", None),
            P("frames"),
            P("frames"),
            P("rows", None),
            P("rows", None),
        ),
        check_vma=False,
    )
```

```python
import functools

import jax
import jax.numpy as jnp
from jax import lax
from jax.experimental import pallas as pl
from jax.experimental.pallas import tpu as pltpu
from jax.sharding import PartitionSpec as P

taps = (1.0 / 256, 8.0 / 256, 28.0 / 256, 56.0 / 256, 70.0 / 256)
calib_zero = -0.25
calib_linear = 1.0
calib_square = 0.15
lanes = 128
reach = 7
near = 4
far = 2
slot = 32
params = pltpu.CompilerParams(vmem_limit_bytes=14 * 1024 * 1024)
vmem = pl.BlockSpec(memory_space=pltpu.VMEM)
smem = pl.BlockSpec(memory_space=pltpu.SMEM)


def cost(mebibytes):
    return pl.CostEstimate(flops=0, bytes_accessed=mebibytes * 2**20, transcendentals=0)


def tile_of(index):
    if isinstance(index, int):
        return slice(index * lanes, (index + 1) * lanes)
    return pl.ds(pl.multiple_of(index * lanes, lanes), lanes)


def by_tiles(step, tiles, group, init=()):
    if group == tiles:
        for index in range(tiles):
            init = step(index, init)
        return init

    def body(index, carry):
        for inner in range(group):
            carry = step(index * group + inner, carry)
        return carry

    return lax.fori_loop(0, tiles // group, body, init)


def lane_of(shape):
    return lax.broadcasted_iota(jnp.int32, shape, len(shape) - 1)


def fold(product):
    return jnp.sum(product.reshape(product.shape[0] // 8, 8, lanes), axis=0)


def vertical(load):
    total = taps[4] * load(4)
    for step in range(4):
        total = total + taps[step] * (load(step) + load(8 - step))
    return total


def moved(before, here, after, step):
    if step > 0:
        return pltpu.roll(jnp.where(lane_of(here.shape) < step, after, here), lanes - step, 1)
    if step < 0:
        return pltpu.roll(jnp.where(lane_of(here.shape) >= lanes + step, before, here), -step, 1)
    return here


def halves(value):
    high = value.astype(jnp.bfloat16)
    low = (value - high.astype(jnp.float32)).astype(jnp.bfloat16)
    return high, low


def cut(value):
    return jnp.concatenate(halves(value), axis=0)


def fill_band(band):
    shape = (lanes, lanes)
    apart = lax.broadcasted_iota(jnp.int32, shape, 0) - lax.broadcasted_iota(jnp.int32, shape, 1)

    def block(offset):
        distance = jnp.abs(apart + offset)
        value = jnp.zeros(shape, jnp.float32)
        for step in range(5):
            value = jnp.where(distance == step, taps[4 - step], value)
        return value.astype(jnp.bfloat16)

    none = jnp.zeros(shape, jnp.bfloat16)
    before, here, after = block(-lanes), block(0), block(lanes)
    for index, pair in enumerate(((before, none), (here, before), (after, here), (none, after))):
        band[index * lanes : (index + 1) * lanes, :] = jnp.concatenate(pair, axis=1)


def chunk_of(t):
    if isinstance(t, int):
        return slice(t * 2 * lanes, (t + 1) * 2 * lanes)
    return pl.ds(pl.multiple_of(t * 2 * lanes, 2 * lanes), 2 * lanes)


def place_tile(windows, index, value):
    for c in (index // 2 - 1, index // 2):
        at = index - 2 * c
        if 0 <= c < windows.shape[0] and at < 4:
            windows[c, :, at * lanes : (at + 1) * lanes] = value


def horizontal(windows, band):
    chunks, height, width = windows.shape
    product = jnp.dot(
        windows[...].reshape(chunks * height, width), band[...], preferred_element_type=jnp.float32
    )
    product = product.reshape(chunks, height, 2 * lanes)
    return product[:, : height // 2] + product[:, height // 2 :]


def by_row_shift(value, rows, direction):
    place = lax.broadcasted_iota(jnp.int32, value.shape, 0) % rows
    unit = 1
    while unit < rows:
        digit = (place // unit) % 4
        result = value
        for times in range(1, 4):
            amount = times * unit
            turned = pltpu.roll(value, amount if direction > 0 else value.shape[1] - amount, 1)
            result = jnp.where(digit == times, turned, result)
        value = result
        unit *= 4
    return value


def at_edge():
    index = lax.axis_index("rows")
    return (index == 0) | (index == lax.axis_size("rows") - 1)


def smooth_kernel(frames, from_odd, from_even, inverse, stack, power, band, rows_in, wide, pieces):
    count, rows, columns = frames.shape
    tiles = columns // lanes
    ring = tiles + 2
    odd = lax.axis_index("rows") % 2 == 1
    edge = at_edge()
    blank = jnp.zeros((2 * count * rows, lanes), jnp.bfloat16)
    place_tile(wide, 0, blank)
    place_tile(wide, tiles + 1, blank)
    fill_band(band)
    pieces[0] = blank
    pieces[tiles + 1] = blank
    pieces[tiles + 2] = blank

    def load_step(t, carry):
        for f in range(count):
            outer = jnp.where(edge, 0.0, from_odd[f, :, tile_of(t)])
            inner = from_even[f, :, tile_of(t)]
            rows_in[f, t, 4:8, :] = jnp.where(odd, inner, outer)
            rows_in[f, t, 8 : 8 + rows, :] = frames[f, :, tile_of(t)]
            rows_in[f, t, 8 + rows : 12 + rows, :] = jnp.where(odd, outer, inner)
        return carry

    def vertical_step(t, carry):
        parts = [vertical(lambda s: rows_in[f, t, pl.ds(4 + s, rows), :]) for f in range(count)]
        place_tile(wide, t + 1, cut(jnp.concatenate(parts, axis=0)))
        return carry

    def horizontal_step(t, totals):
        smooth = smoothed[t]
        result = []
        details = []
        for f in range(count):
            part = smooth[f * rows : (f + 1) * rows]
            inverse[f, :, chunk_of(t)] = 1.0 / part
            details.append(frames[f, :, chunk_of(t)] - part)
            square = details[f] * details[f]
            result.append(totals[f] + fold(square[:, :lanes]) + fold(square[:, lanes:]))
        detail = cut(jnp.concatenate(details, axis=0))
        pieces[2 * t + 1] = detail[:, :lanes]
        pieces[2 * t + 2] = detail[:, lanes:]
        return tuple(result)

    def stack_step(t, carry):
        before, here, after = pieces[t], pieces[t + 1], pieces[t + 2]
        size = count * rows
        for a in range(near):
            turned = moved(before, here, after, 1 - a)
            stack[a * size : (a + 1) * size, tile_of(t)] = turned[:size]
            stack[(near + a) * size : (near + a + 1) * size, tile_of(t)] = turned[size:]
        return carry

    powers = (jnp.zeros((8, lanes), jnp.float32),) * count
    for t in range(tiles):
        load_step(t, 0)
        vertical_step(t, 0)
    smoothed = horizontal(wide, band)
    for t in range(tiles // 2):
        powers = horizontal_step(t, powers)
    for f in range(count):
        power[f * 8 : f * 8 + 8, :] = powers[f]
    pieces[tiles + 3] = pieces[1]
    by_tiles(stack_step, ring, ring)


def column_shift(offset):
    negative = offset < 0
    first = jnp.where(negative, 0, 1)
    amount = jnp.where(negative, offset + lanes, offset)
    back = (lanes - amount) & (lanes - 1)

    def shift(source, t):
        here = source[t + first]
        after = source[t + first + 1]
        return pltpu.roll(jnp.where(lane_of(here.shape) < amount, after, here), back, 1)

    return shift


def reference_rows(raw, smooth, clean, fine, tiles):
    height = clean.shape[1] // 2
    empty = jnp.zeros((2 * height, lanes), jnp.bfloat16)
    for array in (clean, fine):
        array[0] = empty
        array[tiles + 1] = empty
    fine[tiles + 2] = empty
    squares = []
    for t in range(tiles // 2):
        detail = jnp.concatenate([raw(2 * t), raw(2 * t + 1)], axis=1) - smooth(t)
        for array, value in ((clean, cut(smooth(t))), (fine, cut(detail))):
            array[2 * t + 1] = value[:, :lanes]
            array[2 * t + 2] = value[:, lanes:]
        squares.append(detail * detail)
    fine[tiles + 3] = fine[1]
    return squares


def lag_products(stack, fine, stream, folded, base_col, start):
    height = fine.shape[1]
    half = height // 2
    shifts = [column_shift(base_col + near * b - 2) for b in range(far)]
    for t in range(fine.shape[0] - 2):
        for b, shift in enumerate(shifts):
            stream[b * height : (b + 1) * height, tile_of(t)] = shift(fine, t)
    product = lax.dot_general(
        stack[...], stream[...], (((1,), (1,)), ((), ())), preferred_element_type=jnp.float32
    )
    size = product.shape[0] // 2
    folded[...] = jnp.zeros(folded.shape, jnp.float32)
    folded[:, 0 : far * height] = product[:size] + product[size:]
    product = folded[...]
    lane = lane_of(product.shape)
    placed = jnp.zeros_like(product)
    for s in range(2 * far):
        at = s * slot + start
        turned = pltpu.roll(product, at - s * half, 1)
        placed = jnp.where((lane >= at) & (lane < at + half), turned, placed)
    return placed


def near_kernel(
    base, own_odd, own_even, from_even, stack, band, clean, lags, power, rows_in, windows, fine, stream, folded
):
    tiles = own_odd.shape[1] // lanes
    odd = lax.axis_index("rows") % 2 == 1
    height = clean.shape[1] // 2
    empty = jnp.zeros((2 * height, lanes), jnp.bfloat16)
    place_tile(windows, 0, empty)
    place_tile(windows, tiles + 1, empty)
    for t in range(tiles):
        at = tile_of(t)
        outer = own_odd[:, at]
        inner = from_even[:, at]
        rows_in[t, 0:8, :] = jnp.where(odd, inner, outer)
        rows_in[t, 8:16, :] = own_even[:, at]
        rows_in[t, 16:24, :] = jnp.where(odd, outer, inner)
        place_tile(windows, t + 1, cut(vertical(lambda s: rows_in[t, pl.ds(s, height), :])))
    smooth = horizontal(windows, band)
    squares = reference_rows(lambda t: rows_in[t, pl.ds(4, height), :], lambda t: smooth[t], clean, fine, tiles)
    place = lax.broadcasted_iota(jnp.int32, squares[0].shape, 0)
    first = jnp.where(odd, 4, 0)
    own = (place >= first) & (place < first + height - 4)
    total = jnp.zeros((8, lanes), jnp.float32)
    for square in squares:
        square = jnp.where(own, square, 0.0)
        total = total + fold(square[:, :lanes]) + fold(square[:, lanes:])
    power[...] = total
    lags[...] = lag_products(stack, fine, stream, folded, base[0, 1], jnp.where(odd, 0, 8))


def match_kernel(
    base, own_odd, from_odd, near_lags, near_power, stack, power, band, clean, part, rows_in, windows, fine, stream, folded, lags
):
    tiles = own_odd.shape[1] // lanes
    count = power.shape[0] // 8
    rows = folded.shape[0] // (near * count)
    odd = lax.axis_index("rows") % 2 == 1
    edge = at_edge()
    height = clean.shape[1] // 2
    empty = jnp.zeros((2 * height, lanes), jnp.bfloat16)
    place_tile(windows, 0, empty)
    place_tile(windows, tiles + 1, empty)
    for t in range(tiles):
        at = tile_of(t)
        outer = jnp.where(edge, 0.0, from_odd[:, at])
        inner = own_odd[:, at]
        rows_in[t, 0:8, :] = jnp.where(odd, inner, outer)
        rows_in[t, 8:16, :] = jnp.where(odd, outer, inner)
        place_tile(windows, t + 1, cut(vertical(lambda s: rows_in[t, pl.ds(s, height), :])))
    smooth = horizontal(windows, band)
    place = lax.broadcasted_iota(jnp.int32, (height, 2 * lanes), 0)
    first = jnp.where(odd, 0, 4)
    own = (place >= first) & (place < first + 4)
    inside = (place >= jnp.where(edge, first, 0)) & (place < jnp.where(edge, first + 4, height))

    def masked(t):
        return jnp.where(inside, smooth[t], 0.0)

    squares = reference_rows(lambda t: rows_in[t, pl.ds(4, height), :], masked, clean, fine, tiles)
    ref_power = near_power[...]
    for square in squares:
        square = jnp.where(own, square, 0.0)
        ref_power = ref_power + fold(square[:, :lanes]) + fold(square[:, lanes:])
    product = lag_products(stack, fine, stream, folded, base[0, 1], jnp.where(odd, 16, 0))
    product = by_row_shift(product + near_lags[...], rows, -1)
    lags[...] = jnp.zeros(lags.shape, jnp.float32)
    for a in range(near):
        for f in range(count):
            start = (a * count + f) * rows
            lags[f * 8 + a : f * 8 + a + 1, :] = jnp.sum(product[start : start + rows], axis=0, keepdims=True)
    back = 4 * lanes - 1 - base[0, 0]
    across = lax.broadcasted_iota(jnp.int32, (8, lanes), 0)
    lane = lane_of((8, lanes))
    packed = jnp.zeros((8, lanes), jnp.float32)
    for f in range(count):
        block = lags[f * 8 : f * 8 + 8, :]
        for j in range(reach):
            at = (f * reach + j) * reach
            there = back + at - (j // near) * 2 * slot
            high = pltpu.roll(block, there & (lanes - 1), 1)
            low = pltpu.roll(block, (there - slot) & (lanes - 1), 1)
            member = (across == j % near) & (lane >= at) & (lane < at + reach)
            packed = packed + jnp.where(member, high + low, 0.0)
    lags[0:8, :] = jnp.zeros((8, lanes), jnp.float32)
    for f in range(count):
        lags[f : f + 1, :] = jnp.sum(power[f * 8 : f * 8 + 8, :], axis=0, keepdims=True)
    lags[count : count + 1, :] = jnp.sum(ref_power, axis=0, keepdims=True)
    powers = jnp.sum(lags[0:8, :], axis=1, keepdims=True)
    packed = packed + jnp.where(lane == count * reach * reach + across, powers, 0.0)
    packed = jnp.sum(packed, axis=0, keepdims=True)
    for place in range(2):
        offset = base[0, place].astype(jnp.float32)
        packed = jnp.where(lane[0:1] == lanes - 2 + place, offset, packed)
    part[...] = jnp.broadcast_to(packed, part.shape)


def spreader(clean, other, spread, base_col):
    height = clean.shape[1]
    size = height + other.shape[1]
    spare = spread.shape[0] - reach * size
    shifts = [column_shift(base_col + j - 3) for j in range(reach)]

    def spread_tile(t):
        at = tile_of(t)
        for j, shift in enumerate(shifts):
            spread[j * size : j * size + height, at] = shift(clean, t)
            spread[j * size + height : (j + 1) * size, at] = shift(other, t)
        spread[reach * size :, at] = jnp.zeros((spare, lanes), jnp.bfloat16)

    return spread_tile


def blend_weights(totals, count):
    lane = lane_of(totals.shape)
    block = reach * reach

    def pick(index):
        return jnp.sum(jnp.where(lane == index, totals, 0.0), axis=1, keepdims=True)

    ref_power = pick(count * block + count)
    weights = []
    for f in range(count):
        norm_product = jnp.sqrt((pick(count * block + f) + 1e-06) * (ref_power + 1e-06))
        member = (lane >= f * block) & (lane < (f + 1) * block)
        rho = jnp.where(member, totals, 0.0) / norm_product
        squared = rho * rho
        middle = jnp.where(lane == f * block + block // 2, 0.05, 0.0)
        weights.append((squared + middle) / (0.05 + jnp.sum(squared, axis=1, keepdims=True)))
    return weights


def banded(weights, f, rows, first_row, depth):
    wide = rows + 8
    blank = jnp.zeros((weights.shape[0], depth - lanes), jnp.float32)
    weights = jnp.concatenate([weights, blank], axis=1)
    lane = lane_of(weights.shape)
    line = jnp.zeros_like(weights)
    for j in range(reach):
        at = first_row + j * 2 * wide
        amount = at - (f * reach + j) * reach
        amount = jnp.where(amount < 0, amount + depth, amount)
        line = jnp.where((lane >= at) & (lane < at + reach), pltpu.roll(weights, amount, 1), line)
    band = by_row_shift(jnp.broadcast_to(line[0:1], (rows, depth)), rows, 1)
    odd = lax.axis_index("rows") % 2 == 1
    row = lane_of(band.shape) % (2 * wide)
    start = jnp.where(odd, 0, 8)
    inner = (row >= start) & (row < start + rows)
    first = pltpu.roll(jnp.where(inner, band, 0.0), jnp.where(odd, 0, depth - 8), 1)
    second = pltpu.roll(jnp.where(inner, 0.0, band), jnp.where(odd, 2 * rows - 16, 2 * rows), 1)
    return first + pltpu.roll(first, rows, 1) + second + pltpu.roll(second, 8, 1)


def pressures(base, totals, clean, other, spread, inverse):
    count, rows, columns = inverse.shape
    depth = spread.shape[0]
    weights = blend_weights(jnp.broadcast_to(totals[0:1, :], (8, lanes)), count)
    bands = [banded(weights[f], f, rows, 1 + base[0, 0], depth) for f in range(count)]
    mixing = cut(jnp.concatenate(bands, axis=0))
    spread_tile = spreader(clean, other, spread, base[0, 1])

    def chunk_values(t):
        where = chunk_of(t)
        spread_tile(2 * t)
        spread_tile(2 * t + 1)
        product = jnp.dot(mixing, spread[:, where], preferred_element_type=jnp.float32)
        registered = product[: count * rows] + product[count * rows :]
        values = []
        for f in range(count):
            ratio = registered[f * rows : (f + 1) * rows] * inverse[f, :, where]
            values.append(calib_zero + ratio * (calib_linear + calib_square * ratio))
        return values

    return chunk_values


def pressure_kernel(base, totals, clean, other, inverse, pressure, moments, part, spread):
    count, rows, columns = inverse.shape
    chunk_values = pressures(base, totals, clean, other, spread, inverse)

    def step(t, sums):
        where = chunk_of(t)
        values = chunk_values(t)
        squares = [value * value for value in values]
        for f in range(count):
            pressure[f, :, where] = values[f]
        moments[0, :, where] = sum(values[1:], values[0])
        moments[1, :, where] = sum(squares[1:], squares[0])
        result = []
        for total, array in zip(sums, values + squares):
            result.append(total + fold(array[:, :lanes]) + fold(array[:, lanes:]))
        return tuple(result)

    zero = jnp.zeros((8, lanes), jnp.float32)
    sums = by_tiles(step, columns // (2 * lanes), columns // (2 * lanes), (zero,) * (2 * count))
    line = zero
    for k in range(2 * count):
        value = jnp.sum(jnp.sum(sums[k], axis=0, keepdims=True), axis=1, keepdims=True)
        line = line + jnp.where(lane_of(line.shape) == k, value, 0.0)
    part[...] = jnp.broadcast_to(line[0:1], part.shape)


def time_kernel(base, totals, clean, other, inverse, moments, time_mean, time_rms, spread):
    count, rows, columns = inverse.shape
    chunk_values = pressures(base, totals, clean, other, spread, inverse)
    frames = 2 * count

    def step(t, carry):
        where = chunk_of(t)
        first = moments[0, :, where]
        second = moments[1, :, where]
        for value in chunk_values(t):
            first = first + value
            second = second + value * value
        mean = first * (1.0 / frames)
        time_mean[:, where] = mean
        time_rms[:, where] = jnp.sqrt(jnp.maximum(second * (1.0 / frames) - mean * mean, 0.0))
        return carry

    by_tiles(step, columns // (2 * lanes), columns // (2 * lanes))


def paired(value, axis, first):
    size = lax.axis_size(axis)
    partner = list(range(size))
    for i in range(first, size - 1, 2):
        partner[i], partner[i + 1] = i + 1, i
    return lax.ppermute(value, axis, list(enumerate(partner)))


def by_parity(odd, array, height, dim):
    length = array.shape[dim]
    low = lax.slice_in_dim(array, 0, height, axis=dim)
    high = lax.slice_in_dim(array, length - height, length, axis=dim)
    return jnp.where(odd, high, low), jnp.where(odd, low, high)


def from_owner(shard, here, odd, axis, root):
    mine = lax.axis_index(axis) == root
    height = shard.shape[0] // 2
    if lax.axis_size(axis) != 2:
        whole = lax.psum(jnp.where(mine, shard, jnp.zeros_like(shard)), axis)
        return by_parity(odd, whole, height, 0)
    there = by_parity(odd, paired(shard, axis, 0), height, 0)
    here = by_parity(odd, here, height, 0)
    return [jnp.where(mine, own, other) for own, other in zip(here, there)]


def total_over(value, axis):
    size = lax.axis_size(axis)
    if size & (size - 1):
        return lax.psum(value, axis)
    step = 1
    while step < size:
        value = value + lax.ppermute(value, axis, [(i, i ^ step) for i in range(size)])
        step *= 2
    return value


def shards(frames_raw, wind_off, run_owner, search_base):
    count, rows, columns = frames_raw.shape
    tiles = columns // lanes
    ring = tiles + 2
    wide = rows + 8
    depth = near * count * rows
    size = lax.axis_size("rows")
    f32 = jnp.float32
    bf16 = jnp.bfloat16
    struct = functools.partial(jax.ShapeDtypeStruct, dtype=f32)
    odd = lax.axis_index("rows") % 2 == 1
    raw, run = lax.optimization_barrier((jnp.maximum(frames_raw, 0.0), jnp.maximum(wind_off[0], 0.0)))
    owner, offsets = lax.optimization_barrier((run_owner, jnp.clip(search_base, -8, 8)))
    own_odd, own_even = from_owner(wind_off[0], run, odd, "frames", owner[0])
    from_odd = paired(own_odd, "rows", 1)
    from_even = paired(own_even, "rows", 0)
    frames_odd, frames_even = by_parity(odd, raw, 4, 1)
    frames_odd = paired(frames_odd, "rows", 1)
    frames_even = paired(frames_even, "rows", 0)
    frames_odd, own_odd = lax.optimization_barrier((frames_odd, own_odd))
    inverse, stack, power, band = pl.pallas_call(
        smooth_kernel,
        out_shape=(
            struct((count, rows, columns)),
            jax.ShapeDtypeStruct((2 * depth, ring * lanes), bf16),
            struct((8 * count, lanes)),
            jax.ShapeDtypeStruct((4 * lanes, 2 * lanes), bf16),
        ),
        in_specs=[vmem] * 3,
        out_specs=(vmem,) * 4,
        scratch_shapes=[
            pltpu.VMEM((count, tiles, rows + 16, lanes), f32),
            pltpu.VMEM((tiles // 2, 2 * count * rows, 4 * lanes), bf16),
            pltpu.VMEM((ring + 2, 2 * count * rows, lanes), bf16),
        ],
        compiler_params=params,
        cost_estimate=cost(8),
        name="smooth",
    )(raw, frames_odd, frames_even)
    blocks = lax.axis_size("frames")
    peers = size * blocks if blocks == 2 else size
    if blocks == 2:
        other_inverse = paired(inverse, "frames", 0)
    def reference_scratch(height):
        return [
            pltpu.VMEM((tiles, height + 8, lanes), f32),
            pltpu.VMEM((tiles // 2, 2 * height, 4 * lanes), bf16),
            pltpu.VMEM((ring + 2, 2 * height, lanes), bf16),
            pltpu.VMEM((far * 2 * height, ring * lanes), bf16),
            pltpu.VMEM((depth, lanes), f32),
        ]

    clean, near_lags, near_power = pl.pallas_call(
        near_kernel,
        out_shape=(
            jax.ShapeDtypeStruct((tiles + 2, 2 * rows, lanes), bf16),
            struct((depth, lanes)),
            struct((8, lanes)),
        ),
        in_specs=[smem] + [vmem] * 5,
        out_specs=(vmem,) * 3,
        scratch_shapes=reference_scratch(rows),
        compiler_params=params,
        cost_estimate=cost(8),
        name="near",
    )(offsets, own_odd, own_even, from_even, stack, band)
    other, part = pl.pallas_call(
        match_kernel,
        out_shape=(jax.ShapeDtypeStruct((tiles + 2, 16, lanes), bf16), struct((peers, lanes))),
        in_specs=[smem] + [vmem] * 7,
        out_specs=(vmem,) * 2,
        scratch_shapes=reference_scratch(8) + [pltpu.VMEM((8 * count, lanes), f32)],
        compiler_params=params,
        cost_estimate=cost(8),
        name="match",
    )(offsets, own_odd, from_odd, near_lags, near_power, stack, power, band)
    if blocks == 2:
        parts = lax.all_to_all(part, ("rows", "frames"), 0, 0, tiled=True).reshape(size, blocks, lanes)
        mine = lax.axis_index("frames") == 0
        both = jnp.sum(parts, axis=0)
        totals = jnp.where(mine, both[0:1], both[1:2])
        row = jnp.where(mine, both[1:2], both[0:1])
        place = jnp.where(mine, parts[0, 1:2], parts[0, 0:1])[:, lanes - 2 :].astype(jnp.int32)
    else:
        totals = jnp.sum(lax.all_to_all(part, "rows", 0, 0, tiled=True), axis=0, keepdims=True)
    depth = -(-reach * 2 * wide // lanes) * lanes
    spread = pltpu.VMEM((depth, columns), bf16)
    pressure, moments, part = pl.pallas_call(
        pressure_kernel,
        out_shape=(struct((count, rows, columns)), struct((2, rows, columns)), struct((size, lanes))),
        in_specs=[smem] + [vmem] * 4,
        out_specs=(vmem, vmem, vmem),
        scratch_shapes=[spread],
        compiler_params=params,
        cost_estimate=cost(12),
        name="pressure",
    )(offsets, totals, clean, other, inverse)
    if blocks == 2:
        time_mean, time_rms = pl.pallas_call(
            time_kernel,
            out_shape=(struct((rows, columns)), struct((rows, columns))),
            in_specs=[smem] + [vmem] * 5,
            out_specs=(vmem, vmem),
            scratch_shapes=[spread],
            compiler_params=params,
            cost_estimate=cost(12),
            name="time",
        )(place, row, clean, other, other_inverse, moments)
    else:
        whole = total_over(moments, "frames")
        total_frames = count * blocks
        time_mean = whole[0] / total_frames
        time_rms = jnp.sqrt(jnp.maximum(whole[1] / total_frames - time_mean * time_mean, 0.0))
    sums = lax.all_to_all(part, "rows", 0, 0, tiled=True)
    sums, time_mean, time_rms = lax.optimization_barrier((sums, time_mean, time_rms))
    spatial = jnp.sum(sums, axis=0)
    cell_count = rows * columns * size
    frame_mean = spatial[:count] / cell_count
    frame_rms = jnp.sqrt(spatial[count : 2 * count] / cell_count - frame_mean * frame_mean)
    return (pressure, frame_mean, frame_rms, time_mean, time_rms)


def solution(mesh):
    placed = (P("frames", "rows", None), P("frames", "rows", None), P("rows"), P("frames", None))
    return jax.shard_map(
        shards,
        mesh=mesh,
        in_specs=placed,
        out_specs=(
            P("frames", "rows", None),
            P("frames"),
            P("frames"),
            P("rows", None),
            P("rows", None),
        ),
        check_vma=False,
    )
```

```python
import functools

import jax
import jax.numpy as jnp
from jax import lax
from jax.experimental import pallas as pl
from jax.experimental.pallas import tpu as pltpu
from jax.sharding import PartitionSpec as P

taps = (1.0 / 256, 8.0 / 256, 28.0 / 256, 56.0 / 256, 70.0 / 256)
calib_zero = -0.25
calib_linear = 1.0
calib_square = 0.15
lanes = 128
reach = 7
near = 4
far = 2
slot = 32
params = pltpu.CompilerParams(vmem_limit_bytes=14 * 1024 * 1024)
vmem = pl.BlockSpec(memory_space=pltpu.VMEM)
smem = pl.BlockSpec(memory_space=pltpu.SMEM)


def cost(mebibytes):
    return pl.CostEstimate(flops=0, bytes_accessed=mebibytes * 2**20, transcendentals=0)


def tile_of(index):
    if isinstance(index, int):
        return slice(index * lanes, (index + 1) * lanes)
    return pl.ds(pl.multiple_of(index * lanes, lanes), lanes)


def by_tiles(step, tiles, group, init=()):
    if group == tiles:
        for index in range(tiles):
            init = step(index, init)
        return init

    def body(index, carry):
        for inner in range(group):
            carry = step(index * group + inner, carry)
        return carry

    return lax.fori_loop(0, tiles // group, body, init)


def lane_of(shape):
    return lax.broadcasted_iota(jnp.int32, shape, len(shape) - 1)


def fold(product):
    return jnp.sum(product.reshape(product.shape[0] // 8, 8, lanes), axis=0)


def vertical(load):
    total = taps[4] * load(4)
    for step in range(4):
        total = total + taps[step] * (load(step) + load(8 - step))
    return total


def moved(before, here, after, step):
    if step > 0:
        return pltpu.roll(jnp.where(lane_of(here.shape) < step, after, here), lanes - step, 1)
    if step < 0:
        return pltpu.roll(jnp.where(lane_of(here.shape) >= lanes + step, before, here), -step, 1)
    return here


def halves(value):
    high = value.astype(jnp.bfloat16)
    low = (value - high.astype(jnp.float32)).astype(jnp.bfloat16)
    return high, low


def cut(value):
    return jnp.concatenate(halves(value), axis=0)


def fill_band(band):
    shape = (lanes, lanes)
    apart = lax.broadcasted_iota(jnp.int32, shape, 0) - lax.broadcasted_iota(jnp.int32, shape, 1)

    def block(offset):
        distance = jnp.abs(apart + offset)
        value = jnp.zeros(shape, jnp.float32)
        for step in range(5):
            value = jnp.where(distance == step, taps[4 - step], value)
        return value.astype(jnp.bfloat16)

    none = jnp.zeros(shape, jnp.bfloat16)
    before, here, after = block(-lanes), block(0), block(lanes)
    for index, pair in enumerate(((before, none), (here, before), (after, here), (none, after))):
        band[index * lanes : (index + 1) * lanes, :] = jnp.concatenate(pair, axis=1)


def chunk_of(t):
    if isinstance(t, int):
        return slice(t * 2 * lanes, (t + 1) * 2 * lanes)
    return pl.ds(pl.multiple_of(t * 2 * lanes, 2 * lanes), 2 * lanes)


def place_tile(windows, index, value):
    for c in (index // 2 - 1, index // 2):
        at = index - 2 * c
        if 0 <= c < windows.shape[0] and at < 4:
            windows[c, :, at * lanes : (at + 1) * lanes] = value


def horizontal(windows, band):
    chunks, height, width = windows.shape
    product = jnp.dot(
        windows[...].reshape(chunks * height, width), band[...], preferred_element_type=jnp.float32
    )
    product = product.reshape(chunks, height, 2 * lanes)
    return product[:, : height // 2] + product[:, height // 2 :]


def by_row_shift(value, rows, direction):
    place = lax.broadcasted_iota(jnp.int32, value.shape, 0) % rows
    unit = 1
    while unit < rows:
        digit = (place // unit) % 4
        result = value
        for times in range(1, 4):
            amount = times * unit
            turned = pltpu.roll(value, amount if direction > 0 else value.shape[1] - amount, 1)
            result = jnp.where(digit == times, turned, result)
        value = result
        unit *= 4
    return value


def at_edge():
    index = lax.axis_index("rows")
    return (index == 0) | (index == lax.axis_size("rows") - 1)


def smooth_kernel(frames, from_odd, from_even, inverse, stack, power, band, rows_in, wide, pieces):
    count, rows, columns = frames.shape
    tiles = columns // lanes
    ring = tiles + 2
    odd = lax.axis_index("rows") % 2 == 1
    edge = at_edge()
    blank = jnp.zeros((2 * count * rows, lanes), jnp.bfloat16)
    place_tile(wide, 0, blank)
    place_tile(wide, tiles + 1, blank)
    fill_band(band)
    pieces[0] = blank
    pieces[tiles + 1] = blank
    pieces[tiles + 2] = blank

    def load_step(t, carry):
        for f in range(count):
            outer = jnp.where(edge, 0.0, from_odd[f, :, tile_of(t)])
            inner = from_even[f, :, tile_of(t)]
            rows_in[f, t, 4:8, :] = jnp.where(odd, inner, outer)
            rows_in[f, t, 8 : 8 + rows, :] = frames[f, :, tile_of(t)]
            rows_in[f, t, 8 + rows : 12 + rows, :] = jnp.where(odd, outer, inner)
        return carry

    def vertical_step(t, carry):
        parts = [vertical(lambda s: rows_in[f, t, pl.ds(4 + s, rows), :]) for f in range(count)]
        place_tile(wide, t + 1, cut(jnp.concatenate(parts, axis=0)))
        return carry

    def horizontal_step(t, totals):
        smooth = smoothed[t]
        result = []
        details = []
        for f in range(count):
            part = smooth[f * rows : (f + 1) * rows]
            inverse[f, :, chunk_of(t)] = 1.0 / part
            details.append(frames[f, :, chunk_of(t)] - part)
            square = details[f] * details[f]
            result.append(totals[f] + fold(square[:, :lanes]) + fold(square[:, lanes:]))
        detail = cut(jnp.concatenate(details, axis=0))
        pieces[2 * t + 1] = detail[:, :lanes]
        pieces[2 * t + 2] = detail[:, lanes:]
        return tuple(result)

    def stack_step(t, carry):
        before, here, after = pieces[t], pieces[t + 1], pieces[t + 2]
        size = count * rows
        for a in range(near):
            turned = moved(before, here, after, 1 - a)
            stack[a * size : (a + 1) * size, tile_of(t)] = turned[:size]
            stack[(near + a) * size : (near + a + 1) * size, tile_of(t)] = turned[size:]
        return carry

    powers = (jnp.zeros((8, lanes), jnp.float32),) * count
    for t in range(tiles):
        load_step(t, 0)
        vertical_step(t, 0)
    smoothed = horizontal(wide, band)
    for t in range(tiles // 2):
        powers = horizontal_step(t, powers)
    for f in range(count):
        power[f * 8 : f * 8 + 8, :] = powers[f]
    pieces[tiles + 3] = pieces[1]
    by_tiles(stack_step, ring, ring)


def column_shift(offset):
    negative = offset < 0
    first = jnp.where(negative, 0, 1)
    amount = jnp.where(negative, offset + lanes, offset)
    back = (lanes - amount) & (lanes - 1)

    def shift(source, t):
        here = source[t + first]
        after = source[t + first + 1]
        return pltpu.roll(jnp.where(lane_of(here.shape) < amount, after, here), back, 1)

    return shift


def reference_rows(raw, smooth, clean, fine, tiles):
    height = clean.shape[1] // 2
    empty = jnp.zeros((2 * height, lanes), jnp.bfloat16)
    for array in (clean, fine):
        array[0] = empty
        array[tiles + 1] = empty
    fine[tiles + 2] = empty
    squares = []
    for t in range(tiles // 2):
        detail = jnp.concatenate([raw(2 * t), raw(2 * t + 1)], axis=1) - smooth(t)
        for array, value in ((clean, cut(smooth(t))), (fine, cut(detail))):
            array[2 * t + 1] = value[:, :lanes]
            array[2 * t + 2] = value[:, lanes:]
        squares.append(detail * detail)
    fine[tiles + 3] = fine[1]
    return squares


def lag_products(stack, fine, stream, folded, base_col, start):
    height = fine.shape[1]
    half = height // 2
    shifts = [column_shift(base_col + near * b - 2) for b in range(far)]
    for t in range(fine.shape[0] - 2):
        for b, shift in enumerate(shifts):
            stream[b * height : (b + 1) * height, tile_of(t)] = shift(fine, t)
    product = lax.dot_general(
        stack[...], stream[...], (((1,), (1,)), ((), ())), preferred_element_type=jnp.float32
    )
    size = product.shape[0] // 2
    folded[...] = jnp.zeros(folded.shape, jnp.float32)
    folded[:, 0 : far * height] = product[:size] + product[size:]
    product = folded[...]
    lane = lane_of(product.shape)
    placed = jnp.zeros_like(product)
    for s in range(2 * far):
        at = s * slot + start
        turned = pltpu.roll(product, at - s * half, 1)
        placed = jnp.where((lane >= at) & (lane < at + half), turned, placed)
    return placed


def near_kernel(
    base, own_odd, own_even, from_even, stack, band, clean, lags, power, rows_in, windows, fine, stream, folded
):
    tiles = own_odd.shape[1] // lanes
    odd = lax.axis_index("rows") % 2 == 1
    height = clean.shape[1] // 2
    empty = jnp.zeros((2 * height, lanes), jnp.bfloat16)
    place_tile(windows, 0, empty)
    place_tile(windows, tiles + 1, empty)
    for t in range(tiles):
        at = tile_of(t)
        outer = own_odd[:, at]
        inner = from_even[:, at]
        rows_in[t, 0:8, :] = jnp.where(odd, inner, outer)
        rows_in[t, 8:16, :] = own_even[:, at]
        rows_in[t, 16:24, :] = jnp.where(odd, outer, inner)
        place_tile(windows, t + 1, cut(vertical(lambda s: rows_in[t, pl.ds(s, height), :])))
    smooth = horizontal(windows, band)
    squares = reference_rows(lambda t: rows_in[t, pl.ds(4, height), :], lambda t: smooth[t], clean, fine, tiles)
    place = lax.broadcasted_iota(jnp.int32, squares[0].shape, 0)
    first = jnp.where(odd, 4, 0)
    own = (place >= first) & (place < first + height - 4)
    total = jnp.zeros((8, lanes), jnp.float32)
    for square in squares:
        square = jnp.where(own, square, 0.0)
        total = total + fold(square[:, :lanes]) + fold(square[:, lanes:])
    power[...] = total
    lags[...] = lag_products(stack, fine, stream, folded, base[0, 1], jnp.where(odd, 0, 8))


def match_kernel(
    base, own_odd, from_odd, near_lags, near_power, stack, power, band, clean, part, rows_in, windows, fine, stream, folded, lags
):
    tiles = own_odd.shape[1] // lanes
    count = power.shape[0] // 8
    rows = folded.shape[0] // (near * count)
    odd = lax.axis_index("rows") % 2 == 1
    edge = at_edge()
    height = clean.shape[1] // 2
    empty = jnp.zeros((2 * height, lanes), jnp.bfloat16)
    place_tile(windows, 0, empty)
    place_tile(windows, tiles + 1, empty)
    for t in range(tiles):
        at = tile_of(t)
        outer = jnp.where(edge, 0.0, from_odd[:, at])
        inner = own_odd[:, at]
        rows_in[t, 0:8, :] = jnp.where(odd, inner, outer)
        rows_in[t, 8:16, :] = jnp.where(odd, outer, inner)
        place_tile(windows, t + 1, cut(vertical(lambda s: rows_in[t, pl.ds(s, height), :])))
    smooth = horizontal(windows, band)
    place = lax.broadcasted_iota(jnp.int32, (height, 2 * lanes), 0)
    first = jnp.where(odd, 0, 4)
    own = (place >= first) & (place < first + 4)
    inside = (place >= jnp.where(edge, first, 0)) & (place < jnp.where(edge, first + 4, height))

    def masked(t):
        return jnp.where(inside, smooth[t], 0.0)

    squares = reference_rows(lambda t: rows_in[t, pl.ds(4, height), :], masked, clean, fine, tiles)
    ref_power = near_power[...]
    for square in squares:
        square = jnp.where(own, square, 0.0)
        ref_power = ref_power + fold(square[:, :lanes]) + fold(square[:, lanes:])
    product = lag_products(stack, fine, stream, folded, base[0, 1], jnp.where(odd, 16, 0))
    product = by_row_shift(product + near_lags[...], rows, -1)
    lags[...] = jnp.zeros(lags.shape, jnp.float32)
    for a in range(near):
        for f in range(count):
            start = (a * count + f) * rows
            lags[f * 8 + a : f * 8 + a + 1, :] = jnp.sum(product[start : start + rows], axis=0, keepdims=True)
    back = 4 * lanes - 1 - base[0, 0]
    across = lax.broadcasted_iota(jnp.int32, (8, lanes), 0)
    lane = lane_of((8, lanes))
    packed = jnp.zeros((8, lanes), jnp.float32)
    for f in range(count):
        block = lags[f * 8 : f * 8 + 8, :]
        for j in range(reach):
            at = (f * reach + j) * reach
            there = back + at - (j // near) * 2 * slot
            high = pltpu.roll(block, there & (lanes - 1), 1)
            low = pltpu.roll(block, (there - slot) & (lanes - 1), 1)
            member = (across == j % near) & (lane >= at) & (lane < at + reach)
            packed = packed + jnp.where(member, high + low, 0.0)
    lags[0:8, :] = jnp.zeros((8, lanes), jnp.float32)
    for f in range(count):
        lags[f : f + 1, :] = jnp.sum(power[f * 8 : f * 8 + 8, :], axis=0, keepdims=True)
    lags[count : count + 1, :] = jnp.sum(ref_power, axis=0, keepdims=True)
    powers = jnp.sum(lags[0:8, :], axis=1, keepdims=True)
    packed = packed + jnp.where(lane == count * reach * reach + across, powers, 0.0)
    packed = jnp.sum(packed, axis=0, keepdims=True)
    for place in range(2):
        offset = base[0, place].astype(jnp.float32)
        packed = jnp.where(lane[0:1] == lanes - 2 + place, offset, packed)
    part[...] = jnp.broadcast_to(packed, part.shape)


def spreader(clean, spread, base_col):
    size = clean.shape[1]
    shifts = [column_shift(base_col + j - 3) for j in range(reach)]

    def spread_tile(t):
        at = tile_of(t)
        for j, shift in enumerate(shifts):
            spread[j * size : (j + 1) * size, at] = shift(clean, t)
        spread[reach * size :, at] = jnp.zeros((spread.shape[0] - reach * size, lanes), jnp.bfloat16)

    return spread_tile


def shift_kernel(base, clean, spread):
    spread_tile = spreader(clean, spread, base[0, 1])
    for t in range(clean.shape[0] - 2):
        spread_tile(t)


def blend_weights(totals, count):
    lane = lane_of(totals.shape)
    block = reach * reach

    def pick(index):
        return jnp.sum(jnp.where(lane == index, totals, 0.0), axis=1, keepdims=True)

    ref_power = pick(count * block + count)
    weights = []
    for f in range(count):
        norm_product = jnp.sqrt((pick(count * block + f) + 1e-06) * (ref_power + 1e-06))
        member = (lane >= f * block) & (lane < (f + 1) * block)
        rho = jnp.where(member, totals, 0.0) / norm_product
        squared = rho * rho
        middle = jnp.where(lane == f * block + block // 2, 0.05, 0.0)
        weights.append((squared + middle) / (0.05 + jnp.sum(squared, axis=1, keepdims=True)))
    return weights


def banded(weights, f, rows, first_row):
    depth = 8 * slot
    blank = jnp.zeros((weights.shape[0], depth - lanes), jnp.float32)
    weights = jnp.concatenate([weights, blank], axis=1)
    lane = lane_of(weights.shape)
    line = jnp.zeros_like(weights)
    for j in range(reach):
        at = first_row + j * slot
        amount = (at + depth - (f * reach + j) * reach) & (depth - 1)
        line = jnp.where((lane >= at) & (lane < at + reach), pltpu.roll(weights, amount, 1), line)
    band = by_row_shift(jnp.broadcast_to(line[0:1], (rows, depth)), rows, 1)
    odd = lax.axis_index("rows") % 2 == 1
    lane = lane_of(band.shape)
    row = lane & (slot - 1)
    start = jnp.where(odd, 0, 8)
    inner = (row >= start) & (row < start + rows)
    first = pltpu.roll(jnp.where(inner, band, 0.0), (depth - start) & (depth - 1), 1)
    outer = jnp.where(inner, 0.0, band)
    start = jnp.where(odd, 16, 0)
    second = jnp.zeros_like(band)
    for j in range(reach):
        turned = pltpu.roll(outer, (depth - start - j * 16) & (depth - 1), 1)
        second = jnp.where((lane >= j * 16) & (lane < j * 16 + 8), turned, second)
    second = second[:, :lanes]
    return first + pltpu.roll(first, rows, 1), second + pltpu.roll(second, 8, 1)


def pressures(base, totals, first, second, inverse, prepare):
    count, rows, columns = inverse.shape
    weights = blend_weights(jnp.broadcast_to(totals[0:1, :], (8, lanes)), count)
    bands = [banded(weights[f], f, rows, 1 + base[0, 0]) for f in range(count)]
    inner, outer = [cut(jnp.concatenate(parts, axis=0)) for parts in zip(*bands)]

    def chunk_values(t):
        where = chunk_of(t)
        prepare(2 * t)
        prepare(2 * t + 1)
        product = jnp.dot(inner, first[:, where], preferred_element_type=jnp.float32)
        product = product + jnp.dot(outer, second[:, where], preferred_element_type=jnp.float32)
        registered = product[: count * rows] + product[count * rows :]
        values = []
        for f in range(count):
            ratio = registered[f * rows : (f + 1) * rows] * inverse[f, :, where]
            values.append(calib_zero + ratio * (calib_linear + calib_square * ratio))
        return values

    return chunk_values


def pressure_kernel(base, totals, first, other, inverse, pressure, moments, part, second):
    count, rows, columns = inverse.shape
    chunk_values = pressures(base, totals, first, second, inverse, spreader(other, second, base[0, 1]))

    def step(t, sums):
        where = chunk_of(t)
        values = chunk_values(t)
        squares = [value * value for value in values]
        for f in range(count):
            pressure[f, :, where] = values[f]
        moments[0, :, where] = sum(values[1:], values[0])
        moments[1, :, where] = sum(squares[1:], squares[0])
        result = []
        for total, array in zip(sums, values + squares):
            result.append(total + fold(array[:, :lanes]) + fold(array[:, lanes:]))
        return tuple(result)

    zero = jnp.zeros((8, lanes), jnp.float32)
    sums = by_tiles(step, columns // (2 * lanes), columns // (2 * lanes), (zero,) * (2 * count))
    line = zero
    for k in range(2 * count):
        value = jnp.sum(jnp.sum(sums[k], axis=0, keepdims=True), axis=1, keepdims=True)
        line = line + jnp.where(lane_of(line.shape) == k, value, 0.0)
    part[...] = jnp.broadcast_to(line[0:1], part.shape)


def time_kernel(base, totals, clean, other, inverse, moments, time_mean, time_rms, first, second):
    count, rows, columns = inverse.shape
    steps = [spreader(clean, first, base[0, 1]), spreader(other, second, base[0, 1])]

    def prepare(t):
        for step in steps:
            step(t)

    chunk_values = pressures(base, totals, first, second, inverse, prepare)
    frames = 2 * count

    def step(t, carry):
        where = chunk_of(t)
        total = moments[0, :, where]
        squares = moments[1, :, where]
        for value in chunk_values(t):
            total = total + value
            squares = squares + value * value
        mean = total * (1.0 / frames)
        time_mean[:, where] = mean
        time_rms[:, where] = jnp.sqrt(jnp.maximum(squares * (1.0 / frames) - mean * mean, 0.0))
        return carry

    by_tiles(step, columns // (2 * lanes), columns // (2 * lanes))


def paired(value, axis, first):
    size = lax.axis_size(axis)
    partner = list(range(size))
    for i in range(first, size - 1, 2):
        partner[i], partner[i + 1] = i + 1, i
    return lax.ppermute(value, axis, list(enumerate(partner)))


def by_parity(odd, array, height, dim):
    length = array.shape[dim]
    low = lax.slice_in_dim(array, 0, height, axis=dim)
    high = lax.slice_in_dim(array, length - height, length, axis=dim)
    return jnp.where(odd, high, low), jnp.where(odd, low, high)


def from_owner(shard, here, odd, axis, root):
    mine = lax.axis_index(axis) == root
    height = shard.shape[0] // 2
    if lax.axis_size(axis) != 2:
        whole = lax.psum(jnp.where(mine, shard, jnp.zeros_like(shard)), axis)
        return by_parity(odd, whole, height, 0)
    there = by_parity(odd, paired(shard, axis, 0), height, 0)
    here = by_parity(odd, here, height, 0)
    return [jnp.where(mine, own, other) for own, other in zip(here, there)]


def total_over(value, axis):
    size = lax.axis_size(axis)
    if size & (size - 1):
        return lax.psum(value, axis)
    step = 1
    while step < size:
        value = value + lax.ppermute(value, axis, [(i, i ^ step) for i in range(size)])
        step *= 2
    return value


def shards(frames_raw, wind_off, run_owner, search_base):
    count, rows, columns = frames_raw.shape
    tiles = columns // lanes
    ring = tiles + 2
    wide = rows + 8
    depth = near * count * rows
    size = lax.axis_size("rows")
    f32 = jnp.float32
    bf16 = jnp.bfloat16
    struct = functools.partial(jax.ShapeDtypeStruct, dtype=f32)
    odd = lax.axis_index("rows") % 2 == 1
    raw, run = lax.optimization_barrier((jnp.maximum(frames_raw, 0.0), jnp.maximum(wind_off[0], 0.0)))
    owner, offsets = lax.optimization_barrier((run_owner, jnp.clip(search_base, -8, 8)))
    own_odd, own_even = from_owner(wind_off[0], run, odd, "frames", owner[0])
    from_odd = paired(own_odd, "rows", 1)
    from_even = paired(own_even, "rows", 0)
    frames_odd, frames_even = by_parity(odd, raw, 4, 1)
    frames_odd = paired(frames_odd, "rows", 1)
    frames_even = paired(frames_even, "rows", 0)
    frames_odd, own_odd = lax.optimization_barrier((frames_odd, own_odd))
    inverse, stack, power, band = pl.pallas_call(
        smooth_kernel,
        out_shape=(
            struct((count, rows, columns)),
            jax.ShapeDtypeStruct((2 * depth, ring * lanes), bf16),
            struct((8 * count, lanes)),
            jax.ShapeDtypeStruct((4 * lanes, 2 * lanes), bf16),
        ),
        in_specs=[vmem] * 3,
        out_specs=(vmem,) * 4,
        scratch_shapes=[
            pltpu.VMEM((count, tiles, rows + 16, lanes), f32),
            pltpu.VMEM((tiles // 2, 2 * count * rows, 4 * lanes), bf16),
            pltpu.VMEM((ring + 2, 2 * count * rows, lanes), bf16),
        ],
        compiler_params=params,
        cost_estimate=cost(8),
        name="smooth",
    )(raw, frames_odd, frames_even)
    blocks = lax.axis_size("frames")
    peers = size * blocks if blocks == 2 else size
    if blocks == 2:
        other_inverse = paired(inverse, "frames", 0)
    def reference_scratch(height):
        return [
            pltpu.VMEM((tiles, height + 8, lanes), f32),
            pltpu.VMEM((tiles // 2, 2 * height, 4 * lanes), bf16),
            pltpu.VMEM((ring + 2, 2 * height, lanes), bf16),
            pltpu.VMEM((far * 2 * height, ring * lanes), bf16),
            pltpu.VMEM((depth, lanes), f32),
        ]

    clean, near_lags, near_power = pl.pallas_call(
        near_kernel,
        out_shape=(
            jax.ShapeDtypeStruct((tiles + 2, 2 * rows, lanes), bf16),
            struct((depth, lanes)),
            struct((8, lanes)),
        ),
        in_specs=[smem] + [vmem] * 5,
        out_specs=(vmem,) * 3,
        scratch_shapes=reference_scratch(rows),
        compiler_params=params,
        cost_estimate=cost(8),
        name="near",
    )(offsets, own_odd, own_even, from_even, stack, band)
    other, part = pl.pallas_call(
        match_kernel,
        out_shape=(jax.ShapeDtypeStruct((tiles + 2, 16, lanes), bf16), struct((peers, lanes))),
        in_specs=[smem] + [vmem] * 7,
        out_specs=(vmem,) * 2,
        scratch_shapes=reference_scratch(8) + [pltpu.VMEM((8 * count, lanes), f32)],
        compiler_params=params,
        cost_estimate=cost(8),
        name="match",
    )(offsets, own_odd, from_odd, near_lags, near_power, stack, power, band)
    if blocks == 2:
        parts = lax.all_to_all(part, ("rows", "frames"), 0, 0, tiled=True).reshape(size, blocks, lanes)
        mine = lax.axis_index("frames") == 0
        both = jnp.sum(parts, axis=0)
        totals = jnp.where(mine, both[0:1], both[1:2])
        row = jnp.where(mine, both[1:2], both[0:1])
        place = jnp.where(mine, parts[0, 1:2], parts[0, 0:1])[:, lanes - 2 :].astype(jnp.int32)
    else:
        totals = jnp.sum(lax.all_to_all(part, "rows", 0, 0, tiled=True), axis=0, keepdims=True)
    spreads = [(8 * 2 * rows, columns), (8 * 16, columns)]
    first = pl.pallas_call(
        shift_kernel,
        out_shape=jax.ShapeDtypeStruct(spreads[0], bf16),
        in_specs=[smem, vmem],
        out_specs=vmem,
        compiler_params=params,
        cost_estimate=cost(3),
        name="shift",
    )(offsets, clean)
    pressure, moments, part = pl.pallas_call(
        pressure_kernel,
        out_shape=(struct((count, rows, columns)), struct((2, rows, columns)), struct((size, lanes))),
        in_specs=[smem] + [vmem] * 4,
        out_specs=(vmem, vmem, vmem),
        scratch_shapes=[pltpu.VMEM(spreads[1], bf16)],
        compiler_params=params,
        cost_estimate=cost(12),
        name="pressure",
    )(offsets, totals, first, other, inverse)
    if blocks == 2:
        time_mean, time_rms = pl.pallas_call(
            time_kernel,
            out_shape=(struct((rows, columns)), struct((rows, columns))),
            in_specs=[smem] + [vmem] * 5,
            out_specs=(vmem, vmem),
            scratch_shapes=[pltpu.VMEM(shape, bf16) for shape in spreads],
            compiler_params=params,
            cost_estimate=cost(12),
            name="time",
        )(place, row, clean, other, other_inverse, moments)
    else:
        whole = total_over(moments, "frames")
        total_frames = count * blocks
        time_mean = whole[0] / total_frames
        time_rms = jnp.sqrt(jnp.maximum(whole[1] / total_frames - time_mean * time_mean, 0.0))
    sums = lax.all_to_all(part, "rows", 0, 0, tiled=True)
    sums, time_mean, time_rms = lax.optimization_barrier((sums, time_mean, time_rms))
    spatial = jnp.sum(sums, axis=0)
    cell_count = rows * columns * size
    frame_mean = spatial[:count] / cell_count
    frame_rms = jnp.sqrt(spatial[count : 2 * count] / cell_count - frame_mean * frame_mean)
    return (pressure, frame_mean, frame_rms, time_mean, time_rms)


def solution(mesh):
    placed = (P("frames", "rows", None), P("frames", "rows", None), P("rows"), P("frames", None))
    return jax.shard_map(
        shards,
        mesh=mesh,
        in_specs=placed,
        out_specs=(
            P("frames", "rows", None),
            P("frames"),
            P("frames"),
            P("rows", None),
            P("rows", None),
        ),
        check_vma=False,
    )
```

```python
import functools

import jax
import jax.numpy as jnp
from jax import lax
from jax.experimental import pallas as pl
from jax.experimental.pallas import tpu as pltpu
from jax.sharding import PartitionSpec as P

taps = (1.0 / 256, 8.0 / 256, 28.0 / 256, 56.0 / 256, 70.0 / 256)
calib_zero = -0.25
calib_linear = 1.0
calib_square = 0.15
lanes = 128
reach = 7
near = 4
far = 2
slot = 32
params = pltpu.CompilerParams(vmem_limit_bytes=14 * 1024 * 1024)
vmem = pl.BlockSpec(memory_space=pltpu.VMEM)
smem = pl.BlockSpec(memory_space=pltpu.SMEM)


def cost(mebibytes):
    return pl.CostEstimate(flops=0, bytes_accessed=mebibytes * 2**20, transcendentals=0)


def tile_of(index):
    if isinstance(index, int):
        return slice(index * lanes, (index + 1) * lanes)
    return pl.ds(pl.multiple_of(index * lanes, lanes), lanes)


def by_tiles(step, tiles, group, init=()):
    if group == tiles:
        for index in range(tiles):
            init = step(index, init)
        return init

    def body(index, carry):
        for inner in range(group):
            carry = step(index * group + inner, carry)
        return carry

    return lax.fori_loop(0, tiles // group, body, init)


def lane_of(shape):
    return lax.broadcasted_iota(jnp.int32, shape, len(shape) - 1)


def fold(product):
    return jnp.sum(product.reshape(product.shape[0] // 8, 8, lanes), axis=0)


def vertical(load):
    total = taps[4] * load(4)
    for step in range(4):
        total = total + taps[step] * (load(step) + load(8 - step))
    return total


def moved(before, here, after, step):
    if step > 0:
        return pltpu.roll(jnp.where(lane_of(here.shape) < step, after, here), lanes - step, 1)
    if step < 0:
        return pltpu.roll(jnp.where(lane_of(here.shape) >= lanes + step, before, here), -step, 1)
    return here


def halves(value):
    high = value.astype(jnp.bfloat16)
    low = (value - high.astype(jnp.float32)).astype(jnp.bfloat16)
    return high, low


def cut(value):
    return jnp.concatenate(halves(value), axis=0)


def fill_band(band):
    shape = (lanes, lanes)
    apart = lax.broadcasted_iota(jnp.int32, shape, 0) - lax.broadcasted_iota(jnp.int32, shape, 1)

    def block(offset):
        distance = jnp.abs(apart + offset)
        value = jnp.zeros(shape, jnp.float32)
        for step in range(5):
            value = jnp.where(distance == step, taps[4 - step], value)
        return value.astype(jnp.bfloat16)

    none = jnp.zeros(shape, jnp.bfloat16)
    before, here, after = block(-lanes), block(0), block(lanes)
    for index, pair in enumerate(((before, none), (here, before), (after, here), (none, after))):
        band[index * lanes : (index + 1) * lanes, :] = jnp.concatenate(pair, axis=1)


def chunk_of(t):
    if isinstance(t, int):
        return slice(t * 2 * lanes, (t + 1) * 2 * lanes)
    return pl.ds(pl.multiple_of(t * 2 * lanes, 2 * lanes), 2 * lanes)


def place_tile(windows, index, value):
    for c in (index // 2 - 1, index // 2):
        at = index - 2 * c
        if 0 <= c < windows.shape[0] and at < 4:
            windows[c, :, at * lanes : (at + 1) * lanes] = value


def horizontal(windows, band):
    chunks, height, width = windows.shape
    product = jnp.dot(
        windows[...].reshape(chunks * height, width), band[...], preferred_element_type=jnp.float32
    )
    product = product.reshape(chunks, height, 2 * lanes)
    return product[:, : height // 2] + product[:, height // 2 :]


def by_row_shift(value, rows, direction):
    place = lax.broadcasted_iota(jnp.int32, value.shape, 0) % rows
    unit = 1
    while unit < rows:
        digit = (place // unit) % 4
        result = value
        for times in range(1, 4):
            amount = times * unit
            turned = pltpu.roll(value, amount if direction > 0 else value.shape[1] - amount, 1)
            result = jnp.where(digit == times, turned, result)
        value = result
        unit *= 4
    return value


def at_edge():
    index = lax.axis_index("rows")
    return (index == 0) | (index == lax.axis_size("rows") - 1)


def smooth_kernel(frames, from_odd, from_even, inverse, stack, power, band, rows_in, wide, pieces):
    count, rows, columns = frames.shape
    tiles = columns // lanes
    ring = tiles + 2
    odd = lax.axis_index("rows") % 2 == 1
    edge = at_edge()
    blank = jnp.zeros((2 * count * rows, lanes), jnp.bfloat16)
    place_tile(wide, 0, blank)
    place_tile(wide, tiles + 1, blank)
    fill_band(band)
    pieces[0] = blank
    pieces[tiles + 1] = blank
    pieces[tiles + 2] = blank

    def load_step(t, carry):
        for f in range(count):
            outer = jnp.where(edge, 0.0, from_odd[f, :, tile_of(t)])
            inner = from_even[f, :, tile_of(t)]
            rows_in[f, t, 4:8, :] = jnp.where(odd, inner, outer)
            rows_in[f, t, 8 : 8 + rows, :] = frames[f, :, tile_of(t)]
            rows_in[f, t, 8 + rows : 12 + rows, :] = jnp.where(odd, outer, inner)
        return carry

    def vertical_step(t, carry):
        parts = [vertical(lambda s: rows_in[f, t, pl.ds(4 + s, rows), :]) for f in range(count)]
        place_tile(wide, t + 1, cut(jnp.concatenate(parts, axis=0)))
        return carry

    def horizontal_step(t, totals):
        smooth = smoothed[t]
        result = []
        details = []
        for f in range(count):
            part = smooth[f * rows : (f + 1) * rows]
            inverse[f, :, chunk_of(t)] = 1.0 / part
            details.append(frames[f, :, chunk_of(t)] - part)
            square = details[f] * details[f]
            result.append(totals[f] + fold(square[:, :lanes]) + fold(square[:, lanes:]))
        detail = cut(jnp.concatenate(details, axis=0))
        pieces[2 * t + 1] = detail[:, :lanes]
        pieces[2 * t + 2] = detail[:, lanes:]
        return tuple(result)

    def stack_step(t, carry):
        before, here, after = pieces[t], pieces[t + 1], pieces[t + 2]
        size = count * rows
        for a in range(near):
            turned = moved(before, here, after, 1 - a)
            stack[a * size : (a + 1) * size, tile_of(t)] = turned[:size]
            stack[(near + a) * size : (near + a + 1) * size, tile_of(t)] = turned[size:]
        return carry

    powers = (jnp.zeros((8, lanes), jnp.float32),) * count
    for t in range(tiles):
        load_step(t, 0)
        vertical_step(t, 0)
    smoothed = horizontal(wide, band)
    for t in range(tiles // 2):
        powers = horizontal_step(t, powers)
    for f in range(count):
        power[f * 8 : f * 8 + 8, :] = powers[f]
    pieces[tiles + 3] = pieces[1]
    by_tiles(stack_step, ring, ring)


def column_shift(offset):
    negative = offset < 0
    first = jnp.where(negative, 0, 1)
    amount = jnp.where(negative, offset + lanes, offset)
    back = (lanes - amount) & (lanes - 1)

    def shift(source, t):
        here = source[t + first]
        after = source[t + first + 1]
        return pltpu.roll(jnp.where(lane_of(here.shape) < amount, after, here), back, 1)

    return shift


def reference_rows(raw, smooth, clean, fine, tiles):
    height = clean.shape[1] // 2
    empty = jnp.zeros((2 * height, lanes), jnp.bfloat16)
    for array in (clean, fine):
        array[0] = empty
        array[tiles + 1] = empty
    fine[tiles + 2] = empty
    squares = []
    for t in range(tiles // 2):
        detail = jnp.concatenate([raw(2 * t), raw(2 * t + 1)], axis=1) - smooth(t)
        for array, value in ((clean, cut(smooth(t))), (fine, cut(detail))):
            array[2 * t + 1] = value[:, :lanes]
            array[2 * t + 2] = value[:, lanes:]
        squares.append(detail * detail)
    fine[tiles + 3] = fine[1]
    return squares


def lag_products(stack, fine, stream, folded, base_col, start):
    height = fine.shape[1]
    half = height // 2
    shifts = [column_shift(base_col + near * b - 2) for b in range(far)]
    for t in range(fine.shape[0] - 2):
        for b, shift in enumerate(shifts):
            stream[b * height : (b + 1) * height, tile_of(t)] = shift(fine, t)
    product = lax.dot_general(
        stack[...], stream[...], (((1,), (1,)), ((), ())), preferred_element_type=jnp.float32
    )
    size = product.shape[0] // 2
    folded[...] = jnp.zeros(folded.shape, jnp.float32)
    folded[:, 0 : far * height] = product[:size] + product[size:]
    product = folded[...]
    lane = lane_of(product.shape)
    placed = jnp.zeros_like(product)
    for s in range(2 * far):
        at = s * slot + start
        turned = pltpu.roll(product, at - s * half, 1)
        placed = jnp.where((lane >= at) & (lane < at + half), turned, placed)
    return placed


def near_kernel(
    base, own_odd, own_even, from_even, stack, band, clean, lags, power, rows_in, windows, fine, stream, folded
):
    tiles = own_odd.shape[1] // lanes
    odd = lax.axis_index("rows") % 2 == 1
    height = clean.shape[1] // 2
    empty = jnp.zeros((2 * height, lanes), jnp.bfloat16)
    place_tile(windows, 0, empty)
    place_tile(windows, tiles + 1, empty)
    for t in range(tiles):
        at = tile_of(t)
        outer = own_odd[:, at]
        inner = from_even[:, at]
        rows_in[t, 0:8, :] = jnp.where(odd, inner, outer)
        rows_in[t, 8:16, :] = own_even[:, at]
        rows_in[t, 16:24, :] = jnp.where(odd, outer, inner)
        place_tile(windows, t + 1, cut(vertical(lambda s: rows_in[t, pl.ds(s, height), :])))
    smooth = horizontal(windows, band)
    squares = reference_rows(lambda t: rows_in[t, pl.ds(4, height), :], lambda t: smooth[t], clean, fine, tiles)
    place = lax.broadcasted_iota(jnp.int32, squares[0].shape, 0)
    first = jnp.where(odd, 4, 0)
    own = (place >= first) & (place < first + height - 4)
    total = jnp.zeros((8, lanes), jnp.float32)
    for square in squares:
        square = jnp.where(own, square, 0.0)
        total = total + fold(square[:, :lanes]) + fold(square[:, lanes:])
    power[...] = total
    lags[...] = lag_products(stack, fine, stream, folded, base[0, 1], jnp.where(odd, 0, 8))


def match_kernel(
    base, own_odd, from_odd, near_lags, near_power, stack, power, band, clean, part, rows_in, windows, fine, stream, folded, lags
):
    tiles = own_odd.shape[1] // lanes
    count = power.shape[0] // 8
    rows = folded.shape[0] // (near * count)
    odd = lax.axis_index("rows") % 2 == 1
    edge = at_edge()
    height = clean.shape[1] // 2
    empty = jnp.zeros((2 * height, lanes), jnp.bfloat16)
    place_tile(windows, 0, empty)
    place_tile(windows, tiles + 1, empty)
    for t in range(tiles):
        at = tile_of(t)
        outer = jnp.where(edge, 0.0, from_odd[:, at])
        inner = own_odd[:, at]
        rows_in[t, 0:8, :] = jnp.where(odd, inner, outer)
        rows_in[t, 8:16, :] = jnp.where(odd, outer, inner)
        place_tile(windows, t + 1, cut(vertical(lambda s: rows_in[t, pl.ds(s, height), :])))
    smooth = horizontal(windows, band)
    place = lax.broadcasted_iota(jnp.int32, (height, 2 * lanes), 0)
    first = jnp.where(odd, 0, 4)
    own = (place >= first) & (place < first + 4)
    inside = (place >= jnp.where(edge, first, 0)) & (place < jnp.where(edge, first + 4, height))

    def masked(t):
        return jnp.where(inside, smooth[t], 0.0)

    squares = reference_rows(lambda t: rows_in[t, pl.ds(4, height), :], masked, clean, fine, tiles)
    ref_power = near_power[...]
    for square in squares:
        square = jnp.where(own, square, 0.0)
        ref_power = ref_power + fold(square[:, :lanes]) + fold(square[:, lanes:])
    product = lag_products(stack, fine, stream, folded, base[0, 1], jnp.where(odd, 16, 0))
    product = by_row_shift(product + near_lags[...], rows, -1)
    lags[...] = jnp.zeros(lags.shape, jnp.float32)
    for a in range(near):
        for f in range(count):
            start = (a * count + f) * rows
            lags[f * 8 + a : f * 8 + a + 1, :] = jnp.sum(product[start : start + rows], axis=0, keepdims=True)
    back = 4 * lanes - 1 - base[0, 0]
    across = lax.broadcasted_iota(jnp.int32, (8, lanes), 0)
    lane = lane_of((8, lanes))
    packed = jnp.zeros((8, lanes), jnp.float32)
    for f in range(count):
        block = lags[f * 8 : f * 8 + 8, :]
        for j in range(reach):
            at = (f * reach + j) * reach
            there = back + at - (j // near) * 2 * slot
            high = pltpu.roll(block, there & (lanes - 1), 1)
            low = pltpu.roll(block, (there - slot) & (lanes - 1), 1)
            member = (across == j % near) & (lane >= at) & (lane < at + reach)
            packed = packed + jnp.where(member, high + low, 0.0)
    lags[0:8, :] = jnp.zeros((8, lanes), jnp.float32)
    for f in range(count):
        lags[f : f + 1, :] = jnp.sum(power[f * 8 : f * 8 + 8, :], axis=0, keepdims=True)
    lags[count : count + 1, :] = jnp.sum(ref_power, axis=0, keepdims=True)
    powers = jnp.sum(lags[0:8, :], axis=1, keepdims=True)
    packed = packed + jnp.where(lane == count * reach * reach + across, powers, 0.0)
    packed = jnp.sum(packed, axis=0, keepdims=True)
    for place in range(2):
        offset = base[0, place].astype(jnp.float32)
        packed = jnp.where(lane[0:1] == lanes - 2 + place, offset, packed)
    part[...] = jnp.broadcast_to(packed, part.shape)


def spreader(clean, other, spread, base_col):
    height = clean.shape[1]
    size = height + other.shape[1]
    spare = spread.shape[0] - reach * size
    shifts = [column_shift(base_col + j - 3) for j in range(reach)]

    def spread_tile(t):
        at = tile_of(t)
        for j, shift in enumerate(shifts):
            spread[j * size : j * size + height, at] = shift(clean, t)
            spread[j * size + height : (j + 1) * size, at] = shift(other, t)
        spread[reach * size :, at] = jnp.zeros((spare, lanes), jnp.bfloat16)

    return spread_tile


def blend_terms(totals, count):
    lane = lane_of(totals.shape)
    block = reach * reach
    squared = totals * totals

    def pick(array, low, size):
        return jnp.sum(jnp.where((lane >= low) & (lane < low + size), array, 0.0), axis=1, keepdims=True)

    ref_power = pick(totals, count * block + count, 1)
    terms = []
    for f in range(count):
        norm_product = 0.05 * ((pick(totals, count * block + f, 1) + 1e-06) * (ref_power + 1e-06))
        terms.append((norm_product, 1.0 / (norm_product + pick(squared, f * block, block))))
    return squared, terms


def banded(weights, terms, f, rows, first_row, depth):
    wide = rows + 8
    blank = jnp.zeros((weights.shape[0], depth - lanes), jnp.float32)
    weights = jnp.concatenate([weights, blank], axis=1)
    lane = lane_of(weights.shape)
    line = jnp.zeros_like(weights)
    for j in range(reach):
        at = first_row + j * 2 * wide
        amount = at - (f * reach + j) * reach
        amount = jnp.where(amount < 0, amount + depth, amount)
        line = jnp.where((lane >= at) & (lane < at + reach), pltpu.roll(weights, amount, 1), line)
    band = by_row_shift(jnp.broadcast_to(line[0:1], (rows, depth)), rows, 1)
    middle = first_row + reach // 2 * (2 * wide + 1) + lax.broadcasted_iota(jnp.int32, band.shape, 0)
    band = (band + jnp.where(lane_of(band.shape) == middle, terms[0][0:1], 0.0)) * terms[1][0:1]
    odd = lax.axis_index("rows") % 2 == 1
    row = lane_of(band.shape) % (2 * wide)
    start = jnp.where(odd, 0, 8)
    inner = (row >= start) & (row < start + rows)
    first = pltpu.roll(jnp.where(inner, band, 0.0), jnp.where(odd, 0, depth - 8), 1)
    second = pltpu.roll(jnp.where(inner, 0.0, band), jnp.where(odd, 2 * rows - 16, 2 * rows), 1)
    return first + pltpu.roll(first, rows, 1) + second + pltpu.roll(second, 8, 1)


def pressures(base, totals, clean, other, spread, inverse):
    count, rows, columns = inverse.shape
    depth = spread.shape[0]
    squared, terms = blend_terms(jnp.broadcast_to(totals[0:1, :], (8, lanes)), count)
    bands = [banded(squared, terms[f], f, rows, 1 + base[0, 0], depth) for f in range(count)]
    mixing = cut(jnp.concatenate(bands, axis=0))
    spread_tile = spreader(clean, other, spread, base[0, 1])

    def chunk_values(t):
        where = chunk_of(t)
        spread_tile(2 * t)
        spread_tile(2 * t + 1)
        product = jnp.dot(mixing, spread[:, where], preferred_element_type=jnp.float32)
        registered = product[: count * rows] + product[count * rows :]
        values = []
        for f in range(count):
            ratio = registered[f * rows : (f + 1) * rows] * inverse[f, :, where]
            values.append(calib_zero + ratio * (calib_linear + calib_square * ratio))
        return values

    return chunk_values


def pressure_kernel(base, totals, clean, other, inverse, pressure, moments, part, spread):
    count, rows, columns = inverse.shape
    chunk_values = pressures(base, totals, clean, other, spread, inverse)

    def step(t, sums):
        where = chunk_of(t)
        values = chunk_values(t)
        squares = [value * value for value in values]
        for f in range(count):
            pressure[f, :, where] = values[f]
        moments[0, :, where] = sum(values[1:], values[0])
        moments[1, :, where] = sum(squares[1:], squares[0])
        result = []
        for total, array in zip(sums, values + squares):
            result.append(total + fold(array[:, :lanes]) + fold(array[:, lanes:]))
        return tuple(result)

    zero = jnp.zeros((8, lanes), jnp.float32)
    sums = by_tiles(step, columns // (2 * lanes), columns // (2 * lanes), (zero,) * (2 * count))
    line = zero
    for k in range(2 * count):
        value = jnp.sum(jnp.sum(sums[k], axis=0, keepdims=True), axis=1, keepdims=True)
        line = line + jnp.where(lane_of(line.shape) == k, value, 0.0)
    part[...] = jnp.broadcast_to(line[0:1], part.shape)


def time_kernel(base, totals, clean, other, inverse, moments, time_mean, time_rms, spread):
    count, rows, columns = inverse.shape
    chunk_values = pressures(base, totals, clean, other, spread, inverse)
    frames = 2 * count

    def step(t, carry):
        where = chunk_of(t)
        first = moments[0, :, where]
        second = moments[1, :, where]
        for value in chunk_values(t):
            first = first + value
            second = second + value * value
        mean = first * (1.0 / frames)
        time_mean[:, where] = mean
        time_rms[:, where] = jnp.sqrt(jnp.maximum(second * (1.0 / frames) - mean * mean, 0.0))
        return carry

    by_tiles(step, columns // (2 * lanes), columns // (2 * lanes))


def paired(value, axis, first):
    size = lax.axis_size(axis)
    partner = list(range(size))
    for i in range(first, size - 1, 2):
        partner[i], partner[i + 1] = i + 1, i
    return lax.ppermute(value, axis, list(enumerate(partner)))


def by_parity(odd, array, height, dim):
    length = array.shape[dim]
    low = lax.slice_in_dim(array, 0, height, axis=dim)
    high = lax.slice_in_dim(array, length - height, length, axis=dim)
    return jnp.where(odd, high, low), jnp.where(odd, low, high)


def from_owner(shard, here, odd, axis, root):
    mine = lax.axis_index(axis) == root
    height = shard.shape[0] // 2
    if lax.axis_size(axis) != 2:
        whole = lax.psum(jnp.where(mine, shard, jnp.zeros_like(shard)), axis)
        return by_parity(odd, whole, height, 0)
    there = by_parity(odd, paired(shard, axis, 0), height, 0)
    here = by_parity(odd, here, height, 0)
    return [jnp.where(mine, own, other) for own, other in zip(here, there)]


def total_over(value, axis):
    size = lax.axis_size(axis)
    if size & (size - 1):
        return lax.psum(value, axis)
    step = 1
    while step < size:
        value = value + lax.ppermute(value, axis, [(i, i ^ step) for i in range(size)])
        step *= 2
    return value


def shards(frames_raw, wind_off, run_owner, search_base):
    count, rows, columns = frames_raw.shape
    tiles = columns // lanes
    ring = tiles + 2
    wide = rows + 8
    depth = near * count * rows
    size = lax.axis_size("rows")
    f32 = jnp.float32
    bf16 = jnp.bfloat16
    struct = functools.partial(jax.ShapeDtypeStruct, dtype=f32)
    odd = lax.axis_index("rows") % 2 == 1
    raw, run = lax.optimization_barrier((jnp.maximum(frames_raw, 0.0), jnp.maximum(wind_off[0], 0.0)))
    owner, offsets = lax.optimization_barrier((run_owner, jnp.clip(search_base, -8, 8)))
    own_odd, own_even = from_owner(wind_off[0], run, odd, "frames", owner[0])
    from_odd = paired(own_odd, "rows", 1)
    from_even = paired(own_even, "rows", 0)
    frames_odd, frames_even = by_parity(odd, raw, 4, 1)
    frames_odd = paired(frames_odd, "rows", 1)
    frames_even = paired(frames_even, "rows", 0)
    frames_odd, own_odd = lax.optimization_barrier((frames_odd, own_odd))
    inverse, stack, power, band = pl.pallas_call(
        smooth_kernel,
        out_shape=(
            struct((count, rows, columns)),
            jax.ShapeDtypeStruct((2 * depth, ring * lanes), bf16),
            struct((8 * count, lanes)),
            jax.ShapeDtypeStruct((4 * lanes, 2 * lanes), bf16),
        ),
        in_specs=[vmem] * 3,
        out_specs=(vmem,) * 4,
        scratch_shapes=[
            pltpu.VMEM((count, tiles, rows + 16, lanes), f32),
            pltpu.VMEM((tiles // 2, 2 * count * rows, 4 * lanes), bf16),
            pltpu.VMEM((ring + 2, 2 * count * rows, lanes), bf16),
        ],
        compiler_params=params,
        cost_estimate=cost(8),
        name="smooth",
    )(raw, frames_odd, frames_even)
    blocks = lax.axis_size("frames")
    peers = size * blocks if blocks == 2 else size
    if blocks == 2:
        other_inverse = paired(inverse, "frames", 0)
    def reference_scratch(height):
        return [
            pltpu.VMEM((tiles, height + 8, lanes), f32),
            pltpu.VMEM((tiles // 2, 2 * height, 4 * lanes), bf16),
            pltpu.VMEM((ring + 2, 2 * height, lanes), bf16),
            pltpu.VMEM((far * 2 * height, ring * lanes), bf16),
            pltpu.VMEM((depth, lanes), f32),
        ]

    clean, near_lags, near_power = pl.pallas_call(
        near_kernel,
        out_shape=(
            jax.ShapeDtypeStruct((tiles + 2, 2 * rows, lanes), bf16),
            struct((depth, lanes)),
            struct((8, lanes)),
        ),
        in_specs=[smem] + [vmem] * 5,
        out_specs=(vmem,) * 3,
        scratch_shapes=reference_scratch(rows),
        compiler_params=params,
        cost_estimate=cost(8),
        name="near",
    )(offsets, own_odd, own_even, from_even, stack, band)
    other, part = pl.pallas_call(
        match_kernel,
        out_shape=(jax.ShapeDtypeStruct((tiles + 2, 16, lanes), bf16), struct((peers, lanes))),
        in_specs=[smem] + [vmem] * 7,
        out_specs=(vmem,) * 2,
        scratch_shapes=reference_scratch(8) + [pltpu.VMEM((8 * count, lanes), f32)],
        compiler_params=params,
        cost_estimate=cost(8),
        name="match",
    )(offsets, own_odd, from_odd, near_lags, near_power, stack, power, band)
    if blocks == 2:
        parts = lax.all_to_all(part, ("rows", "frames"), 0, 0, tiled=True).reshape(size, blocks, lanes)
        mine = lax.axis_index("frames") == 0
        both = jnp.sum(parts, axis=0)
        totals = jnp.where(mine, both[0:1], both[1:2])
        row = jnp.where(mine, both[1:2], both[0:1])
        place = jnp.where(mine, parts[0, 1:2], parts[0, 0:1])[:, lanes - 2 :].astype(jnp.int32)
    else:
        totals = jnp.sum(lax.all_to_all(part, "rows", 0, 0, tiled=True), axis=0, keepdims=True)
    depth = -(-reach * 2 * wide // lanes) * lanes
    spread = pltpu.VMEM((depth, columns), bf16)
    pressure, moments, part = pl.pallas_call(
        pressure_kernel,
        out_shape=(struct((count, rows, columns)), struct((2, rows, columns)), struct((size, lanes))),
        in_specs=[smem] + [vmem] * 4,
        out_specs=(vmem, vmem, vmem),
        scratch_shapes=[spread],
        compiler_params=params,
        cost_estimate=cost(12),
        name="pressure",
    )(offsets, totals, clean, other, inverse)
    if blocks == 2:
        time_mean, time_rms = pl.pallas_call(
            time_kernel,
            out_shape=(struct((rows, columns)), struct((rows, columns))),
            in_specs=[smem] + [vmem] * 5,
            out_specs=(vmem, vmem),
            scratch_shapes=[spread],
            compiler_params=params,
            cost_estimate=cost(12),
            name="time",
        )(place, row, clean, other, other_inverse, moments)
    else:
        whole = total_over(moments, "frames")
        total_frames = count * blocks
        time_mean = whole[0] / total_frames
        time_rms = jnp.sqrt(jnp.maximum(whole[1] / total_frames - time_mean * time_mean, 0.0))
    sums = lax.all_to_all(part, "rows", 0, 0, tiled=True)
    sums, time_mean, time_rms = lax.optimization_barrier((sums, time_mean, time_rms))
    spatial = jnp.sum(sums, axis=0)
    cell_count = rows * columns * size
    frame_mean = spatial[:count] / cell_count
    frame_rms = jnp.sqrt(spatial[count : 2 * count] / cell_count - frame_mean * frame_mean)
    return (pressure, frame_mean, frame_rms, time_mean, time_rms)


def solution(mesh):
    placed = (P("frames", "rows", None), P("frames", "rows", None), P("rows"), P("frames", None))
    return jax.shard_map(
        shards,
        mesh=mesh,
        in_specs=placed,
        out_specs=(
            P("frames", "rows", None),
            P("frames"),
            P("frames"),
            P("rows", None),
            P("rows", None),
        ),
        check_vma=False,
    )
```

```python
import functools

import jax
import jax.numpy as jnp
from jax import lax
from jax.experimental import pallas as pl
from jax.experimental.pallas import tpu as pltpu
from jax.sharding import PartitionSpec as P

taps = (1.0 / 256, 8.0 / 256, 28.0 / 256, 56.0 / 256, 70.0 / 256)
calib_zero = -0.25
calib_linear = 1.0
calib_square = 0.15
lanes = 128
reach = 7
near = 4
far = 2
slot = 32
params = pltpu.CompilerParams(vmem_limit_bytes=14 * 1024 * 1024)
vmem = pl.BlockSpec(memory_space=pltpu.VMEM)
smem = pl.BlockSpec(memory_space=pltpu.SMEM)


def cost(mebibytes):
    return pl.CostEstimate(flops=0, bytes_accessed=mebibytes * 2**20, transcendentals=0)


def tile_of(index):
    if isinstance(index, int):
        return slice(index * lanes, (index + 1) * lanes)
    return pl.ds(pl.multiple_of(index * lanes, lanes), lanes)


def by_tiles(step, tiles, group, init=()):
    if group == tiles:
        for index in range(tiles):
            init = step(index, init)
        return init

    def body(index, carry):
        for inner in range(group):
            carry = step(index * group + inner, carry)
        return carry

    return lax.fori_loop(0, tiles // group, body, init)


def lane_of(shape):
    return lax.broadcasted_iota(jnp.int32, shape, len(shape) - 1)


def fold(product):
    return jnp.sum(product.reshape(product.shape[0] // 8, 8, lanes), axis=0)


def vertical(load):
    total = taps[4] * load(4)
    for step in range(4):
        total = total + taps[step] * (load(step) + load(8 - step))
    return total


def moved(before, here, after, step):
    if step > 0:
        return pltpu.roll(jnp.where(lane_of(here.shape) < step, after, here), lanes - step, 1)
    if step < 0:
        return pltpu.roll(jnp.where(lane_of(here.shape) >= lanes + step, before, here), -step, 1)
    return here


def halves(value):
    high = value.astype(jnp.bfloat16)
    low = (value - high.astype(jnp.float32)).astype(jnp.bfloat16)
    return high, low


def cut(value):
    return jnp.concatenate(halves(value), axis=0)


def fill_band(band):
    shape = (lanes, lanes)
    apart = lax.broadcasted_iota(jnp.int32, shape, 0) - lax.broadcasted_iota(jnp.int32, shape, 1)

    def block(offset):
        distance = jnp.abs(apart + offset)
        value = jnp.zeros(shape, jnp.float32)
        for step in range(5):
            value = jnp.where(distance == step, taps[4 - step], value)
        return value.astype(jnp.bfloat16)

    none = jnp.zeros(shape, jnp.bfloat16)
    before, here, after = block(-lanes), block(0), block(lanes)
    for index, pair in enumerate(((before, none), (here, before), (after, here), (none, after))):
        band[index * lanes : (index + 1) * lanes, :] = jnp.concatenate(pair, axis=1)


def chunk_of(t):
    if isinstance(t, int):
        return slice(t * 2 * lanes, (t + 1) * 2 * lanes)
    return pl.ds(pl.multiple_of(t * 2 * lanes, 2 * lanes), 2 * lanes)


def place_tile(windows, index, value):
    for c in (index // 2 - 1, index // 2):
        at = index - 2 * c
        if 0 <= c < windows.shape[0] and at < 4:
            windows[c, :, at * lanes : (at + 1) * lanes] = value


def horizontal(windows, band):
    chunks, height, width = windows.shape
    product = jnp.dot(
        windows[...].reshape(chunks * height, width), band[...], preferred_element_type=jnp.float32
    )
    product = product.reshape(chunks, height, 2 * lanes)
    return product[:, : height // 2] + product[:, height // 2 :]


def by_row_shift(value, rows, direction):
    place = lax.broadcasted_iota(jnp.int32, value.shape, 0) % rows
    unit = 1
    while unit < rows:
        digit = (place // unit) % 4
        result = value
        for times in range(1, 4):
            amount = times * unit
            turned = pltpu.roll(value, amount if direction > 0 else value.shape[1] - amount, 1)
            result = jnp.where(digit == times, turned, result)
        value = result
        unit *= 4
    return value


def at_edge():
    index = lax.axis_index("rows")
    return (index == 0) | (index == lax.axis_size("rows") - 1)


def smooth_kernel(frames, from_odd, from_even, inverse, stack, power, band, rows_in, wide, pieces):
    count, rows, columns = frames.shape
    tiles = columns // lanes
    ring = tiles + 2
    odd = lax.axis_index("rows") % 2 == 1
    edge = at_edge()
    blank = jnp.zeros((2 * count * rows, lanes), jnp.bfloat16)
    place_tile(wide, 0, blank)
    place_tile(wide, tiles + 1, blank)
    fill_band(band)
    pieces[0] = blank
    pieces[tiles + 1] = blank
    pieces[tiles + 2] = blank

    def load_step(t, carry):
        for f in range(count):
            outer = jnp.where(edge, 0.0, from_odd[f, :, tile_of(t)])
            inner = from_even[f, :, tile_of(t)]
            rows_in[f, t, 4:8, :] = jnp.where(odd, inner, outer)
            rows_in[f, t, 8 : 8 + rows, :] = frames[f, :, tile_of(t)]
            rows_in[f, t, 8 + rows : 12 + rows, :] = jnp.where(odd, outer, inner)
        return carry

    def vertical_step(t, carry):
        parts = [vertical(lambda s: rows_in[f, t, pl.ds(4 + s, rows), :]) for f in range(count)]
        place_tile(wide, t + 1, cut(jnp.concatenate(parts, axis=0)))
        return carry

    def horizontal_step(t, totals):
        smooth = smoothed[t]
        result = []
        details = []
        for f in range(count):
            part = smooth[f * rows : (f + 1) * rows]
            inverse[f, :, chunk_of(t)] = 1.0 / part
            details.append(frames[f, :, chunk_of(t)] - part)
            square = details[f] * details[f]
            result.append(totals[f] + fold(square[:, :lanes]) + fold(square[:, lanes:]))
        detail = cut(jnp.concatenate(details, axis=0))
        pieces[2 * t + 1] = detail[:, :lanes]
        pieces[2 * t + 2] = detail[:, lanes:]
        return tuple(result)

    def stack_step(t, carry):
        before, here, after = pieces[t], pieces[t + 1], pieces[t + 2]
        size = count * rows
        for a in range(near):
            turned = moved(before, here, after, 1 - a)
            stack[a * size : (a + 1) * size, tile_of(t)] = turned[:size]
            stack[(near + a) * size : (near + a + 1) * size, tile_of(t)] = turned[size:]
        return carry

    powers = (jnp.zeros((8, lanes), jnp.float32),) * count
    for t in range(tiles):
        load_step(t, 0)
        vertical_step(t, 0)
    smoothed = horizontal(wide, band)
    for t in range(tiles // 2):
        powers = horizontal_step(t, powers)
    for f in range(count):
        power[f * 8 : f * 8 + 8, :] = powers[f]
    pieces[tiles + 3] = pieces[1]
    by_tiles(stack_step, ring, ring)


def column_shift(offset):
    negative = offset < 0
    first = jnp.where(negative, 0, 1)
    amount = jnp.where(negative, offset + lanes, offset)
    back = (lanes - amount) & (lanes - 1)

    def shift(source, t):
        here = source[t + first]
        after = source[t + first + 1]
        return pltpu.roll(jnp.where(lane_of(here.shape) < amount, after, here), back, 1)

    return shift


def reference_rows(raw, smooth, clean, fine, tiles):
    height = clean.shape[1] // 2
    empty = jnp.zeros((2 * height, lanes), jnp.bfloat16)
    for array in (clean, fine):
        array[0] = empty
        array[tiles + 1] = empty
    fine[tiles + 2] = empty
    squares = []
    for t in range(tiles // 2):
        detail = jnp.concatenate([raw(2 * t), raw(2 * t + 1)], axis=1) - smooth(t)
        for array, value in ((clean, cut(smooth(t))), (fine, cut(detail))):
            array[2 * t + 1] = value[:, :lanes]
            array[2 * t + 2] = value[:, lanes:]
        squares.append(detail * detail)
    fine[tiles + 3] = fine[1]
    return squares


def lag_products(stack, fine, stream, folded, base_col, start):
    height = fine.shape[1]
    half = height // 2
    shifts = [column_shift(base_col + near * b - 2) for b in range(far)]
    for t in range(fine.shape[0] - 2):
        for b, shift in enumerate(shifts):
            stream[b * height : (b + 1) * height, tile_of(t)] = shift(fine, t)
    product = lax.dot_general(
        stack[...], stream[...], (((1,), (1,)), ((), ())), preferred_element_type=jnp.float32
    )
    size = product.shape[0] // 2
    folded[...] = jnp.zeros(folded.shape, jnp.float32)
    folded[:, 0 : far * height] = product[:size] + product[size:]
    product = folded[...]
    lane = lane_of(product.shape)
    placed = jnp.zeros_like(product)
    for s in range(2 * far):
        at = s * slot + start
        turned = pltpu.roll(product, at - s * half, 1)
        placed = jnp.where((lane >= at) & (lane < at + half), turned, placed)
    return placed


def near_kernel(
    base, own_odd, own_even, from_even, stack, band, clean, lags, power, rows_in, windows, fine, stream, folded
):
    tiles = own_odd.shape[1] // lanes
    odd = lax.axis_index("rows") % 2 == 1
    height = clean.shape[1] // 2
    empty = jnp.zeros((2 * height, lanes), jnp.bfloat16)
    place_tile(windows, 0, empty)
    place_tile(windows, tiles + 1, empty)
    for t in range(tiles):
        at = tile_of(t)
        outer = own_odd[:, at]
        inner = from_even[:, at]
        rows_in[t, 0:8, :] = jnp.where(odd, inner, outer)
        rows_in[t, 8:16, :] = own_even[:, at]
        rows_in[t, 16:24, :] = jnp.where(odd, outer, inner)
        place_tile(windows, t + 1, cut(vertical(lambda s: rows_in[t, pl.ds(s, height), :])))
    smooth = horizontal(windows, band)
    squares = reference_rows(lambda t: rows_in[t, pl.ds(4, height), :], lambda t: smooth[t], clean, fine, tiles)
    place = lax.broadcasted_iota(jnp.int32, squares[0].shape, 0)
    first = jnp.where(odd, 4, 0)
    own = (place >= first) & (place < first + height - 4)
    total = jnp.zeros((8, lanes), jnp.float32)
    for square in squares:
        square = jnp.where(own, square, 0.0)
        total = total + fold(square[:, :lanes]) + fold(square[:, lanes:])
    power[...] = total
    lags[...] = lag_products(stack, fine, stream, folded, base[0, 1], jnp.where(odd, 0, 8))


def match_kernel(
    base, own_odd, from_odd, near_lags, near_power, stack, power, band, clean, part, rows_in, windows, fine, stream, folded, lags
):
    tiles = own_odd.shape[1] // lanes
    count = power.shape[0] // 8
    rows = folded.shape[0] // (near * count)
    odd = lax.axis_index("rows") % 2 == 1
    edge = at_edge()
    height = clean.shape[1] // 2
    empty = jnp.zeros((2 * height, lanes), jnp.bfloat16)
    place_tile(windows, 0, empty)
    place_tile(windows, tiles + 1, empty)
    for t in range(tiles):
        at = tile_of(t)
        outer = jnp.where(edge, 0.0, from_odd[:, at])
        inner = own_odd[:, at]
        rows_in[t, 0:8, :] = jnp.where(odd, inner, outer)
        rows_in[t, 8:16, :] = jnp.where(odd, outer, inner)
        place_tile(windows, t + 1, cut(vertical(lambda s: rows_in[t, pl.ds(s, height), :])))
    smooth = horizontal(windows, band)
    place = lax.broadcasted_iota(jnp.int32, (height, 2 * lanes), 0)
    first = jnp.where(odd, 0, 4)
    own = (place >= first) & (place < first + 4)
    inside = (place >= jnp.where(edge, first, 0)) & (place < jnp.where(edge, first + 4, height))

    def masked(t):
        return jnp.where(inside, smooth[t], 0.0)

    squares = reference_rows(lambda t: rows_in[t, pl.ds(4, height), :], masked, clean, fine, tiles)
    ref_power = near_power[...]
    for square in squares:
        square = jnp.where(own, square, 0.0)
        ref_power = ref_power + fold(square[:, :lanes]) + fold(square[:, lanes:])
    product = lag_products(stack, fine, stream, folded, base[0, 1], jnp.where(odd, 16, 0))
    product = by_row_shift(product + near_lags[...], rows, -1)
    lags[...] = jnp.zeros(lags.shape, jnp.float32)
    for a in range(near):
        for f in range(count):
            start = (a * count + f) * rows
            lags[f * 8 + a : f * 8 + a + 1, :] = jnp.sum(product[start : start + rows], axis=0, keepdims=True)
    back = 4 * lanes - 1 - base[0, 0]
    across = lax.broadcasted_iota(jnp.int32, (8, lanes), 0)
    lane = lane_of((8, lanes))
    packed = jnp.zeros((8, lanes), jnp.float32)
    for f in range(count):
        block = lags[f * 8 : f * 8 + 8, :]
        for j in range(reach):
            at = (f * reach + j) * reach
            there = back + at - (j // near) * 2 * slot
            high = pltpu.roll(block, there & (lanes - 1), 1)
            low = pltpu.roll(block, (there - slot) & (lanes - 1), 1)
            member = (across == j % near) & (lane >= at) & (lane < at + reach)
            packed = packed + jnp.where(member, high + low, 0.0)
    lags[0:8, :] = jnp.zeros((8, lanes), jnp.float32)
    for f in range(count):
        lags[f : f + 1, :] = jnp.sum(power[f * 8 : f * 8 + 8, :], axis=0, keepdims=True)
    lags[count : count + 1, :] = jnp.sum(ref_power, axis=0, keepdims=True)
    powers = jnp.sum(lags[0:8, :], axis=1, keepdims=True)
    packed = packed + jnp.where(lane == count * reach * reach + across, powers, 0.0)
    packed = jnp.sum(packed, axis=0, keepdims=True)
    for place in range(2):
        offset = base[0, place].astype(jnp.float32)
        packed = jnp.where(lane[0:1] == lanes - 2 + place, offset, packed)
    part[...] = jnp.broadcast_to(packed, part.shape)


def spreader(clean, other, spread, base_col):
    height = clean.shape[1]
    size = height + other.shape[1]
    spare = spread.shape[0] - reach * size
    shifts = [column_shift(base_col + j - 3) for j in range(reach)]

    def spread_tile(t):
        at = tile_of(t)
        for j, shift in enumerate(shifts):
            spread[j * size : j * size + height, at] = shift(clean, t)
            spread[j * size + height : (j + 1) * size, at] = shift(other, t)
        spread[reach * size :, at] = jnp.zeros((spare, lanes), jnp.bfloat16)

    return spread_tile


def blend_terms(totals, count):
    lane = lane_of(totals.shape)
    block = reach * reach
    squared = totals * totals

    def pick(array, low, size):
        return jnp.sum(jnp.where((lane >= low) & (lane < low + size), array, 0.0), axis=1, keepdims=True)

    ref_power = pick(totals, count * block + count, 1)
    terms = []
    for f in range(count):
        norm_product = 0.05 * ((pick(totals, count * block + f, 1) + 1e-06) * (ref_power + 1e-06))
        terms.append((norm_product, 1.0 / (norm_product + pick(squared, f * block, block))))
    return squared, terms


def banded(weights, terms, f, rows, first_row, depth):
    wide = rows + 8
    blank = jnp.zeros((weights.shape[0], depth - lanes), jnp.float32)
    weights = jnp.concatenate([weights, blank], axis=1)
    lane = lane_of(weights.shape)
    line = jnp.zeros_like(weights)
    for j in range(reach):
        at = first_row + j * 2 * wide
        amount = at - (f * reach + j) * reach
        amount = jnp.where(amount < 0, amount + depth, amount)
        line = jnp.where((lane >= at) & (lane < at + reach), pltpu.roll(weights, amount, 1), line)
    band = by_row_shift(jnp.broadcast_to(line[0:1], (rows, depth)), rows, 1)
    middle = first_row + reach // 2 * (2 * wide + 1) + lax.broadcasted_iota(jnp.int32, band.shape, 0)
    band = (band + jnp.where(lane_of(band.shape) == middle, terms[0][0:1], 0.0)) * terms[1][0:1]
    odd = lax.axis_index("rows") % 2 == 1
    row = lane_of(band.shape) % (2 * wide)
    start = jnp.where(odd, 0, 8)
    inner = (row >= start) & (row < start + rows)
    first = pltpu.roll(jnp.where(inner, band, 0.0), jnp.where(odd, 0, depth - 8), 1)
    second = pltpu.roll(jnp.where(inner, 0.0, band), jnp.where(odd, 2 * rows - 16, 2 * rows), 1)
    return first + pltpu.roll(first, rows, 1) + second + pltpu.roll(second, 8, 1)


def pressures(base, totals, clean, other, spread, inverse):
    count, rows, columns = inverse.shape
    depth = spread.shape[0]
    squared, terms = blend_terms(jnp.broadcast_to(totals[0:1, :], (8, lanes)), count)
    bands = [banded(squared, terms[f], f, rows, 1 + base[0, 0], depth) for f in range(count)]
    mixing = cut(jnp.concatenate(bands, axis=0))
    spread_tile = spreader(clean, other, spread, base[0, 1])

    def chunk_values(t):
        where = chunk_of(t)
        spread_tile(2 * t)
        spread_tile(2 * t + 1)
        product = jnp.dot(mixing, spread[:, where], preferred_element_type=jnp.float32)
        registered = product[: count * rows] + product[count * rows :]
        values = []
        for f in range(count):
            ratio = registered[f * rows : (f + 1) * rows] * inverse[f, :, where]
            values.append(calib_zero + ratio * (calib_linear + calib_square * ratio))
        return values

    return chunk_values


def pressure_kernel(base, totals, clean, other, inverse, pressure, moments, part, spread):
    count, rows, columns = inverse.shape
    chunk_values = pressures(base, totals, clean, other, spread, inverse)

    def step(t, sums):
        where = chunk_of(t)
        values = chunk_values(t)
        squares = [value * value for value in values]
        for f in range(count):
            pressure[f, :, where] = values[f]
        moments[0, :, where] = sum(values[1:], values[0])
        moments[1, :, where] = sum(squares[1:], squares[0])
        result = []
        for total, array in zip(sums, values + squares):
            result.append(total + fold(array[:, :lanes]) + fold(array[:, lanes:]))
        return tuple(result)

    zero = jnp.zeros((8, lanes), jnp.float32)
    sums = by_tiles(step, columns // (2 * lanes), columns // (2 * lanes), (zero,) * (2 * count))
    line = zero
    for k in range(2 * count):
        value = jnp.sum(jnp.sum(sums[k], axis=0, keepdims=True), axis=1, keepdims=True)
        line = line + jnp.where(lane_of(line.shape) == k, value, 0.0)
    part[...] = jnp.broadcast_to(line[0:1], part.shape)


def time_kernel(base, totals, clean, other, inverse, moments, time_mean, time_rms, spread):
    count, rows, columns = inverse.shape
    chunk_values = pressures(base, totals, clean, other, spread, inverse)
    frames = 2 * count

    def step(t, carry):
        where = chunk_of(t)
        first = moments[0, :, where]
        second = moments[1, :, where]
        for value in chunk_values(t):
            first = first + value
            second = second + value * value
        mean = first * (1.0 / frames)
        time_mean[:, where] = mean
        time_rms[:, where] = jnp.sqrt(jnp.maximum(second * (1.0 / frames) - mean * mean, 0.0))
        return carry

    by_tiles(step, columns // (2 * lanes), columns // (2 * lanes))


def paired(value, axis, first):
    size = lax.axis_size(axis)
    partner = list(range(size))
    for i in range(first, size - 1, 2):
        partner[i], partner[i + 1] = i + 1, i
    return lax.ppermute(value, axis, list(enumerate(partner)))


def by_parity(odd, array, height, dim):
    length = array.shape[dim]
    low = lax.slice_in_dim(array, 0, height, axis=dim)
    high = lax.slice_in_dim(array, length - height, length, axis=dim)
    return jnp.where(odd, high, low), jnp.where(odd, low, high)


def from_owner(shard, here, odd, axis, root):
    mine = lax.axis_index(axis) == root
    height = shard.shape[0] // 2
    if lax.axis_size(axis) != 2:
        whole = lax.psum(jnp.where(mine, shard, jnp.zeros_like(shard)), axis)
        return by_parity(odd, whole, height, 0)
    there = by_parity(odd, paired(shard, axis, 0), height, 0)
    here = by_parity(odd, here, height, 0)
    return [jnp.where(mine, own, other) for own, other in zip(here, there)]


def middle_first(size):
    order = sorted(range(size), key=lambda i: (abs(2 * i + 1 - size), i))
    return order


def total_over(value, axis):
    size = lax.axis_size(axis)
    if size & (size - 1):
        return lax.psum(value, axis)
    step = 1
    while step < size:
        value = value + lax.ppermute(value, axis, [(i, i ^ step) for i in range(size)])
        step *= 2
    return value


def shards(frames_raw, wind_off, run_owner, search_base):
    count, rows, columns = frames_raw.shape
    tiles = columns // lanes
    ring = tiles + 2
    wide = rows + 8
    depth = near * count * rows
    size = lax.axis_size("rows")
    f32 = jnp.float32
    bf16 = jnp.bfloat16
    struct = functools.partial(jax.ShapeDtypeStruct, dtype=f32)
    odd = lax.axis_index("rows") % 2 == 1
    raw, run = lax.optimization_barrier((jnp.maximum(frames_raw, 0.0), jnp.maximum(wind_off[0], 0.0)))
    owner, offsets = lax.optimization_barrier((run_owner, jnp.clip(search_base, -8, 8)))
    own_odd, own_even = from_owner(wind_off[0], run, odd, "frames", owner[0])
    from_odd = paired(own_odd, "rows", 1)
    from_even = paired(own_even, "rows", 0)
    frames_odd, frames_even = by_parity(odd, raw, 4, 1)
    frames_odd = paired(frames_odd, "rows", 1)
    frames_even = paired(frames_even, "rows", 0)
    frames_odd, own_odd = lax.optimization_barrier((frames_odd, own_odd))
    inverse, stack, power, band = pl.pallas_call(
        smooth_kernel,
        out_shape=(
            struct((count, rows, columns)),
            jax.ShapeDtypeStruct((2 * depth, ring * lanes), bf16),
            struct((8 * count, lanes)),
            jax.ShapeDtypeStruct((4 * lanes, 2 * lanes), bf16),
        ),
        in_specs=[vmem] * 3,
        out_specs=(vmem,) * 4,
        scratch_shapes=[
            pltpu.VMEM((count, tiles, rows + 16, lanes), f32),
            pltpu.VMEM((tiles // 2, 2 * count * rows, 4 * lanes), bf16),
            pltpu.VMEM((ring + 2, 2 * count * rows, lanes), bf16),
        ],
        compiler_params=params,
        cost_estimate=cost(8),
        name="smooth",
    )(raw, frames_odd, frames_even)
    blocks = lax.axis_size("frames")
    peers = size * blocks if blocks == 2 else size
    if blocks == 2:
        other_inverse = paired(inverse, "frames", 0)
    def reference_scratch(height):
        return [
            pltpu.VMEM((tiles, height + 8, lanes), f32),
            pltpu.VMEM((tiles // 2, 2 * height, 4 * lanes), bf16),
            pltpu.VMEM((ring + 2, 2 * height, lanes), bf16),
            pltpu.VMEM((far * 2 * height, ring * lanes), bf16),
            pltpu.VMEM((depth, lanes), f32),
        ]

    clean, near_lags, near_power = pl.pallas_call(
        near_kernel,
        out_shape=(
            jax.ShapeDtypeStruct((tiles + 2, 2 * rows, lanes), bf16),
            struct((depth, lanes)),
            struct((8, lanes)),
        ),
        in_specs=[smem] + [vmem] * 5,
        out_specs=(vmem,) * 3,
        scratch_shapes=reference_scratch(rows),
        compiler_params=params,
        cost_estimate=cost(8),
        name="near",
    )(offsets, own_odd, own_even, from_even, stack, band)
    other, part = pl.pallas_call(
        match_kernel,
        out_shape=(jax.ShapeDtypeStruct((tiles + 2, 16, lanes), bf16), struct((peers, lanes))),
        in_specs=[smem] + [vmem] * 7,
        out_specs=(vmem,) * 2,
        scratch_shapes=reference_scratch(8) + [pltpu.VMEM((8 * count, lanes), f32)],
        compiler_params=params,
        cost_estimate=cost(8),
        name="match",
    )(offsets, own_odd, from_odd, near_lags, near_power, stack, power, band)
    if blocks == 2:
        order = [i * blocks + f for i in middle_first(size) for f in range(blocks)]
        parts = lax.all_to_all(part, ("rows", "frames"), 0, 0, axis_index_groups=[order], tiled=True)
        parts = parts.reshape(size, blocks, lanes)
        mine = lax.axis_index("frames") == 0
        both = jnp.sum(parts, axis=0)
        totals = jnp.where(mine, both[0:1], both[1:2])
        row = jnp.where(mine, both[1:2], both[0:1])
        place = jnp.where(mine, parts[0, 1:2], parts[0, 0:1])[:, lanes - 2 :].astype(jnp.int32)
    else:
        totals = jnp.sum(lax.all_to_all(part, "rows", 0, 0, tiled=True), axis=0, keepdims=True)
    depth = -(-reach * 2 * wide // lanes) * lanes
    spread = pltpu.VMEM((depth, columns), bf16)
    pressure, moments, part = pl.pallas_call(
        pressure_kernel,
        out_shape=(struct((count, rows, columns)), struct((2, rows, columns)), struct((size, lanes))),
        in_specs=[smem] + [vmem] * 4,
        out_specs=(vmem, vmem, vmem),
        scratch_shapes=[spread],
        compiler_params=params,
        cost_estimate=cost(12),
        name="pressure",
    )(offsets, totals, clean, other, inverse)
    if blocks == 2:
        time_mean, time_rms = pl.pallas_call(
            time_kernel,
            out_shape=(struct((rows, columns)), struct((rows, columns))),
            in_specs=[smem] + [vmem] * 5,
            out_specs=(vmem, vmem),
            scratch_shapes=[spread],
            compiler_params=params,
            cost_estimate=cost(12),
            name="time",
        )(place, row, clean, other, other_inverse, moments)
    else:
        whole = total_over(moments, "frames")
        total_frames = count * blocks
        time_mean = whole[0] / total_frames
        time_rms = jnp.sqrt(jnp.maximum(whole[1] / total_frames - time_mean * time_mean, 0.0))
    sums = lax.all_to_all(part, "rows", 0, 0, axis_index_groups=[middle_first(size)], tiled=True)
    sums, time_mean, time_rms = lax.optimization_barrier((sums, time_mean, time_rms))
    spatial = jnp.sum(sums, axis=0)
    cell_count = rows * columns * size
    frame_mean = spatial[:count] / cell_count
    frame_rms = jnp.sqrt(spatial[count : 2 * count] / cell_count - frame_mean * frame_mean)
    return (pressure, frame_mean, frame_rms, time_mean, time_rms)


def solution(mesh):
    placed = (P("frames", "rows", None), P("frames", "rows", None), P("rows"), P("frames", None))
    return jax.shard_map(
        shards,
        mesh=mesh,
        in_specs=placed,
        out_specs=(
            P("frames", "rows", None),
            P("frames"),
            P("frames"),
            P("rows", None),
            P("rows", None),
        ),
        check_vma=False,
    )
```

```python
import functools

import jax
import jax.numpy as jnp
from jax import lax
from jax.experimental import pallas as pl
from jax.experimental.pallas import tpu as pltpu
from jax.sharding import PartitionSpec as P

taps = (1.0 / 256, 8.0 / 256, 28.0 / 256, 56.0 / 256, 70.0 / 256)
calib_zero = -0.25
calib_linear = 1.0
calib_square = 0.15
lanes = 128
reach = 7
near = 4
far = 2
slot = 32
params = pltpu.CompilerParams(vmem_limit_bytes=14 * 1024 * 1024)
vmem = pl.BlockSpec(memory_space=pltpu.VMEM)
smem = pl.BlockSpec(memory_space=pltpu.SMEM)


def cost(mebibytes):
    return pl.CostEstimate(flops=0, bytes_accessed=mebibytes * 2**20, transcendentals=0)


def tile_of(index):
    if isinstance(index, int):
        return slice(index * lanes, (index + 1) * lanes)
    return pl.ds(pl.multiple_of(index * lanes, lanes), lanes)


def by_tiles(step, tiles, group, init=()):
    if group == tiles:
        for index in range(tiles):
            init = step(index, init)
        return init

    def body(index, carry):
        for inner in range(group):
            carry = step(index * group + inner, carry)
        return carry

    return lax.fori_loop(0, tiles // group, body, init)


def lane_of(shape):
    return lax.broadcasted_iota(jnp.int32, shape, len(shape) - 1)


def fold(product):
    return jnp.sum(product.reshape(product.shape[0] // 8, 8, lanes), axis=0)


def vertical(load):
    total = taps[4] * load(4)
    for step in range(4):
        total = total + taps[step] * (load(step) + load(8 - step))
    return total


def moved(before, here, after, step):
    if step > 0:
        return pltpu.roll(jnp.where(lane_of(here.shape) < step, after, here), lanes - step, 1)
    if step < 0:
        return pltpu.roll(jnp.where(lane_of(here.shape) >= lanes + step, before, here), -step, 1)
    return here


def halves(value):
    high = value.astype(jnp.bfloat16)
    low = (value - high.astype(jnp.float32)).astype(jnp.bfloat16)
    return high, low


def cut(value):
    return jnp.concatenate(halves(value), axis=0)


def fill_band(band):
    shape = (lanes, lanes)
    apart = lax.broadcasted_iota(jnp.int32, shape, 0) - lax.broadcasted_iota(jnp.int32, shape, 1)

    def block(offset):
        distance = jnp.abs(apart + offset)
        value = jnp.zeros(shape, jnp.float32)
        for step in range(5):
            value = jnp.where(distance == step, taps[4 - step], value)
        return value.astype(jnp.bfloat16)

    none = jnp.zeros(shape, jnp.bfloat16)
    before, here, after = block(-lanes), block(0), block(lanes)
    for index, pair in enumerate(((before, none), (here, before), (after, here), (none, after))):
        band[index * lanes : (index + 1) * lanes, :] = jnp.concatenate(pair, axis=1)


def chunk_of(t):
    if isinstance(t, int):
        return slice(t * 2 * lanes, (t + 1) * 2 * lanes)
    return pl.ds(pl.multiple_of(t * 2 * lanes, 2 * lanes), 2 * lanes)


def place_tile(windows, index, value):
    for c in (index // 2 - 1, index // 2):
        at = index - 2 * c
        if 0 <= c < windows.shape[0] and at < 4:
            windows[c, :, at * lanes : (at + 1) * lanes] = value


def horizontal(windows, band):
    chunks, height, width = windows.shape
    product = jnp.dot(
        windows[...].reshape(chunks * height, width), band[...], preferred_element_type=jnp.float32
    )
    product = product.reshape(chunks, height, 2 * lanes)
    return product[:, : height // 2] + product[:, height // 2 :]


def by_row_shift(value, rows, direction):
    place = lax.broadcasted_iota(jnp.int32, value.shape, 0) % rows
    unit = 1
    while unit < rows:
        digit = (place // unit) % 4
        result = value
        for times in range(1, 4):
            amount = times * unit
            turned = pltpu.roll(value, amount if direction > 0 else value.shape[1] - amount, 1)
            result = jnp.where(digit == times, turned, result)
        value = result
        unit *= 4
    return value


def at_edge():
    index = lax.axis_index("rows")
    return (index == 0) | (index == lax.axis_size("rows") - 1)


def smooth_kernel(frames, from_odd, from_even, inverse, stack, power, band, rows_in, wide, pieces):
    count, rows, columns = frames.shape
    tiles = columns // lanes
    ring = tiles + 2
    odd = lax.axis_index("rows") % 2 == 1
    edge = at_edge()
    blank = jnp.zeros((2 * count * rows, lanes), jnp.bfloat16)
    place_tile(wide, 0, blank)
    place_tile(wide, tiles + 1, blank)
    fill_band(band)
    pieces[0] = blank
    pieces[tiles + 1] = blank
    pieces[tiles + 2] = blank

    def load_step(t, carry):
        for f in range(count):
            outer = jnp.where(edge, 0.0, from_odd[f, :, tile_of(t)])
            inner = from_even[f, :, tile_of(t)]
            rows_in[f, t, 4:8, :] = jnp.where(odd, inner, outer)
            rows_in[f, t, 8 : 8 + rows, :] = frames[f, :, tile_of(t)]
            rows_in[f, t, 8 + rows : 12 + rows, :] = jnp.where(odd, outer, inner)
        return carry

    def vertical_step(t, carry):
        parts = [vertical(lambda s: rows_in[f, t, pl.ds(4 + s, rows), :]) for f in range(count)]
        place_tile(wide, t + 1, cut(jnp.concatenate(parts, axis=0)))
        return carry

    def horizontal_step(t, totals):
        smooth = smoothed[t]
        result = []
        details = []
        for f in range(count):
            part = smooth[f * rows : (f + 1) * rows]
            inverse[f, :, chunk_of(t)] = 1.0 / part
            details.append(frames[f, :, chunk_of(t)] - part)
            square = details[f] * details[f]
            result.append(totals[f] + fold(square[:, :lanes]) + fold(square[:, lanes:]))
        detail = cut(jnp.concatenate(details, axis=0))
        pieces[2 * t + 1] = detail[:, :lanes]
        pieces[2 * t + 2] = detail[:, lanes:]
        return tuple(result)

    def stack_step(t, carry):
        before, here, after = pieces[t], pieces[t + 1], pieces[t + 2]
        size = count * rows
        for a in range(near):
            turned = moved(before, here, after, 1 - a)
            stack[a * size : (a + 1) * size, tile_of(t)] = turned[:size]
            stack[(near + a) * size : (near + a + 1) * size, tile_of(t)] = turned[size:]
        return carry

    powers = (jnp.zeros((8, lanes), jnp.float32),) * count
    for t in range(tiles):
        load_step(t, 0)
        vertical_step(t, 0)
    smoothed = horizontal(wide, band)
    for t in range(tiles // 2):
        powers = horizontal_step(t, powers)
    for f in range(count):
        power[f * 8 : f * 8 + 8, :] = powers[f]
    pieces[tiles + 3] = pieces[1]
    by_tiles(stack_step, ring, ring)


def column_shift(offset):
    negative = offset < 0
    first = jnp.where(negative, 0, 1)
    amount = jnp.where(negative, offset + lanes, offset)
    back = (lanes - amount) & (lanes - 1)

    def shift(source, t):
        here = source[t + first]
        after = source[t + first + 1]
        return pltpu.roll(jnp.where(lane_of(here.shape) < amount, after, here), back, 1)

    return shift


def reference_rows(raw, smooth, clean, fine, tiles):
    height = clean.shape[1] // 2
    empty = jnp.zeros((2 * height, lanes), jnp.bfloat16)
    for array in (clean, fine):
        array[0] = empty
        array[tiles + 1] = empty
    fine[tiles + 2] = empty
    squares = []
    for t in range(tiles // 2):
        detail = jnp.concatenate([raw(2 * t), raw(2 * t + 1)], axis=1) - smooth(t)
        for array, value in ((clean, cut(smooth(t))), (fine, cut(detail))):
            array[2 * t + 1] = value[:, :lanes]
            array[2 * t + 2] = value[:, lanes:]
        squares.append(detail * detail)
    fine[tiles + 3] = fine[1]
    return squares


def lag_products(stack, fine, stream, folded, base_col, start):
    height = fine.shape[1]
    half = height // 2
    shifts = [column_shift(base_col + near * b - 2) for b in range(far)]
    for t in range(fine.shape[0] - 2):
        for b, shift in enumerate(shifts):
            stream[b * height : (b + 1) * height, tile_of(t)] = shift(fine, t)
    product = lax.dot_general(
        stack[...], stream[...], (((1,), (1,)), ((), ())), preferred_element_type=jnp.float32
    )
    size = product.shape[0] // 2
    folded[...] = jnp.zeros(folded.shape, jnp.float32)
    folded[:, 0 : far * height] = product[:size] + product[size:]
    product = folded[...]
    lane = lane_of(product.shape)
    placed = jnp.zeros_like(product)
    for s in range(2 * far):
        at = s * slot + start
        turned = pltpu.roll(product, at - s * half, 1)
        placed = jnp.where((lane >= at) & (lane < at + half), turned, placed)
    return placed


def near_kernel(
    base, own_odd, own_even, from_even, stack, band, clean, lags, power, rows_in, windows, fine, stream, folded
):
    tiles = own_odd.shape[1] // lanes
    odd = lax.axis_index("rows") % 2 == 1
    height = clean.shape[1] // 2
    empty = jnp.zeros((2 * height, lanes), jnp.bfloat16)
    place_tile(windows, 0, empty)
    place_tile(windows, tiles + 1, empty)
    for t in range(tiles):
        at = tile_of(t)
        outer = own_odd[:, at]
        inner = from_even[:, at]
        rows_in[t, 0:8, :] = jnp.where(odd, inner, outer)
        rows_in[t, 8:16, :] = own_even[:, at]
        rows_in[t, 16:24, :] = jnp.where(odd, outer, inner)
        place_tile(windows, t + 1, cut(vertical(lambda s: rows_in[t, pl.ds(s, height), :])))
    smooth = horizontal(windows, band)
    squares = reference_rows(lambda t: rows_in[t, pl.ds(4, height), :], lambda t: smooth[t], clean, fine, tiles)
    place = lax.broadcasted_iota(jnp.int32, squares[0].shape, 0)
    first = jnp.where(odd, 4, 0)
    own = (place >= first) & (place < first + height - 4)
    total = jnp.zeros((8, lanes), jnp.float32)
    for square in squares:
        square = jnp.where(own, square, 0.0)
        total = total + fold(square[:, :lanes]) + fold(square[:, lanes:])
    power[...] = total
    lags[...] = lag_products(stack, fine, stream, folded, base[0, 1], jnp.where(odd, 0, 8))


def match_kernel(
    base, own_odd, from_odd, near_lags, near_power, stack, power, band, clean, part, rows_in, windows, fine, stream, folded, lags
):
    tiles = own_odd.shape[1] // lanes
    count = power.shape[0] // 8
    rows = folded.shape[0] // (near * count)
    odd = lax.axis_index("rows") % 2 == 1
    edge = at_edge()
    height = clean.shape[1] // 2
    empty = jnp.zeros((2 * height, lanes), jnp.bfloat16)
    place_tile(windows, 0, empty)
    place_tile(windows, tiles + 1, empty)
    for t in range(tiles):
        at = tile_of(t)
        outer = jnp.where(edge, 0.0, from_odd[:, at])
        inner = own_odd[:, at]
        rows_in[t, 0:8, :] = jnp.where(odd, inner, outer)
        rows_in[t, 8:16, :] = jnp.where(odd, outer, inner)
        place_tile(windows, t + 1, cut(vertical(lambda s: rows_in[t, pl.ds(s, height), :])))
    smooth = horizontal(windows, band)
    place = lax.broadcasted_iota(jnp.int32, (height, 2 * lanes), 0)
    first = jnp.where(odd, 0, 4)
    own = (place >= first) & (place < first + 4)
    inside = (place >= jnp.where(edge, first, 0)) & (place < jnp.where(edge, first + 4, height))

    def masked(t):
        return jnp.where(inside, smooth[t], 0.0)

    squares = reference_rows(lambda t: rows_in[t, pl.ds(4, height), :], masked, clean, fine, tiles)
    ref_power = near_power[...]
    for square in squares:
        square = jnp.where(own, square, 0.0)
        ref_power = ref_power + fold(square[:, :lanes]) + fold(square[:, lanes:])
    product = lag_products(stack, fine, stream, folded, base[0, 1], jnp.where(odd, 16, 0))
    product = by_row_shift(product + near_lags[...], rows, -1)
    lags[...] = jnp.zeros(lags.shape, jnp.float32)
    for a in range(near):
        for f in range(count):
            start = (a * count + f) * rows
            lags[f * 8 + a : f * 8 + a + 1, :] = jnp.sum(product[start : start + rows], axis=0, keepdims=True)
    back = 4 * lanes - 1 - base[0, 0]
    across = lax.broadcasted_iota(jnp.int32, (8, lanes), 0)
    lane = lane_of((8, lanes))
    packed = jnp.zeros((8, lanes), jnp.float32)
    for f in range(count):
        block = lags[f * 8 : f * 8 + 8, :]
        for j in range(reach):
            at = (f * reach + j) * reach
            there = back + at - (j // near) * 2 * slot
            high = pltpu.roll(block, there & (lanes - 1), 1)
            low = pltpu.roll(block, (there - slot) & (lanes - 1), 1)
            member = (across == j % near) & (lane >= at) & (lane < at + reach)
            packed = packed + jnp.where(member, high + low, 0.0)
    lags[0:8, :] = jnp.zeros((8, lanes), jnp.float32)
    for f in range(count):
        lags[f : f + 1, :] = jnp.sum(power[f * 8 : f * 8 + 8, :], axis=0, keepdims=True)
    lags[count : count + 1, :] = jnp.sum(ref_power, axis=0, keepdims=True)
    powers = jnp.sum(lags[0:8, :], axis=1, keepdims=True)
    packed = packed + jnp.where(lane == count * reach * reach + across, powers, 0.0)
    packed = jnp.sum(packed, axis=0, keepdims=True)
    for place in range(2):
        offset = base[0, place].astype(jnp.float32)
        packed = jnp.where(lane[0:1] == lanes - 2 + place, offset, packed)
    part[...] = jnp.broadcast_to(packed, part.shape)


def spreader(clean, other, spread, base_col):
    height = clean.shape[1]
    size = height + other.shape[1]
    spare = spread.shape[0] - reach * size
    shifts = [column_shift(base_col + j - 3) for j in range(reach)]

    def spread_tile(t):
        at = tile_of(t)
        for j, shift in enumerate(shifts):
            spread[j * size : j * size + height, at] = shift(clean, t)
            spread[j * size + height : (j + 1) * size, at] = shift(other, t)
        spread[reach * size :, at] = jnp.zeros((spare, lanes), jnp.bfloat16)

    return spread_tile


def blend_terms(totals, count):
    lane = lane_of(totals.shape)
    block = reach * reach
    squared = totals * totals

    def pick(array, low, size):
        return jnp.sum(jnp.where((lane >= low) & (lane < low + size), array, 0.0), axis=1, keepdims=True)

    ref_power = pick(totals, count * block + count, 1)
    terms = []
    for f in range(count):
        norm_product = 0.05 * ((pick(totals, count * block + f, 1) + 1e-06) * (ref_power + 1e-06))
        terms.append((norm_product, 1.0 / (norm_product + pick(squared, f * block, block))))
    return squared, terms


def banded(weights, terms, f, rows, first_row, depth):
    wide = rows + 8
    blank = jnp.zeros((weights.shape[0], depth - lanes), jnp.float32)
    weights = jnp.concatenate([weights, blank], axis=1)
    lane = lane_of(weights.shape)
    line = jnp.zeros_like(weights)
    for j in range(reach):
        at = first_row + j * 2 * wide
        amount = at - (f * reach + j) * reach
        amount = jnp.where(amount < 0, amount + depth, amount)
        line = jnp.where((lane >= at) & (lane < at + reach), pltpu.roll(weights, amount, 1), line)
    band = by_row_shift(jnp.broadcast_to(line[0:1], (rows, depth)), rows, 1)
    middle = first_row + reach // 2 * (2 * wide + 1) + lax.broadcasted_iota(jnp.int32, band.shape, 0)
    band = (band + jnp.where(lane_of(band.shape) == middle, terms[0][0:1], 0.0)) * terms[1][0:1]
    odd = lax.axis_index("rows") % 2 == 1
    row = lane_of(band.shape) % (2 * wide)
    start = jnp.where(odd, 0, 8)
    inner = (row >= start) & (row < start + rows)
    first = pltpu.roll(jnp.where(inner, band, 0.0), jnp.where(odd, 0, depth - 8), 1)
    second = pltpu.roll(jnp.where(inner, 0.0, band), jnp.where(odd, 2 * rows - 16, 2 * rows), 1)
    return first + pltpu.roll(first, rows, 1) + second + pltpu.roll(second, 8, 1)


def pressures(base, totals, clean, other, spread, inverse):
    count, rows, columns = inverse.shape
    depth = spread.shape[0]
    squared, terms = blend_terms(jnp.broadcast_to(totals[0:1, :], (8, lanes)), count)
    bands = [banded(squared, terms[f], f, rows, 1 + base[0, 0], depth) for f in range(count)]
    mixing = cut(jnp.concatenate(bands, axis=0))
    spread_tile = spreader(clean, other, spread, base[0, 1])

    def chunk_values(t):
        where = chunk_of(t)
        spread_tile(2 * t)
        spread_tile(2 * t + 1)
        product = jnp.dot(mixing, spread[:, where], preferred_element_type=jnp.float32)
        registered = product[: count * rows] + product[count * rows :]
        values = []
        for f in range(count):
            ratio = registered[f * rows : (f + 1) * rows] * inverse[f, :, where]
            values.append(calib_zero + ratio * (calib_linear + calib_square * ratio))
        return values

    return chunk_values


def pressure_kernel(base, totals, clean, other, inverse, pressure, moments, part, spread):
    count, rows, columns = inverse.shape
    chunk_values = pressures(base, totals, clean, other, spread, inverse)

    def step(t, sums):
        where = chunk_of(t)
        values = chunk_values(t)
        squares = [value * value for value in values]
        for f in range(count):
            pressure[f, :, where] = values[f]
        moments[0, :, where] = sum(values[1:], values[0])
        moments[1, :, where] = sum(squares[1:], squares[0])
        result = []
        for total, array in zip(sums, values + squares):
            result.append(total + fold(array[:, :lanes]) + fold(array[:, lanes:]))
        return tuple(result)

    zero = jnp.zeros((8, lanes), jnp.float32)
    sums = by_tiles(step, columns // (2 * lanes), columns // (2 * lanes), (zero,) * (2 * count))
    line = zero
    for k in range(2 * count):
        value = jnp.sum(jnp.sum(sums[k], axis=0, keepdims=True), axis=1, keepdims=True)
        line = line + jnp.where(lane_of(line.shape) == k, value, 0.0)
    part[...] = jnp.broadcast_to(line[0:1], part.shape)


def time_kernel(base, totals, clean, other, inverse, moments, time_mean, time_rms, spread):
    count, rows, columns = inverse.shape
    chunk_values = pressures(base, totals, clean, other, spread, inverse)
    frames = 2 * count

    def step(t, carry):
        where = chunk_of(t)
        first = moments[0, :, where]
        second = moments[1, :, where]
        for value in chunk_values(t):
            first = first + value
            second = second + value * value
        mean = first * (1.0 / frames)
        time_mean[:, where] = mean
        time_rms[:, where] = jnp.sqrt(jnp.maximum(second * (1.0 / frames) - mean * mean, 0.0))
        return carry

    by_tiles(step, columns // (2 * lanes), columns // (2 * lanes))


def paired(value, axis, first):
    size = lax.axis_size(axis)
    partner = list(range(size))
    for i in range(first, size - 1, 2):
        partner[i], partner[i + 1] = i + 1, i
    return lax.ppermute(value, axis, list(enumerate(partner)))


def by_parity(odd, array, height, dim):
    length = array.shape[dim]
    low = lax.slice_in_dim(array, 0, height, axis=dim)
    high = lax.slice_in_dim(array, length - height, length, axis=dim)
    return jnp.where(odd, high, low), jnp.where(odd, low, high)


def from_owner(shard, here, odd, axis, root):
    mine = lax.axis_index(axis) == root
    height = shard.shape[0] // 2
    if lax.axis_size(axis) != 2:
        whole = lax.psum(jnp.where(mine, shard, jnp.zeros_like(shard)), axis)
        return by_parity(odd, whole, height, 0)
    there = by_parity(odd, paired(shard, axis, 0), height, 0)
    here = by_parity(odd, here, height, 0)
    return [jnp.where(mine, own, other) for own, other in zip(here, there)]


def middle_first(size):
    order = sorted(range(size), key=lambda i: (abs(2 * i + 1 - size), i))
    return order


def total_over(value, axis):
    size = lax.axis_size(axis)
    if size & (size - 1):
        return lax.psum(value, axis)
    step = 1
    while step < size:
        value = value + lax.ppermute(value, axis, [(i, i ^ step) for i in range(size)])
        step *= 2
    return value


def shards(frames_raw, wind_off, run_owner, search_base):
    count, rows, columns = frames_raw.shape
    tiles = columns // lanes
    ring = tiles + 2
    wide = rows + 8
    depth = near * count * rows
    size = lax.axis_size("rows")
    f32 = jnp.float32
    bf16 = jnp.bfloat16
    struct = functools.partial(jax.ShapeDtypeStruct, dtype=f32)
    odd = lax.axis_index("rows") % 2 == 1
    raw, run = lax.optimization_barrier((jnp.maximum(frames_raw, 0.0), jnp.maximum(wind_off[0], 0.0)))
    owner, offsets = lax.optimization_barrier((run_owner, jnp.clip(search_base, -8, 8)))
    own_odd, own_even = from_owner(wind_off[0], run, odd, "frames", owner[0])
    from_odd = paired(own_odd, "rows", 1)
    from_even = paired(own_even, "rows", 0)
    frames_odd, frames_even = by_parity(odd, raw, 4, 1)
    frames_odd = paired(frames_odd, "rows", 1)
    frames_even = paired(frames_even, "rows", 0)
    frames_odd, own_odd = lax.optimization_barrier((frames_odd, own_odd))
    inverse, stack, power, band = pl.pallas_call(
        smooth_kernel,
        out_shape=(
            struct((count, rows, columns)),
            jax.ShapeDtypeStruct((2 * depth, ring * lanes), bf16),
            struct((8 * count, lanes)),
            jax.ShapeDtypeStruct((4 * lanes, 2 * lanes), bf16),
        ),
        in_specs=[vmem] * 3,
        out_specs=(vmem,) * 4,
        scratch_shapes=[
            pltpu.VMEM((count, tiles, rows + 16, lanes), f32),
            pltpu.VMEM((tiles // 2, 2 * count * rows, 4 * lanes), bf16),
            pltpu.VMEM((ring + 2, 2 * count * rows, lanes), bf16),
        ],
        compiler_params=params,
        cost_estimate=cost(8),
        name="smooth",
    )(raw, frames_odd, frames_even)
    blocks = lax.axis_size("frames")
    def reference_scratch(height):
        return [
            pltpu.VMEM((tiles, height + 8, lanes), f32),
            pltpu.VMEM((tiles // 2, 2 * height, 4 * lanes), bf16),
            pltpu.VMEM((ring + 2, 2 * height, lanes), bf16),
            pltpu.VMEM((far * 2 * height, ring * lanes), bf16),
            pltpu.VMEM((depth, lanes), f32),
        ]

    clean, near_lags, near_power = pl.pallas_call(
        near_kernel,
        out_shape=(
            jax.ShapeDtypeStruct((tiles + 2, 2 * rows, lanes), bf16),
            struct((depth, lanes)),
            struct((8, lanes)),
        ),
        in_specs=[smem] + [vmem] * 5,
        out_specs=(vmem,) * 3,
        scratch_shapes=reference_scratch(rows),
        compiler_params=params,
        cost_estimate=cost(8),
        name="near",
    )(offsets, own_odd, own_even, from_even, stack, band)
    other, part = pl.pallas_call(
        match_kernel,
        out_shape=(jax.ShapeDtypeStruct((tiles + 2, 16, lanes), bf16), struct((size, lanes))),
        in_specs=[smem] + [vmem] * 7,
        out_specs=(vmem,) * 2,
        scratch_shapes=reference_scratch(8) + [pltpu.VMEM((8 * count, lanes), f32)],
        compiler_params=params,
        cost_estimate=cost(8),
        name="match",
    )(offsets, own_odd, from_odd, near_lags, near_power, stack, power, band)
    if blocks == 2:
        inverse_out, part = lax.optimization_barrier((inverse, part))
        other_inverse = paired(inverse_out, "frames", 0)
    order = [middle_first(size)]
    parts = lax.all_to_all(part, "rows", 0, 0, axis_index_groups=order, tiled=True)
    totals = jnp.sum(parts, axis=0, keepdims=True)
    depth = -(-reach * 2 * wide // lanes) * lanes
    spread = pltpu.VMEM((depth, columns), bf16)
    pressure, moments, part = pl.pallas_call(
        pressure_kernel,
        out_shape=(struct((count, rows, columns)), struct((2, rows, columns)), struct((size, lanes))),
        in_specs=[smem] + [vmem] * 4,
        out_specs=(vmem, vmem, vmem),
        scratch_shapes=[spread],
        compiler_params=params,
        cost_estimate=cost(12),
        name="pressure",
    )(offsets, totals, clean, other, inverse)
    if blocks == 2:
        row, part = lax.optimization_barrier((totals, part))
        row = paired(row, "frames", 0)
        place = (row[:, lanes - 2 :] / size).astype(jnp.int32)
        time_mean, time_rms = pl.pallas_call(
            time_kernel,
            out_shape=(struct((rows, columns)), struct((rows, columns))),
            in_specs=[smem] + [vmem] * 5,
            out_specs=(vmem, vmem),
            scratch_shapes=[spread],
            compiler_params=params,
            cost_estimate=cost(12),
            name="time",
        )(place, row, clean, other, other_inverse, moments)
    else:
        whole = total_over(moments, "frames")
        total_frames = count * blocks
        time_mean = whole[0] / total_frames
        time_rms = jnp.sqrt(jnp.maximum(whole[1] / total_frames - time_mean * time_mean, 0.0))
    sums = lax.all_to_all(part, "rows", 0, 0, axis_index_groups=order, tiled=True)
    sums, time_mean, time_rms = lax.optimization_barrier((sums, time_mean, time_rms))
    spatial = jnp.sum(sums, axis=0)
    cell_count = rows * columns * size
    frame_mean = spatial[:count] / cell_count
    frame_rms = jnp.sqrt(spatial[count : 2 * count] / cell_count - frame_mean * frame_mean)
    return (pressure, frame_mean, frame_rms, time_mean, time_rms)


def solution(mesh):
    placed = (P("frames", "rows", None), P("frames", "rows", None), P("rows"), P("frames", None))
    return jax.shard_map(
        shards,
        mesh=mesh,
        in_specs=placed,
        out_specs=(
            P("frames", "rows", None),
            P("frames"),
            P("frames"),
            P("rows", None),
            P("rows", None),
        ),
        check_vma=False,
    )
```

```python
import functools

import jax
import jax.numpy as jnp
from jax import lax
from jax.experimental import pallas as pl
from jax.experimental.pallas import tpu as pltpu
from jax.sharding import PartitionSpec as P

taps = (1.0 / 256, 8.0 / 256, 28.0 / 256, 56.0 / 256, 70.0 / 256)
calib_zero = -0.25
calib_linear = 1.0
calib_square = 0.15
lanes = 128
reach = 7
near = 4
far = 2
slot = 32
params = pltpu.CompilerParams(vmem_limit_bytes=14 * 1024 * 1024)
vmem = pl.BlockSpec(memory_space=pltpu.VMEM)
smem = pl.BlockSpec(memory_space=pltpu.SMEM)


def cost(mebibytes):
    return pl.CostEstimate(flops=0, bytes_accessed=mebibytes * 2**20, transcendentals=0)


def tile_of(index):
    if isinstance(index, int):
        return slice(index * lanes, (index + 1) * lanes)
    return pl.ds(pl.multiple_of(index * lanes, lanes), lanes)


def by_tiles(step, tiles, group, init=()):
    if group == tiles:
        for index in range(tiles):
            init = step(index, init)
        return init

    def body(index, carry):
        for inner in range(group):
            carry = step(index * group + inner, carry)
        return carry

    return lax.fori_loop(0, tiles // group, body, init)


def lane_of(shape):
    return lax.broadcasted_iota(jnp.int32, shape, len(shape) - 1)


def fold(product):
    return jnp.sum(product.reshape(product.shape[0] // 8, 8, lanes), axis=0)


def vertical(load):
    total = taps[4] * load(4)
    for step in range(4):
        total = total + taps[step] * (load(step) + load(8 - step))
    return total


def moved(before, here, after, step):
    if step > 0:
        return pltpu.roll(jnp.where(lane_of(here.shape) < step, after, here), lanes - step, 1)
    if step < 0:
        return pltpu.roll(jnp.where(lane_of(here.shape) >= lanes + step, before, here), -step, 1)
    return here


def halves(value):
    high = value.astype(jnp.bfloat16)
    low = (value - high.astype(jnp.float32)).astype(jnp.bfloat16)
    return high, low


def cut(value):
    return jnp.concatenate(halves(value), axis=0)


def fill_band(band):
    shape = (lanes, lanes)
    apart = lax.broadcasted_iota(jnp.int32, shape, 0) - lax.broadcasted_iota(jnp.int32, shape, 1)

    def block(offset):
        distance = jnp.abs(apart + offset)
        value = jnp.zeros(shape, jnp.float32)
        for step in range(5):
            value = jnp.where(distance == step, taps[4 - step], value)
        return value.astype(jnp.bfloat16)

    none = jnp.zeros(shape, jnp.bfloat16)
    before, here, after = block(-lanes), block(0), block(lanes)
    for index, pair in enumerate(((before, none), (here, before), (after, here), (none, after))):
        band[index * lanes : (index + 1) * lanes, :] = jnp.concatenate(pair, axis=1)


def chunk_of(t):
    if isinstance(t, int):
        return slice(t * 2 * lanes, (t + 1) * 2 * lanes)
    return pl.ds(pl.multiple_of(t * 2 * lanes, 2 * lanes), 2 * lanes)


def place_tile(windows, index, value):
    for c in (index // 2 - 1, index // 2):
        at = index - 2 * c
        if 0 <= c < windows.shape[0] and at < 4:
            windows[c, :, at * lanes : (at + 1) * lanes] = value


def horizontal(windows, band):
    chunks, height, width = windows.shape
    product = jnp.dot(
        windows[...].reshape(chunks * height, width), band[...], preferred_element_type=jnp.float32
    )
    product = product.reshape(chunks, height, 2 * lanes)
    return product[:, : height // 2] + product[:, height // 2 :]


def by_row_shift(value, rows, direction):
    place = lax.broadcasted_iota(jnp.int32, value.shape, 0) % rows
    unit = 1
    while unit < rows:
        digit = (place // unit) % 4
        result = value
        for times in range(1, 4):
            amount = times * unit
            turned = pltpu.roll(value, amount if direction > 0 else value.shape[1] - amount, 1)
            result = jnp.where(digit == times, turned, result)
        value = result
        unit *= 4
    return value


def at_edge():
    index = lax.axis_index("rows")
    return (index == 0) | (index == lax.axis_size("rows") - 1)


def smooth_kernel(frames, from_odd, from_even, inverse, stack, power, band, rows_in, wide, pieces):
    count, rows, columns = frames.shape
    tiles = columns // lanes
    ring = tiles + 2
    odd = lax.axis_index("rows") % 2 == 1
    edge = at_edge()
    blank = jnp.zeros((2 * count * rows, lanes), jnp.bfloat16)
    place_tile(wide, 0, blank)
    place_tile(wide, tiles + 1, blank)
    fill_band(band)
    pieces[0] = blank
    pieces[tiles + 1] = blank
    pieces[tiles + 2] = blank

    def load_step(t, carry):
        for f in range(count):
            outer = jnp.where(edge, 0.0, from_odd[f, :, tile_of(t)])
            inner = from_even[f, :, tile_of(t)]
            rows_in[f, t, 4:8, :] = jnp.where(odd, inner, outer)
            rows_in[f, t, 8 : 8 + rows, :] = frames[f, :, tile_of(t)]
            rows_in[f, t, 8 + rows : 12 + rows, :] = jnp.where(odd, outer, inner)
        return carry

    def vertical_step(t, carry):
        parts = [vertical(lambda s: rows_in[f, t, pl.ds(4 + s, rows), :]) for f in range(count)]
        place_tile(wide, t + 1, cut(jnp.concatenate(parts, axis=0)))
        return carry

    def horizontal_step(t, totals):
        smooth = smoothed[t]
        result = []
        details = []
        for f in range(count):
            part = smooth[f * rows : (f + 1) * rows]
            inverse[f, :, chunk_of(t)] = 1.0 / part
            details.append(frames[f, :, chunk_of(t)] - part)
            square = details[f] * details[f]
            result.append(totals[f] + fold(square[:, :lanes]) + fold(square[:, lanes:]))
        detail = cut(jnp.concatenate(details, axis=0))
        pieces[2 * t + 1] = detail[:, :lanes]
        pieces[2 * t + 2] = detail[:, lanes:]
        return tuple(result)

    def stack_step(t, carry):
        before, here, after = pieces[t], pieces[t + 1], pieces[t + 2]
        size = count * rows
        for a in range(near):
            turned = moved(before, here, after, 1 - a)
            stack[a * size : (a + 1) * size, tile_of(t)] = turned[:size]
            stack[(near + a) * size : (near + a + 1) * size, tile_of(t)] = turned[size:]
        return carry

    powers = (jnp.zeros((8, lanes), jnp.float32),) * count
    for t in range(tiles):
        load_step(t, 0)
        vertical_step(t, 0)
    smoothed = horizontal(wide, band)
    for t in range(tiles // 2):
        powers = horizontal_step(t, powers)
    for f in range(count):
        power[f * 8 : f * 8 + 8, :] = powers[f]
    pieces[tiles + 3] = pieces[1]
    by_tiles(stack_step, ring, ring)


def column_shift(offset):
    negative = offset < 0
    first = jnp.where(negative, 0, 1)
    amount = jnp.where(negative, offset + lanes, offset)
    back = (lanes - amount) & (lanes - 1)

    def shift(source, t):
        here = source[t + first]
        after = source[t + first + 1]
        return pltpu.roll(jnp.where(lane_of(here.shape) < amount, after, here), back, 1)

    return shift


def reference_rows(raw, smooth, clean, fine, tiles):
    height = clean.shape[1] // 2
    empty = jnp.zeros((2 * height, lanes), jnp.bfloat16)
    for array in (clean, fine):
        array[0] = empty
        array[tiles + 1] = empty
    fine[tiles + 2] = empty
    squares = []
    for t in range(tiles // 2):
        detail = jnp.concatenate([raw(2 * t), raw(2 * t + 1)], axis=1) - smooth(t)
        for array, value in ((clean, cut(smooth(t))), (fine, cut(detail))):
            array[2 * t + 1] = value[:, :lanes]
            array[2 * t + 2] = value[:, lanes:]
        squares.append(detail * detail)
    fine[tiles + 3] = fine[1]
    return squares


def lag_products(stack, fine, stream, folded, base_col, start):
    height = fine.shape[1]
    half = height // 2
    shifts = [column_shift(base_col + near * b - 2) for b in range(far)]
    for t in range(fine.shape[0] - 2):
        for b, shift in enumerate(shifts):
            stream[b * height : (b + 1) * height, tile_of(t)] = shift(fine, t)
    product = lax.dot_general(
        stack[...], stream[...], (((1,), (1,)), ((), ())), preferred_element_type=jnp.float32
    )
    size = product.shape[0] // 2
    folded[...] = jnp.zeros(folded.shape, jnp.float32)
    folded[:, 0 : far * height] = product[:size] + product[size:]
    product = folded[...]
    lane = lane_of(product.shape)
    placed = jnp.zeros_like(product)
    for s in range(2 * far):
        at = s * slot + start
        turned = pltpu.roll(product, at - s * half, 1)
        placed = jnp.where((lane >= at) & (lane < at + half), turned, placed)
    return placed


def near_kernel(
    base, own_odd, own_even, from_even, stack, band, clean, lags, power, rows_in, windows, fine, stream, folded
):
    tiles = own_odd.shape[1] // lanes
    odd = lax.axis_index("rows") % 2 == 1
    height = clean.shape[1] // 2
    empty = jnp.zeros((2 * height, lanes), jnp.bfloat16)
    place_tile(windows, 0, empty)
    place_tile(windows, tiles + 1, empty)
    for t in range(tiles):
        at = tile_of(t)
        outer = own_odd[:, at]
        inner = from_even[:, at]
        rows_in[t, 0:8, :] = jnp.where(odd, inner, outer)
        rows_in[t, 8:16, :] = own_even[:, at]
        rows_in[t, 16:24, :] = jnp.where(odd, outer, inner)
        place_tile(windows, t + 1, cut(vertical(lambda s: rows_in[t, pl.ds(s, height), :])))
    smooth = horizontal(windows, band)
    squares = reference_rows(lambda t: rows_in[t, pl.ds(4, height), :], lambda t: smooth[t], clean, fine, tiles)
    place = lax.broadcasted_iota(jnp.int32, squares[0].shape, 0)
    first = jnp.where(odd, 4, 0)
    own = (place >= first) & (place < first + height - 4)
    total = jnp.zeros((8, lanes), jnp.float32)
    for square in squares:
        square = jnp.where(own, square, 0.0)
        total = total + fold(square[:, :lanes]) + fold(square[:, lanes:])
    power[...] = total
    lags[...] = lag_products(stack, fine, stream, folded, base[0, 1], jnp.where(odd, 0, 8))


def match_kernel(
    base, own_odd, from_odd, near_lags, near_power, stack, power, band, clean, part, rows_in, windows, fine, stream, folded, lags
):
    tiles = own_odd.shape[1] // lanes
    count = power.shape[0] // 8
    rows = folded.shape[0] // (near * count)
    odd = lax.axis_index("rows") % 2 == 1
    edge = at_edge()
    height = clean.shape[1] // 2
    empty = jnp.zeros((2 * height, lanes), jnp.bfloat16)
    place_tile(windows, 0, empty)
    place_tile(windows, tiles + 1, empty)
    for t in range(tiles):
        at = tile_of(t)
        outer = jnp.where(edge, 0.0, from_odd[:, at])
        inner = own_odd[:, at]
        rows_in[t, 0:8, :] = jnp.where(odd, inner, outer)
        rows_in[t, 8:16, :] = jnp.where(odd, outer, inner)
        place_tile(windows, t + 1, cut(vertical(lambda s: rows_in[t, pl.ds(s, height), :])))
    smooth = horizontal(windows, band)
    place = lax.broadcasted_iota(jnp.int32, (height, 2 * lanes), 0)
    first = jnp.where(odd, 0, 4)
    own = (place >= first) & (place < first + 4)
    inside = (place >= jnp.where(edge, first, 0)) & (place < jnp.where(edge, first + 4, height))

    def masked(t):
        return jnp.where(inside, smooth[t], 0.0)

    squares = reference_rows(lambda t: rows_in[t, pl.ds(4, height), :], masked, clean, fine, tiles)
    ref_power = near_power[...]
    for square in squares:
        square = jnp.where(own, square, 0.0)
        ref_power = ref_power + fold(square[:, :lanes]) + fold(square[:, lanes:])
    product = lag_products(stack, fine, stream, folded, base[0, 1], jnp.where(odd, 16, 0))
    product = by_row_shift(product + near_lags[...], rows, -1)
    lags[...] = jnp.zeros(lags.shape, jnp.float32)
    for a in range(near):
        for f in range(count):
            start = (a * count + f) * rows
            lags[f * 8 + a : f * 8 + a + 1, :] = jnp.sum(product[start : start + rows], axis=0, keepdims=True)
    back = 4 * lanes - 1 - base[0, 0]
    across = lax.broadcasted_iota(jnp.int32, (8, lanes), 0)
    lane = lane_of((8, lanes))
    packed = jnp.zeros((8, lanes), jnp.float32)
    for f in range(count):
        block = lags[f * 8 : f * 8 + 8, :]
        for j in range(reach):
            at = (f * reach + j) * reach
            there = back + at - (j // near) * 2 * slot
            high = pltpu.roll(block, there & (lanes - 1), 1)
            low = pltpu.roll(block, (there - slot) & (lanes - 1), 1)
            member = (across == j % near) & (lane >= at) & (lane < at + reach)
            packed = packed + jnp.where(member, high + low, 0.0)
    lags[0:8, :] = jnp.zeros((8, lanes), jnp.float32)
    for f in range(count):
        lags[f : f + 1, :] = jnp.sum(power[f * 8 : f * 8 + 8, :], axis=0, keepdims=True)
    lags[count : count + 1, :] = jnp.sum(ref_power, axis=0, keepdims=True)
    powers = jnp.sum(lags[0:8, :], axis=1, keepdims=True)
    packed = packed + jnp.where(lane == count * reach * reach + across, powers, 0.0)
    packed = jnp.sum(packed, axis=0, keepdims=True)
    for place in range(2):
        offset = base[0, place].astype(jnp.float32)
        packed = jnp.where(lane[0:1] == lanes - 2 + place, offset, packed)
    part[...] = jnp.broadcast_to(packed, part.shape)


def spreader(clean, other, spread, base_col):
    height = clean.shape[1]
    size = height + other.shape[1]
    spare = spread.shape[0] - reach * size
    shifts = [column_shift(base_col + j - 3) for j in range(reach)]

    def spread_tile(t):
        at = tile_of(t)
        for j, shift in enumerate(shifts):
            spread[j * size : j * size + height, at] = shift(clean, t)
            spread[j * size + height : (j + 1) * size, at] = shift(other, t)
        spread[reach * size :, at] = jnp.zeros((spare, lanes), jnp.bfloat16)

    return spread_tile


def blend_terms(totals, count):
    lane = lane_of(totals.shape)
    block = reach * reach
    squared = totals * totals

    def pick(array, low, size):
        return jnp.sum(jnp.where((lane >= low) & (lane < low + size), array, 0.0), axis=1, keepdims=True)

    ref_power = pick(totals, count * block + count, 1)
    terms = []
    for f in range(count):
        norm_product = 0.05 * ((pick(totals, count * block + f, 1) + 1e-06) * (ref_power + 1e-06))
        terms.append((norm_product, 1.0 / (norm_product + pick(squared, f * block, block))))
    return squared, terms


def banded(weights, terms, f, rows, first_row, depth):
    wide = rows + 8
    blank = jnp.zeros((weights.shape[0], depth - lanes), jnp.float32)
    weights = jnp.concatenate([weights, blank], axis=1)
    lane = lane_of(weights.shape)
    line = jnp.zeros_like(weights)
    for j in range(reach):
        at = first_row + j * 2 * wide
        amount = at - (f * reach + j) * reach
        amount = jnp.where(amount < 0, amount + depth, amount)
        line = jnp.where((lane >= at) & (lane < at + reach), pltpu.roll(weights, amount, 1), line)
    band = by_row_shift(jnp.broadcast_to(line[0:1], (rows, depth)), rows, 1)
    middle = first_row + reach // 2 * (2 * wide + 1) + lax.broadcasted_iota(jnp.int32, band.shape, 0)
    band = (band + jnp.where(lane_of(band.shape) == middle, terms[0][0:1], 0.0)) * terms[1][0:1]
    odd = lax.axis_index("rows") % 2 == 1
    row = lane_of(band.shape) % (2 * wide)
    start = jnp.where(odd, 0, 8)
    inner = (row >= start) & (row < start + rows)
    first = pltpu.roll(jnp.where(inner, band, 0.0), jnp.where(odd, 0, depth - 8), 1)
    second = pltpu.roll(jnp.where(inner, 0.0, band), jnp.where(odd, 2 * rows - 16, 2 * rows), 1)
    return first + pltpu.roll(first, rows, 1) + second + pltpu.roll(second, 8, 1)


def pressures(base, totals, clean, other, spread, inverse):
    count, rows, columns = inverse.shape
    depth = spread.shape[0]
    squared, terms = blend_terms(jnp.broadcast_to(totals[0:1, :], (8, lanes)), count)
    bands = [banded(squared, terms[f], f, rows, 1 + base[0, 0], depth) for f in range(count)]
    mixing = cut(jnp.concatenate(bands, axis=0))
    spread_tile = spreader(clean, other, spread, base[0, 1])

    def chunk_values(t):
        where = chunk_of(t)
        spread_tile(2 * t)
        spread_tile(2 * t + 1)
        product = jnp.dot(mixing, spread[:, where], preferred_element_type=jnp.float32)
        registered = product[: count * rows] + product[count * rows :]
        values = []
        for f in range(count):
            ratio = registered[f * rows : (f + 1) * rows] * inverse[f, :, where]
            values.append(calib_zero + ratio * (calib_linear + calib_square * ratio))
        return values

    return chunk_values


def pressure_kernel(base, totals, clean, other, inverse, pressure, moments, part, spread):
    count, rows, columns = inverse.shape
    chunk_values = pressures(base, totals, clean, other, spread, inverse)

    def step(t, sums):
        where = chunk_of(t)
        values = chunk_values(t)
        squares = [value * value for value in values]
        for f in range(count):
            pressure[f, :, where] = values[f]
        moments[0, :, where] = sum(values[1:], values[0])
        moments[1, :, where] = sum(squares[1:], squares[0])
        result = []
        for total, array in zip(sums, values + squares):
            result.append(total + fold(array[:, :lanes]) + fold(array[:, lanes:]))
        return tuple(result)

    zero = jnp.zeros((8, lanes), jnp.float32)
    sums = by_tiles(step, columns // (2 * lanes), columns // (2 * lanes), (zero,) * (2 * count))
    line = zero
    for k in range(2 * count):
        value = jnp.sum(jnp.sum(sums[k], axis=0, keepdims=True), axis=1, keepdims=True)
        line = line + jnp.where(lane_of(line.shape) == k, value, 0.0)
    part[...] = jnp.broadcast_to(line[0:1], part.shape)


def time_kernel(base, totals, clean, other, inverse, moments, time_mean, time_rms, spread):
    count, rows, columns = inverse.shape
    chunk_values = pressures(base, totals, clean, other, spread, inverse)
    frames = 2 * count

    def step(t, carry):
        where = chunk_of(t)
        first = moments[0, :, where]
        second = moments[1, :, where]
        for value in chunk_values(t):
            first = first + value
            second = second + value * value
        mean = first * (1.0 / frames)
        time_mean[:, where] = mean
        time_rms[:, where] = jnp.sqrt(jnp.maximum(second * (1.0 / frames) - mean * mean, 0.0))
        return carry

    by_tiles(step, columns // (2 * lanes), columns // (2 * lanes))


def paired(value, axis, first):
    size = lax.axis_size(axis)
    partner = list(range(size))
    for i in range(first, size - 1, 2):
        partner[i], partner[i + 1] = i + 1, i
    return lax.ppermute(value, axis, list(enumerate(partner)))


def by_parity(odd, array, height, dim):
    length = array.shape[dim]
    low = lax.slice_in_dim(array, 0, height, axis=dim)
    high = lax.slice_in_dim(array, length - height, length, axis=dim)
    return jnp.where(odd, high, low), jnp.where(odd, low, high)


def from_owner(shard, here, odd, axis, root):
    mine = lax.axis_index(axis) == root
    height = shard.shape[0] // 2
    if lax.axis_size(axis) != 2:
        whole = lax.psum(jnp.where(mine, shard, jnp.zeros_like(shard)), axis)
        return by_parity(odd, whole, height, 0)
    there = by_parity(odd, paired(shard, axis, 0), height, 0)
    here = by_parity(odd, here, height, 0)
    return [jnp.where(mine, own, other) for own, other in zip(here, there)]


def middle_first(size):
    order = sorted(range(size), key=lambda i: (abs(2 * i + 1 - size), i))
    return order


def total_over(value, axis):
    size = lax.axis_size(axis)
    if size & (size - 1):
        return lax.psum(value, axis)
    step = 1
    while step < size:
        value = value + lax.ppermute(value, axis, [(i, i ^ step) for i in range(size)])
        step *= 2
    return value


def shards(frames_raw, wind_off, run_owner, search_base):
    count, rows, columns = frames_raw.shape
    tiles = columns // lanes
    ring = tiles + 2
    wide = rows + 8
    depth = near * count * rows
    size = lax.axis_size("rows")
    f32 = jnp.float32
    bf16 = jnp.bfloat16
    struct = functools.partial(jax.ShapeDtypeStruct, dtype=f32)
    odd = lax.axis_index("rows") % 2 == 1
    raw, run = lax.optimization_barrier((jnp.maximum(frames_raw, 0.0), jnp.maximum(wind_off[0], 0.0)))
    owner, offsets = lax.optimization_barrier((run_owner, jnp.clip(search_base, -8, 8)))
    own_odd, own_even = from_owner(wind_off[0], run, odd, "frames", owner[0])
    from_odd = paired(own_odd, "rows", 1)
    from_even = paired(own_even, "rows", 0)
    frames_odd, frames_even = by_parity(odd, raw, 4, 1)
    frames_odd = paired(frames_odd, "rows", 1)
    frames_even = paired(frames_even, "rows", 0)
    frames_odd, own_odd = lax.optimization_barrier((frames_odd, own_odd))
    inverse, stack, power, band = pl.pallas_call(
        smooth_kernel,
        out_shape=(
            struct((count, rows, columns)),
            jax.ShapeDtypeStruct((2 * depth, ring * lanes), bf16),
            struct((8 * count, lanes)),
            jax.ShapeDtypeStruct((4 * lanes, 2 * lanes), bf16),
        ),
        in_specs=[vmem] * 3,
        out_specs=(vmem,) * 4,
        scratch_shapes=[
            pltpu.VMEM((count, tiles, rows + 16, lanes), f32),
            pltpu.VMEM((tiles // 2, 2 * count * rows, 4 * lanes), bf16),
            pltpu.VMEM((ring + 2, 2 * count * rows, lanes), bf16),
        ],
        compiler_params=params,
        cost_estimate=cost(8),
        name="smooth",
    )(raw, frames_odd, frames_even)
    blocks = lax.axis_size("frames")
    def reference_scratch(height):
        return [
            pltpu.VMEM((tiles, height + 8, lanes), f32),
            pltpu.VMEM((tiles // 2, 2 * height, 4 * lanes), bf16),
            pltpu.VMEM((ring + 2, 2 * height, lanes), bf16),
            pltpu.VMEM((far * 2 * height, ring * lanes), bf16),
            pltpu.VMEM((depth, lanes), f32),
        ]

    clean, near_lags, near_power = pl.pallas_call(
        near_kernel,
        out_shape=(
            jax.ShapeDtypeStruct((tiles + 2, 2 * rows, lanes), bf16),
            struct((depth, lanes)),
            struct((8, lanes)),
        ),
        in_specs=[smem] + [vmem] * 5,
        out_specs=(vmem,) * 3,
        scratch_shapes=reference_scratch(rows),
        compiler_params=params,
        cost_estimate=cost(8),
        name="near",
    )(offsets, own_odd, own_even, from_even, stack, band)
    other, part = pl.pallas_call(
        match_kernel,
        out_shape=(jax.ShapeDtypeStruct((tiles + 2, 16, lanes), bf16), struct((size, lanes))),
        in_specs=[smem] + [vmem] * 7,
        out_specs=(vmem,) * 2,
        scratch_shapes=reference_scratch(8) + [pltpu.VMEM((8 * count, lanes), f32)],
        compiler_params=params,
        cost_estimate=cost(8),
        name="match",
    )(offsets, own_odd, from_odd, near_lags, near_power, stack, power, band)
    if blocks == 2:
        inverse_out, part = lax.optimization_barrier((inverse, part))
        other_inverse = paired(inverse_out, "frames", 0)
    order = [middle_first(size)]
    parts = lax.all_to_all(part, "rows", 0, 0, axis_index_groups=order, tiled=True)
    totals = jnp.sum(parts, axis=0, keepdims=True)
    depth = -(-reach * 2 * wide // lanes) * lanes
    spread = pltpu.VMEM((depth, columns), bf16)
    pressure, moments, part = pl.pallas_call(
        pressure_kernel,
        out_shape=(struct((count, rows, columns)), struct((2, rows, columns)), struct((size, lanes))),
        in_specs=[smem] + [vmem] * 4,
        out_specs=(vmem, vmem, vmem),
        scratch_shapes=[spread],
        compiler_params=params,
        cost_estimate=cost(12),
        name="pressure",
    )(offsets, totals, clean, other, inverse)
    if blocks == 2:
        row, part = lax.optimization_barrier((totals, part))
        row = paired(row, "frames", 0)
        place = (row[:, lanes - 2 :] / size).astype(jnp.int32)
        time_mean, time_rms = pl.pallas_call(
            time_kernel,
            out_shape=(struct((rows, columns)), struct((rows, columns))),
            in_specs=[smem] + [vmem] * 5,
            out_specs=(vmem, vmem),
            scratch_shapes=[spread],
            compiler_params=params,
            cost_estimate=cost(12),
            name="time",
        )(place, row, clean, other, other_inverse, moments)
    else:
        whole = total_over(moments, "frames")
        total_frames = count * blocks
        time_mean = whole[0] / total_frames
        time_rms = jnp.sqrt(jnp.maximum(whole[1] / total_frames - time_mean * time_mean, 0.0))
    turned = [[(i + size // 2 - 1) % size for i in range(size)]]
    sums = lax.all_to_all(part, "rows", 0, 0, axis_index_groups=turned, tiled=True)
    sums, time_mean, time_rms = lax.optimization_barrier((sums, time_mean, time_rms))
    spatial = jnp.sum(sums, axis=0)
    cell_count = rows * columns * size
    frame_mean = spatial[:count] / cell_count
    frame_rms = jnp.sqrt(spatial[count : 2 * count] / cell_count - frame_mean * frame_mean)
    return (pressure, frame_mean, frame_rms, time_mean, time_rms)


def solution(mesh):
    placed = (P("frames", "rows", None), P("frames", "rows", None), P("rows"), P("frames", None))
    return jax.shard_map(
        shards,
        mesh=mesh,
        in_specs=placed,
        out_specs=(
            P("frames", "rows", None),
            P("frames"),
            P("frames"),
            P("rows", None),
            P("rows", None),
        ),
        check_vma=False,
    )
```

```python
import functools

import jax
import jax.numpy as jnp
from jax import lax
from jax.experimental import pallas as pl
from jax.experimental.pallas import tpu as pltpu
from jax.sharding import PartitionSpec as P

taps = (1.0 / 256, 8.0 / 256, 28.0 / 256, 56.0 / 256, 70.0 / 256)
calib_zero = -0.25
calib_linear = 1.0
calib_square = 0.15
lanes = 128
reach = 7
near = 4
far = 2
slot = 32
params = pltpu.CompilerParams(vmem_limit_bytes=14 * 1024 * 1024)
vmem = pl.BlockSpec(memory_space=pltpu.VMEM)
smem = pl.BlockSpec(memory_space=pltpu.SMEM)


def cost(mebibytes):
    return pl.CostEstimate(flops=0, bytes_accessed=mebibytes * 2**20, transcendentals=0)


def tile_of(index):
    if isinstance(index, int):
        return slice(index * lanes, (index + 1) * lanes)
    return pl.ds(pl.multiple_of(index * lanes, lanes), lanes)


def by_tiles(step, tiles, group, init=()):
    if group == tiles:
        for index in range(tiles):
            init = step(index, init)
        return init

    def body(index, carry):
        for inner in range(group):
            carry = step(index * group + inner, carry)
        return carry

    return lax.fori_loop(0, tiles // group, body, init)


def lane_of(shape):
    return lax.broadcasted_iota(jnp.int32, shape, len(shape) - 1)


def fold(product):
    return jnp.sum(product.reshape(product.shape[0] // 8, 8, lanes), axis=0)


def vertical(load):
    total = taps[4] * load(4)
    for step in range(4):
        total = total + taps[step] * (load(step) + load(8 - step))
    return total


def moved(before, here, after, step):
    if step > 0:
        return pltpu.roll(jnp.where(lane_of(here.shape) < step, after, here), lanes - step, 1)
    if step < 0:
        return pltpu.roll(jnp.where(lane_of(here.shape) >= lanes + step, before, here), -step, 1)
    return here


def halves(value):
    high = value.astype(jnp.bfloat16)
    low = (value - high.astype(jnp.float32)).astype(jnp.bfloat16)
    return high, low


def cut(value):
    return jnp.concatenate(halves(value), axis=0)


def fill_band(band):
    shape = (lanes, lanes)
    apart = lax.broadcasted_iota(jnp.int32, shape, 0) - lax.broadcasted_iota(jnp.int32, shape, 1)

    def block(offset):
        distance = jnp.abs(apart + offset)
        value = jnp.zeros(shape, jnp.float32)
        for step in range(5):
            value = jnp.where(distance == step, taps[4 - step], value)
        return value.astype(jnp.bfloat16)

    none = jnp.zeros(shape, jnp.bfloat16)
    before, here, after = block(-lanes), block(0), block(lanes)
    for index, pair in enumerate(((before, none), (here, before), (after, here), (none, after))):
        band[index * lanes : (index + 1) * lanes, :] = jnp.concatenate(pair, axis=1)


def chunk_of(t):
    if isinstance(t, int):
        return slice(t * 2 * lanes, (t + 1) * 2 * lanes)
    return pl.ds(pl.multiple_of(t * 2 * lanes, 2 * lanes), 2 * lanes)


def place_tile(windows, index, value):
    for c in (index // 2 - 1, index // 2):
        at = index - 2 * c
        if 0 <= c < windows.shape[0] and at < 4:
            windows[c, :, at * lanes : (at + 1) * lanes] = value


def horizontal(windows, band):
    chunks, height, width = windows.shape
    product = jnp.dot(
        windows[...].reshape(chunks * height, width), band[...], preferred_element_type=jnp.float32
    )
    product = product.reshape(chunks, height, 2 * lanes)
    return product[:, : height // 2] + product[:, height // 2 :]


def by_row_shift(value, rows, direction):
    place = lax.broadcasted_iota(jnp.int32, value.shape, 0) % rows
    unit = 1
    while unit < rows:
        digit = (place // unit) % 4
        result = value
        for times in range(1, 4):
            amount = times * unit
            turned = pltpu.roll(value, amount if direction > 0 else value.shape[1] - amount, 1)
            result = jnp.where(digit == times, turned, result)
        value = result
        unit *= 4
    return value


def at_edge():
    index = lax.axis_index("rows")
    return (index == 0) | (index == lax.axis_size("rows") - 1)


def smooth_kernel(frames, from_odd, from_even, inverse, stack, power, band, rows_in, wide, pieces):
    count, rows, columns = frames.shape
    tiles = columns // lanes
    ring = tiles + 2
    odd = lax.axis_index("rows") % 2 == 1
    edge = at_edge()
    blank = jnp.zeros((2 * count * rows, lanes), jnp.bfloat16)
    place_tile(wide, 0, blank)
    place_tile(wide, tiles + 1, blank)
    fill_band(band)
    pieces[0] = blank
    pieces[tiles + 1] = blank
    pieces[tiles + 2] = blank

    def load_step(t, carry):
        for f in range(count):
            outer = jnp.where(edge, 0.0, from_odd[f, :, tile_of(t)])
            inner = from_even[f, :, tile_of(t)]
            rows_in[f, t, 4:8, :] = jnp.where(odd, inner, outer)
            rows_in[f, t, 8 : 8 + rows, :] = frames[f, :, tile_of(t)]
            rows_in[f, t, 8 + rows : 12 + rows, :] = jnp.where(odd, outer, inner)
        return carry

    def vertical_step(t, carry):
        parts = [vertical(lambda s: rows_in[f, t, pl.ds(4 + s, rows), :]) for f in range(count)]
        place_tile(wide, t + 1, cut(jnp.concatenate(parts, axis=0)))
        return carry

    def horizontal_step(t, totals):
        smooth = smoothed[t]
        result = []
        details = []
        for f in range(count):
            part = smooth[f * rows : (f + 1) * rows]
            inverse[f, :, chunk_of(t)] = 1.0 / part
            details.append(frames[f, :, chunk_of(t)] - part)
            square = details[f] * details[f]
            result.append(totals[f] + fold(square[:, :lanes]) + fold(square[:, lanes:]))
        detail = cut(jnp.concatenate(details, axis=0))
        pieces[2 * t + 1] = detail[:, :lanes]
        pieces[2 * t + 2] = detail[:, lanes:]
        return tuple(result)

    def stack_step(t, carry):
        before, here, after = pieces[t], pieces[t + 1], pieces[t + 2]
        size = count * rows
        for a in range(near):
            turned = moved(before, here, after, 1 - a)
            stack[a * size : (a + 1) * size, tile_of(t)] = turned[:size]
            stack[(near + a) * size : (near + a + 1) * size, tile_of(t)] = turned[size:]
        return carry

    powers = (jnp.zeros((8, lanes), jnp.float32),) * count
    for t in range(tiles):
        load_step(t, 0)
        vertical_step(t, 0)
    smoothed = horizontal(wide, band)
    for t in range(tiles // 2):
        powers = horizontal_step(t, powers)
    for f in range(count):
        power[f * 8 : f * 8 + 8, :] = powers[f]
    pieces[tiles + 3] = pieces[1]
    by_tiles(stack_step, ring, ring)


def column_shift(offset):
    negative = offset < 0
    first = jnp.where(negative, 0, 1)
    amount = jnp.where(negative, offset + lanes, offset)
    back = (lanes - amount) & (lanes - 1)

    def shift(source, t):
        here = source[t + first]
        after = source[t + first + 1]
        return pltpu.roll(jnp.where(lane_of(here.shape) < amount, after, here), back, 1)

    return shift


def reference_rows(raw, smooth, clean, fine, tiles):
    height = clean.shape[1] // 2
    empty = jnp.zeros((2 * height, lanes), jnp.bfloat16)
    for array in (clean, fine):
        array[0] = empty
        array[tiles + 1] = empty
    fine[tiles + 2] = empty
    squares = []
    for t in range(tiles // 2):
        detail = jnp.concatenate([raw(2 * t), raw(2 * t + 1)], axis=1) - smooth(t)
        for array, value in ((clean, cut(smooth(t))), (fine, cut(detail))):
            array[2 * t + 1] = value[:, :lanes]
            array[2 * t + 2] = value[:, lanes:]
        squares.append(detail * detail)
    fine[tiles + 3] = fine[1]
    return squares


def lag_products(stack, fine, stream, folded, base_col, start):
    height = fine.shape[1]
    half = height // 2
    shifts = [column_shift(base_col + near * b - 2) for b in range(far)]
    for t in range(fine.shape[0] - 2):
        for b, shift in enumerate(shifts):
            stream[b * height : (b + 1) * height, tile_of(t)] = shift(fine, t)
    product = lax.dot_general(
        stack[...], stream[...], (((1,), (1,)), ((), ())), preferred_element_type=jnp.float32
    )
    size = product.shape[0] // 2
    folded[...] = jnp.zeros(folded.shape, jnp.float32)
    folded[:, 0 : far * height] = product[:size] + product[size:]
    product = folded[...]
    lane = lane_of(product.shape)
    placed = jnp.zeros_like(product)
    for s in range(2 * far):
        at = s * slot + start
        turned = pltpu.roll(product, at - s * half, 1)
        placed = jnp.where((lane >= at) & (lane < at + half), turned, placed)
    return placed


def near_kernel(
    base, own_odd, own_even, from_even, stack, band, clean, lags, power, rows_in, windows, fine, stream, folded
):
    tiles = own_odd.shape[1] // lanes
    odd = lax.axis_index("rows") % 2 == 1
    height = clean.shape[1] // 2
    empty = jnp.zeros((2 * height, lanes), jnp.bfloat16)
    place_tile(windows, 0, empty)
    place_tile(windows, tiles + 1, empty)
    for t in range(tiles):
        at = tile_of(t)
        outer = own_odd[:, at]
        inner = from_even[:, at]
        rows_in[t, 0:8, :] = jnp.where(odd, inner, outer)
        rows_in[t, 8:16, :] = own_even[:, at]
        rows_in[t, 16:24, :] = jnp.where(odd, outer, inner)
        place_tile(windows, t + 1, cut(vertical(lambda s: rows_in[t, pl.ds(s, height), :])))
    smooth = horizontal(windows, band)
    squares = reference_rows(lambda t: rows_in[t, pl.ds(4, height), :], lambda t: smooth[t], clean, fine, tiles)
    place = lax.broadcasted_iota(jnp.int32, squares[0].shape, 0)
    first = jnp.where(odd, 4, 0)
    own = (place >= first) & (place < first + height - 4)
    total = jnp.zeros((8, lanes), jnp.float32)
    for square in squares:
        square = jnp.where(own, square, 0.0)
        total = total + fold(square[:, :lanes]) + fold(square[:, lanes:])
    power[...] = total
    lags[...] = lag_products(stack, fine, stream, folded, base[0, 1], jnp.where(odd, 0, 8))


def match_kernel(
    base, own_odd, from_odd, near_lags, near_power, stack, power, band, clean, part, rows_in, windows, fine, stream, folded, lags
):
    tiles = own_odd.shape[1] // lanes
    count = power.shape[0] // 8
    rows = folded.shape[0] // (near * count)
    odd = lax.axis_index("rows") % 2 == 1
    edge = at_edge()
    height = clean.shape[1] // 2
    empty = jnp.zeros((2 * height, lanes), jnp.bfloat16)
    place_tile(windows, 0, empty)
    place_tile(windows, tiles + 1, empty)
    for t in range(tiles):
        at = tile_of(t)
        outer = jnp.where(edge, 0.0, from_odd[:, at])
        inner = own_odd[:, at]
        rows_in[t, 0:8, :] = jnp.where(odd, inner, outer)
        rows_in[t, 8:16, :] = jnp.where(odd, outer, inner)
        place_tile(windows, t + 1, cut(vertical(lambda s: rows_in[t, pl.ds(s, height), :])))
    smooth = horizontal(windows, band)
    place = lax.broadcasted_iota(jnp.int32, (height, 2 * lanes), 0)
    first = jnp.where(odd, 0, 4)
    own = (place >= first) & (place < first + 4)
    inside = (place >= jnp.where(edge, first, 0)) & (place < jnp.where(edge, first + 4, height))

    def masked(t):
        return jnp.where(inside, smooth[t], 0.0)

    squares = reference_rows(lambda t: rows_in[t, pl.ds(4, height), :], masked, clean, fine, tiles)
    ref_power = near_power[...]
    for square in squares:
        square = jnp.where(own, square, 0.0)
        ref_power = ref_power + fold(square[:, :lanes]) + fold(square[:, lanes:])
    product = lag_products(stack, fine, stream, folded, base[0, 1], jnp.where(odd, 16, 0))
    product = by_row_shift(product + near_lags[...], rows, -1)
    lags[...] = jnp.zeros(lags.shape, jnp.float32)
    for a in range(near):
        for f in range(count):
            start = (a * count + f) * rows
            lags[f * 8 + a : f * 8 + a + 1, :] = jnp.sum(product[start : start + rows], axis=0, keepdims=True)
    back = 4 * lanes - 1 - base[0, 0]
    across = lax.broadcasted_iota(jnp.int32, (8, lanes), 0)
    lane = lane_of((8, lanes))
    packed = jnp.zeros((8, lanes), jnp.float32)
    for f in range(count):
        block = lags[f * 8 : f * 8 + 8, :]
        for j in range(reach):
            at = (f * reach + j) * reach
            there = back + at - (j // near) * 2 * slot
            high = pltpu.roll(block, there & (lanes - 1), 1)
            low = pltpu.roll(block, (there - slot) & (lanes - 1), 1)
            member = (across == j % near) & (lane >= at) & (lane < at + reach)
            packed = packed + jnp.where(member, high + low, 0.0)
    lags[0:8, :] = jnp.zeros((8, lanes), jnp.float32)
    for f in range(count):
        lags[f : f + 1, :] = jnp.sum(power[f * 8 : f * 8 + 8, :], axis=0, keepdims=True)
    lags[count : count + 1, :] = jnp.sum(ref_power, axis=0, keepdims=True)
    powers = jnp.sum(lags[0:8, :], axis=1, keepdims=True)
    packed = packed + jnp.where(lane == count * reach * reach + across, powers, 0.0)
    packed = jnp.sum(packed, axis=0, keepdims=True)
    for place in range(2):
        offset = base[0, place].astype(jnp.float32)
        packed = jnp.where(lane[0:1] == lanes - 2 + place, offset, packed)
    part[...] = jnp.broadcast_to(packed, part.shape)


def spreader(clean, other, spread, base_col):
    height = clean.shape[1]
    size = height + other.shape[1]
    spare = spread.shape[0] - reach * size
    shifts = [column_shift(base_col + j - 3) for j in range(reach)]

    def spread_tile(t):
        at = tile_of(t)
        for j, shift in enumerate(shifts):
            spread[j * size : j * size + height, at] = shift(clean, t)
            spread[j * size + height : (j + 1) * size, at] = shift(other, t)
        spread[reach * size :, at] = jnp.zeros((spare, lanes), jnp.bfloat16)

    return spread_tile


def blend_terms(totals, count):
    lane = lane_of(totals.shape)
    block = reach * reach
    squared = totals * totals

    def pick(array, low, size):
        return jnp.sum(jnp.where((lane >= low) & (lane < low + size), array, 0.0), axis=1, keepdims=True)

    ref_power = pick(totals, count * block + count, 1)
    terms = []
    for f in range(count):
        norm_product = 0.05 * ((pick(totals, count * block + f, 1) + 1e-06) * (ref_power + 1e-06))
        terms.append((norm_product, 1.0 / (norm_product + pick(squared, f * block, block))))
    return squared, terms


def banded(weights, terms, f, rows, first_row, depth):
    wide = rows + 8
    blank = jnp.zeros((weights.shape[0], depth - lanes), jnp.float32)
    weights = jnp.concatenate([weights, blank], axis=1)
    lane = lane_of(weights.shape)
    line = jnp.zeros_like(weights)
    for j in range(reach):
        at = first_row + j * 2 * wide
        amount = at - (f * reach + j) * reach
        amount = jnp.where(amount < 0, amount + depth, amount)
        line = jnp.where((lane >= at) & (lane < at + reach), pltpu.roll(weights, amount, 1), line)
    band = by_row_shift(jnp.broadcast_to(line[0:1], (rows, depth)), rows, 1)
    middle = first_row + reach // 2 * (2 * wide + 1) + lax.broadcasted_iota(jnp.int32, band.shape, 0)
    band = (band + jnp.where(lane_of(band.shape) == middle, terms[0][0:1], 0.0)) * terms[1][0:1]
    odd = lax.axis_index("rows") % 2 == 1
    row = lane_of(band.shape) % (2 * wide)
    start = jnp.where(odd, 0, 8)
    inner = (row >= start) & (row < start + rows)
    first = pltpu.roll(jnp.where(inner, band, 0.0), jnp.where(odd, 0, depth - 8), 1)
    second = pltpu.roll(jnp.where(inner, 0.0, band), jnp.where(odd, 2 * rows - 16, 2 * rows), 1)
    return first + pltpu.roll(first, rows, 1) + second + pltpu.roll(second, 8, 1)


def pressures(base, totals, clean, other, spread, inverse):
    count, rows, columns = inverse.shape
    depth = spread.shape[0]
    squared, terms = blend_terms(jnp.broadcast_to(totals[0:1, :], (8, lanes)), count)
    bands = [banded(squared, terms[f], f, rows, 1 + base[0, 0], depth) for f in range(count)]
    mixing = cut(jnp.concatenate(bands, axis=0))
    spread_tile = spreader(clean, other, spread, base[0, 1])

    def chunk_values(t):
        where = chunk_of(t)
        spread_tile(2 * t)
        spread_tile(2 * t + 1)
        product = jnp.dot(mixing, spread[:, where], preferred_element_type=jnp.float32)
        registered = product[: count * rows] + product[count * rows :]
        values = []
        for f in range(count):
            ratio = registered[f * rows : (f + 1) * rows] * inverse[f, :, where]
            values.append(calib_zero + ratio * (calib_linear + calib_square * ratio))
        return values

    return chunk_values


def pressure_kernel(base, totals, clean, other, inverse, pressure, moments, part, spread):
    count, rows, columns = inverse.shape
    chunk_values = pressures(base, totals, clean, other, spread, inverse)

    def step(t, sums):
        where = chunk_of(t)
        values = chunk_values(t)
        squares = [value * value for value in values]
        for f in range(count):
            pressure[f, :, where] = values[f]
        moments[0, :, where] = sum(values[1:], values[0])
        moments[1, :, where] = sum(squares[1:], squares[0])
        result = []
        for total, array in zip(sums, values + squares):
            result.append(total + fold(array[:, :lanes]) + fold(array[:, lanes:]))
        return tuple(result)

    zero = jnp.zeros((8, lanes), jnp.float32)
    sums = by_tiles(step, columns // (2 * lanes), columns // (2 * lanes), (zero,) * (2 * count))
    line = zero
    for k in range(2 * count):
        value = jnp.sum(jnp.sum(sums[k], axis=0, keepdims=True), axis=1, keepdims=True)
        line = line + jnp.where(lane_of(line.shape) == k, value, 0.0)
    part[...] = jnp.broadcast_to(line[0:1], part.shape)


def time_kernel(base, totals, clean, other, inverse, moments, time_mean, time_rms, spread):
    count, rows, columns = inverse.shape
    chunk_values = pressures(base, totals, clean, other, spread, inverse)
    frames = 2 * count

    def step(t, carry):
        where = chunk_of(t)
        first = moments[0, :, where]
        second = moments[1, :, where]
        for value in chunk_values(t):
            first = first + value
            second = second + value * value
        mean = first * (1.0 / frames)
        time_mean[:, where] = mean
        time_rms[:, where] = jnp.sqrt(jnp.maximum(second * (1.0 / frames) - mean * mean, 0.0))
        return carry

    by_tiles(step, columns // (2 * lanes), columns // (2 * lanes))


def paired(value, axis, first):
    size = lax.axis_size(axis)
    partner = list(range(size))
    for i in range(first, size - 1, 2):
        partner[i], partner[i + 1] = i + 1, i
    return lax.ppermute(value, axis, list(enumerate(partner)))


def by_parity(odd, array, height, dim):
    length = array.shape[dim]
    low = lax.slice_in_dim(array, 0, height, axis=dim)
    high = lax.slice_in_dim(array, length - height, length, axis=dim)
    return jnp.where(odd, high, low), jnp.where(odd, low, high)


def from_owner(shard, here, odd, axis, root):
    mine = lax.axis_index(axis) == root
    height = shard.shape[0] // 2
    if lax.axis_size(axis) != 2:
        whole = lax.psum(jnp.where(mine, shard, jnp.zeros_like(shard)), axis)
        return by_parity(odd, whole, height, 0)
    here = by_parity(odd, here, height, 0)
    there = [paired(half, axis, 0) for half in here]
    return [jnp.where(mine, own, other) for own, other in zip(here, there)]


def middle_first(size):
    order = sorted(range(size), key=lambda i: (abs(2 * i + 1 - size), i))
    return order


def total_over(value, axis):
    size = lax.axis_size(axis)
    if size & (size - 1):
        return lax.psum(value, axis)
    step = 1
    while step < size:
        value = value + lax.ppermute(value, axis, [(i, i ^ step) for i in range(size)])
        step *= 2
    return value


def shards(frames_raw, wind_off, run_owner, search_base):
    count, rows, columns = frames_raw.shape
    tiles = columns // lanes
    ring = tiles + 2
    wide = rows + 8
    depth = near * count * rows
    size = lax.axis_size("rows")
    f32 = jnp.float32
    bf16 = jnp.bfloat16
    struct = functools.partial(jax.ShapeDtypeStruct, dtype=f32)
    odd = lax.axis_index("rows") % 2 == 1
    run = lax.optimization_barrier(jnp.maximum(wind_off[0], 0.0))
    raw = lax.optimization_barrier(jnp.maximum(frames_raw, 0.0))
    owner, offsets = lax.optimization_barrier((run_owner, jnp.clip(search_base, -8, 8)))
    own_odd, own_even = from_owner(wind_off[0], run, odd, "frames", owner[0])
    from_odd = paired(own_odd, "rows", 1)
    frames_odd, frames_even = by_parity(odd, raw, 4, 1)
    frames_odd = paired(frames_odd, "rows", 1)
    frames_even = paired(frames_even, "rows", 0)
    frames_odd, own_odd = lax.optimization_barrier((frames_odd, own_odd))
    inverse, stack, power, band = pl.pallas_call(
        smooth_kernel,
        out_shape=(
            struct((count, rows, columns)),
            jax.ShapeDtypeStruct((2 * depth, ring * lanes), bf16),
            struct((8 * count, lanes)),
            jax.ShapeDtypeStruct((4 * lanes, 2 * lanes), bf16),
        ),
        in_specs=[vmem] * 3,
        out_specs=(vmem,) * 4,
        scratch_shapes=[
            pltpu.VMEM((count, tiles, rows + 16, lanes), f32),
            pltpu.VMEM((tiles // 2, 2 * count * rows, 4 * lanes), bf16),
            pltpu.VMEM((ring + 2, 2 * count * rows, lanes), bf16),
        ],
        compiler_params=params,
        cost_estimate=cost(8),
        name="smooth",
    )(raw, frames_odd, frames_even)
    own_even, power = lax.optimization_barrier((own_even, power))
    from_even = paired(own_even, "rows", 0)
    blocks = lax.axis_size("frames")
    def reference_scratch(height):
        return [
            pltpu.VMEM((tiles, height + 8, lanes), f32),
            pltpu.VMEM((tiles // 2, 2 * height, 4 * lanes), bf16),
            pltpu.VMEM((ring + 2, 2 * height, lanes), bf16),
            pltpu.VMEM((far * 2 * height, ring * lanes), bf16),
            pltpu.VMEM((depth, lanes), f32),
        ]

    clean, near_lags, near_power = pl.pallas_call(
        near_kernel,
        out_shape=(
            jax.ShapeDtypeStruct((tiles + 2, 2 * rows, lanes), bf16),
            struct((depth, lanes)),
            struct((8, lanes)),
        ),
        in_specs=[smem] + [vmem] * 5,
        out_specs=(vmem,) * 3,
        scratch_shapes=reference_scratch(rows),
        compiler_params=params,
        cost_estimate=cost(8),
        name="near",
    )(offsets, own_odd, own_even, from_even, stack, band)
    other, part = pl.pallas_call(
        match_kernel,
        out_shape=(jax.ShapeDtypeStruct((tiles + 2, 16, lanes), bf16), struct((size, lanes))),
        in_specs=[smem] + [vmem] * 7,
        out_specs=(vmem,) * 2,
        scratch_shapes=reference_scratch(8) + [pltpu.VMEM((8 * count, lanes), f32)],
        compiler_params=params,
        cost_estimate=cost(8),
        name="match",
    )(offsets, own_odd, from_odd, near_lags, near_power, stack, power, band)
    if blocks == 2:
        inverse_out, part = lax.optimization_barrier((inverse, part))
        other_inverse = paired(inverse_out, "frames", 0)
    order = [middle_first(size)]
    parts = lax.all_to_all(part, "rows", 0, 0, axis_index_groups=order, tiled=True)
    totals = jnp.sum(parts, axis=0, keepdims=True)
    depth = -(-reach * 2 * wide // lanes) * lanes
    spread = pltpu.VMEM((depth, columns), bf16)
    pressure, moments, part = pl.pallas_call(
        pressure_kernel,
        out_shape=(struct((count, rows, columns)), struct((2, rows, columns)), struct((size, lanes))),
        in_specs=[smem] + [vmem] * 4,
        out_specs=(vmem, vmem, vmem),
        scratch_shapes=[spread],
        compiler_params=params,
        cost_estimate=cost(12),
        name="pressure",
    )(offsets, totals, clean, other, inverse)
    if blocks == 2:
        row, part = lax.optimization_barrier((totals, part))
        row = paired(row, "frames", 0)
        place = (row[:, lanes - 2 :] / size).astype(jnp.int32)
        time_mean, time_rms = pl.pallas_call(
            time_kernel,
            out_shape=(struct((rows, columns)), struct((rows, columns))),
            in_specs=[smem] + [vmem] * 5,
            out_specs=(vmem, vmem),
            scratch_shapes=[spread],
            compiler_params=params,
            cost_estimate=cost(12),
            name="time",
        )(place, row, clean, other, other_inverse, moments)
    else:
        whole = total_over(moments, "frames")
        total_frames = count * blocks
        time_mean = whole[0] / total_frames
        time_rms = jnp.sqrt(jnp.maximum(whole[1] / total_frames - time_mean * time_mean, 0.0))
    sums = lax.all_to_all(part, "rows", 0, 0, axis_index_groups=order, tiled=True)
    sums, time_mean, time_rms = lax.optimization_barrier((sums, time_mean, time_rms))
    spatial = jnp.sum(sums, axis=0)
    cell_count = rows * columns * size
    frame_mean = spatial[:count] / cell_count
    frame_rms = jnp.sqrt(spatial[count : 2 * count] / cell_count - frame_mean * frame_mean)
    return (pressure, frame_mean, frame_rms, time_mean, time_rms)


def solution(mesh):
    placed = (P("frames", "rows", None), P("frames", "rows", None), P("rows"), P("frames", None))
    return jax.shard_map(
        shards,
        mesh=mesh,
        in_specs=placed,
        out_specs=(
            P("frames", "rows", None),
            P("frames"),
            P("frames"),
            P("rows", None),
            P("rows", None),
        ),
        check_vma=False,
    )
```

```python
import functools

import jax
import jax.numpy as jnp
from jax import lax
from jax.experimental import pallas as pl
from jax.experimental.pallas import tpu as pltpu
from jax.sharding import PartitionSpec as P

taps = (1.0 / 256, 8.0 / 256, 28.0 / 256, 56.0 / 256, 70.0 / 256)
calib_zero = -0.25
calib_linear = 1.0
calib_square = 0.15
lanes = 128
reach = 7
near = 4
far = 2
slot = 32
params = pltpu.CompilerParams(vmem_limit_bytes=14 * 1024 * 1024)
vmem = pl.BlockSpec(memory_space=pltpu.VMEM)
smem = pl.BlockSpec(memory_space=pltpu.SMEM)


def cost(mebibytes):
    return pl.CostEstimate(flops=0, bytes_accessed=mebibytes * 2**20, transcendentals=0)


def tile_of(index):
    if isinstance(index, int):
        return slice(index * lanes, (index + 1) * lanes)
    return pl.ds(pl.multiple_of(index * lanes, lanes), lanes)


def by_tiles(step, tiles, group, init=()):
    if group == tiles:
        for index in range(tiles):
            init = step(index, init)
        return init

    def body(index, carry):
        for inner in range(group):
            carry = step(index * group + inner, carry)
        return carry

    return lax.fori_loop(0, tiles // group, body, init)


def lane_of(shape):
    return lax.broadcasted_iota(jnp.int32, shape, len(shape) - 1)


def fold(product):
    return jnp.sum(product.reshape(product.shape[0] // 8, 8, lanes), axis=0)


def vertical(load):
    total = taps[4] * load(4)
    for step in range(4):
        total = total + taps[step] * (load(step) + load(8 - step))
    return total


def moved(before, here, after, step):
    if step > 0:
        return pltpu.roll(jnp.where(lane_of(here.shape) < step, after, here), lanes - step, 1)
    if step < 0:
        return pltpu.roll(jnp.where(lane_of(here.shape) >= lanes + step, before, here), -step, 1)
    return here


def halves(value):
    high = value.astype(jnp.bfloat16)
    low = (value - high.astype(jnp.float32)).astype(jnp.bfloat16)
    return high, low


def cut(value):
    return jnp.concatenate(halves(value), axis=0)


def fill_band(band):
    shape = (lanes, lanes)
    apart = lax.broadcasted_iota(jnp.int32, shape, 0) - lax.broadcasted_iota(jnp.int32, shape, 1)

    def block(offset):
        distance = jnp.abs(apart + offset)
        value = jnp.zeros(shape, jnp.float32)
        for step in range(5):
            value = jnp.where(distance == step, taps[4 - step], value)
        return value.astype(jnp.bfloat16)

    none = jnp.zeros(shape, jnp.bfloat16)
    before, here, after = block(-lanes), block(0), block(lanes)
    for index, pair in enumerate(((before, none), (here, before), (after, here), (none, after))):
        band[index * lanes : (index + 1) * lanes, :] = jnp.concatenate(pair, axis=1)


def chunk_of(t):
    if isinstance(t, int):
        return slice(t * 2 * lanes, (t + 1) * 2 * lanes)
    return pl.ds(pl.multiple_of(t * 2 * lanes, 2 * lanes), 2 * lanes)


def place_tile(windows, index, value):
    for c in (index // 2 - 1, index // 2):
        at = index - 2 * c
        if 0 <= c < windows.shape[0] and at < 4:
            windows[c, :, at * lanes : (at + 1) * lanes] = value


def horizontal(windows, band):
    chunks, height, width = windows.shape
    product = jnp.dot(
        windows[...].reshape(chunks * height, width), band[...], preferred_element_type=jnp.float32
    )
    product = product.reshape(chunks, height, 2 * lanes)
    return product[:, : height // 2] + product[:, height // 2 :]


def by_row_shift(value, rows, direction):
    place = lax.broadcasted_iota(jnp.int32, value.shape, 0) % rows
    unit = 1
    while unit < rows:
        digit = (place // unit) % 4
        result = value
        for times in range(1, 4):
            amount = times * unit
            turned = pltpu.roll(value, amount if direction > 0 else value.shape[1] - amount, 1)
            result = jnp.where(digit == times, turned, result)
        value = result
        unit *= 4
    return value


def at_edge():
    index = lax.axis_index("rows")
    return (index == 0) | (index == lax.axis_size("rows") - 1)


def smooth_kernel(frames, from_odd, from_even, inverse, stack, power, band, rows_in, wide, pieces):
    count, rows, columns = frames.shape
    tiles = columns // lanes
    ring = tiles + 2
    odd = lax.axis_index("rows") % 2 == 1
    edge = at_edge()
    blank = jnp.zeros((2 * count * rows, lanes), jnp.bfloat16)
    place_tile(wide, 0, blank)
    place_tile(wide, tiles + 1, blank)
    fill_band(band)
    pieces[0] = blank
    pieces[tiles + 1] = blank
    pieces[tiles + 2] = blank

    def load_step(t, carry):
        for f in range(count):
            outer = jnp.where(edge, 0.0, from_odd[f, :, tile_of(t)])
            inner = from_even[f, :, tile_of(t)]
            rows_in[f, t, 4:8, :] = jnp.where(odd, inner, outer)
            rows_in[f, t, 8 : 8 + rows, :] = frames[f, :, tile_of(t)]
            rows_in[f, t, 8 + rows : 12 + rows, :] = jnp.where(odd, outer, inner)
        return carry

    def vertical_step(t, carry):
        parts = [vertical(lambda s: rows_in[f, t, pl.ds(4 + s, rows), :]) for f in range(count)]
        place_tile(wide, t + 1, cut(jnp.concatenate(parts, axis=0)))
        return carry

    def horizontal_step(t, totals):
        smooth = smoothed[t]
        result = []
        details = []
        for f in range(count):
            part = smooth[f * rows : (f + 1) * rows]
            inverse[f, :, chunk_of(t)] = 1.0 / part
            details.append(frames[f, :, chunk_of(t)] - part)
            square = details[f] * details[f]
            result.append(totals[f] + fold(square[:, :lanes]) + fold(square[:, lanes:]))
        detail = cut(jnp.concatenate(details, axis=0))
        pieces[2 * t + 1] = detail[:, :lanes]
        pieces[2 * t + 2] = detail[:, lanes:]
        return tuple(result)

    def stack_step(t, carry):
        before, here, after = pieces[t], pieces[t + 1], pieces[t + 2]
        size = count * rows
        for a in range(near):
            turned = moved(before, here, after, 1 - a)
            stack[a * size : (a + 1) * size, tile_of(t)] = turned[:size]
            stack[(near + a) * size : (near + a + 1) * size, tile_of(t)] = turned[size:]
        return carry

    powers = (jnp.zeros((8, lanes), jnp.float32),) * count
    for t in range(tiles):
        load_step(t, 0)
        vertical_step(t, 0)
    smoothed = horizontal(wide, band)
    for t in range(tiles // 2):
        powers = horizontal_step(t, powers)
    for f in range(count):
        power[f * 8 : f * 8 + 8, :] = powers[f]
    pieces[tiles + 3] = pieces[1]
    by_tiles(stack_step, ring, ring)


def column_shift(offset):
    negative = offset < 0
    first = jnp.where(negative, 0, 1)
    amount = jnp.where(negative, offset + lanes, offset)
    back = (lanes - amount) & (lanes - 1)

    def shift(source, t):
        here = source[t + first]
        after = source[t + first + 1]
        return pltpu.roll(jnp.where(lane_of(here.shape) < amount, after, here), back, 1)

    return shift


def reference_rows(raw, smooth, clean, fine, tiles):
    height = clean.shape[1] // 2
    empty = jnp.zeros((2 * height, lanes), jnp.bfloat16)
    for array in (clean, fine):
        array[0] = empty
        array[tiles + 1] = empty
    fine[tiles + 2] = empty
    squares = []
    for t in range(tiles // 2):
        detail = jnp.concatenate([raw(2 * t), raw(2 * t + 1)], axis=1) - smooth(t)
        for array, value in ((clean, cut(smooth(t))), (fine, cut(detail))):
            array[2 * t + 1] = value[:, :lanes]
            array[2 * t + 2] = value[:, lanes:]
        squares.append(detail * detail)
    fine[tiles + 3] = fine[1]
    return squares


def lag_products(stack, fine, stream, folded, base_col, start):
    height = fine.shape[1]
    half = height // 2
    shifts = [column_shift(base_col + near * b - 2) for b in range(far)]
    for t in range(fine.shape[0] - 2):
        for b, shift in enumerate(shifts):
            stream[b * height : (b + 1) * height, tile_of(t)] = shift(fine, t)
    product = lax.dot_general(
        stack[...], stream[...], (((1,), (1,)), ((), ())), preferred_element_type=jnp.float32
    )
    size = product.shape[0] // 2
    folded[...] = jnp.zeros(folded.shape, jnp.float32)
    folded[:, 0 : far * height] = product[:size] + product[size:]
    product = folded[...]
    lane = lane_of(product.shape)
    placed = jnp.zeros_like(product)
    for s in range(2 * far):
        at = s * slot + start
        turned = pltpu.roll(product, at - s * half, 1)
        placed = jnp.where((lane >= at) & (lane < at + half), turned, placed)
    return placed


def near_kernel(
    base, own_odd, own_even, from_even, stack, band, clean, lags, power, rows_in, windows, fine, stream, folded
):
    tiles = own_odd.shape[1] // lanes
    odd = lax.axis_index("rows") % 2 == 1
    height = clean.shape[1] // 2
    empty = jnp.zeros((2 * height, lanes), jnp.bfloat16)
    place_tile(windows, 0, empty)
    place_tile(windows, tiles + 1, empty)
    for t in range(tiles):
        at = tile_of(t)
        outer = own_odd[:, at]
        inner = from_even[:, at]
        rows_in[t, 0:8, :] = jnp.where(odd, inner, outer)
        rows_in[t, 8:16, :] = own_even[:, at]
        rows_in[t, 16:24, :] = jnp.where(odd, outer, inner)
        place_tile(windows, t + 1, cut(vertical(lambda s: rows_in[t, pl.ds(s, height), :])))
    smooth = horizontal(windows, band)
    squares = reference_rows(lambda t: rows_in[t, pl.ds(4, height), :], lambda t: smooth[t], clean, fine, tiles)
    place = lax.broadcasted_iota(jnp.int32, squares[0].shape, 0)
    first = jnp.where(odd, 4, 0)
    own = (place >= first) & (place < first + height - 4)
    total = jnp.zeros((8, lanes), jnp.float32)
    for square in squares:
        square = jnp.where(own, square, 0.0)
        total = total + fold(square[:, :lanes]) + fold(square[:, lanes:])
    power[...] = total
    lags[...] = lag_products(stack, fine, stream, folded, base[0, 1], jnp.where(odd, 0, 8))


def match_kernel(
    base, own_odd, from_odd, near_lags, near_power, stack, power, band, clean, part, rows_in, windows, fine, stream, folded, lags
):
    tiles = own_odd.shape[1] // lanes
    count = power.shape[0] // 8
    rows = folded.shape[0] // (near * count)
    odd = lax.axis_index("rows") % 2 == 1
    edge = at_edge()
    height = clean.shape[1] // 2
    empty = jnp.zeros((2 * height, lanes), jnp.bfloat16)
    place_tile(windows, 0, empty)
    place_tile(windows, tiles + 1, empty)
    for t in range(tiles):
        at = tile_of(t)
        outer = jnp.where(edge, 0.0, from_odd[:, at])
        inner = own_odd[:, at]
        rows_in[t, 0:8, :] = jnp.where(odd, inner, outer)
        rows_in[t, 8:16, :] = jnp.where(odd, outer, inner)
        place_tile(windows, t + 1, cut(vertical(lambda s: rows_in[t, pl.ds(s, height), :])))
    smooth = horizontal(windows, band)
    place = lax.broadcasted_iota(jnp.int32, (height, 2 * lanes), 0)
    first = jnp.where(odd, 0, 4)
    own = (place >= first) & (place < first + 4)
    inside = (place >= jnp.where(edge, first, 0)) & (place < jnp.where(edge, first + 4, height))

    def masked(t):
        return jnp.where(inside, smooth[t], 0.0)

    squares = reference_rows(lambda t: rows_in[t, pl.ds(4, height), :], masked, clean, fine, tiles)
    ref_power = near_power[...]
    for square in squares:
        square = jnp.where(own, square, 0.0)
        ref_power = ref_power + fold(square[:, :lanes]) + fold(square[:, lanes:])
    product = lag_products(stack, fine, stream, folded, base[0, 1], jnp.where(odd, 16, 0))
    product = by_row_shift(product + near_lags[...], rows, -1)
    lags[...] = jnp.zeros(lags.shape, jnp.float32)
    for a in range(near):
        for f in range(count):
            start = (a * count + f) * rows
            lags[f * 8 + a : f * 8 + a + 1, :] = jnp.sum(product[start : start + rows], axis=0, keepdims=True)
    back = 4 * lanes - 1 - base[0, 0]
    across = lax.broadcasted_iota(jnp.int32, (8, lanes), 0)
    lane = lane_of((8, lanes))
    packed = jnp.zeros((8, lanes), jnp.float32)
    for f in range(count):
        block = lags[f * 8 : f * 8 + 8, :]
        for j in range(reach):
            at = (f * reach + j) * reach
            there = back + at - (j // near) * 2 * slot
            high = pltpu.roll(block, there & (lanes - 1), 1)
            low = pltpu.roll(block, (there - slot) & (lanes - 1), 1)
            member = (across == j % near) & (lane >= at) & (lane < at + reach)
            packed = packed + jnp.where(member, high + low, 0.0)
    lags[0:8, :] = jnp.zeros((8, lanes), jnp.float32)
    for f in range(count):
        lags[f : f + 1, :] = jnp.sum(power[f * 8 : f * 8 + 8, :], axis=0, keepdims=True)
    lags[count : count + 1, :] = jnp.sum(ref_power, axis=0, keepdims=True)
    powers = jnp.sum(lags[0:8, :], axis=1, keepdims=True)
    packed = packed + jnp.where(lane == count * reach * reach + across, powers, 0.0)
    packed = jnp.sum(packed, axis=0, keepdims=True)
    for place in range(2):
        offset = base[0, place].astype(jnp.float32)
        packed = jnp.where(lane[0:1] == lanes - 2 + place, offset, packed)
    part[...] = jnp.broadcast_to(packed, part.shape)


def spreader(clean, other, spread, base_col):
    height = clean.shape[1]
    size = height + other.shape[1]
    spare = spread.shape[0] - reach * size
    shifts = [column_shift(base_col + j - 3) for j in range(reach)]

    def spread_tile(t):
        at = tile_of(t)
        for j, shift in enumerate(shifts):
            spread[j * size : j * size + height, at] = shift(clean, t)
            spread[j * size + height : (j + 1) * size, at] = shift(other, t)
        spread[reach * size :, at] = jnp.zeros((spare, lanes), jnp.bfloat16)

    return spread_tile


def blend_terms(totals, count):
    lane = lane_of(totals.shape)
    block = reach * reach
    squared = totals * totals

    def pick(array, low, size):
        return jnp.sum(jnp.where((lane >= low) & (lane < low + size), array, 0.0), axis=1, keepdims=True)

    ref_power = pick(totals, count * block + count, 1)
    terms = []
    for f in range(count):
        norm_product = 0.05 * ((pick(totals, count * block + f, 1) + 1e-06) * (ref_power + 1e-06))
        terms.append((norm_product, 1.0 / (norm_product + pick(squared, f * block, block))))
    return squared, terms


def banded(weights, terms, f, rows, first_row, depth):
    wide = rows + 8
    blank = jnp.zeros((weights.shape[0], depth - lanes), jnp.float32)
    weights = jnp.concatenate([weights, blank], axis=1)
    lane = lane_of(weights.shape)
    line = jnp.zeros_like(weights)
    for j in range(reach):
        at = first_row + j * 2 * wide
        amount = at - (f * reach + j) * reach
        amount = jnp.where(amount < 0, amount + depth, amount)
        line = jnp.where((lane >= at) & (lane < at + reach), pltpu.roll(weights, amount, 1), line)
    band = by_row_shift(jnp.broadcast_to(line[0:1], (rows, depth)), rows, 1)
    middle = first_row + reach // 2 * (2 * wide + 1) + lax.broadcasted_iota(jnp.int32, band.shape, 0)
    band = (band + jnp.where(lane_of(band.shape) == middle, terms[0][0:1], 0.0)) * terms[1][0:1]
    odd = lax.axis_index("rows") % 2 == 1
    row = lane_of(band.shape) % (2 * wide)
    start = jnp.where(odd, 0, 8)
    inner = (row >= start) & (row < start + rows)
    first = pltpu.roll(jnp.where(inner, band, 0.0), jnp.where(odd, 0, depth - 8), 1)
    second = pltpu.roll(jnp.where(inner, 0.0, band), jnp.where(odd, 2 * rows - 16, 2 * rows), 1)
    return first + pltpu.roll(first, rows, 1) + second + pltpu.roll(second, 8, 1)


def pressures(base, totals, clean, other, spread, inverse):
    count, rows, columns = inverse.shape
    depth = spread.shape[0]
    squared, terms = blend_terms(jnp.broadcast_to(totals[0:1, :], (8, lanes)), count)
    bands = [banded(squared, terms[f], f, rows, 1 + base[0, 0], depth) for f in range(count)]
    mixing = cut(jnp.concatenate(bands, axis=0))
    spread_tile = spreader(clean, other, spread, base[0, 1])

    def chunk_values(t):
        where = chunk_of(t)
        spread_tile(2 * t)
        spread_tile(2 * t + 1)
        product = jnp.dot(mixing, spread[:, where], preferred_element_type=jnp.float32)
        registered = product[: count * rows] + product[count * rows :]
        values = []
        for f in range(count):
            ratio = registered[f * rows : (f + 1) * rows] * inverse[f, :, where]
            values.append(calib_zero + ratio * (calib_linear + calib_square * ratio))
        return values

    return chunk_values


def pressure_kernel(base, totals, clean, other, inverse, pressure, moments, part, spread):
    count, rows, columns = inverse.shape
    chunk_values = pressures(base, totals, clean, other, spread, inverse)

    def step(t, sums):
        where = chunk_of(t)
        values = chunk_values(t)
        squares = [value * value for value in values]
        for f in range(count):
            pressure[f, :, where] = values[f]
        moments[0, :, where] = sum(values[1:], values[0])
        moments[1, :, where] = sum(squares[1:], squares[0])
        result = []
        for total, array in zip(sums, values + squares):
            result.append(total + fold(array[:, :lanes]) + fold(array[:, lanes:]))
        return tuple(result)

    zero = jnp.zeros((8, lanes), jnp.float32)
    sums = by_tiles(step, columns // (2 * lanes), columns // (2 * lanes), (zero,) * (2 * count))
    line = zero
    for k in range(2 * count):
        value = jnp.sum(jnp.sum(sums[k], axis=0, keepdims=True), axis=1, keepdims=True)
        line = line + jnp.where(lane_of(line.shape) == k, value, 0.0)
    part[...] = jnp.broadcast_to(line[0:1], part.shape)


def time_kernel(base, totals, clean, other, inverse, moments, time_mean, time_rms, spread):
    count, rows, columns = inverse.shape
    chunk_values = pressures(base, totals, clean, other, spread, inverse)
    frames = 2 * count

    def step(t, carry):
        where = chunk_of(t)
        first = moments[0, :, where]
        second = moments[1, :, where]
        for value in chunk_values(t):
            first = first + value
            second = second + value * value
        mean = first * (1.0 / frames)
        time_mean[:, where] = mean
        time_rms[:, where] = jnp.sqrt(jnp.maximum(second * (1.0 / frames) - mean * mean, 0.0))
        return carry

    by_tiles(step, columns // (2 * lanes), columns // (2 * lanes))


def paired(value, axis, first):
    size = lax.axis_size(axis)
    partner = list(range(size))
    for i in range(first, size - 1, 2):
        partner[i], partner[i + 1] = i + 1, i
    return lax.ppermute(value, axis, list(enumerate(partner)))


def by_parity(odd, array, height, dim):
    length = array.shape[dim]
    low = lax.slice_in_dim(array, 0, height, axis=dim)
    high = lax.slice_in_dim(array, length - height, length, axis=dim)
    return jnp.where(odd, high, low), jnp.where(odd, low, high)


def from_owner(shard, here, odd, axis, root):
    mine = lax.axis_index(axis) == root
    height = shard.shape[0] // 2
    if lax.axis_size(axis) != 2:
        whole = lax.psum(jnp.where(mine, shard, jnp.zeros_like(shard)), axis)
        return by_parity(odd, whole, height, 0)
    there = by_parity(odd, paired(shard, axis, 0), height, 0)
    here = by_parity(odd, here, height, 0)
    return [jnp.where(mine, own, other) for own, other in zip(here, there)]


def begun_at(first, size):
    return [[(i + first) % size for i in range(size)]]


def total_over(value, axis):
    size = lax.axis_size(axis)
    if size & (size - 1):
        return lax.psum(value, axis)
    step = 1
    while step < size:
        value = value + lax.ppermute(value, axis, [(i, i ^ step) for i in range(size)])
        step *= 2
    return value


def shards(frames_raw, wind_off, run_owner, search_base):
    count, rows, columns = frames_raw.shape
    tiles = columns // lanes
    ring = tiles + 2
    wide = rows + 8
    depth = near * count * rows
    size = lax.axis_size("rows")
    f32 = jnp.float32
    bf16 = jnp.bfloat16
    struct = functools.partial(jax.ShapeDtypeStruct, dtype=f32)
    odd = lax.axis_index("rows") % 2 == 1
    raw, run = lax.optimization_barrier((jnp.maximum(frames_raw, 0.0), jnp.maximum(wind_off[0], 0.0)))
    owner, offsets = lax.optimization_barrier((run_owner, jnp.clip(search_base, -8, 8)))
    own_odd, own_even = from_owner(wind_off[0], run, odd, "frames", owner[0])
    from_odd = paired(own_odd, "rows", 1)
    from_even = paired(own_even, "rows", 0)
    frames_odd, frames_even = by_parity(odd, raw, 4, 1)
    frames_odd = paired(frames_odd, "rows", 1)
    frames_even = paired(frames_even, "rows", 0)
    frames_odd, own_odd = lax.optimization_barrier((frames_odd, own_odd))
    inverse, stack, power, band = pl.pallas_call(
        smooth_kernel,
        out_shape=(
            struct((count, rows, columns)),
            jax.ShapeDtypeStruct((2 * depth, ring * lanes), bf16),
            struct((8 * count, lanes)),
            jax.ShapeDtypeStruct((4 * lanes, 2 * lanes), bf16),
        ),
        in_specs=[vmem] * 3,
        out_specs=(vmem,) * 4,
        scratch_shapes=[
            pltpu.VMEM((count, tiles, rows + 16, lanes), f32),
            pltpu.VMEM((tiles // 2, 2 * count * rows, 4 * lanes), bf16),
            pltpu.VMEM((ring + 2, 2 * count * rows, lanes), bf16),
        ],
        compiler_params=params,
        cost_estimate=cost(8),
        name="smooth",
    )(raw, frames_odd, frames_even)
    blocks = lax.axis_size("frames")
    def reference_scratch(height):
        return [
            pltpu.VMEM((tiles, height + 8, lanes), f32),
            pltpu.VMEM((tiles // 2, 2 * height, 4 * lanes), bf16),
            pltpu.VMEM((ring + 2, 2 * height, lanes), bf16),
            pltpu.VMEM((far * 2 * height, ring * lanes), bf16),
            pltpu.VMEM((depth, lanes), f32),
        ]

    clean, near_lags, near_power = pl.pallas_call(
        near_kernel,
        out_shape=(
            jax.ShapeDtypeStruct((tiles + 2, 2 * rows, lanes), bf16),
            struct((depth, lanes)),
            struct((8, lanes)),
        ),
        in_specs=[smem] + [vmem] * 5,
        out_specs=(vmem,) * 3,
        scratch_shapes=reference_scratch(rows),
        compiler_params=params,
        cost_estimate=cost(8),
        name="near",
    )(offsets, own_odd, own_even, from_even, stack, band)
    other, part = pl.pallas_call(
        match_kernel,
        out_shape=(jax.ShapeDtypeStruct((tiles + 2, 16, lanes), bf16), struct((size, lanes))),
        in_specs=[smem] + [vmem] * 7,
        out_specs=(vmem,) * 2,
        scratch_shapes=reference_scratch(8) + [pltpu.VMEM((8 * count, lanes), f32)],
        compiler_params=params,
        cost_estimate=cost(8),
        name="match",
    )(offsets, own_odd, from_odd, near_lags, near_power, stack, power, band)
    if blocks == 2:
        inverse_out, part = lax.optimization_barrier((inverse, part))
        other_inverse = paired(inverse_out, "frames", 0)
    parts = lax.all_to_all(part, "rows", 0, 0, axis_index_groups=begun_at(size // 2, size), tiled=True)
    totals = jnp.sum(parts, axis=0, keepdims=True)
    depth = -(-reach * 2 * wide // lanes) * lanes
    spread = pltpu.VMEM((depth, columns), bf16)
    pressure, moments, part = pl.pallas_call(
        pressure_kernel,
        out_shape=(struct((count, rows, columns)), struct((2, rows, columns)), struct((size, lanes))),
        in_specs=[smem] + [vmem] * 4,
        out_specs=(vmem, vmem, vmem),
        scratch_shapes=[spread],
        compiler_params=params,
        cost_estimate=cost(12),
        name="pressure",
    )(offsets, totals, clean, other, inverse)
    if blocks == 2:
        row, part = lax.optimization_barrier((totals, part))
        row = paired(row, "frames", 0)
        place = (row[:, lanes - 2 :] / size).astype(jnp.int32)
        time_mean, time_rms = pl.pallas_call(
            time_kernel,
            out_shape=(struct((rows, columns)), struct((rows, columns))),
            in_specs=[smem] + [vmem] * 5,
            out_specs=(vmem, vmem),
            scratch_shapes=[spread],
            compiler_params=params,
            cost_estimate=cost(12),
            name="time",
        )(place, row, clean, other, other_inverse, moments)
    else:
        whole = total_over(moments, "frames")
        total_frames = count * blocks
        time_mean = whole[0] / total_frames
        time_rms = jnp.sqrt(jnp.maximum(whole[1] / total_frames - time_mean * time_mean, 0.0))
    sums = lax.all_to_all(part, "rows", 0, 0, axis_index_groups=begun_at(size // 2 + 1, size), tiled=True)
    sums, time_mean, time_rms = lax.optimization_barrier((sums, time_mean, time_rms))
    spatial = jnp.sum(sums, axis=0)
    cell_count = rows * columns * size
    frame_mean = spatial[:count] / cell_count
    frame_rms = jnp.sqrt(spatial[count : 2 * count] / cell_count - frame_mean * frame_mean)
    return (pressure, frame_mean, frame_rms, time_mean, time_rms)


def solution(mesh):
    placed = (P("frames", "rows", None), P("frames", "rows", None), P("rows"), P("frames", None))
    return jax.shard_map(
        shards,
        mesh=mesh,
        in_specs=placed,
        out_specs=(
            P("frames", "rows", None),
            P("frames"),
            P("frames"),
            P("rows", None),
            P("rows", None),
        ),
        check_vma=False,
    )
```

```python
import functools

import jax
import jax.numpy as jnp
from jax import lax
from jax.experimental import pallas as pl
from jax.experimental.pallas import tpu as pltpu
from jax.sharding import PartitionSpec as P

taps = (1.0 / 256, 8.0 / 256, 28.0 / 256, 56.0 / 256, 70.0 / 256)
calib_zero = -0.25
calib_linear = 1.0
calib_square = 0.15
lanes = 128
reach = 7
near = 4
far = 2
slot = 32
params = pltpu.CompilerParams(vmem_limit_bytes=14 * 1024 * 1024)
vmem = pl.BlockSpec(memory_space=pltpu.VMEM)
smem = pl.BlockSpec(memory_space=pltpu.SMEM)


def cost(mebibytes):
    return pl.CostEstimate(flops=0, bytes_accessed=mebibytes * 2**20, transcendentals=0)


def tile_of(index):
    if isinstance(index, int):
        return slice(index * lanes, (index + 1) * lanes)
    return pl.ds(pl.multiple_of(index * lanes, lanes), lanes)


def by_tiles(step, tiles, group, init=()):
    if group == tiles:
        for index in range(tiles):
            init = step(index, init)
        return init

    def body(index, carry):
        for inner in range(group):
            carry = step(index * group + inner, carry)
        return carry

    return lax.fori_loop(0, tiles // group, body, init)


def lane_of(shape):
    return lax.broadcasted_iota(jnp.int32, shape, len(shape) - 1)


def fold(product):
    return jnp.sum(product.reshape(product.shape[0] // 8, 8, lanes), axis=0)


def vertical(load):
    total = taps[4] * load(4)
    for step in range(4):
        total = total + taps[step] * (load(step) + load(8 - step))
    return total


def moved(before, here, after, step):
    if step > 0:
        return pltpu.roll(jnp.where(lane_of(here.shape) < step, after, here), lanes - step, 1)
    if step < 0:
        return pltpu.roll(jnp.where(lane_of(here.shape) >= lanes + step, before, here), -step, 1)
    return here


def halves(value):
    high = value.astype(jnp.bfloat16)
    low = (value - high.astype(jnp.float32)).astype(jnp.bfloat16)
    return high, low


def cut(value):
    return jnp.concatenate(halves(value), axis=0)


def fill_band(band):
    shape = (lanes, lanes)
    apart = lax.broadcasted_iota(jnp.int32, shape, 0) - lax.broadcasted_iota(jnp.int32, shape, 1)

    def block(offset):
        distance = jnp.abs(apart + offset)
        value = jnp.zeros(shape, jnp.float32)
        for step in range(5):
            value = jnp.where(distance == step, taps[4 - step], value)
        return value.astype(jnp.bfloat16)

    none = jnp.zeros(shape, jnp.bfloat16)
    before, here, after = block(-lanes), block(0), block(lanes)
    for index, pair in enumerate(((before, none), (here, before), (after, here), (none, after))):
        band[index * lanes : (index + 1) * lanes, :] = jnp.concatenate(pair, axis=1)


def chunk_of(t):
    if isinstance(t, int):
        return slice(t * 2 * lanes, (t + 1) * 2 * lanes)
    return pl.ds(pl.multiple_of(t * 2 * lanes, 2 * lanes), 2 * lanes)


def place_tile(windows, index, value):
    for c in (index // 2 - 1, index // 2):
        at = index - 2 * c
        if 0 <= c < windows.shape[0] and at < 4:
            windows[c, :, at * lanes : (at + 1) * lanes] = value


def horizontal(windows, band):
    chunks, height, width = windows.shape
    product = jnp.dot(
        windows[...].reshape(chunks * height, width), band[...], preferred_element_type=jnp.float32
    )
    product = product.reshape(chunks, height, 2 * lanes)
    return product[:, : height // 2] + product[:, height // 2 :]


def by_row_shift(value, rows, direction):
    place = lax.broadcasted_iota(jnp.int32, value.shape, 0) % rows
    unit = 1
    while unit < rows:
        digit = (place // unit) % 4
        result = value
        for times in range(1, 4):
            amount = times * unit
            turned = pltpu.roll(value, amount if direction > 0 else value.shape[1] - amount, 1)
            result = jnp.where(digit == times, turned, result)
        value = result
        unit *= 4
    return value


def at_edge():
    index = lax.axis_index("rows")
    return (index == 0) | (index == lax.axis_size("rows") - 1)


def smooth_kernel(frames, from_odd, from_even, inverse, stack, power, band, rows_in, wide, pieces):
    count, rows, columns = frames.shape
    tiles = columns // lanes
    ring = tiles + 2
    odd = lax.axis_index("rows") % 2 == 1
    edge = at_edge()
    blank = jnp.zeros((2 * count * rows, lanes), jnp.bfloat16)
    place_tile(wide, 0, blank)
    place_tile(wide, tiles + 1, blank)
    fill_band(band)
    pieces[0] = blank
    pieces[tiles + 1] = blank
    pieces[tiles + 2] = blank

    def load_step(t, carry):
        for f in range(count):
            outer = jnp.where(edge, 0.0, from_odd[f, :, tile_of(t)])
            inner = from_even[f, :, tile_of(t)]
            rows_in[f, t, 4:8, :] = jnp.where(odd, inner, outer)
            rows_in[f, t, 8 : 8 + rows, :] = frames[f, :, tile_of(t)]
            rows_in[f, t, 8 + rows : 12 + rows, :] = jnp.where(odd, outer, inner)
        return carry

    def vertical_step(t, carry):
        parts = [vertical(lambda s: rows_in[f, t, pl.ds(4 + s, rows), :]) for f in range(count)]
        place_tile(wide, t + 1, cut(jnp.concatenate(parts, axis=0)))
        return carry

    def horizontal_step(t, totals):
        smooth = smoothed[t]
        result = []
        details = []
        for f in range(count):
            part = smooth[f * rows : (f + 1) * rows]
            inverse[f, :, chunk_of(t)] = 1.0 / part
            details.append(frames[f, :, chunk_of(t)] - part)
            square = details[f] * details[f]
            result.append(totals[f] + fold(square[:, :lanes]) + fold(square[:, lanes:]))
        detail = cut(jnp.concatenate(details, axis=0))
        pieces[2 * t + 1] = detail[:, :lanes]
        pieces[2 * t + 2] = detail[:, lanes:]
        return tuple(result)

    def stack_step(t, carry):
        before, here, after = pieces[t], pieces[t + 1], pieces[t + 2]
        size = count * rows
        for a in range(near):
            turned = moved(before, here, after, 1 - a)
            stack[a * size : (a + 1) * size, tile_of(t)] = turned[:size]
            stack[(near + a) * size : (near + a + 1) * size, tile_of(t)] = turned[size:]
        return carry

    powers = (jnp.zeros((8, lanes), jnp.float32),) * count
    for t in range(tiles):
        load_step(t, 0)
        vertical_step(t, 0)
    smoothed = horizontal(wide, band)
    for t in range(tiles // 2):
        powers = horizontal_step(t, powers)
    for f in range(count):
        power[f * 8 : f * 8 + 8, :] = powers[f]
    pieces[tiles + 3] = pieces[1]
    by_tiles(stack_step, ring, ring)


def column_shift(offset):
    negative = offset < 0
    first = jnp.where(negative, 0, 1)
    amount = jnp.where(negative, offset + lanes, offset)
    back = (lanes - amount) & (lanes - 1)

    def shift(source, t):
        here = source[t + first]
        after = source[t + first + 1]
        return pltpu.roll(jnp.where(lane_of(here.shape) < amount, after, here), back, 1)

    return shift


def reference_rows(raw, smooth, clean, fine, tiles):
    height = clean.shape[1] // 2
    empty = jnp.zeros((2 * height, lanes), jnp.bfloat16)
    for array in (clean, fine):
        array[0] = empty
        array[tiles + 1] = empty
    fine[tiles + 2] = empty
    squares = []
    for t in range(tiles // 2):
        detail = jnp.concatenate([raw(2 * t), raw(2 * t + 1)], axis=1) - smooth(t)
        for array, value in ((clean, cut(smooth(t))), (fine, cut(detail))):
            array[2 * t + 1] = value[:, :lanes]
            array[2 * t + 2] = value[:, lanes:]
        squares.append(detail * detail)
    fine[tiles + 3] = fine[1]
    return squares


def lag_products(stack, fine, stream, folded, base_col, start):
    height = fine.shape[1]
    half = height // 2
    shifts = [column_shift(base_col + near * b - 2) for b in range(far)]
    for t in range(fine.shape[0] - 2):
        for b, shift in enumerate(shifts):
            stream[b * height : (b + 1) * height, tile_of(t)] = shift(fine, t)
    product = lax.dot_general(
        stack[...], stream[...], (((1,), (1,)), ((), ())), preferred_element_type=jnp.float32
    )
    size = product.shape[0] // 2
    folded[...] = jnp.zeros(folded.shape, jnp.float32)
    folded[:, 0 : far * height] = product[:size] + product[size:]
    product = folded[...]
    lane = lane_of(product.shape)
    placed = jnp.zeros_like(product)
    for s in range(2 * far):
        at = s * slot + start
        turned = pltpu.roll(product, at - s * half, 1)
        placed = jnp.where((lane >= at) & (lane < at + half), turned, placed)
    return placed


def near_kernel(
    base, own_odd, own_even, from_even, stack, band, clean, lags, power, rows_in, windows, fine, stream, folded
):
    tiles = own_odd.shape[1] // lanes
    odd = lax.axis_index("rows") % 2 == 1
    height = clean.shape[1] // 2
    empty = jnp.zeros((2 * height, lanes), jnp.bfloat16)
    place_tile(windows, 0, empty)
    place_tile(windows, tiles + 1, empty)
    for t in range(tiles):
        at = tile_of(t)
        outer = own_odd[:, at]
        inner = from_even[:, at]
        rows_in[t, 0:8, :] = jnp.where(odd, inner, outer)
        rows_in[t, 8:16, :] = own_even[:, at]
        rows_in[t, 16:24, :] = jnp.where(odd, outer, inner)
        place_tile(windows, t + 1, cut(vertical(lambda s: rows_in[t, pl.ds(s, height), :])))
    smooth = horizontal(windows, band)
    squares = reference_rows(lambda t: rows_in[t, pl.ds(4, height), :], lambda t: smooth[t], clean, fine, tiles)
    place = lax.broadcasted_iota(jnp.int32, squares[0].shape, 0)
    first = jnp.where(odd, 4, 0)
    own = (place >= first) & (place < first + height - 4)
    total = jnp.zeros((8, lanes), jnp.float32)
    for square in squares:
        square = jnp.where(own, square, 0.0)
        total = total + fold(square[:, :lanes]) + fold(square[:, lanes:])
    power[...] = total
    lags[...] = lag_products(stack, fine, stream, folded, base[0, 1], jnp.where(odd, 0, 8))


def match_kernel(
    base, own_odd, from_odd, near_lags, near_power, stack, power, band, clean, part, rows_in, windows, fine, stream, folded, lags
):
    tiles = own_odd.shape[1] // lanes
    count = power.shape[0] // 8
    rows = folded.shape[0] // (near * count)
    odd = lax.axis_index("rows") % 2 == 1
    edge = at_edge()
    height = clean.shape[1] // 2
    empty = jnp.zeros((2 * height, lanes), jnp.bfloat16)
    place_tile(windows, 0, empty)
    place_tile(windows, tiles + 1, empty)
    for t in range(tiles):
        at = tile_of(t)
        outer = jnp.where(edge, 0.0, from_odd[:, at])
        inner = own_odd[:, at]
        rows_in[t, 0:8, :] = jnp.where(odd, inner, outer)
        rows_in[t, 8:16, :] = jnp.where(odd, outer, inner)
        place_tile(windows, t + 1, cut(vertical(lambda s: rows_in[t, pl.ds(s, height), :])))
    smooth = horizontal(windows, band)
    place = lax.broadcasted_iota(jnp.int32, (height, 2 * lanes), 0)
    first = jnp.where(odd, 0, 4)
    own = (place >= first) & (place < first + 4)
    inside = (place >= jnp.where(edge, first, 0)) & (place < jnp.where(edge, first + 4, height))

    def masked(t):
        return jnp.where(inside, smooth[t], 0.0)

    squares = reference_rows(lambda t: rows_in[t, pl.ds(4, height), :], masked, clean, fine, tiles)
    ref_power = near_power[...]
    for square in squares:
        square = jnp.where(own, square, 0.0)
        ref_power = ref_power + fold(square[:, :lanes]) + fold(square[:, lanes:])
    product = lag_products(stack, fine, stream, folded, base[0, 1], jnp.where(odd, 16, 0))
    product = by_row_shift(product + near_lags[...], rows, -1)
    lags[...] = jnp.zeros(lags.shape, jnp.float32)
    for a in range(near):
        for f in range(count):
            start = (a * count + f) * rows
            lags[f * 8 + a : f * 8 + a + 1, :] = jnp.sum(product[start : start + rows], axis=0, keepdims=True)
    back = 4 * lanes - 1 - base[0, 0]
    across = lax.broadcasted_iota(jnp.int32, (8, lanes), 0)
    lane = lane_of((8, lanes))
    packed = jnp.zeros((8, lanes), jnp.float32)
    for f in range(count):
        block = lags[f * 8 : f * 8 + 8, :]
        for j in range(reach):
            at = (f * reach + j) * reach
            there = back + at - (j // near) * 2 * slot
            high = pltpu.roll(block, there & (lanes - 1), 1)
            low = pltpu.roll(block, (there - slot) & (lanes - 1), 1)
            member = (across == j % near) & (lane >= at) & (lane < at + reach)
            packed = packed + jnp.where(member, high + low, 0.0)
    lags[0:8, :] = jnp.zeros((8, lanes), jnp.float32)
    for f in range(count):
        lags[f : f + 1, :] = jnp.sum(power[f * 8 : f * 8 + 8, :], axis=0, keepdims=True)
    lags[count : count + 1, :] = jnp.sum(ref_power, axis=0, keepdims=True)
    powers = jnp.sum(lags[0:8, :], axis=1, keepdims=True)
    packed = packed + jnp.where(lane == count * reach * reach + across, powers, 0.0)
    packed = jnp.sum(packed, axis=0, keepdims=True)
    for place in range(2):
        offset = base[0, place].astype(jnp.float32)
        packed = jnp.where(lane[0:1] == lanes - 2 + place, offset, packed)
    part[...] = jnp.broadcast_to(packed, part.shape)


def spreader(clean, other, spread, base_col):
    height = clean.shape[1]
    size = height + other.shape[1]
    spare = spread.shape[0] - reach * size
    shifts = [column_shift(base_col + j - 3) for j in range(reach)]

    def spread_tile(t):
        at = tile_of(t)
        for j, shift in enumerate(shifts):
            spread[j * size : j * size + height, at] = shift(clean, t)
            spread[j * size + height : (j + 1) * size, at] = shift(other, t)
        spread[reach * size :, at] = jnp.zeros((spare, lanes), jnp.bfloat16)

    return spread_tile


def blend_terms(totals, count):
    lane = lane_of(totals.shape)
    block = reach * reach
    squared = totals * totals

    def pick(array, low, size):
        return jnp.sum(jnp.where((lane >= low) & (lane < low + size), array, 0.0), axis=1, keepdims=True)

    ref_power = pick(totals, count * block + count, 1)
    terms = []
    for f in range(count):
        norm_product = 0.05 * ((pick(totals, count * block + f, 1) + 1e-06) * (ref_power + 1e-06))
        terms.append((norm_product, 1.0 / (norm_product + pick(squared, f * block, block))))
    return squared, terms


def banded(weights, terms, f, rows, first_row, depth):
    wide = rows + 8
    blank = jnp.zeros((weights.shape[0], depth - lanes), jnp.float32)
    weights = jnp.concatenate([weights, blank], axis=1)
    lane = lane_of(weights.shape)
    line = jnp.zeros_like(weights)
    for j in range(reach):
        at = first_row + j * 2 * wide
        amount = at - (f * reach + j) * reach
        amount = jnp.where(amount < 0, amount + depth, amount)
        line = jnp.where((lane >= at) & (lane < at + reach), pltpu.roll(weights, amount, 1), line)
    band = by_row_shift(jnp.broadcast_to(line[0:1], (rows, depth)), rows, 1)
    middle = first_row + reach // 2 * (2 * wide + 1) + lax.broadcasted_iota(jnp.int32, band.shape, 0)
    band = (band + jnp.where(lane_of(band.shape) == middle, terms[0][0:1], 0.0)) * terms[1][0:1]
    odd = lax.axis_index("rows") % 2 == 1
    row = lane_of(band.shape) % (2 * wide)
    start = jnp.where(odd, 0, 8)
    inner = (row >= start) & (row < start + rows)
    first = pltpu.roll(jnp.where(inner, band, 0.0), jnp.where(odd, 0, depth - 8), 1)
    second = pltpu.roll(jnp.where(inner, 0.0, band), jnp.where(odd, 2 * rows - 16, 2 * rows), 1)
    return first + pltpu.roll(first, rows, 1) + second + pltpu.roll(second, 8, 1)


def pressures(base, totals, clean, other, spread, inverse):
    count, rows, columns = inverse.shape
    depth = spread.shape[0]
    squared, terms = blend_terms(jnp.broadcast_to(totals[0:1, :], (8, lanes)), count)
    bands = [banded(squared, terms[f], f, rows, 1 + base[0, 0], depth) for f in range(count)]
    mixing = cut(jnp.concatenate(bands, axis=0))
    spread_tile = spreader(clean, other, spread, base[0, 1])

    def chunk_values(t):
        where = chunk_of(t)
        spread_tile(2 * t)
        spread_tile(2 * t + 1)
        product = jnp.dot(mixing, spread[:, where], preferred_element_type=jnp.float32)
        registered = product[: count * rows] + product[count * rows :]
        values = []
        for f in range(count):
            ratio = registered[f * rows : (f + 1) * rows] * inverse[f, :, where]
            values.append(calib_zero + ratio * (calib_linear + calib_square * ratio))
        return values

    return chunk_values


def pressure_kernel(base, totals, clean, other, inverse, pressure, moments, part, spread):
    count, rows, columns = inverse.shape
    chunk_values = pressures(base, totals, clean, other, spread, inverse)

    def step(t, sums):
        where = chunk_of(t)
        values = chunk_values(t)
        squares = [value * value for value in values]
        for f in range(count):
            pressure[f, :, where] = values[f]
        moments[0, :, where] = sum(values[1:], values[0])
        moments[1, :, where] = sum(squares[1:], squares[0])
        result = []
        for total, array in zip(sums, values + squares):
            result.append(total + fold(array[:, :lanes]) + fold(array[:, lanes:]))
        return tuple(result)

    zero = jnp.zeros((8, lanes), jnp.float32)
    sums = by_tiles(step, columns // (2 * lanes), columns // (2 * lanes), (zero,) * (2 * count))
    line = zero
    for k in range(2 * count):
        value = jnp.sum(jnp.sum(sums[k], axis=0, keepdims=True), axis=1, keepdims=True)
        line = line + jnp.where(lane_of(line.shape) == k, value, 0.0)
    part[...] = jnp.broadcast_to(line[0:1], part.shape)


def time_kernel(base, totals, clean, other, inverse, moments, time_mean, time_rms, spread):
    count, rows, columns = inverse.shape
    chunk_values = pressures(base, totals, clean, other, spread, inverse)
    frames = 2 * count

    def step(t, carry):
        where = chunk_of(t)
        first = moments[0, :, where]
        second = moments[1, :, where]
        for value in chunk_values(t):
            first = first + value
            second = second + value * value
        mean = first * (1.0 / frames)
        time_mean[:, where] = mean
        time_rms[:, where] = jnp.sqrt(jnp.maximum(second * (1.0 / frames) - mean * mean, 0.0))
        return carry

    by_tiles(step, columns // (2 * lanes), columns // (2 * lanes))


def paired(value, axis, first):
    size = lax.axis_size(axis)
    partner = list(range(size))
    for i in range(first, size - 1, 2):
        partner[i], partner[i + 1] = i + 1, i
    return lax.ppermute(value, axis, list(enumerate(partner)))


def by_parity(odd, array, height, dim):
    length = array.shape[dim]
    low = lax.slice_in_dim(array, 0, height, axis=dim)
    high = lax.slice_in_dim(array, length - height, length, axis=dim)
    return jnp.where(odd, high, low), jnp.where(odd, low, high)


def from_owner(shard, here, odd, axis, root):
    mine = lax.axis_index(axis) == root
    height = shard.shape[0] // 2
    if lax.axis_size(axis) != 2:
        whole = lax.psum(jnp.where(mine, shard, jnp.zeros_like(shard)), axis)
        return by_parity(odd, whole, height, 0)
    there = by_parity(odd, paired(shard, axis, 0), height, 0)
    here = by_parity(odd, here, height, 0)
    return [jnp.where(mine, own, other) for own, other in zip(here, there)]


def begun_at(first, size):
    return [[(i + first) % size for i in range(size)]]


def total_over(value, axis):
    size = lax.axis_size(axis)
    if size & (size - 1):
        return lax.psum(value, axis)
    step = 1
    while step < size:
        value = value + lax.ppermute(value, axis, [(i, i ^ step) for i in range(size)])
        step *= 2
    return value


def shards(frames_raw, wind_off, run_owner, search_base):
    count, rows, columns = frames_raw.shape
    tiles = columns // lanes
    ring = tiles + 2
    wide = rows + 8
    depth = near * count * rows
    size = lax.axis_size("rows")
    f32 = jnp.float32
    bf16 = jnp.bfloat16
    struct = functools.partial(jax.ShapeDtypeStruct, dtype=f32)
    odd = lax.axis_index("rows") % 2 == 1
    raw, run = lax.optimization_barrier((jnp.maximum(frames_raw, 0.0), jnp.maximum(wind_off[0], 0.0)))
    owner, offsets = lax.optimization_barrier((run_owner, jnp.clip(search_base, -8, 8)))
    own_odd, own_even = from_owner(wind_off[0], run, odd, "frames", owner[0])
    from_odd = paired(own_odd, "rows", 1)
    from_even = paired(own_even, "rows", 0)
    frames_odd, frames_even = by_parity(odd, raw, 4, 1)
    frames_odd = paired(frames_odd, "rows", 1)
    frames_even = paired(frames_even, "rows", 0)
    frames_odd, own_odd = lax.optimization_barrier((frames_odd, own_odd))
    inverse, stack, power, band = pl.pallas_call(
        smooth_kernel,
        out_shape=(
            struct((count, rows, columns)),
            jax.ShapeDtypeStruct((2 * depth, ring * lanes), bf16),
            struct((8 * count, lanes)),
            jax.ShapeDtypeStruct((4 * lanes, 2 * lanes), bf16),
        ),
        in_specs=[vmem] * 3,
        out_specs=(vmem,) * 4,
        scratch_shapes=[
            pltpu.VMEM((count, tiles, rows + 16, lanes), f32),
            pltpu.VMEM((tiles // 2, 2 * count * rows, 4 * lanes), bf16),
            pltpu.VMEM((ring + 2, 2 * count * rows, lanes), bf16),
        ],
        compiler_params=params,
        cost_estimate=cost(8),
        name="smooth",
    )(raw, frames_odd, frames_even)
    blocks = lax.axis_size("frames")
    def reference_scratch(height):
        return [
            pltpu.VMEM((tiles, height + 8, lanes), f32),
            pltpu.VMEM((tiles // 2, 2 * height, 4 * lanes), bf16),
            pltpu.VMEM((ring + 2, 2 * height, lanes), bf16),
            pltpu.VMEM((far * 2 * height, ring * lanes), bf16),
            pltpu.VMEM((depth, lanes), f32),
        ]

    clean, near_lags, near_power = pl.pallas_call(
        near_kernel,
        out_shape=(
            jax.ShapeDtypeStruct((tiles + 2, 2 * rows, lanes), bf16),
            struct((depth, lanes)),
            struct((8, lanes)),
        ),
        in_specs=[smem] + [vmem] * 5,
        out_specs=(vmem,) * 3,
        scratch_shapes=reference_scratch(rows),
        compiler_params=params,
        cost_estimate=cost(8),
        name="near",
    )(offsets, own_odd, own_even, from_even, stack, band)
    other, part = pl.pallas_call(
        match_kernel,
        out_shape=(jax.ShapeDtypeStruct((tiles + 2, 16, lanes), bf16), struct((size, lanes))),
        in_specs=[smem] + [vmem] * 7,
        out_specs=(vmem,) * 2,
        scratch_shapes=reference_scratch(8) + [pltpu.VMEM((8 * count, lanes), f32)],
        compiler_params=params,
        cost_estimate=cost(8),
        name="match",
    )(offsets, own_odd, from_odd, near_lags, near_power, stack, power, band)
    if blocks == 2:
        inverse_out, part = lax.optimization_barrier((inverse, part))
        other_inverse = paired(inverse_out, "frames", 0)
    parts = lax.all_to_all(part, "rows", 0, 0, axis_index_groups=begun_at(size // 2 + 1, size), tiled=True)
    totals = jnp.sum(parts, axis=0, keepdims=True)
    depth = -(-reach * 2 * wide // lanes) * lanes
    spread = pltpu.VMEM((depth, columns), bf16)
    pressure, moments, part = pl.pallas_call(
        pressure_kernel,
        out_shape=(struct((count, rows, columns)), struct((2, rows, columns)), struct((size, lanes))),
        in_specs=[smem] + [vmem] * 4,
        out_specs=(vmem, vmem, vmem),
        scratch_shapes=[spread],
        compiler_params=params,
        cost_estimate=cost(12),
        name="pressure",
    )(offsets, totals, clean, other, inverse)
    if blocks == 2:
        row, part = lax.optimization_barrier((totals, part))
        row = paired(row, "frames", 0)
        place = (row[:, lanes - 2 :] / size).astype(jnp.int32)
        time_mean, time_rms = pl.pallas_call(
            time_kernel,
            out_shape=(struct((rows, columns)), struct((rows, columns))),
            in_specs=[smem] + [vmem] * 5,
            out_specs=(vmem, vmem),
            scratch_shapes=[spread],
            compiler_params=params,
            cost_estimate=cost(12),
            name="time",
        )(place, row, clean, other, other_inverse, moments)
    else:
        whole = total_over(moments, "frames")
        total_frames = count * blocks
        time_mean = whole[0] / total_frames
        time_rms = jnp.sqrt(jnp.maximum(whole[1] / total_frames - time_mean * time_mean, 0.0))
    sums = lax.all_to_all(part, "rows", 0, 0, axis_index_groups=begun_at(size // 2, size), tiled=True)
    sums, time_mean, time_rms = lax.optimization_barrier((sums, time_mean, time_rms))
    spatial = jnp.sum(sums, axis=0)
    cell_count = rows * columns * size
    frame_mean = spatial[:count] / cell_count
    frame_rms = jnp.sqrt(spatial[count : 2 * count] / cell_count - frame_mean * frame_mean)
    return (pressure, frame_mean, frame_rms, time_mean, time_rms)


def solution(mesh):
    placed = (P("frames", "rows", None), P("frames", "rows", None), P("rows"), P("frames", None))
    return jax.shard_map(
        shards,
        mesh=mesh,
        in_specs=placed,
        out_specs=(
            P("frames", "rows", None),
            P("frames"),
            P("frames"),
            P("rows", None),
            P("rows", None),
        ),
        check_vma=False,
    )
```

```python
import functools

import jax
import jax.numpy as jnp
from jax import lax
from jax.experimental import pallas as pl
from jax.experimental.pallas import tpu as pltpu
from jax.sharding import PartitionSpec as P

taps = (1.0 / 256, 8.0 / 256, 28.0 / 256, 56.0 / 256, 70.0 / 256)
calib_zero = -0.25
calib_linear = 1.0
calib_square = 0.15
lanes = 128
reach = 7
near = 4
far = 2
slot = 32
params = pltpu.CompilerParams(vmem_limit_bytes=14 * 1024 * 1024)
vmem = pl.BlockSpec(memory_space=pltpu.VMEM)
smem = pl.BlockSpec(memory_space=pltpu.SMEM)


def cost(mebibytes):
    return pl.CostEstimate(flops=0, bytes_accessed=mebibytes * 2**20, transcendentals=0)


def tile_of(index):
    if isinstance(index, int):
        return slice(index * lanes, (index + 1) * lanes)
    return pl.ds(pl.multiple_of(index * lanes, lanes), lanes)


def by_tiles(step, tiles, group, init=()):
    if group == tiles:
        for index in range(tiles):
            init = step(index, init)
        return init

    def body(index, carry):
        for inner in range(group):
            carry = step(index * group + inner, carry)
        return carry

    return lax.fori_loop(0, tiles // group, body, init)


def lane_of(shape):
    return lax.broadcasted_iota(jnp.int32, shape, len(shape) - 1)


def fold(product):
    return jnp.sum(product.reshape(product.shape[0] // 8, 8, lanes), axis=0)


def vertical(load):
    total = taps[4] * load(4)
    for step in range(4):
        total = total + taps[step] * (load(step) + load(8 - step))
    return total


def moved(before, here, after, step):
    if step > 0:
        return pltpu.roll(jnp.where(lane_of(here.shape) < step, after, here), lanes - step, 1)
    if step < 0:
        return pltpu.roll(jnp.where(lane_of(here.shape) >= lanes + step, before, here), -step, 1)
    return here


def halves(value):
    high = value.astype(jnp.bfloat16)
    low = (value - high.astype(jnp.float32)).astype(jnp.bfloat16)
    return high, low


def cut(value):
    return jnp.concatenate(halves(value), axis=0)


def fill_band(band):
    shape = (lanes, lanes)
    apart = lax.broadcasted_iota(jnp.int32, shape, 0) - lax.broadcasted_iota(jnp.int32, shape, 1)

    def block(offset):
        distance = jnp.abs(apart + offset)
        value = jnp.zeros(shape, jnp.float32)
        for step in range(5):
            value = jnp.where(distance == step, taps[4 - step], value)
        return value.astype(jnp.bfloat16)

    none = jnp.zeros(shape, jnp.bfloat16)
    before, here, after = block(-lanes), block(0), block(lanes)
    for index, pair in enumerate(((before, none), (here, before), (after, here), (none, after))):
        band[index * lanes : (index + 1) * lanes, :] = jnp.concatenate(pair, axis=1)


def chunk_of(t):
    if isinstance(t, int):
        return slice(t * 2 * lanes, (t + 1) * 2 * lanes)
    return pl.ds(pl.multiple_of(t * 2 * lanes, 2 * lanes), 2 * lanes)


def place_tile(windows, index, value):
    for c in (index // 2 - 1, index // 2):
        at = index - 2 * c
        if 0 <= c < windows.shape[0] and at < 4:
            windows[c, :, at * lanes : (at + 1) * lanes] = value


def horizontal(windows, band):
    chunks, height, width = windows.shape
    product = jnp.dot(
        windows[...].reshape(chunks * height, width), band[...], preferred_element_type=jnp.float32
    )
    product = product.reshape(chunks, height, 2 * lanes)
    return product[:, : height // 2] + product[:, height // 2 :]


def by_row_shift(value, rows, direction):
    place = lax.broadcasted_iota(jnp.int32, value.shape, 0) % rows
    unit = 1
    while unit < rows:
        digit = (place // unit) % 4
        result = value
        for times in range(1, 4):
            amount = times * unit
            turned = pltpu.roll(value, amount if direction > 0 else value.shape[1] - amount, 1)
            result = jnp.where(digit == times, turned, result)
        value = result
        unit *= 4
    return value


def at_edge():
    index = lax.axis_index("rows")
    return (index == 0) | (index == lax.axis_size("rows") - 1)


def smooth_kernel(frames, from_odd, from_even, inverse, stack, power, band, rows_in, wide, pieces):
    count, rows, columns = frames.shape
    tiles = columns // lanes
    ring = tiles + 2
    odd = lax.axis_index("rows") % 2 == 1
    edge = at_edge()
    blank = jnp.zeros((2 * count * rows, lanes), jnp.bfloat16)
    place_tile(wide, 0, blank)
    place_tile(wide, tiles + 1, blank)
    fill_band(band)
    pieces[0] = blank
    pieces[tiles + 1] = blank
    pieces[tiles + 2] = blank

    def load_step(t, carry):
        for f in range(count):
            outer = jnp.where(edge, 0.0, from_odd[f, :, tile_of(t)])
            inner = from_even[f, :, tile_of(t)]
            rows_in[f, t, 4:8, :] = jnp.where(odd, inner, outer)
            rows_in[f, t, 8 : 8 + rows, :] = frames[f, :, tile_of(t)]
            rows_in[f, t, 8 + rows : 12 + rows, :] = jnp.where(odd, outer, inner)
        return carry

    def vertical_step(t, carry):
        parts = [vertical(lambda s: rows_in[f, t, pl.ds(4 + s, rows), :]) for f in range(count)]
        place_tile(wide, t + 1, cut(jnp.concatenate(parts, axis=0)))
        return carry

    def horizontal_step(t, totals):
        smooth = smoothed[t]
        result = []
        details = []
        for f in range(count):
            part = smooth[f * rows : (f + 1) * rows]
            inverse[f, :, chunk_of(t)] = 1.0 / part
            details.append(frames[f, :, chunk_of(t)] - part)
            square = details[f] * details[f]
            result.append(totals[f] + fold(square[:, :lanes]) + fold(square[:, lanes:]))
        detail = cut(jnp.concatenate(details, axis=0))
        pieces[2 * t + 1] = detail[:, :lanes]
        pieces[2 * t + 2] = detail[:, lanes:]
        return tuple(result)

    def stack_step(t, carry):
        before, here, after = pieces[t], pieces[t + 1], pieces[t + 2]
        size = count * rows
        for a in range(near):
            turned = moved(before, here, after, 1 - a)
            stack[a * size : (a + 1) * size, tile_of(t)] = turned[:size]
            stack[(near + a) * size : (near + a + 1) * size, tile_of(t)] = turned[size:]
        return carry

    powers = (jnp.zeros((8, lanes), jnp.float32),) * count
    for t in range(tiles):
        load_step(t, 0)
        vertical_step(t, 0)
    smoothed = horizontal(wide, band)
    for t in range(tiles // 2):
        powers = horizontal_step(t, powers)
    for f in range(count):
        power[f * 8 : f * 8 + 8, :] = powers[f]
    pieces[tiles + 3] = pieces[1]
    by_tiles(stack_step, ring, ring)


def column_shift(offset):
    negative = offset < 0
    first = jnp.where(negative, 0, 1)
    amount = jnp.where(negative, offset + lanes, offset)
    back = (lanes - amount) & (lanes - 1)

    def shift(source, t):
        here = source[t + first]
        after = source[t + first + 1]
        return pltpu.roll(jnp.where(lane_of(here.shape) < amount, after, here), back, 1)

    return shift


def reference_rows(raw, smooth, clean, fine, tiles):
    height = clean.shape[1] // 2
    empty = jnp.zeros((2 * height, lanes), jnp.bfloat16)
    for array in (clean, fine):
        array[0] = empty
        array[tiles + 1] = empty
    fine[tiles + 2] = empty
    squares = []
    for t in range(tiles // 2):
        detail = jnp.concatenate([raw(2 * t), raw(2 * t + 1)], axis=1) - smooth(t)
        for array, value in ((clean, cut(smooth(t))), (fine, cut(detail))):
            array[2 * t + 1] = value[:, :lanes]
            array[2 * t + 2] = value[:, lanes:]
        squares.append(detail * detail)
    fine[tiles + 3] = fine[1]
    return squares


def lag_products(stack, fine, stream, folded, base_col, start):
    height = fine.shape[1]
    half = height // 2
    shifts = [column_shift(base_col + near * b - 2) for b in range(far)]
    for t in range(fine.shape[0] - 2):
        for b, shift in enumerate(shifts):
            stream[b * height : (b + 1) * height, tile_of(t)] = shift(fine, t)
    product = lax.dot_general(
        stack[...], stream[...], (((1,), (1,)), ((), ())), preferred_element_type=jnp.float32
    )
    size = product.shape[0] // 2
    folded[...] = jnp.zeros(folded.shape, jnp.float32)
    folded[:, 0 : far * height] = product[:size] + product[size:]
    product = folded[...]
    lane = lane_of(product.shape)
    placed = jnp.zeros_like(product)
    for s in range(2 * far):
        at = s * slot + start
        turned = pltpu.roll(product, at - s * half, 1)
        placed = jnp.where((lane >= at) & (lane < at + half), turned, placed)
    return placed


def near_kernel(
    base, own_odd, own_even, from_even, stack, band, clean, lags, power, rows_in, windows, fine, stream, folded
):
    tiles = own_odd.shape[1] // lanes
    odd = lax.axis_index("rows") % 2 == 1
    height = clean.shape[1] // 2
    empty = jnp.zeros((2 * height, lanes), jnp.bfloat16)
    place_tile(windows, 0, empty)
    place_tile(windows, tiles + 1, empty)
    for t in range(tiles):
        at = tile_of(t)
        outer = own_odd[:, at]
        inner = from_even[:, at]
        rows_in[t, 0:8, :] = jnp.where(odd, inner, outer)
        rows_in[t, 8:16, :] = own_even[:, at]
        rows_in[t, 16:24, :] = jnp.where(odd, outer, inner)
        place_tile(windows, t + 1, cut(vertical(lambda s: rows_in[t, pl.ds(s, height), :])))
    smooth = horizontal(windows, band)
    squares = reference_rows(lambda t: rows_in[t, pl.ds(4, height), :], lambda t: smooth[t], clean, fine, tiles)
    place = lax.broadcasted_iota(jnp.int32, squares[0].shape, 0)
    first = jnp.where(odd, 4, 0)
    own = (place >= first) & (place < first + height - 4)
    total = jnp.zeros((8, lanes), jnp.float32)
    for square in squares:
        square = jnp.where(own, square, 0.0)
        total = total + fold(square[:, :lanes]) + fold(square[:, lanes:])
    power[...] = total
    lags[...] = lag_products(stack, fine, stream, folded, base[0, 1], jnp.where(odd, 0, 8))


def match_kernel(
    base, own_odd, from_odd, near_lags, near_power, stack, power, band, clean, part, rows_in, windows, fine, stream, folded, lags
):
    tiles = own_odd.shape[1] // lanes
    count = power.shape[0] // 8
    rows = folded.shape[0] // (near * count)
    odd = lax.axis_index("rows") % 2 == 1
    edge = at_edge()
    height = clean.shape[1] // 2
    empty = jnp.zeros((2 * height, lanes), jnp.bfloat16)
    place_tile(windows, 0, empty)
    place_tile(windows, tiles + 1, empty)
    for t in range(tiles):
        at = tile_of(t)
        outer = jnp.where(edge, 0.0, from_odd[:, at])
        inner = own_odd[:, at]
        rows_in[t, 0:8, :] = jnp.where(odd, inner, outer)
        rows_in[t, 8:16, :] = jnp.where(odd, outer, inner)
        place_tile(windows, t + 1, cut(vertical(lambda s: rows_in[t, pl.ds(s, height), :])))
    smooth = horizontal(windows, band)
    place = lax.broadcasted_iota(jnp.int32, (height, 2 * lanes), 0)
    first = jnp.where(odd, 0, 4)
    own = (place >= first) & (place < first + 4)
    inside = (place >= jnp.where(edge, first, 0)) & (place < jnp.where(edge, first + 4, height))

    def masked(t):
        return jnp.where(inside, smooth[t], 0.0)

    squares = reference_rows(lambda t: rows_in[t, pl.ds(4, height), :], masked, clean, fine, tiles)
    ref_power = near_power[...]
    for square in squares:
        square = jnp.where(own, square, 0.0)
        ref_power = ref_power + fold(square[:, :lanes]) + fold(square[:, lanes:])
    product = lag_products(stack, fine, stream, folded, base[0, 1], jnp.where(odd, 16, 0))
    product = by_row_shift(product + near_lags[...], rows, -1)
    lags[...] = jnp.zeros(lags.shape, jnp.float32)
    for a in range(near):
        for f in range(count):
            start = (a * count + f) * rows
            lags[f * 8 + a : f * 8 + a + 1, :] = jnp.sum(product[start : start + rows], axis=0, keepdims=True)
    back = 4 * lanes - 1 - base[0, 0]
    across = lax.broadcasted_iota(jnp.int32, (8, lanes), 0)
    lane = lane_of((8, lanes))
    packed = jnp.zeros((8, lanes), jnp.float32)
    for f in range(count):
        block = lags[f * 8 : f * 8 + 8, :]
        for j in range(reach):
            at = (f * reach + j) * reach
            there = back + at - (j // near) * 2 * slot
            high = pltpu.roll(block, there & (lanes - 1), 1)
            low = pltpu.roll(block, (there - slot) & (lanes - 1), 1)
            member = (across == j % near) & (lane >= at) & (lane < at + reach)
            packed = packed + jnp.where(member, high + low, 0.0)
    lags[0:8, :] = jnp.zeros((8, lanes), jnp.float32)
    for f in range(count):
        lags[f : f + 1, :] = jnp.sum(power[f * 8 : f * 8 + 8, :], axis=0, keepdims=True)
    lags[count : count + 1, :] = jnp.sum(ref_power, axis=0, keepdims=True)
    powers = jnp.sum(lags[0:8, :], axis=1, keepdims=True)
    packed = packed + jnp.where(lane == count * reach * reach + across, powers, 0.0)
    packed = jnp.sum(packed, axis=0, keepdims=True)
    for place in range(2):
        offset = base[0, place].astype(jnp.float32)
        packed = jnp.where(lane[0:1] == lanes - 2 + place, offset, packed)
    part[...] = jnp.broadcast_to(packed, part.shape)


def spreader(clean, other, spread, base_col):
    height = clean.shape[1]
    size = height + other.shape[1]
    spare = spread.shape[0] - reach * size
    shifts = [column_shift(base_col + j - 3) for j in range(reach)]

    def spread_tile(t):
        at = tile_of(t)
        for j, shift in enumerate(shifts):
            spread[j * size : j * size + height, at] = shift(clean, t)
            spread[j * size + height : (j + 1) * size, at] = shift(other, t)
        spread[reach * size :, at] = jnp.zeros((spare, lanes), jnp.bfloat16)

    return spread_tile


def blend_terms(totals, count):
    lane = lane_of(totals.shape)
    block = reach * reach
    squared = totals * totals

    def pick(array, low, size):
        return jnp.sum(jnp.where((lane >= low) & (lane < low + size), array, 0.0), axis=1, keepdims=True)

    ref_power = pick(totals, count * block + count, 1)
    terms = []
    for f in range(count):
        norm_product = 0.05 * ((pick(totals, count * block + f, 1) + 1e-06) * (ref_power + 1e-06))
        terms.append((norm_product, 1.0 / (norm_product + pick(squared, f * block, block))))
    return squared, terms


def banded(weights, terms, f, rows, first_row, depth):
    wide = rows + 8
    blank = jnp.zeros((weights.shape[0], depth - lanes), jnp.float32)
    weights = jnp.concatenate([weights, blank], axis=1)
    lane = lane_of(weights.shape)
    line = jnp.zeros_like(weights)
    for j in range(reach):
        at = first_row + j * 2 * wide
        amount = at - (f * reach + j) * reach
        amount = jnp.where(amount < 0, amount + depth, amount)
        line = jnp.where((lane >= at) & (lane < at + reach), pltpu.roll(weights, amount, 1), line)
    band = by_row_shift(jnp.broadcast_to(line[0:1], (rows, depth)), rows, 1)
    middle = first_row + reach // 2 * (2 * wide + 1) + lax.broadcasted_iota(jnp.int32, band.shape, 0)
    band = (band + jnp.where(lane_of(band.shape) == middle, terms[0][0:1], 0.0)) * terms[1][0:1]
    odd = lax.axis_index("rows") % 2 == 1
    row = lane_of(band.shape) % (2 * wide)
    start = jnp.where(odd, 0, 8)
    inner = (row >= start) & (row < start + rows)
    first = pltpu.roll(jnp.where(inner, band, 0.0), jnp.where(odd, 0, depth - 8), 1)
    second = pltpu.roll(jnp.where(inner, 0.0, band), jnp.where(odd, 2 * rows - 16, 2 * rows), 1)
    return first + pltpu.roll(first, rows, 1) + second + pltpu.roll(second, 8, 1)


def pressures(base, totals, clean, other, spread, inverse):
    count, rows, columns = inverse.shape
    depth = spread.shape[0]
    squared, terms = blend_terms(jnp.broadcast_to(totals[0:1, :], (8, lanes)), count)
    bands = [banded(squared, terms[f], f, rows, 1 + base[0, 0], depth) for f in range(count)]
    mixing = cut(jnp.concatenate(bands, axis=0))
    spread_tile = spreader(clean, other, spread, base[0, 1])

    def chunk_values(t):
        where = chunk_of(t)
        spread_tile(2 * t)
        spread_tile(2 * t + 1)
        product = jnp.dot(mixing, spread[:, where], preferred_element_type=jnp.float32)
        registered = product[: count * rows] + product[count * rows :]
        values = []
        for f in range(count):
            ratio = registered[f * rows : (f + 1) * rows] * inverse[f, :, where]
            values.append(calib_zero + ratio * (calib_linear + calib_square * ratio))
        return values

    return chunk_values


def pressure_kernel(base, totals, clean, other, inverse, pressure, moments, part, spread):
    count, rows, columns = inverse.shape
    chunk_values = pressures(base, totals, clean, other, spread, inverse)

    def step(t, sums):
        where = chunk_of(t)
        values = chunk_values(t)
        squares = [value * value for value in values]
        for f in range(count):
            pressure[f, :, where] = values[f]
        moments[0, :, where] = sum(values[1:], values[0])
        moments[1, :, where] = sum(squares[1:], squares[0])
        result = []
        for total, array in zip(sums, values + squares):
            result.append(total + fold(array[:, :lanes]) + fold(array[:, lanes:]))
        return tuple(result)

    zero = jnp.zeros((8, lanes), jnp.float32)
    sums = by_tiles(step, columns // (2 * lanes), columns // (2 * lanes), (zero,) * (2 * count))
    line = zero
    for k in range(2 * count):
        value = jnp.sum(jnp.sum(sums[k], axis=0, keepdims=True), axis=1, keepdims=True)
        line = line + jnp.where(lane_of(line.shape) == k, value, 0.0)
    part[...] = jnp.broadcast_to(line[0:1], part.shape)


def time_kernel(base, totals, clean, other, inverse, moments, time_mean, time_rms, spread):
    count, rows, columns = inverse.shape
    chunk_values = pressures(base, totals, clean, other, spread, inverse)
    frames = 2 * count

    def step(t, carry):
        where = chunk_of(t)
        first = moments[0, :, where]
        second = moments[1, :, where]
        for value in chunk_values(t):
            first = first + value
            second = second + value * value
        mean = first * (1.0 / frames)
        time_mean[:, where] = mean
        time_rms[:, where] = jnp.sqrt(jnp.maximum(second * (1.0 / frames) - mean * mean, 0.0))
        return carry

    by_tiles(step, columns // (2 * lanes), columns // (2 * lanes))


def paired(value, axis, first):
    size = lax.axis_size(axis)
    partner = list(range(size))
    for i in range(first, size - 1, 2):
        partner[i], partner[i + 1] = i + 1, i
    return lax.ppermute(value, axis, list(enumerate(partner)))


def by_parity(odd, array, height, dim):
    length = array.shape[dim]
    low = lax.slice_in_dim(array, 0, height, axis=dim)
    high = lax.slice_in_dim(array, length - height, length, axis=dim)
    return jnp.where(odd, high, low), jnp.where(odd, low, high)


def from_owner(shard, here, odd, axis, root):
    mine = lax.axis_index(axis) == root
    height = shard.shape[0] // 2
    if lax.axis_size(axis) != 2:
        whole = lax.psum(jnp.where(mine, shard, jnp.zeros_like(shard)), axis)
        return by_parity(odd, whole, height, 0)
    there = by_parity(odd, paired(shard, axis, 0), height, 0)
    here = by_parity(odd, here, height, 0)
    return [jnp.where(mine, own, other) for own, other in zip(here, there)]


def begun_at(first, size):
    return [[(i + first) % size for i in range(size)]]


def total_over(value, axis):
    size = lax.axis_size(axis)
    if size & (size - 1):
        return lax.psum(value, axis)
    step = 1
    while step < size:
        value = value + lax.ppermute(value, axis, [(i, i ^ step) for i in range(size)])
        step *= 2
    return value


def shards(frames_raw, wind_off, run_owner, search_base):
    count, rows, columns = frames_raw.shape
    tiles = columns // lanes
    ring = tiles + 2
    wide = rows + 8
    depth = near * count * rows
    size = lax.axis_size("rows")
    f32 = jnp.float32
    bf16 = jnp.bfloat16
    struct = functools.partial(jax.ShapeDtypeStruct, dtype=f32)
    odd = lax.axis_index("rows") % 2 == 1
    raw, run = lax.optimization_barrier((jnp.maximum(frames_raw, 0.0), jnp.maximum(wind_off[0], 0.0)))
    owner, offsets = lax.optimization_barrier((run_owner, jnp.clip(search_base, -8, 8)))
    own_odd, own_even = from_owner(wind_off[0], run, odd, "frames", owner[0])
    from_odd = paired(own_odd, "rows", 1)
    from_even = paired(own_even, "rows", 0)
    frames_odd, frames_even = by_parity(odd, raw, 4, 1)
    frames_odd = paired(frames_odd, "rows", 1)
    frames_even = paired(frames_even, "rows", 0)
    frames_odd, own_odd = lax.optimization_barrier((frames_odd, own_odd))
    inverse, stack, power, band = pl.pallas_call(
        smooth_kernel,
        out_shape=(
            struct((count, rows, columns)),
            jax.ShapeDtypeStruct((2 * depth, ring * lanes), bf16),
            struct((8 * count, lanes)),
            jax.ShapeDtypeStruct((4 * lanes, 2 * lanes), bf16),
        ),
        in_specs=[vmem] * 3,
        out_specs=(vmem,) * 4,
        scratch_shapes=[
            pltpu.VMEM((count, tiles, rows + 16, lanes), f32),
            pltpu.VMEM((tiles // 2, 2 * count * rows, 4 * lanes), bf16),
            pltpu.VMEM((ring + 2, 2 * count * rows, lanes), bf16),
        ],
        compiler_params=params,
        cost_estimate=cost(8),
        name="smooth",
    )(raw, frames_odd, frames_even)
    blocks = lax.axis_size("frames")
    def reference_scratch(height):
        return [
            pltpu.VMEM((tiles, height + 8, lanes), f32),
            pltpu.VMEM((tiles // 2, 2 * height, 4 * lanes), bf16),
            pltpu.VMEM((ring + 2, 2 * height, lanes), bf16),
            pltpu.VMEM((far * 2 * height, ring * lanes), bf16),
            pltpu.VMEM((depth, lanes), f32),
        ]

    clean, near_lags, near_power = pl.pallas_call(
        near_kernel,
        out_shape=(
            jax.ShapeDtypeStruct((tiles + 2, 2 * rows, lanes), bf16),
            struct((depth, lanes)),
            struct((8, lanes)),
        ),
        in_specs=[smem] + [vmem] * 5,
        out_specs=(vmem,) * 3,
        scratch_shapes=reference_scratch(rows),
        compiler_params=params,
        cost_estimate=cost(8),
        name="near",
    )(offsets, own_odd, own_even, from_even, stack, band)
    other, part = pl.pallas_call(
        match_kernel,
        out_shape=(jax.ShapeDtypeStruct((tiles + 2, 16, lanes), bf16), struct((size, lanes))),
        in_specs=[smem] + [vmem] * 7,
        out_specs=(vmem,) * 2,
        scratch_shapes=reference_scratch(8) + [pltpu.VMEM((8 * count, lanes), f32)],
        compiler_params=params,
        cost_estimate=cost(8),
        name="match",
    )(offsets, own_odd, from_odd, near_lags, near_power, stack, power, band)
    if blocks == 2:
        inverse_out, part = lax.optimization_barrier((inverse, part))
        other_inverse = paired(inverse_out, "frames", 0)
    parts = lax.all_to_all(part, "rows", 0, 0, axis_index_groups=begun_at(size // 2, size), tiled=True)
    totals = jnp.sum(parts, axis=0, keepdims=True)
    depth = -(-reach * 2 * wide // lanes) * lanes
    spread = pltpu.VMEM((depth, columns), bf16)
    pressure, moments, part = pl.pallas_call(
        pressure_kernel,
        out_shape=(struct((count, rows, columns)), struct((2, rows, columns)), struct((size, lanes))),
        in_specs=[smem] + [vmem] * 4,
        out_specs=(vmem, vmem, vmem),
        scratch_shapes=[spread],
        compiler_params=params,
        cost_estimate=cost(12),
        name="pressure",
    )(offsets, totals, clean, other, inverse)
    if blocks == 2:
        row, part = lax.optimization_barrier((totals, part))
        row = paired(row, "frames", 0)
        place = (row[:, lanes - 2 :] / size).astype(jnp.int32)
        time_mean, time_rms = pl.pallas_call(
            time_kernel,
            out_shape=(struct((rows, columns)), struct((rows, columns))),
            in_specs=[smem] + [vmem] * 5,
            out_specs=(vmem, vmem),
            scratch_shapes=[spread],
            compiler_params=params,
            cost_estimate=cost(12),
            name="time",
        )(place, row, clean, other, other_inverse, moments)
    else:
        whole = total_over(moments, "frames")
        total_frames = count * blocks
        time_mean = whole[0] / total_frames
        time_rms = jnp.sqrt(jnp.maximum(whole[1] / total_frames - time_mean * time_mean, 0.0))
    sums = lax.all_to_all(part, "rows", 0, 0, axis_index_groups=begun_at(size // 2 + 2, size), tiled=True)
    sums, time_mean, time_rms = lax.optimization_barrier((sums, time_mean, time_rms))
    spatial = jnp.sum(sums, axis=0)
    cell_count = rows * columns * size
    frame_mean = spatial[:count] / cell_count
    frame_rms = jnp.sqrt(spatial[count : 2 * count] / cell_count - frame_mean * frame_mean)
    return (pressure, frame_mean, frame_rms, time_mean, time_rms)


def solution(mesh):
    placed = (P("frames", "rows", None), P("frames", "rows", None), P("rows"), P("frames", None))
    return jax.shard_map(
        shards,
        mesh=mesh,
        in_specs=placed,
        out_specs=(
            P("frames", "rows", None),
            P("frames"),
            P("frames"),
            P("rows", None),
            P("rows", None),
        ),
        check_vma=False,
    )
```
